32 devices in a mesh: gx: 16 (over z, y, x), gy: 2 (over core).
Axes of the slice: x: 2, y: 2, z: 4, core: 2. Of those that a mesh axis runs over, the one named last changes fastest.
Arguments:
- tokens_in: bfloat16 [4096, 2048], P('gx'), may hold values from -6 to 6
- doc_ids: int32 [16, 256], P('gx'), may hold values from 0 to 3, never falling along the last dimension, each value on 1 to 128 neighbouring positions
- routes: int32 [4096, 8], P('gx'), may hold values from 0 to 15, all different within a row; in each aligned block of 256 rows (0 to 255, 256 to 511, ...) at most 160 rows name the same one
- q_weight: bfloat16 [2048, 4096], P('gx', 'gy'), may hold values from -0.125 to 0.125
- key_matrix: bfloat16 [2048, 512], P('gx', 'gy'), may hold values from -0.125 to 0.125
- value_matrix: bfloat16 [2048, 512], P('gx', 'gy'), may hold values from -0.125 to 0.125
- out_weight: bfloat16 [2048, 4096], P('gx', 'gy'), may hold values from -0.75 to 0.75
- router_weight: bfloat16 [2048, 16], P('gx'), may hold values from -0.0625 to 0.0625
- attn_gain: float32 [2048], replicated, may hold values from 0.1 to 1.9
- ffn_gain: float32 [2048], replicated, may hold values from 0.1 to 1.9
- query_norm_gain: float32 [128], replicated, may hold values from 0.5 to 2
- k_gain: float32 [128], replicated, may hold values from 0.5 to 2
- gate_weight: bfloat16 [16, 2048, 768], P('gx', None, 'gy'), may hold values from -0.125 to 0.125
- up_weight: bfloat16 [16, 2048, 768], P('gx', None, 'gy'), may hold values from -0.125 to 0.125
- down_weight: bfloat16 [16, 768, 2048], P('gx', 'gy'), may hold values from -0.625 to 0.625
- cotangent: bfloat16 [4096, 2048], P('gx'), may hold values from -6 to 6
Outputs:
- output: bfloat16 [4096, 2048], P('gx')
- grad_input: bfloat16 [4096, 2048], P('gx')
- grad_q: float32 [2048, 4096], P('gx', 'gy')
- grad_k: float32 [2048, 512], P('gx', 'gy')
- grad_v: float32 [2048, 512], P('gx', 'gy')
- grad_out: float32 [2048, 4096], P('gx', 'gy')
- grad_router: float32 [2048, 16], P('gx')
- grad_attn_gain: float32 [2048], replicated
- grad_ffn_gain: float32 [2048], replicated
- grad_q_gain: float32 [128], replicated
- grad_k_gain: float32 [128], replicated
- grad_gate: float32 [16, 2048, 768], P('gx', None, 'gy')
- grad_up: float32 [16, 2048, 768], P('gx', None, 'gy')
- grad_down: float32 [16, 768, 2048], P('gx', 'gy')
The draws below stay inside these ranges and needn't reach their ends.
Inputs may be any that keep to these rules, and one draw needn't show every extreme that they name: `routes`: each row names 8 different experts. Among the 256 rows of one index of gx no expert is named by more than 160 rows, and in every draw some expert is named by exactly 160 rows of some index. `doc_ids`: along a sequence the document numbers never fall; each document takes 1 to half of 256 positions, and one takes exactly half.
All inputs are finite; a program needn't handle non-finite values.
Results may differ from the reference program's by a relative error of at most 0.018.
Values may be sent and summed in bfloat16 or wider, within the bound.
A program may use at most 256 MiB of HBM per device.

```python
import math
import jax
import jax.numpy as jnp
import numpy as np
from jax import lax

MODEL_DIM = 2048
QUERY_HEADS = 32
KEY_VALUE_HEADS = 4
HEAD_DIM = 128
FF = 768
TOP = 8
DOCS = 4
TOK_DEV = 256
EXPERTS = 16
SEQS = 16
TOKENS = 4096
CAP = 160
N_GX = 16
N_GY = 2


def gain_values(key):
    return jax.random.uniform(key, (HEAD_DIM,), jnp.float32, 0.5, 2.0)


def draw_query_norm_gain(key, part):
    return gain_values(jax.random.fold_in(key, 17))


def draw_k_gain(key, part):
    return gain_values(jax.random.fold_in(key, 29))


def strengthened(array, key, source, target, blocks, factor):
    def block_of(position):
        return (jnp.arange(array.shape[position]) // (array.shape[position] // blocks)).reshape((-1,) + (1,) * (array.ndim - 1 - position))

    near = jax.random.permutation(key, blocks)[block_of(target)]
    other_side = (block_of(target) + blocks // 2) % blocks
    return jnp.where((block_of(source) == near) | (block_of(source) == other_side), factor * array, array)


def level_of(key, shape, shards, smallest, largest):
    gain, own = 1.0, jax.random.fold_in(key, 6)
    for axis_at, blocks in shards:
        heights = jnp.exp(jax.random.uniform(jax.random.fold_in(own, axis_at), (blocks,), jnp.float32, smallest / len(shards), largest / len(shards)))
        gain = gain * jnp.repeat(heights, shape[axis_at] // blocks).reshape([-1 if axis == axis_at else 1 for axis in range(len(shape))])
    return gain


def profile(count, total, reach, lean):
    portions = [(1 << 20) // math.isqrt(rank ** lean) + 1 for rank in range(2, count + 1)]
    spare, holding = total - reach - (count - 1), [1] * (count - 1)
    while spare > 0:
        free = [i for i in range(count - 1) if holding[i] < reach]
        pool, left = sum([portions[i] for i in free]), spare
        for i in free:
            addition = min(reach - holding[i], max(1, left * portions[i] // pool), spare)
            holding[i] = holding[i] + addition
            spare = spare - addition
    return np.array([reach] + holding)


def ragged_sizes(rng, amount, total, bound, skew):
    if amount == 2:
        one = jax.random.randint(rng, (), max(1, total - bound), min(bound, total - 1) + 1)
        return jnp.stack([one, total - one])
    sizes = jnp.asarray(profile(amount, total, bound, skew), jnp.int32)
    twos = (amount - 1) // 2
    giver, taker = sizes[1:1 + 2 * twos:2], sizes[2:2 + 2 * twos:2]
    margin = jnp.minimum(giver - 1, bound - taker)
    moved = jax.random.randint(jax.random.fold_in(rng, 1), (twos,), 0, 1 << 20) % (margin + 1)
    sizes = sizes.at[1:1 + 2 * twos:2].set(giver - moved).at[2:2 + 2 * twos:2].set(taker + moved)
    return sizes[jax.random.permutation(jax.random.fold_in(rng, 2), amount)]


def assign_block(rng, own, number, rows, amount, top, most, lean):
    ranking = jax.random.permutation(rng, amount)
    heavy_load, usual = load_shares(amount, rows * top, most, lean, True), load_shares(amount, rows * top, most, lean, False)
    places = jnp.arange(amount)

    def named(sizes, rotation):
        used = int((sizes > 0).sum())
        fixed = max(1, used // 4)
        moved = fixed + (places - fixed + rotation * (used - fixed)) % max(1, amount - fixed)
        return jnp.zeros((amount,), jnp.int32).at[ranking[jnp.where(places < fixed, places, moved)]].set(jnp.asarray(sizes, jnp.int32))

    sizes = jnp.where(number % 4 == 0, named(heavy_load, number // 4), named(usual, number - number // 4 - 1))
    mixed = jax.random.permutation(jax.random.fold_in(own, 3), amount)
    source_of, taker = mixed[0:amount // 2 * 2:2], mixed[1:amount // 2 * 2:2]
    margin = jnp.minimum(sizes[source_of] - 1, most - sizes[taker]) // 2
    margin = jnp.where((source_of == ranking[0]) | (taker == ranking[0]) | (sizes[taker] == 0), 0, jnp.maximum(margin, 0))
    moved = jax.random.randint(jax.random.fold_in(own, 4), (amount // 2,), 0, 1 << 20) % (margin + 1)
    sizes = sizes.at[source_of].add(-moved).at[taker].add(moved)
    members = jnp.searchsorted(jnp.cumsum(sizes), jnp.arange(rows * top), side="right").astype(jnp.int32)
    grid = members.reshape(top, rows).T
    grid = grid[jax.random.permutation(jax.random.fold_in(own, 1), rows)]
    rotation = jax.random.randint(jax.random.fold_in(own, 2), (rows, 1), 0, top)
    return jnp.take_along_axis(grid, (jnp.arange(top)[None, :] + rotation) % top, axis=1)


def load_shares(count, total, bound, slope, full):
    weights = [(1 << 20) // math.isqrt(grade ** slope) + 1 for grade in range(1, count + 1)]
    largest = bound if full else min(bound, max(-(-total // count), total * weights[0] // sum(weights)))
    least = 1 if total - largest >= count - 1 else 0
    given, surplus = [largest] + [least] * (count - 1), total - largest - least * (count - 1)
    while surplus > 0:
        candidates = [i for i in range(1, count) if given[i] < largest] or [i for i in range(1, count) if given[i] < bound]
        pool, remaining = sum([weights[i] for i in candidates]), surplus
        for i in candidates:
            addition = min(bound - given[i], max(1, remaining * weights[i] // pool), surplus)
            given[i] = given[i] + addition
            surplus = surplus - addition
    return np.array(given)


def scatter_about(own_key, shape, spread, most, split=(), held_as=jnp.bfloat16):
    level = level_of(own_key, shape, split, -0.22, 0.18) if split else 1.0
    values = jax.random.normal(own_key, shape, jnp.float32) * spread * level
    return jnp.minimum(jnp.maximum(values, -most), most).astype(held_as)


def noise_with(rng, extent, width, limit, pieces, heavy, kind=jnp.bfloat16):
    drawn = width * jax.random.normal(rng, extent, jnp.float32)
    if pieces:
        drawn = drawn * level_of(rng, extent, pieces, -0.22, 0.18)
    return jnp.clip(strengthened(drawn, jax.random.fold_in(rng, 3), *heavy), -limit, limit).astype(kind)


def setup_inputs(seed: int = 0) -> dict:
    splits = jax.random.split(jax.random.key(seed), 17)
    tokens_in = noise_with(splits[0], (TOKENS, MODEL_DIM), 1.0, 6.0, ((0, 16),), (0, 1, 16, 2.0))
    doc_ids = jax.vmap(lambda own: jnp.searchsorted(jnp.cumsum(ragged_sizes(own, DOCS, TOK_DEV, TOK_DEV // 2, 2)), jnp.arange(TOK_DEV), side="right"))(jax.random.split(splits[1], SEQS)).reshape((SEQS, TOK_DEV)).astype(jnp.int32)
    routes_keys = jax.random.split(jax.random.fold_in(splits[2], 1), TOKENS // TOK_DEV)
    routes_turns = jax.random.permutation(jax.random.fold_in(splits[2], 3), TOKENS // TOK_DEV)
    routes = jax.vmap(lambda own, number: assign_block(jax.random.fold_in(splits[2], 2), own, number, TOK_DEV, EXPERTS, TOP, CAP, 2))(routes_keys, routes_turns).reshape((TOKENS, TOP))
    q_weight = scatter_about(splits[3], (MODEL_DIM, QUERY_HEADS * HEAD_DIM), MODEL_DIM ** -0.5, 0.125, ((0, 16), (1, 2)))
    key_matrix = scatter_about(splits[4], (MODEL_DIM, KEY_VALUE_HEADS * HEAD_DIM), MODEL_DIM ** -0.5, 0.125, ((0, 16), (1, 2)))
    value_matrix = scatter_about(splits[5], (MODEL_DIM, KEY_VALUE_HEADS * HEAD_DIM), MODEL_DIM ** -0.5, 0.125, ((0, 16), (1, 2)))
    out_weight = scatter_about(splits[6], (MODEL_DIM, QUERY_HEADS * HEAD_DIM), (max(QUERY_HEADS * HEAD_DIM // 64, 1)) ** -0.5, 0.75, ((0, 16), (1, 2)))
    router_weight = scatter_about(splits[7], (MODEL_DIM, EXPERTS), (4 * MODEL_DIM) ** -0.5, 0.0625, ((0, 16),))
    attn_gain = jnp.clip(1.0 + 0.18 * jax.random.normal(splits[8], (MODEL_DIM,), jnp.float32), 0.1, 1.9)
    ffn_gain = jnp.clip(1.0 + 0.18 * jax.random.normal(splits[9], (MODEL_DIM,), jnp.float32), 0.1, 1.9)
    query_norm_gain = draw_query_norm_gain(jax.random.fold_in(splits[16], 71), 0)
    k_gain = draw_k_gain(jax.random.fold_in(splits[16], 71), 0)
    gate_weight = scatter_about(splits[12], (EXPERTS, MODEL_DIM, FF), MODEL_DIM ** -0.5, 0.125, ((0, 16), (2, 2)))
    up_weight = scatter_about(splits[13], (EXPERTS, MODEL_DIM, FF), MODEL_DIM ** -0.5, 0.125, ((0, 16), (2, 2)))
    down_weight = scatter_about(splits[14], (EXPERTS, FF, MODEL_DIM), (FF // 8) ** -0.5, 0.625, ((0, 16), (1, 2)))
    cotangent = noise_with(splits[15], (TOKENS, MODEL_DIM), 1.0, 6.0, ((0, 16),), (0, 1, 16, 2.0))
    return dict(tokens_in=tokens_in, doc_ids=doc_ids, routes=routes, q_weight=q_weight, key_matrix=key_matrix, value_matrix=value_matrix, out_weight=out_weight, router_weight=router_weight, attn_gain=attn_gain, ffn_gain=ffn_gain, query_norm_gain=query_norm_gain, k_gain=k_gain, gate_weight=gate_weight, up_weight=up_weight, down_weight=down_weight, cotangent=cotangent)


EPSILON = 1e-06
THETA = 1000000.0
HIGH_PRECISION = lax.Precision.HIGHEST

@jax.custom_vjp
def lower_precision(v):
    return lax.optimization_barrier(v.astype(jnp.bfloat16)).astype(jnp.float32)

@jax.custom_vjp
def lower_backward(v):
    return v

def low_keep(v):
    return (lower_precision(v), None)

def low_pass(kept, grad):
    return (grad,)

def back_keep(v):
    return (v, None)

def back_low(kept, grad):
    return (lower_precision(grad),)
lower_precision.defvjp(low_keep, low_pass)
lower_backward.defvjp(back_keep, back_low)

def root_mean_scale(values):
    return lax.rsqrt(lax.optimization_barrier(jnp.mean(values * values, axis=-1, keepdims=True)) + EPSILON)

def rotary_embedding(values):
    sequence_length = values.shape[0]
    half_width = values.shape[-1] // 2
    frequencies = THETA ** (-(2.0 * jnp.arange(half_width, dtype=jnp.float32)) / values.shape[-1])
    angles = jnp.arange(sequence_length, dtype=jnp.float32)[:, None] * frequencies[None, :]
    cosine = jnp.cos(angles)[:, None, :]
    sine_table = jnp.sin(angles)[:, None, :]
    lead_half = values[..., :half_width]
    tail_half = values[..., half_width:]
    return jnp.concatenate([lead_half * cosine - tail_half * sine_table, tail_half * cosine + lead_half * sine_table], axis=-1)

def attend(seq_tokens, seq_docs, q_weight, key_matrix, value_matrix, out_weight, attn_gain, query_norm_gain, k_gain):
    sequence_length = seq_tokens.shape[0]
    query_group_count = QUERY_HEADS // KEY_VALUE_HEADS
    normalized_input = lower_precision(seq_tokens * root_mean_scale(seq_tokens) * attn_gain)
    query_unrotated = lower_backward(jnp.dot(normalized_input, q_weight, precision=HIGH_PRECISION)).reshape(sequence_length, QUERY_HEADS, HEAD_DIM)
    key_unrotated = lower_backward(jnp.dot(normalized_input, key_matrix, precision=HIGH_PRECISION)).reshape(sequence_length, KEY_VALUE_HEADS, HEAD_DIM)
    value_rows = lower_precision(lower_backward(jnp.dot(normalized_input, value_matrix, precision=HIGH_PRECISION))).reshape(sequence_length, KEY_VALUE_HEADS, HEAD_DIM)
    query_rows = lower_precision(rotary_embedding(query_unrotated * root_mean_scale(query_unrotated) * query_norm_gain)).reshape(sequence_length, KEY_VALUE_HEADS, query_group_count, HEAD_DIM)
    keys_rows = lower_precision(rotary_embedding(key_unrotated * root_mean_scale(key_unrotated) * k_gain))
    scores = lower_backward(jnp.einsum('qngd,knd->ngqk', query_rows, keys_rows, precision=HIGH_PRECISION) / math.sqrt(HEAD_DIM))
    positions = jnp.arange(sequence_length)
    allowed = (positions[None, :] <= positions[:, None]) & (seq_docs[None, :] == seq_docs[:, None])
    scores = jnp.where(allowed, scores, -1e+30)
    row_peak = lax.optimization_barrier(jnp.max(scores, axis=-1, keepdims=True))
    attn_exps = jnp.exp(scores - row_peak)
    attn_probs = lower_precision(attn_exps / lax.optimization_barrier(jnp.sum(attn_exps, axis=-1, keepdims=True)))
    attended = jnp.einsum('ngqk,knd->qngd', attn_probs, value_rows, precision=HIGH_PRECISION)
    attended = lower_precision(lower_backward(attended)).reshape(sequence_length, QUERY_HEADS * HEAD_DIM)
    return lower_backward(jnp.dot(attended, out_weight.T, precision=HIGH_PRECISION))

def slot_table(routes):
    pair_ids = routes.reshape(N_GX, TOK_DEV * TOP).astype(jnp.int32)
    expert_iota = jnp.arange(EXPERTS, dtype=jnp.int32)
    route_hits = (pair_ids[:, :, None] == expert_iota).astype(jnp.int32)
    earlier = (jnp.cumsum(route_hits, axis=1) - route_hits).astype(jnp.int32)
    slot_rank = lax.optimization_barrier(jnp.sum(earlier * route_hits, axis=2)).astype(jnp.int32)
    slot_row = (jnp.arange(N_GX, dtype=jnp.int32)[:, None] * CAP + slot_rank).astype(jnp.int32)
    pair_index = jnp.arange(TOKENS * TOP, dtype=jnp.int32).reshape(N_GX, TOK_DEV * TOP)
    empty_table = jnp.full((EXPERTS, N_GX * CAP), -1, jnp.int32)
    return empty_table.at[pair_ids, slot_row].set(pair_index)

def expert_rows(normed_ffn, gate_flat, w_gate, w_up, w_down, slot_pair):
    valid_slot = slot_pair >= 0
    safe_pair = jnp.where(valid_slot, slot_pair, 0).astype(jnp.int32)
    token_index = (safe_pair // TOP).astype(jnp.int32)
    inputs = lower_backward(jnp.where(valid_slot[:, None], normed_ffn[token_index], 0.0))
    block_width = FF // N_GY
    summed = jnp.zeros((inputs.shape[0], MODEL_DIM), inputs.dtype)
    for block_index in range(N_GY):
        inner_rows = lower_backward(inputs)
        start = block_index * block_width
        gate_in = lower_backward(jnp.dot(inner_rows, w_gate[:, start:start + block_width], precision=HIGH_PRECISION))
        up_in = lower_backward(jnp.dot(inner_rows, w_up[:, start:start + block_width], precision=HIGH_PRECISION))
        activated = lower_precision(jax.nn.silu(gate_in) * up_in)
        summed = summed + lower_precision(jnp.dot(activated, w_down[start:start + block_width, :], precision=HIGH_PRECISION))
    returned = lower_backward(lower_precision(summed))
    gate_scale = jnp.where(valid_slot, gate_flat[safe_pair], 0.0)
    return returned * gate_scale[:, None]

def layer(tokens_in, q_weight, key_matrix, value_matrix, out_weight, router_weight, attn_gain, ffn_gain, query_norm_gain, k_gain, gate_weight, up_weight, down_weight, doc_ids, routes, slot_pair):

    def attend_one(bundle):
        return attend(bundle[0], bundle[1], q_weight, key_matrix, value_matrix, out_weight, attn_gain, query_norm_gain, k_gain)
    attn_rows = lax.map(jax.checkpoint(attend_one), (tokens_in.reshape(SEQS, TOK_DEV, MODEL_DIM), doc_ids))
    residual = tokens_in + attn_rows.reshape(TOKENS, MODEL_DIM)
    normed_ffn = lower_precision(residual * root_mean_scale(residual) * ffn_gain)
    logits = lower_backward(jnp.dot(normed_ffn, router_weight, precision=HIGH_PRECISION))
    chosen = jnp.take_along_axis(logits, routes, axis=1)
    gate_exps = jnp.exp(chosen)
    gate_values = gate_exps / lax.optimization_barrier(jnp.sum(gate_exps, axis=1, keepdims=True))
    gate_flat = gate_values.reshape(-1)
    checked_rows = jax.checkpoint(expert_rows)

    def scan_step(moe_sum, expert_items):
        weighted = checked_rows(normed_ffn, gate_flat, expert_items[0], expert_items[1], expert_items[2], expert_items[3])
        target = jnp.where(expert_items[3] >= 0, expert_items[3] // TOP, TOKENS).astype(jnp.int32)
        return (moe_sum.at[target].add(weighted, mode='drop'), None)
    moe_total = lax.scan(scan_step, jnp.zeros_like(tokens_in), (gate_weight, up_weight, down_weight, slot_pair))[0]
    return residual + moe_total

def reference(tokens_in, doc_ids, routes, q_weight, key_matrix, value_matrix, out_weight, router_weight, attn_gain, ffn_gain, query_norm_gain, k_gain, gate_weight, up_weight, down_weight, cotangent):
    slot_pair = slot_table(routes)
    floats = tuple((item.astype(jnp.float32) for item in (tokens_in, q_weight, key_matrix, value_matrix, out_weight, router_weight, attn_gain, ffn_gain, query_norm_gain, k_gain, gate_weight, up_weight, down_weight)))

    def forward(tokens_f, wq_f, wk_f, wv_f, wo_f, wr_f, gain_one, gain_two, gain_q, gain_k, wg_f, wu_f, wd_f):
        return layer(tokens_f, wq_f, wk_f, wv_f, wo_f, wr_f, gain_one, gain_two, gain_q, gain_k, wg_f, wu_f, wd_f, doc_ids, routes, slot_pair)
    result, pullback = jax.vjp(forward, *floats)
    gradients = pullback(cotangent.astype(jnp.float32))
    return (result.astype(jnp.bfloat16), gradients[0].astype(jnp.bfloat16), gradients[1], gradients[2], gradients[3], gradients[4], gradients[5], gradients[6], gradients[7], gradients[8], gradients[9], gradients[10], gradients[11], gradients[12])
```

```python
import math

import jax
import jax.numpy as jnp
from jax import lax
from jax.sharding import PartitionSpec as P

QUERY_HEADS = 32
KEY_VALUE_HEADS = 4
HEAD_DIM = 128
TOP = 8


EPSILON = 1e-06
THETA = 1000000.0


def root_mean_scale(values):
    return lax.rsqrt(jnp.mean(values * values, axis=-1, keepdims=True) + EPSILON)


def rotary_tables(sequence_length, head_width):
    half_width = head_width // 2
    frequencies = THETA ** (-(2.0 * jnp.arange(half_width, dtype=jnp.float32)) / head_width)
    angles = jnp.arange(sequence_length, dtype=jnp.float32)[:, None] * frequencies[None, :]
    return (jnp.cos(angles)[:, None, :], jnp.sin(angles)[:, None, :])


def rotate(values, cosine, sine_table):
    half_width = values.shape[-1] // 2
    lead_half = values[..., :half_width]
    tail_half = values[..., half_width:]
    return jnp.concatenate(
        [lead_half * cosine - tail_half * sine_table, tail_half * cosine + lead_half * sine_table],
        axis=-1,
    )


def norm_back(grad_normed, normed_unit, scale_rows):
    return scale_rows * (
        grad_normed - normed_unit * jnp.mean(grad_normed * normed_unit, axis=-1, keepdims=True)
    )


def contract(first_op, second_op, first_dim, second_dim):
    return lax.dot_general(
        first_op,
        second_op,
        (((first_dim,), (second_dim,)), ((), ())),
        preferred_element_type=jnp.float32,
    )


def scatter_sum(term):
    low = lax.psum_scatter(term.astype(jnp.bfloat16), "gx", scatter_dimension=0, tiled=True)
    return low.astype(jnp.float32)


def sparse_experts(normed_ffn, logits, route_hits, routes, cotangent, w_gate, w_up, w_down):
    sequence_length, model_width = normed_ffn.shape
    experts_all = logits.shape[1]
    devices_gx = lax.axis_size("gx")
    part_width = model_width // lax.axis_size("gy")
    capacity = 5 * sequence_length * TOP // (4 * experts_all)
    pairs_count = sequence_length * TOP
    hits_float = route_hits.astype(jnp.float32)
    chosen = jnp.sum(logits[:, None, :] * hits_float, axis=-1)
    gate_exps = jnp.exp(chosen)
    gate_values = gate_exps / jnp.sum(gate_exps, axis=1, keepdims=True)
    flat_hits = route_hits.reshape(pairs_count, experts_all).astype(jnp.int32)
    slot_rank = jnp.sum((jnp.cumsum(flat_hits, axis=0) - flat_hits) * flat_hits, axis=1)
    slot_dest = routes.reshape(-1) * capacity + slot_rank
    slot_pair = (
        jnp.full((experts_all * capacity,), pairs_count, jnp.int32)
        .at[slot_dest]
        .set(jnp.arange(pairs_count, dtype=jnp.int32))
    )
    slot_token = jnp.where(slot_pair < pairs_count, slot_pair // TOP, sequence_length)

    def to_experts(buffer):
        arrived = lax.all_to_all(buffer, "gx", split_axis=0, concat_axis=0, tiled=True)
        return arrived.reshape(devices_gx * capacity, model_width)

    def from_experts(partial_rows):
        share_rows = lax.psum_scatter(
            partial_rows.astype(jnp.bfloat16), "gy", scatter_dimension=1, tiled=True
        )
        returned = lax.all_to_all(
            share_rows.reshape(devices_gx, capacity, part_width),
            "gx",
            split_axis=0,
            concat_axis=0,
            tiled=True,
        )
        whole_rows = lax.all_gather(returned, "gy", axis=2, tiled=True)
        return whole_rows.reshape(devices_gx * capacity, model_width)

    send_rows = jnp.take(normed_ffn, slot_token, axis=0, mode="fill", fill_value=0)
    expert_in = to_experts(send_rows.reshape(devices_gx, capacity, model_width))
    gate_in = jnp.dot(expert_in, w_gate, preferred_element_type=jnp.float32)
    up_in = jnp.dot(expert_in, w_up, preferred_element_type=jnp.float32)
    gate_sigmoid = jax.nn.sigmoid(gate_in)
    gate_swish = gate_in * gate_sigmoid
    activated = (gate_swish * up_in).astype(jnp.bfloat16)
    expert_part = jnp.dot(activated, w_down, preferred_element_type=jnp.float32)
    expert_out = from_experts(expert_part)
    pair_rows = jnp.take(expert_out, slot_dest, axis=0).reshape(sequence_length, TOP, model_width)
    mixed_rows = jnp.einsum(
        "tk,tkd->td", gate_values, pair_rows, preferred_element_type=jnp.float32
    )
    grad_out_f = cotangent.astype(jnp.float32)
    grad_gates = jnp.einsum("td,tkd->tk", grad_out_f, pair_rows, preferred_element_type=jnp.float32)
    grad_chosen = gate_values * (
        grad_gates - jnp.sum(gate_values * grad_gates, axis=1, keepdims=True)
    )
    grad_logits = jnp.sum(grad_chosen[:, :, None] * hits_float, axis=1).astype(jnp.bfloat16)
    slot_gate = jnp.take(gate_values.reshape(-1), slot_pair, mode="fill", fill_value=0.0)
    grad_send = (
        jnp.take(grad_out_f, slot_token, axis=0, mode="fill", fill_value=0) * slot_gate[:, None]
    )
    grad_expert_out = to_experts(
        grad_send.astype(jnp.bfloat16).reshape(devices_gx, capacity, model_width)
    )
    grad_act = contract(grad_expert_out, w_down, 1, 1)
    down_term = contract(activated, grad_expert_out, 0, 0)
    grad_gate_in = (
        grad_act * up_in * gate_sigmoid * (1.0 + gate_in * (1.0 - gate_sigmoid))
    ).astype(jnp.bfloat16)
    grad_up_in = (grad_act * gate_swish).astype(jnp.bfloat16)
    gate_term = contract(expert_in, grad_gate_in, 0, 0)
    up_term = contract(expert_in, grad_up_in, 0, 0)
    grad_in_part = contract(grad_gate_in, w_gate, 1, 1) + contract(grad_up_in, w_up, 1, 1)
    grad_rows = from_experts(grad_in_part)
    grad_pairs = jnp.take(grad_rows, slot_dest, axis=0).reshape(sequence_length, TOP, model_width)
    grad_rows_sum = jnp.sum(grad_pairs.astype(jnp.float32), axis=1)
    return mixed_rows, grad_rows_sum, grad_logits, (gate_term[None], up_term[None], down_term[None])


def swap_cores(rows):
    return lax.ppermute(rows, "gy", [(0, 1), (1, 0)])


def dense_experts(normed_ffn, logits, route_hits, cotangent, w_gate, w_up, w_down):
    sequence_length, model_width = normed_ffn.shape
    devices_gx = lax.axis_size("gx")
    half_rows = sequence_length // lax.axis_size("gy")
    my_core = lax.axis_index("gy")
    my_expert = lax.axis_index("gx")

    def own_half(rows):
        return lax.dynamic_slice_in_dim(rows, my_core * half_rows, half_rows, 0)

    def to_experts(rows):
        own_rows = lax.all_gather(own_half(rows), "gx", axis=0, tiled=True)
        return (own_rows, swap_cores(own_rows))

    def both_halves(own_rows):
        other = swap_cores(own_rows)
        return jnp.where(
            my_core == 0,
            jnp.concatenate([own_rows, other], axis=0),
            jnp.concatenate([other, own_rows], axis=0),
        )

    def from_experts(partial_rows):
        there = swap_cores(partial_rows(1).astype(jnp.bfloat16))
        own_rows = (partial_rows(0) + there).astype(jnp.bfloat16)
        summed = lax.psum_scatter(own_rows, "gx", scatter_dimension=0, tiled=True)
        return both_halves(summed).astype(jnp.float32)

    def dot(left, right):
        return jnp.dot(left, right, preferred_element_type=jnp.float32)

    gate_exps = jnp.exp(jnp.where(jnp.any(route_hits, axis=1), logits, -1e30))
    gate_all = gate_exps / jnp.sum(gate_exps, axis=1, keepdims=True)
    grad_sets = to_experts(cotangent)
    row_sets = to_experts(normed_ffn)
    gate_sets = to_experts(gate_all)
    weighted, gate_terms, grad_gate_in, grad_up_in = [], [], [], []
    for part in range(2):
        gate_rows = lax.dynamic_slice_in_dim(gate_sets[part], my_expert, 1, 1)
        gate_in = dot(row_sets[part], w_gate)
        up_in = dot(row_sets[part], w_up)
        grad_hidden = contract(grad_sets[part], w_down, 1, 1)
        gate_sigmoid = jax.nn.sigmoid(gate_in)
        gate_swish = gate_in * gate_sigmoid
        activated = gate_swish * up_in
        gate_terms.append(jnp.sum(activated * grad_hidden, axis=1))
        weighted.append((gate_rows * activated).astype(jnp.bfloat16))
        grad_act = gate_rows * grad_hidden
        grad_gate_in.append(
            (grad_act * up_in * gate_sigmoid * (1.0 + gate_in * (1.0 - gate_sigmoid))).astype(jnp.bfloat16)
        )
        grad_up_in.append((grad_act * gate_swish).astype(jnp.bfloat16))
    mixed_rows = from_experts(lambda part: dot(weighted[part], w_down))
    grad_rows_sum = from_experts(
        lambda part: contract(grad_gate_in[part], w_gate, 1, 1) + contract(grad_up_in[part], w_up, 1, 1)
    )
    down_term, gate_term, up_term = (
        contract(first[0], second[0], 0, 0) + contract(first[1], second[1], 0, 0)
        for first, second in ((weighted, grad_sets), (row_sets, grad_gate_in), (row_sets, grad_up_in))
    )
    own_terms = gate_terms[0] + swap_cores(gate_terms[1])
    back = lax.all_to_all(own_terms.reshape(devices_gx, half_rows), "gx", split_axis=0, concat_axis=0, tiled=True)
    grad_gates = both_halves(back.T)
    grad_logits = (
        gate_all * (grad_gates - jnp.sum(gate_all * grad_gates, axis=1, keepdims=True))
    ).astype(jnp.bfloat16)
    return mixed_rows, grad_rows_sum, grad_logits, (gate_term[None], up_term[None], down_term[None])


def on_device(
    tokens_in,
    doc_ids,
    routes,
    q_weight,
    key_matrix,
    value_matrix,
    out_weight,
    router_weight,
    attn_gain,
    ffn_gain,
    query_norm_gain,
    k_gain,
    gate_weight,
    up_weight,
    down_weight,
    cotangent,
):
    sequence_length = tokens_in.shape[0]
    model_width = tokens_in.shape[1]
    devices_gx = lax.axis_size("gx")
    devices_gy = lax.axis_size("gy")
    part_width = model_width // devices_gy
    experts_all = router_weight.shape[1]
    query_group_count = QUERY_HEADS // KEY_VALUE_HEADS
    inv_root = 1.0 / math.sqrt(HEAD_DIM)
    q_full, k_full, v_full, o_full, router_full = (
        lax.all_gather(q_weight, "gx", axis=0, tiled=True),
        lax.all_gather(key_matrix, "gx", axis=0, tiled=True),
        lax.all_gather(value_matrix, "gx", axis=0, tiled=True),
        lax.all_gather(out_weight, "gx", axis=0, tiled=True),
        lax.all_gather(router_weight, "gx", axis=0, tiled=True),
    )
    heads_local = q_full.shape[1] // HEAD_DIM
    kv_local = k_full.shape[1] // HEAD_DIM
    inputs_f = tokens_in.astype(jnp.float32)
    scale_one = root_mean_scale(inputs_f)
    unit_one = inputs_f * scale_one
    normalized_input = (unit_one * attn_gain).astype(jnp.bfloat16)
    query_unrotated = jnp.dot(normalized_input, q_full, preferred_element_type=jnp.float32).reshape(
        sequence_length, heads_local, HEAD_DIM
    )
    key_unrotated = jnp.dot(normalized_input, k_full, preferred_element_type=jnp.float32).reshape(
        sequence_length, kv_local, HEAD_DIM
    )
    value_rows = (
        jnp.dot(normalized_input, v_full, preferred_element_type=jnp.float32)
        .astype(jnp.bfloat16)
        .reshape(sequence_length, kv_local, HEAD_DIM)
    )
    cosine, sine_table = rotary_tables(sequence_length, HEAD_DIM)
    q_scale = root_mean_scale(query_unrotated)
    q_unit = query_unrotated * q_scale
    query_rows = (
        rotate(q_unit * query_norm_gain, cosine, sine_table)
        .astype(jnp.bfloat16)
        .reshape(sequence_length, kv_local, query_group_count, HEAD_DIM)
    )
    k_scale = root_mean_scale(key_unrotated)
    k_unit = key_unrotated * k_scale
    keys_rows = rotate(k_unit * k_gain, cosine, sine_table).astype(jnp.bfloat16)
    positions = jnp.arange(sequence_length)
    documents = doc_ids[0]
    allowed = (positions[None, :] <= positions[:, None]) & (
        documents[None, :] == documents[:, None]
    )

    def score_block():
        raw_scores = (
            jnp.einsum("qngd,knd->ngqk", query_rows, keys_rows, preferred_element_type=jnp.float32)
            * inv_root
        )
        return jnp.where(allowed, raw_scores, -1e30)

    scores = score_block()
    row_peak = jnp.max(scores, axis=-1, keepdims=True)
    attn_exps = jnp.exp(scores - row_peak)
    row_total = jnp.sum(attn_exps, axis=-1, keepdims=True)
    log_total = row_peak + jnp.log(row_total)
    probs_low = (attn_exps / row_total).astype(jnp.bfloat16)
    attended = jnp.einsum(
        "ngqk,knd->qngd", probs_low, value_rows, preferred_element_type=jnp.float32
    )
    attended = attended.reshape(sequence_length, heads_local * HEAD_DIM).astype(jnp.bfloat16)
    attn_part = contract(attended, o_full, 1, 1)
    attn_total = attn_part + swap_cores(attn_part)
    residual = inputs_f + attn_total
    scale_two = root_mean_scale(residual)
    unit_two = residual * scale_two
    normed_ffn = (unit_two * ffn_gain).astype(jnp.bfloat16)
    logits = jnp.dot(normed_ffn, router_full, preferred_element_type=jnp.float32)
    expert_iota = jnp.arange(experts_all, dtype=jnp.int32)
    route_hits = routes[:, :, None] == expert_iota
    if experts_all <= 2 * TOP:
        mixed_rows, grad_rows_sum, grad_logits, expert_grads = dense_experts(
            normed_ffn, logits, route_hits, cotangent, gate_weight[0], up_weight[0], down_weight[0]
        )
    else:
        mixed_rows, grad_rows_sum, grad_logits, expert_grads = sparse_experts(
            normed_ffn, logits, route_hits, routes, cotangent, gate_weight[0], up_weight[0], down_weight[0]
        )
    output = (residual + mixed_rows).astype(jnp.bfloat16)
    grad_out_f = cotangent.astype(jnp.float32)
    router_term = contract(normed_ffn, grad_logits, 0, 0)
    grad_ffn_in = contract(grad_logits, router_full, 1, 1) + grad_rows_sum
    ffn_gain_term = jnp.sum(grad_ffn_in * unit_two, axis=0)
    grad_residual = grad_out_f + norm_back(grad_ffn_in * ffn_gain, unit_two, scale_two)
    grad_attn = grad_residual.astype(jnp.bfloat16)
    out_term = contract(grad_attn, attended, 0, 0)
    grad_attended = jnp.dot(grad_attn, o_full, preferred_element_type=jnp.float32).astype(
        jnp.bfloat16
    )
    grad_attended = grad_attended.reshape(sequence_length, kv_local, query_group_count, HEAD_DIM)
    probs_again = jnp.exp(score_block() - log_total)
    probs_again_low = probs_again.astype(jnp.bfloat16)
    grad_values = jnp.einsum(
        "ngqk,qngd->knd", probs_again_low, grad_attended, preferred_element_type=jnp.float32
    )
    grad_probs = jnp.einsum(
        "qngd,knd->ngqk", grad_attended, value_rows, preferred_element_type=jnp.float32
    )
    prob_inner = jnp.sum(probs_again * grad_probs, axis=-1, keepdims=True)
    grad_scores = (probs_again * (grad_probs - prob_inner)).astype(jnp.bfloat16)
    grad_queries = (
        jnp.einsum("ngqk,knd->qngd", grad_scores, keys_rows, preferred_element_type=jnp.float32)
        * inv_root
    )
    grad_keys = (
        jnp.einsum("ngqk,qngd->knd", grad_scores, query_rows, preferred_element_type=jnp.float32)
        * inv_root
    )
    grad_q_rot = rotate(
        grad_queries.reshape(sequence_length, heads_local, HEAD_DIM), cosine, -sine_table
    )
    grad_k_rot = rotate(grad_keys, cosine, -sine_table)
    q_gain_term = jnp.sum(grad_q_rot * q_unit, axis=(0, 1))
    k_gain_term = jnp.sum(grad_k_rot * k_unit, axis=(0, 1))
    grad_q_raw = (
        norm_back(grad_q_rot * query_norm_gain, q_unit, q_scale)
        .astype(jnp.bfloat16)
        .reshape(sequence_length, heads_local * HEAD_DIM)
    )
    grad_k_raw = (
        norm_back(grad_k_rot * k_gain, k_unit, k_scale)
        .astype(jnp.bfloat16)
        .reshape(sequence_length, kv_local * HEAD_DIM)
    )
    grad_v_raw = grad_values.astype(jnp.bfloat16).reshape(sequence_length, kv_local * HEAD_DIM)
    q_term = contract(normalized_input, grad_q_raw, 0, 0)
    k_term = contract(normalized_input, grad_k_raw, 0, 0)
    v_term = contract(normalized_input, grad_v_raw, 0, 0)
    grad_normed_part = (
        contract(grad_q_raw, q_full, 1, 1)
        + contract(grad_k_raw, k_full, 1, 1)
        + contract(grad_v_raw, v_full, 1, 1)
    )
    grad_normed = grad_normed_part + swap_cores(grad_normed_part)
    attn_gain_term = jnp.sum(grad_normed * unit_one, axis=0)
    grad_input = (grad_residual + norm_back(grad_normed * attn_gain, unit_one, scale_one)).astype(
        jnp.bfloat16
    )
    grad_q, grad_k, grad_v, grad_out, grad_router = (
        scatter_sum(q_term),
        scatter_sum(k_term),
        scatter_sum(v_term),
        scatter_sum(out_term),
        lax.psum_scatter(router_term, "gx", scatter_dimension=0, tiled=True),
    )
    own_mask = (jnp.arange(model_width) // part_width == lax.axis_index("gy")).astype(jnp.float32)
    gain_attn, gain_ffn, gain_query, gain_key = lax.psum(
        (attn_gain_term * own_mask, ffn_gain_term * own_mask, q_gain_term, k_gain_term),
        ("gx", "gy"),
    )
    return (
        output,
        grad_input,
        grad_q,
        grad_k,
        grad_v,
        grad_out,
        grad_router,
        gain_attn,
        gain_ffn,
        gain_query,
        gain_key,
        expert_grads[0],
        expert_grads[1],
        expert_grads[2],
    )


def solution(mesh):
    return jax.shard_map(
        on_device,
        mesh=mesh,
        in_specs=(
            P("gx", None),
            P("gx", None),
            P("gx", None),
            P("gx", "gy"),
            P("gx", "gy"),
            P("gx", "gy"),
            P("gx", "gy"),
            P("gx", None),
            P(),
            P(),
            P(),
            P(),
            P("gx", None, "gy"),
            P("gx", None, "gy"),
            P("gx", "gy", None),
            P("gx", None),
        ),
        out_specs=(
            P("gx", None),
            P("gx", None),
            P("gx", "gy"),
            P("gx", "gy"),
            P("gx", "gy"),
            P("gx", "gy"),
            P("gx", None),
            P(),
            P(),
            P(),
            P(),
            P("gx", None, "gy"),
            P("gx", None, "gy"),
            P("gx", "gy", None),
        ),
        check_vma=False,
    )
```

```python
import functools
import math

import jax
import jax.numpy as jnp
from jax import lax
from jax.experimental import pallas as pl
from jax.experimental.pallas import tpu as pltpu
from jax.sharding import PartitionSpec as P

QUERY_HEADS = 32
KEY_VALUE_HEADS = 4
HEAD_DIM = 128
LANES = 128
TOP = 8


EPSILON = 1e-06
THETA = 1000000.0


def root_mean_scale(values):
    return lax.rsqrt(jnp.mean(values * values, axis=-1, keepdims=True) + EPSILON)


def rotary_tables(sequence_length, head_width):
    half_width = head_width // 2
    frequencies = THETA ** (-(2.0 * jnp.arange(half_width, dtype=jnp.float32)) / head_width)
    angles = jnp.arange(sequence_length, dtype=jnp.float32)[:, None] * frequencies[None, :]
    return (jnp.cos(angles)[:, None, :], jnp.sin(angles)[:, None, :])


def rotate(values, cosine, sine_table):
    half_width = values.shape[-1] // 2
    lead_half = values[..., :half_width]
    tail_half = values[..., half_width:]
    return jnp.concatenate(
        [lead_half * cosine - tail_half * sine_table, tail_half * cosine + lead_half * sine_table],
        axis=-1,
    )


def norm_back(grad_normed, normed_unit, scale_rows):
    return scale_rows * (
        grad_normed - normed_unit * jnp.mean(grad_normed * normed_unit, axis=-1, keepdims=True)
    )


def contract(first_op, second_op, first_dim, second_dim):
    return lax.dot_general(
        first_op,
        second_op,
        (((first_dim,), (second_dim,)), ((), ())),
        preferred_element_type=jnp.float32,
    )


MESH = pl.DeviceIdType.MESH
LEVELS = 4
PLANE = 4


def cut_rows(rows):
    near, far = 3 * rows // 4, rows // 4
    return (
        (0, near),
        ((0, near // 2), (near // 2, near // 2)),
        (near, far),
        ((near, far // 2), (near + far // 2, far // 2)),
    )


def neighbours():
    me, core = lax.axis_index("gx"), lax.axis_index("gy")
    level = me // PLANE
    x_side = me + 1 - 2 * (me % 2)
    y_side = me + 2 - 4 * ((me // 2) % 2)
    return me, core, level, x_side, y_side


def greet(level, targets, with_core, me, core):
    barrier = pltpu.get_barrier_semaphore()

    def hello(device):
        pl.semaphore_signal(barrier, inc=1, device_id=device, device_id_type=MESH)

    for target in targets:
        hello((target, core))
    if with_core:
        hello((me, 1 - core))

    @pl.when(level > 0)
    def _():
        hello((me - PLANE, core))

    @pl.when(level < LEVELS - 1)
    def _():
        hello((me + PLANE, core))

    inner = jnp.where(level > 0, 1, 0) + jnp.where(level < LEVELS - 1, 1, 0)
    pl.semaphore_wait(barrier, len(targets) + int(with_core) + inner)


def when(condition, action):
    if condition is None:
        action()
    else:
        pl.when(condition)(action)


def gather_kernel(count, paired, *refs):
    ins, outs = refs[:count], refs[count : 2 * count]
    pairs = refs[2 * count : 3 * count] if paired else ()
    send_sem, recv_sem, local_sem = refs[-5:-2] if paired else refs[-3:]
    if paired:
        pair_send, pair_recv = refs[-2:]
    me, core, level, x_side, y_side = neighbours()
    whole_a, half_a, whole_b, half_b = cut_rows(ins[0].shape[0])
    greet(level, (x_side, y_side), paired, me, core)
    has_up, has_down = level < LEVELS - 1, level > 0
    up, down = (me + PLANE, core), (me - PLANE, core)
    to_x, to_y = (x_side, core), (y_side, core)
    sent, mirrored = [], []

    def place(array, first, number, span):
        return array.at[pl.ds(first, number), pl.ds(*span)]

    def send(condition, k, slot, source, first, number, span, target):
        def copy():
            here = ins[k].at[pl.ds(*span)] if source == "own" else place(outs[k], first, number, span)
            there = outs[k].at[first, pl.ds(*span)] if source == "own" else place(outs[k], first, number, span)
            return pltpu.make_async_remote_copy(
                here, there, send_sem.at[k, slot], recv_sem.at[k, slot], device_id=target, device_id_type=MESH
            )

        when(condition, lambda: copy().start())
        sent.append((condition, copy))

    def mirror(condition, k, first, number, span):
        if not paired:
            return
        slot = len(mirrored)

        def copy():
            here = place(outs[k], first, number, span)
            return pltpu.make_async_remote_copy(
                here,
                place(pairs[k], first, number, span),
                pair_send.at[slot],
                pair_recv.at[slot],
                device_id=(me, 1 - core),
                device_id_type=MESH,
            )

        when(condition, lambda: copy().start())
        mirrored.append((condition, copy))

    def arrive(condition, k, slot, first, number, span):
        def wait():
            pltpu.make_async_remote_copy(
                place(outs[k], first, number, span),
                place(outs[k], first, number, span),
                send_sem.at[k, slot],
                recv_sem.at[k, slot],
                device_id=to_x,
                device_id_type=MESH,
            ).wait_recv()

        when(condition, wait)
        mirror(condition, k, first, number, span)

    def slot_of(group, index):
        return 6 + 7 * group + index

    last = 6 + 28
    everyone = range(count)
    for k in everyone:
        pltpu.make_async_copy(ins[k], outs[k].at[me], local_sem.at[k]).start()
        send(None, k, last, "own", me, 1, whole_b, to_x)
        send(None, k, last + 1, "own", me, 1, whole_b, to_y)
        send(has_up, k, 0, "own", me, 1, whole_a, up)
        send(has_down, k, 3, "own", me, 1, whole_a, down)
        send(None, k, slot_of(0, 0), "own", me, 1, whole_a, to_x)
        send(None, k, slot_of(1, 0), "own", me, 1, whole_a, to_y)
    diagonal = x_side + y_side - me
    for k in everyone:
        arrive(None, k, last, x_side, 1, whole_b)
        send(None, k, last + 3, "out", x_side, 1, half_b[1], to_y)
        arrive(None, k, last + 1, y_side, 1, whole_b)
        send(None, k, last + 2, "out", y_side, 1, half_b[0], to_x)
    for k in everyone:
        pltpu.make_async_copy(ins[k], outs[k].at[me], local_sem.at[k]).wait()
        mirror(None, k, me, 1, (0, ins[k].shape[0]))
        arrive(None, k, last + 2, diagonal, 1, half_b[0])
        arrive(None, k, last + 3, diagonal, 1, half_b[1])
        send(has_up, k, last + 4, "out", PLANE * level, PLANE, whole_b, up)
        send(has_down, k, last + 7, "out", PLANE * level, PLANE, whole_b, down)

    def round_members(step):
        if step == 0:
            return [(None, 0, 0)]
        return [(level >= step, step, -step), (level + step < LEVELS, 3 + step, step)]

    def cross(k, step):
        for condition, index, distance in round_members(step):
            first = x_side + PLANE * distance
            arrive(condition, k, slot_of(0, index), first, 1, whole_a)
            send(condition, k, slot_of(3, index), "out", first, 1, half_a[1], to_y)
            first = y_side + PLANE * distance
            arrive(condition, k, slot_of(1, index), first, 1, whole_a)
            send(condition, k, slot_of(2, index), "out", first, 1, half_a[0], to_x)

    for step in range(1, LEVELS):
        for k in everyone:
            for condition, index, distance in round_members(step):
                first = me + PLANE * distance
                rising = distance < 0
                arrive(condition, k, step - 1 if rising else 2 + step, first, 1, whole_a)
                if step < LEVELS - 1:
                    onward = condition & (has_up if rising else has_down)
                    send(onward, k, step if rising else 3 + step, "out", first, 1, whole_a, up if rising else down)
                send(condition, k, slot_of(0, index), "out", first, 1, whole_a, to_x)
                send(condition, k, slot_of(1, index), "out", first, 1, whole_a, to_y)
            cross(k, step - 1)
            for condition, index, distance in round_members(step):
                first = PLANE * (level + distance)
                rising = distance < 0
                arrive(condition, k, last + (3 if rising else 6) + step, first, PLANE, whole_b)
                if step < LEVELS - 1:
                    onward = condition & (has_up if rising else has_down)
                    slot = last + (4 if rising else 7) + step
                    send(onward, k, slot, "out", first, PLANE, whole_b, up if rising else down)
    for k in everyone:
        cross(k, LEVELS - 1)
    for k in everyone:
        for step in range(LEVELS):
            for condition, index, distance in round_members(step):
                first = diagonal + PLANE * distance
                arrive(condition, k, slot_of(2, index), first, 1, half_a[0])
                arrive(condition, k, slot_of(3, index), first, 1, half_a[1])
    for condition, copy in sent:
        when(condition, lambda copy=copy: copy().wait_send())
    for condition, copy in mirrored:
        when(condition, lambda copy=copy: copy().wait())


GATHER_SLOTS = 6 + 28 + 10


def gather_blocks(arrays, collective_id, paired=False):
    count, blocks = len(arrays), lax.axis_size("gx")
    shapes = [jax.ShapeDtypeStruct((blocks, *a.shape), a.dtype) for a in arrays]
    scratch = [
        pltpu.SemaphoreType.DMA((count, GATHER_SLOTS)),
        pltpu.SemaphoreType.DMA((count, GATHER_SLOTS)),
        pltpu.SemaphoreType.DMA((count,)),
    ]
    if paired:
        scratch += [pltpu.SemaphoreType.DMA((count * (GATHER_SLOTS + 1),))] * 2
    return pl.pallas_call(
        functools.partial(gather_kernel, count, paired),
        out_shape=shapes * (2 if paired else 1),
        in_specs=[pl.BlockSpec(memory_space=pl.ANY)] * count,
        out_specs=[pl.BlockSpec(memory_space=pl.ANY)] * (count * (2 if paired else 1)),
        scratch_shapes=scratch,
        compiler_params=pltpu.CompilerParams(collective_id=collective_id, has_side_effects=True),
    )(*arrays)


def scatter_kernel(count, paired, *refs):
    n_in = 2 * count if paired else count
    ins, aways, outs = refs[:count], refs[count:n_in], refs[n_in : n_in + count]
    held = refs[n_in + count :]
    per = 8 + int(paired)
    parts = [held[per * k : per * (k + 1)] for k in range(count)]
    rest = held[per * count :]
    send_sem, recv_sem, chain_send, chain_recv, local_sem = rest[:5]
    me, core, level, x_side, y_side = neighbours()
    rows = ins[0].shape[1]
    whole_a, half_a, whole_b, half_b = cut_rows(rows)
    greet(level, (x_side, y_side), paired, me, core)
    up, down = (me + PLANE, core), (me - PLANE, core)
    to_x, to_y = (x_side, core), (y_side, core)
    x_at, y_at, own_at = x_side % PLANE, y_side % PLANE, me % PLANE
    diagonal_at = (x_side + y_side - me) % PLANE
    forward = jnp.where(level < 2, 1, 0)
    order = [
        3 * forward,
        2 * forward + (1 - forward),
        level + 1 - 2 * (level % 2),
        level,
    ]
    sent = []

    def send(condition, source, target_ref, ssem, rsem, target):
        def copy():
            return pltpu.make_async_remote_copy(
                source, target_ref, ssem, rsem, device_id=target, device_id_type=MESH
            )

        when(condition, lambda: copy().start())
        sent.append((condition, copy))

    def arrive(condition, target_ref, rsem):
        def wait():
            pltpu.make_async_remote_copy(
                target_ref, target_ref, rsem, rsem, device_id=to_x, device_id_type=MESH
            ).wait_recv()

        when(condition, wait)

    def add(condition, height, target, *terms, step=16):
        def run():
            def body(i, carry):
                at = pl.multiple_of(i * step, step)
                total = target(at, step)[...].astype(jnp.float32)
                for term in terms:
                    total = total + term(at, step)[...].astype(jnp.float32)
                target(at, step)[...] = total.astype(jnp.bfloat16)
                return carry

            lax.fori_loop(0, height // step, body, 0)

        when(condition, run)

    def rows_of(ref, *index, start=0):
        return lambda at, step: ref.at[(*index, pl.ds(start + at, step))]

    def load(k, to_level):
        return pltpu.make_async_copy(
            ins[k].at[pl.ds(PLANE * to_level, PLANE)],
            parts[k][0].at[pl.ds(PLANE * to_level, PLANE)],
            local_sem.at[k, to_level],
        )

    def hand(k, to_level):
        pair_send, pair_recv = rest[5:7]
        return pltpu.make_async_remote_copy(
            aways[k].at[pl.ds(PLANE * to_level, PLANE)],
            parts[k][8].at[pl.ds(PLANE * to_level, PLANE)],
            pair_send.at[k, to_level],
            pair_recv.at[k, to_level],
            device_id=(me, 1 - core),
            device_id_type=MESH,
        )

    everyone = range(count)
    for to_level in order:
        for k in everyone:
            load(k, to_level).start()
            if paired:
                hand(k, to_level).start()

    def chain(k, which, to_level, block, slots, spread):
        rising, falling = to_level > level, to_level < level
        begins = (rising & (level == 0)) | (falling & (level == LEVELS - 1))
        middle = (rising | falling) & jnp.logical_not(begins)
        arrive(middle, slots.at[to_level], chain_recv.at[k, which, to_level])
        spread(middle, to_level)
        send(rising, block, slots.at[to_level], chain_send.at[k, which, to_level], chain_recv.at[k, which, to_level], up)
        at = jnp.where(to_level == level - 1, LEVELS, to_level)
        send(falling, block, slots.at[at], chain_send.at[k, which, to_level], chain_recv.at[k, which, at], down)

    for turn, to_level in enumerate(order):
        first = PLANE * to_level
        for k in everyone:
            mine, half_y, half_x, full_x, full_y, slots_a, slots_b, side_b = parts[k][:8]
            load(k, to_level).wait()
            if paired:
                hand(k, to_level).wait()
                for column in range(PLANE):
                    add(None, rows, rows_of(mine, first + column), rows_of(parts[k][8], first + column))
            height = half_a[0][1]
            sems = [(send_sem.at[k, 6 * turn + i], recv_sem.at[k, 6 * turn + i]) for i in range(6)]
            send(None, mine.at[first + diagonal_at, pl.ds(*half_a[0])], half_y.at[turn], *sems[0], to_y)
            send(None, mine.at[first + diagonal_at, pl.ds(*half_a[1])], half_x.at[turn], *sems[1], to_x)
            send(None, mine.at[first + x_at, pl.ds(*half_a[1])], full_x.at[turn, pl.ds(*half_a[1])], *sems[2], to_x)
            send(None, mine.at[first + y_at, pl.ds(*half_a[0])], full_y.at[turn, pl.ds(*half_a[0])], *sems[3], to_y)

            def spread_b(condition, to_level, mine=mine, slots_b=slots_b, first=first):
                for column in range(PLANE):
                    add(
                        condition,
                        whole_b[1],
                        rows_of(mine, first + column, start=whole_b[0]),
                        rows_of(slots_b, to_level, column),
                    )

            chain(k, 1, to_level, mine.at[pl.ds(first, PLANE), pl.ds(*whole_b)], slots_b, spread_b)
            arrive(None, half_y.at[turn], recv_sem.at[k, 6 * turn])
            add(None, height, rows_of(mine, first + x_at), rows_of(half_y, turn))
            send(None, mine.at[first + x_at, pl.ds(*half_a[0])], full_x.at[turn, pl.ds(*half_a[0])], *sems[4], to_x)
            arrive(None, half_x.at[turn], recv_sem.at[k, 6 * turn + 1])
            add(None, height, rows_of(mine, first + y_at, start=height), rows_of(half_x, turn))
            send(None, mine.at[first + y_at, pl.ds(*half_a[1])], full_y.at[turn, pl.ds(*half_a[1])], *sems[5], to_y)
        if turn:
            finish_plane(turn - 1)
        else:

            def finish_plane(turn):
                to_level = order[turn]
                first = PLANE * to_level
                for k in everyone:
                    mine, half_y, half_x, full_x, full_y, slots_a, slots_b, side_b = parts[k][:8]
                    arrive(None, full_x.at[turn, pl.ds(*half_a[1])], recv_sem.at[k, 6 * turn + 2])
                    arrive(None, full_y.at[turn, pl.ds(*half_a[0])], recv_sem.at[k, 6 * turn + 3])
                    arrive(None, full_x.at[turn, pl.ds(*half_a[0])], recv_sem.at[k, 6 * turn + 4])
                    arrive(None, full_y.at[turn, pl.ds(*half_a[1])], recv_sem.at[k, 6 * turn + 5])
                    if turn == LEVELS - 1:
                        continue
                    add(None, whole_a[1], rows_of(mine, first + own_at), rows_of(full_x, turn), rows_of(full_y, turn))

                    def spread_a(condition, to_level, mine=mine, slots_a=slots_a, first=first):
                        add(condition, whole_a[1], rows_of(mine, first + own_at), rows_of(slots_a, to_level))

                    chain(k, 0, to_level, mine.at[first + own_at, pl.ds(*whole_a)], slots_a, spread_a)

    first = PLANE * level
    has_below, has_above = level > 0, level < LEVELS - 1
    for k in everyone:
        mine, half_y, half_x, full_x, full_y, slots_a, slots_b, side_b = parts[k][:8]
        for condition, slot in ((has_below, level), (has_above, LEVELS)):
            arrive(condition, slots_b.at[slot], chain_recv.at[k, 1, slot])
            for column in range(PLANE):
                add(
                    condition,
                    whole_b[1],
                    rows_of(mine, first + column, start=whole_b[0]),
                    rows_of(slots_b, slot, column),
                )
        sems = [(send_sem.at[k, 24 + i], recv_sem.at[k, 24 + i]) for i in range(4)]
        short = half_b[0][1]
        send(None, mine.at[first + diagonal_at, pl.ds(*half_b[0])], side_b.at[pl.ds(0, short)], *sems[0], to_y)
        send(None, mine.at[first + diagonal_at, pl.ds(*half_b[1])], side_b.at[pl.ds(short, short)], *sems[1], to_x)
    for k in everyone:
        mine, half_y, half_x, full_x, full_y, slots_a, slots_b, side_b = parts[k][:8]
        sems = [(send_sem.at[k, 24 + i], recv_sem.at[k, 24 + i]) for i in range(4)]
        short = half_b[0][1]
        arrive(None, side_b.at[pl.ds(0, short)], recv_sem.at[k, 24])
        add(None, short, rows_of(mine, first + x_at, start=half_b[0][0]), rows_of(side_b))
        send(None, mine.at[first + x_at, pl.ds(*whole_b)], side_b.at[pl.ds(2 * short, 2 * short)], *sems[2], to_x)
        arrive(None, side_b.at[pl.ds(short, short)], recv_sem.at[k, 25])
        add(None, short, rows_of(mine, first + y_at, start=half_b[1][0]), rows_of(side_b, start=short))
        send(None, mine.at[first + y_at, pl.ds(*whole_b)], side_b.at[pl.ds(4 * short, 2 * short)], *sems[3], to_y)
    finish_plane(LEVELS - 1)
    base = core * rows if paired else 0
    step = 16
    for k in everyone:
        mine, half_y, half_x, full_x, full_y, slots_a, slots_b, side_b = parts[k][:8]
        out = outs[k]
        for condition, slot in ((has_below, level), (has_above, LEVELS)):
            arrive(condition, slots_a.at[slot], chain_recv.at[k, 0, slot])

        def tail_a(i, carry, out=out, mine=mine, slots_a=slots_a, full_x=full_x, full_y=full_y):
            at = pl.multiple_of(i * step, step)
            span = pl.ds(at, step)
            turn = LEVELS - 1
            total = mine[first + own_at, span].astype(jnp.float32)
            total = total + full_x[turn, span].astype(jnp.float32) + full_y[turn, span].astype(jnp.float32)
            out[pl.ds(pl.multiple_of(base + at, step), step)] = total
            return carry

        lax.fori_loop(0, whole_a[1] // step, tail_a, 0)
        for condition, slot in ((has_below, level), (has_above, LEVELS)):

            def more(condition=condition, slot=slot, out=out, slots_a=slots_a):
                def body(i, carry):
                    at = pl.multiple_of(i * step, step)
                    span = pl.ds(pl.multiple_of(base + at, step), step)
                    out[span] = out[span] + slots_a[slot, pl.ds(at, step)].astype(jnp.float32)
                    return carry

                lax.fori_loop(0, whole_a[1] // step, body, 0)

            when(condition, more)
        short = half_b[0][1]
        arrive(None, side_b.at[pl.ds(2 * short, 2 * short)], recv_sem.at[k, 26])
        arrive(None, side_b.at[pl.ds(4 * short, 2 * short)], recv_sem.at[k, 27])

        def tail_b(i, carry, out=out, mine=mine, side_b=side_b):
            at = pl.multiple_of(i * step, step)
            total = mine[first + own_at, pl.ds(whole_b[0] + at, step)].astype(jnp.float32)
            total = total + side_b[pl.ds(2 * short + at, step)].astype(jnp.float32)
            total = total + side_b[pl.ds(4 * short + at, step)].astype(jnp.float32)
            out[pl.ds(pl.multiple_of(base + whole_b[0] + at, step), step)] = total
            return carry

        lax.fori_loop(0, whole_b[1] // step, tail_b, 0)
        if paired:
            ready_send, ready_recv = rest[7:9]
            span = pl.ds(pl.multiple_of(base, rows), rows)
            pltpu.make_async_remote_copy(
                out.at[span],
                out.at[span],
                ready_send.at[k],
                ready_recv.at[k],
                device_id=(me, 1 - core),
                device_id_type=MESH,
            ).start()
    for k in everyone:
        if paired:
            ready_send, ready_recv = rest[7:9]
            there = pl.ds(pl.multiple_of((1 - core) * rows, rows), rows)
            copy = pltpu.make_async_remote_copy(
                outs[k].at[there],
                outs[k].at[there],
                ready_send.at[k],
                ready_recv.at[k],
                device_id=(me, 1 - core),
                device_id_type=MESH,
            )
            copy.wait_send()
            copy.wait_recv()
    for condition, copy in sent:
        when(condition, lambda copy=copy: copy().wait_send())


def scatter_sums(arrays, collective_id, away=()):
    count, paired = len(arrays), bool(away)
    low = jnp.bfloat16
    scratch = []
    for a in arrays:
        blocks, rows, width = a.shape
        near, far = 3 * rows // 4, rows // 4
        scratch += [
            pltpu.VMEM((blocks, rows, width), low),
            pltpu.VMEM((LEVELS, near // 2, width), low),
            pltpu.VMEM((LEVELS, near // 2, width), low),
            pltpu.VMEM((LEVELS, near, width), low),
            pltpu.VMEM((LEVELS, near, width), low),
            pltpu.VMEM((LEVELS + 1, near, width), low),
            pltpu.VMEM((LEVELS + 1, PLANE, far, width), low),
            pltpu.VMEM((3 * far, width), low),
        ]
        if paired:
            scratch += [pltpu.VMEM((blocks, rows, width), low)]
    dma = pltpu.SemaphoreType.DMA
    scratch += [dma((count, 28)), dma((count, 28)), dma((count, 2, 5)), dma((count, 2, 5)), dma((count, LEVELS))]
    if paired:
        scratch += [dma((count, LEVELS)), dma((count, LEVELS)), dma((count,)), dma((count,))]
    return pl.pallas_call(
        functools.partial(scatter_kernel, count, paired),
        out_shape=[
            jax.ShapeDtypeStruct(((2 if paired else 1) * a.shape[1], a.shape[2]), jnp.float32) for a in arrays
        ],
        in_specs=[pl.BlockSpec(memory_space=pl.ANY)] * (count * (2 if paired else 1)),
        out_specs=[pl.BlockSpec(memory_space=pltpu.VMEM)] * count,
        scratch_shapes=scratch,
        compiler_params=pltpu.CompilerParams(
            collective_id=collective_id, has_side_effects=True, vmem_limit_bytes=60 * 1024 * 1024
        ),
    )(*arrays, *away)


def total_kernel(in_ref, out_ref, slots, send_sem, recv_sem):
    me, core, level, x_side, y_side = neighbours()
    near = me + PLANE - 2 * PLANE * (level % 2)
    far = me + 2 * PLANE - 4 * PLANE * (level // 2)
    partners = ((me, 1 - core), (x_side, core), (y_side, core), (near, core), (far, core))
    barrier = pltpu.get_barrier_semaphore()
    for partner in partners:
        pl.semaphore_signal(barrier, inc=1, device_id=partner, device_id_type=MESH)
    pl.semaphore_wait(barrier, len(partners))
    slots[0] = in_ref[...]
    for turn, partner in enumerate(partners):
        copy = pltpu.make_async_remote_copy(
            slots.at[2 * turn],
            slots.at[2 * turn + 1],
            send_sem.at[turn],
            recv_sem.at[turn],
            device_id=partner,
            device_id_type=MESH,
        )
        copy.start()
        copy.wait_recv()
        slots[2 * turn + 2] = slots[2 * turn] + slots[2 * turn + 1]
        copy.wait_send()
    out_ref[...] = slots[2 * len(partners)]


def total_everywhere(rows, collective_id):
    return pl.pallas_call(
        total_kernel,
        out_shape=jax.ShapeDtypeStruct(rows.shape, rows.dtype),
        in_specs=[pl.BlockSpec(memory_space=pltpu.VMEM)],
        out_specs=pl.BlockSpec(memory_space=pltpu.VMEM),
        scratch_shapes=[
            pltpu.VMEM((11, *rows.shape), rows.dtype),
            pltpu.SemaphoreType.DMA((5,)),
            pltpu.SemaphoreType.DMA((5,)),
        ],
        compiler_params=pltpu.CompilerParams(collective_id=collective_id, has_side_effects=True),
    )(rows)


def kernels_fit():
    return lax.axis_size("gx") == LEVELS * PLANE and lax.axis_size("gy") == 2


def gather_rows(arrays):
    if kernels_fit():
        return [rows.reshape(-1, rows.shape[-1]) for rows in gather_blocks(arrays, 1)]
    return [lax.all_gather(rows, "gx", axis=0, tiled=True) for rows in arrays]


def scatter_rows(terms):
    if kernels_fit():
        blocks = lax.axis_size("gx")
        return scatter_sums([term.astype(jnp.bfloat16).reshape(blocks, -1, term.shape[-1]) for term in terms], 2)
    return [lax.psum_scatter(term, "gx", scatter_dimension=0, tiled=True) for term in terms]


def total_of(vectors):
    if not kernels_fit():
        return lax.psum(vectors, ("gx", "gy"))
    lengths = [vector.shape[0] // HEAD_DIM for vector in vectors]
    rows = jnp.concatenate([vector.reshape(-1, HEAD_DIM) for vector in vectors], axis=0)
    rows = jnp.pad(rows, ((0, -rows.shape[0] % 8), (0, 0)))
    rows = total_everywhere(rows, 3)
    sums, at = [], 0
    for length in lengths:
        sums.append(rows[at : at + length].reshape(-1))
        at += length
    return sums


def two_parts(values):
    high = values.astype(jnp.bfloat16)
    return high, (values - high.astype(jnp.float32)).astype(jnp.bfloat16)


def sparse_experts(normed_ffn, logits, route_hits, routes, cotangent, w_gate, w_up, w_down):
    sequence_length, model_width = normed_ffn.shape
    experts_all = logits.shape[1]
    devices_gx = lax.axis_size("gx")
    part_width = model_width // lax.axis_size("gy")
    capacity = 5 * sequence_length * TOP // (4 * experts_all)
    pairs_count = sequence_length * TOP
    hits_float = route_hits.astype(jnp.float32)
    chosen = jnp.sum(logits[:, None, :] * hits_float, axis=-1)
    gate_exps = jnp.exp(chosen)
    gate_values = gate_exps / jnp.sum(gate_exps, axis=1, keepdims=True)
    flat_hits = route_hits.reshape(pairs_count, experts_all).astype(jnp.int32)
    slot_rank = jnp.sum((jnp.cumsum(flat_hits, axis=0) - flat_hits) * flat_hits, axis=1)
    slot_dest = routes.reshape(-1) * capacity + slot_rank
    slot_pair = (
        jnp.full((experts_all * capacity,), pairs_count, jnp.int32)
        .at[slot_dest]
        .set(jnp.arange(pairs_count, dtype=jnp.int32))
    )
    slot_token = jnp.where(slot_pair < pairs_count, slot_pair // TOP, sequence_length)

    def to_experts(buffer):
        arrived = lax.all_to_all(buffer, "gx", split_axis=0, concat_axis=0, tiled=True)
        return arrived.reshape(devices_gx * capacity, model_width)

    def from_experts(partial_rows):
        share_rows = lax.psum_scatter(
            partial_rows.astype(jnp.bfloat16), "gy", scatter_dimension=1, tiled=True
        )
        returned = lax.all_to_all(
            share_rows.reshape(devices_gx, capacity, part_width),
            "gx",
            split_axis=0,
            concat_axis=0,
            tiled=True,
        )
        whole_rows = lax.all_gather(returned, "gy", axis=2, tiled=True)
        return whole_rows.reshape(devices_gx * capacity, model_width)

    send_rows = jnp.take(normed_ffn, slot_token, axis=0, mode="fill", fill_value=0)
    expert_in = to_experts(send_rows.reshape(devices_gx, capacity, model_width))
    gate_in = jnp.dot(expert_in, w_gate, preferred_element_type=jnp.float32)
    up_in = jnp.dot(expert_in, w_up, preferred_element_type=jnp.float32)
    gate_sigmoid = jax.nn.sigmoid(gate_in)
    gate_swish = gate_in * gate_sigmoid
    activated = (gate_swish * up_in).astype(jnp.bfloat16)
    expert_part = jnp.dot(activated, w_down, preferred_element_type=jnp.float32)
    expert_out = from_experts(expert_part)
    pair_rows = jnp.take(expert_out, slot_dest, axis=0).reshape(sequence_length, TOP, model_width)
    mixed_rows = jnp.einsum(
        "tk,tkd->td", gate_values, pair_rows, preferred_element_type=jnp.float32
    )
    grad_out_f = cotangent.astype(jnp.float32)
    grad_gates = jnp.einsum("td,tkd->tk", grad_out_f, pair_rows, preferred_element_type=jnp.float32)
    grad_chosen = gate_values * (
        grad_gates - jnp.sum(gate_values * grad_gates, axis=1, keepdims=True)
    )
    grad_logits = jnp.sum(grad_chosen[:, :, None] * hits_float, axis=1).astype(jnp.bfloat16)
    slot_gate = jnp.take(gate_values.reshape(-1), slot_pair, mode="fill", fill_value=0.0)
    grad_send = (
        jnp.take(grad_out_f, slot_token, axis=0, mode="fill", fill_value=0) * slot_gate[:, None]
    )
    grad_expert_out = to_experts(
        grad_send.astype(jnp.bfloat16).reshape(devices_gx, capacity, model_width)
    )
    grad_act = contract(grad_expert_out, w_down, 1, 1)
    down_term = contract(activated, grad_expert_out, 0, 0)
    grad_gate_in = (
        grad_act * up_in * gate_sigmoid * (1.0 + gate_in * (1.0 - gate_sigmoid))
    ).astype(jnp.bfloat16)
    grad_up_in = (grad_act * gate_swish).astype(jnp.bfloat16)
    gate_term = contract(expert_in, grad_gate_in, 0, 0)
    up_term = contract(expert_in, grad_up_in, 0, 0)
    grad_in_part = contract(grad_gate_in, w_gate, 1, 1) + contract(grad_up_in, w_up, 1, 1)
    grad_rows = from_experts(grad_in_part)
    grad_pairs = jnp.take(grad_rows, slot_dest, axis=0).reshape(sequence_length, TOP, model_width)
    grad_rows_sum = jnp.sum(grad_pairs.astype(jnp.float32), axis=1)
    return mixed_rows, grad_rows_sum, grad_logits, (gate_term[None], up_term[None], down_term[None])


def swap_cores(rows):
    return lax.ppermute(rows, "gy", [(0, 1), (1, 0)])


def dense_experts(normed_ffn, logits, route_hits, cotangent, w_gate, w_up, w_down):
    sequence_length, model_width = normed_ffn.shape
    devices_gx = lax.axis_size("gx")
    half_rows = sequence_length // lax.axis_size("gy")
    my_core = lax.axis_index("gy")
    my_expert = lax.axis_index("gx")
    experts_all = logits.shape[1]

    def own_half(rows):
        return lax.dynamic_slice_in_dim(rows, my_core * half_rows, half_rows, 0)

    def dot(left, right):
        return jnp.dot(left, right, preferred_element_type=jnp.float32)

    gate_exps = jnp.exp(jnp.where(jnp.any(route_hits, axis=1), logits, -1e30))
    gate_all = gate_exps / jnp.sum(gate_exps, axis=1, keepdims=True)
    gate_lanes = jnp.pad(jnp.concatenate(two_parts(gate_all), axis=1), ((0, 0), (0, LANES - 2 * experts_all)))
    row_lanes = jnp.concatenate([own_half(normed_ffn), own_half(gate_lanes)], axis=1)
    gathered = gather_blocks([row_lanes, own_half(cotangent)], 4, paired=True)
    gathered = [rows.reshape(-1, rows.shape[-1]) for rows in gathered]
    row_sets = [gathered[part][:, :model_width] for part in (0, 2)]
    gate_sets = [gathered[part][:, model_width:] for part in (0, 2)]
    grad_sets = [gathered[1], gathered[3]]
    lane = jnp.arange(LANES)
    gate_pick = ((lane % experts_all == my_expert) & (lane < 2 * experts_all)).astype(jnp.bfloat16)
    high_lane = (lane == 2 * experts_all * my_core + my_expert).astype(jnp.bfloat16)
    low_lane = (lane == 2 * experts_all * my_core + experts_all + my_expert).astype(jnp.bfloat16)
    weighted, gate_terms, grad_gate_in, grad_up_in = [], [], [], []
    for part in range(2):
        gate_rows = jnp.sum(gate_sets[part].astype(jnp.float32) * gate_pick, axis=1, keepdims=True)
        gate_in = dot(row_sets[part], w_gate)
        up_in = dot(row_sets[part], w_up)
        grad_hidden = contract(grad_sets[part], w_down, 1, 1)
        gate_sigmoid = jax.nn.sigmoid(gate_in)
        gate_swish = gate_in * gate_sigmoid
        activated = gate_swish * up_in
        gate_terms.append(jnp.sum(activated * grad_hidden, axis=1))
        weighted.append((gate_rows * activated).astype(jnp.bfloat16))
        grad_act = gate_rows * grad_hidden
        grad_gate_in.append(
            (grad_act * up_in * gate_sigmoid * (1.0 + gate_in * (1.0 - gate_sigmoid))).astype(jnp.bfloat16)
        )
        grad_up_in.append((grad_act * gate_swish).astype(jnp.bfloat16))
    def blocks_of(rows):
        return rows.reshape(devices_gx, half_rows, rows.shape[-1])

    mixed_parts, term_parts, back_parts = [], [], []
    for part in range(2):
        mixed_parts.append(blocks_of(dot(weighted[part], w_down).astype(jnp.bfloat16)))
        high, low = two_parts(gate_terms[part])
        term_parts.append(blocks_of(high[:, None] * high_lane + low[:, None] * low_lane))
        grad_in = contract(grad_gate_in[part], w_gate, 1, 1) + contract(grad_up_in[part], w_up, 1, 1)
        back_parts.append(blocks_of(grad_in.astype(jnp.bfloat16)))
    mixed_rows, term_lanes = scatter_sums([mixed_parts[0], term_parts[0]], 5, [mixed_parts[1], term_parts[1]])
    (grad_rows_sum,) = scatter_sums([back_parts[0]], 6, [back_parts[1]])
    down_term, gate_term, up_term = (
        contract(first[0], second[0], 0, 0) + contract(first[1], second[1], 0, 0)
        for first, second in ((weighted, grad_sets), (row_sets, grad_gate_in), (row_sets, grad_up_in))
    )
    grad_gates = jnp.sum(term_lanes[:, : 4 * experts_all].reshape(sequence_length, 4, experts_all), axis=1)
    grad_logits = (
        gate_all * (grad_gates - jnp.sum(gate_all * grad_gates, axis=1, keepdims=True))
    ).astype(jnp.bfloat16)
    return mixed_rows, grad_rows_sum, grad_logits, (gate_term[None], up_term[None], down_term[None])


def on_device(
    tokens_in,
    doc_ids,
    routes,
    q_weight,
    key_matrix,
    value_matrix,
    out_weight,
    router_weight,
    attn_gain,
    ffn_gain,
    query_norm_gain,
    k_gain,
    gate_weight,
    up_weight,
    down_weight,
    cotangent,
):
    sequence_length = tokens_in.shape[0]
    model_width = tokens_in.shape[1]
    devices_gx = lax.axis_size("gx")
    devices_gy = lax.axis_size("gy")
    part_width = model_width // devices_gy
    experts_all = router_weight.shape[1]
    query_group_count = QUERY_HEADS // KEY_VALUE_HEADS
    inv_root = 1.0 / math.sqrt(HEAD_DIM)
    router_lanes = jnp.pad(router_weight, ((0, 0), (0, LANES - experts_all)))
    in_full, o_full = gather_rows(
        [jnp.concatenate([q_weight, key_matrix, value_matrix, router_lanes], axis=1), out_weight]
    )
    q_width, kv_width = q_weight.shape[1], key_matrix.shape[1]
    qkv_width = q_width + 2 * kv_width
    qkv_full = in_full[:, :qkv_width]
    router_full = in_full[:, qkv_width : qkv_width + experts_all]
    heads_local = q_width // HEAD_DIM
    kv_local = kv_width // HEAD_DIM
    inputs_f = tokens_in.astype(jnp.float32)
    scale_one = root_mean_scale(inputs_f)
    unit_one = inputs_f * scale_one
    normalized_input = (unit_one * attn_gain).astype(jnp.bfloat16)
    qkv_rows = jnp.dot(normalized_input, qkv_full, preferred_element_type=jnp.float32)
    query_unrotated = qkv_rows[:, :q_width].reshape(sequence_length, heads_local, HEAD_DIM)
    key_unrotated = qkv_rows[:, q_width : q_width + kv_width].reshape(sequence_length, kv_local, HEAD_DIM)
    value_rows = (
        qkv_rows[:, q_width + kv_width :].astype(jnp.bfloat16).reshape(sequence_length, kv_local, HEAD_DIM)
    )
    cosine, sine_table = rotary_tables(sequence_length, HEAD_DIM)
    q_scale = root_mean_scale(query_unrotated)
    q_unit = query_unrotated * q_scale
    query_rows = (
        rotate(q_unit * query_norm_gain, cosine, sine_table)
        .astype(jnp.bfloat16)
        .reshape(sequence_length, kv_local, query_group_count, HEAD_DIM)
    )
    k_scale = root_mean_scale(key_unrotated)
    k_unit = key_unrotated * k_scale
    keys_rows = rotate(k_unit * k_gain, cosine, sine_table).astype(jnp.bfloat16)
    positions = jnp.arange(sequence_length)
    documents = doc_ids[0]
    allowed = (positions[None, :] <= positions[:, None]) & (
        documents[None, :] == documents[:, None]
    )

    def score_block():
        raw_scores = (
            jnp.einsum("qngd,knd->ngqk", query_rows, keys_rows, preferred_element_type=jnp.float32)
            * inv_root
        )
        return jnp.where(allowed, raw_scores, -1e30)

    scores = score_block()
    row_peak = jnp.max(scores, axis=-1, keepdims=True)
    attn_exps = jnp.exp(scores - row_peak)
    row_total = jnp.sum(attn_exps, axis=-1, keepdims=True)
    log_total = row_peak + jnp.log(row_total)
    probs_low = (attn_exps / row_total).astype(jnp.bfloat16)
    attended = jnp.einsum(
        "ngqk,knd->qngd", probs_low, value_rows, preferred_element_type=jnp.float32
    )
    attended = attended.reshape(sequence_length, heads_local * HEAD_DIM).astype(jnp.bfloat16)
    attn_part = contract(attended, o_full, 1, 1)
    attn_total = attn_part + swap_cores(attn_part)
    residual = inputs_f + attn_total
    scale_two = root_mean_scale(residual)
    unit_two = residual * scale_two
    normed_ffn = (unit_two * ffn_gain).astype(jnp.bfloat16)
    logits = jnp.dot(normed_ffn, router_full, preferred_element_type=jnp.float32)
    expert_iota = jnp.arange(experts_all, dtype=jnp.int32)
    route_hits = routes[:, :, None] == expert_iota
    if experts_all <= 2 * TOP:
        mixed_rows, grad_rows_sum, grad_logits, expert_grads = dense_experts(
            normed_ffn, logits, route_hits, cotangent, gate_weight[0], up_weight[0], down_weight[0]
        )
    else:
        mixed_rows, grad_rows_sum, grad_logits, expert_grads = sparse_experts(
            normed_ffn, logits, route_hits, routes, cotangent, gate_weight[0], up_weight[0], down_weight[0]
        )
    output = (residual + mixed_rows).astype(jnp.bfloat16)
    grad_out_f = cotangent.astype(jnp.float32)
    router_term = contract(normed_ffn, grad_logits, 0, 0)
    grad_ffn_in = contract(grad_logits, router_full, 1, 1) + grad_rows_sum
    ffn_gain_term = jnp.sum(grad_ffn_in * unit_two, axis=0)
    grad_residual = grad_out_f + norm_back(grad_ffn_in * ffn_gain, unit_two, scale_two)
    grad_attn = grad_residual.astype(jnp.bfloat16)
    out_term = contract(grad_attn, attended, 0, 0)
    grad_attended = jnp.dot(grad_attn, o_full, preferred_element_type=jnp.float32).astype(
        jnp.bfloat16
    )
    grad_attended = grad_attended.reshape(sequence_length, kv_local, query_group_count, HEAD_DIM)
    probs_again = jnp.exp(score_block() - log_total)
    probs_again_low = probs_again.astype(jnp.bfloat16)
    grad_values = jnp.einsum(
        "ngqk,qngd->knd", probs_again_low, grad_attended, preferred_element_type=jnp.float32
    )
    grad_probs = jnp.einsum(
        "qngd,knd->ngqk", grad_attended, value_rows, preferred_element_type=jnp.float32
    )
    prob_inner = jnp.sum(probs_again * grad_probs, axis=-1, keepdims=True)
    grad_scores = (probs_again * (grad_probs - prob_inner)).astype(jnp.bfloat16)
    grad_queries = (
        jnp.einsum("ngqk,knd->qngd", grad_scores, keys_rows, preferred_element_type=jnp.float32)
        * inv_root
    )
    grad_keys = (
        jnp.einsum("ngqk,qngd->knd", grad_scores, query_rows, preferred_element_type=jnp.float32)
        * inv_root
    )
    grad_q_rot = rotate(
        grad_queries.reshape(sequence_length, heads_local, HEAD_DIM), cosine, -sine_table
    )
    grad_k_rot = rotate(grad_keys, cosine, -sine_table)
    q_gain_term = jnp.sum(grad_q_rot * q_unit, axis=(0, 1))
    k_gain_term = jnp.sum(grad_k_rot * k_unit, axis=(0, 1))
    grad_q_raw = (
        norm_back(grad_q_rot * query_norm_gain, q_unit, q_scale)
        .astype(jnp.bfloat16)
        .reshape(sequence_length, heads_local * HEAD_DIM)
    )
    grad_k_raw = (
        norm_back(grad_k_rot * k_gain, k_unit, k_scale)
        .astype(jnp.bfloat16)
        .reshape(sequence_length, kv_local * HEAD_DIM)
    )
    grad_v_raw = grad_values.astype(jnp.bfloat16).reshape(sequence_length, kv_local * HEAD_DIM)
    grad_qkv = jnp.concatenate([grad_q_raw, grad_k_raw, grad_v_raw], axis=1)
    qkv_term = contract(normalized_input, grad_qkv, 0, 0)
    grad_normed_part = contract(grad_qkv, qkv_full, 1, 1)
    grad_normed = grad_normed_part + swap_cores(grad_normed_part)
    attn_gain_term = jnp.sum(grad_normed * unit_one, axis=0)
    grad_input = (grad_residual + norm_back(grad_normed * attn_gain, unit_one, scale_one)).astype(
        jnp.bfloat16
    )
    router_lanes = jnp.pad(router_term, ((0, 0), (0, LANES - experts_all)))
    grad_in, grad_out, grad_router = scatter_rows([qkv_term, out_term, router_lanes])
    grad_q = grad_in[:, :q_width]
    grad_k = grad_in[:, q_width : q_width + kv_width]
    grad_v = grad_in[:, q_width + kv_width :]
    grad_router = grad_router[:, :experts_all]
    own_mask = (jnp.arange(model_width) // part_width == lax.axis_index("gy")).astype(jnp.float32)
    gain_attn, gain_ffn, gain_query, gain_key = total_of(
        (attn_gain_term * own_mask, ffn_gain_term * own_mask, q_gain_term, k_gain_term)
    )
    return (
        output,
        grad_input,
        grad_q,
        grad_k,
        grad_v,
        grad_out,
        grad_router,
        gain_attn,
        gain_ffn,
        gain_query,
        gain_key,
        expert_grads[0],
        expert_grads[1],
        expert_grads[2],
    )


def solution(mesh):
    return jax.shard_map(
        on_device,
        mesh=mesh,
        in_specs=(
            P("gx", None),
            P("gx", None),
            P("gx", None),
            P("gx", "gy"),
            P("gx", "gy"),
            P("gx", "gy"),
            P("gx", "gy"),
            P("gx", None),
            P(),
            P(),
            P(),
            P(),
            P("gx", None, "gy"),
            P("gx", None, "gy"),
            P("gx", "gy", None),
            P("gx", None),
        ),
        out_specs=(
            P("gx", None),
            P("gx", None),
            P("gx", "gy"),
            P("gx", "gy"),
            P("gx", "gy"),
            P("gx", "gy"),
            P("gx", None),
            P(),
            P(),
            P(),
            P(),
            P("gx", None, "gy"),
            P("gx", None, "gy"),
            P("gx", "gy", None),
        ),
        check_vma=False,
    )
```

```python
import functools
import math

import jax
import jax.numpy as jnp
from jax import lax
from jax.experimental import pallas as pl
from jax.experimental.pallas import tpu as pltpu
from jax.sharding import PartitionSpec as P

QUERY_HEADS = 32
KEY_VALUE_HEADS = 4
HEAD_DIM = 128
LANES = 128
TOP = 8


EPSILON = 1e-06
THETA = 1000000.0


def root_mean_scale(values):
    return lax.rsqrt(jnp.mean(values * values, axis=-1, keepdims=True) + EPSILON)


def rotary_tables(sequence_length, head_width):
    half_width = head_width // 2
    frequencies = THETA ** (-(2.0 * jnp.arange(half_width, dtype=jnp.float32)) / head_width)
    angles = jnp.arange(sequence_length, dtype=jnp.float32)[:, None] * frequencies[None, :]
    return (jnp.cos(angles)[:, None, :], jnp.sin(angles)[:, None, :])


def rotate(values, cosine, sine_table):
    half_width = values.shape[-1] // 2
    lead_half = values[..., :half_width]
    tail_half = values[..., half_width:]
    return jnp.concatenate(
        [lead_half * cosine - tail_half * sine_table, tail_half * cosine + lead_half * sine_table],
        axis=-1,
    )


def norm_back(grad_normed, normed_unit, scale_rows):
    return scale_rows * (
        grad_normed - normed_unit * jnp.mean(grad_normed * normed_unit, axis=-1, keepdims=True)
    )


def contract(first_op, second_op, first_dim, second_dim):
    return lax.dot_general(
        first_op,
        second_op,
        (((first_dim,), (second_dim,)), ((), ())),
        preferred_element_type=jnp.float32,
    )


MESH = pl.DeviceIdType.MESH
LEVELS = 4
PLANE = 4


def cut_rows(rows):
    near, far = 3 * rows // 4, rows // 4
    return (
        (0, near),
        ((0, near // 2), (near // 2, near // 2)),
        (near, far),
        ((near, far // 2), (near + far // 2, far // 2)),
    )


def neighbours():
    me, core = lax.axis_index("gx"), lax.axis_index("gy")
    level = me // PLANE
    x_side = me + 1 - 2 * (me % 2)
    y_side = me + 2 - 4 * ((me // 2) % 2)
    return me, core, level, x_side, y_side


def greet(level, targets, with_core, me, core):
    barrier = pltpu.get_barrier_semaphore()

    def hello(device):
        pl.semaphore_signal(barrier, inc=1, device_id=device, device_id_type=MESH)

    for target in targets:
        hello((target, core))
    if with_core:
        hello((me, 1 - core))

    @pl.when(level > 0)
    def _():
        hello((me - PLANE, core))

    @pl.when(level < LEVELS - 1)
    def _():
        hello((me + PLANE, core))

    inner = jnp.where(level > 0, 1, 0) + jnp.where(level < LEVELS - 1, 1, 0)
    pl.semaphore_wait(barrier, len(targets) + int(with_core) + inner)


def when(condition, action):
    if condition is None:
        action()
    else:
        pl.when(condition)(action)


def gather_kernel(count, with_pair, *refs):
    paired = sum(with_pair)
    ins, outs, pairs = refs[:count], refs[count : 2 * count], list(refs[2 * count : 2 * count + paired])
    pairs = [pairs.pop(0) if wanted else None for wanted in with_pair]
    sems = refs[2 * count + paired :]
    steps = gather_steps(ins, outs, pairs, sems)
    for step in steps.order:
        step()
    steps.end()


class gather_steps:
    def __init__(self, ins, outs, pairs, sems):
        self.ins, self.outs, self.pairs = ins, outs, pairs
        self.send_sem, self.recv_sem, self.local_sem, self.pair_send, self.pair_recv = sems
        self.me, self.core, self.level, self.x_side, self.y_side = neighbours()
        self.diagonal = self.x_side + self.y_side - self.me
        self.spans = cut_rows(ins[0].shape[0])
        self.has_up, self.has_down = self.level < LEVELS - 1, self.level > 0
        self.up, self.down = (self.me + PLANE, self.core), (self.me - PLANE, self.core)
        self.to_x, self.to_y = (self.x_side, self.core), (self.y_side, self.core)
        self.sent, self.mirrored, self.everyone = [], [], range(len(ins))
        greet(self.level, (self.x_side, self.y_side), any(p is not None for p in pairs), self.me, self.core)
        self.order = [
            self.start,
            self.side_small,
            lambda: self.column(1),
            lambda: self.cross(0),
            lambda: self.column(2),
            self.start_planes,
            lambda: self.cross(1),
            lambda: self.column(3),
            lambda: self.planes(1),
            lambda: self.cross(2),
            lambda: self.planes(2),
            lambda: self.cross(3),
            lambda: self.planes(3),
            lambda: [self.halves(step) for step in range(LEVELS)],
        ]

    def send(self, condition, k, slot, source, first, number, span, target):
        def copy():
            there = self.outs[k].at[pl.ds(first, number), pl.ds(*span)]
            here = there
            if source == "own":
                here, there = self.ins[k].at[pl.ds(*span)], self.outs[k].at[first, pl.ds(*span)]
            return pltpu.make_async_remote_copy(
                here,
                there,
                self.send_sem.at[k, slot],
                self.recv_sem.at[k, slot],
                device_id=target,
                device_id_type=MESH,
            )

        when(condition, lambda: copy().start())
        self.sent.append((condition, copy))

    def mirror(self, condition, k, first, number, span, group):
        if self.pairs[k] is None:
            return
        slot = len(self.mirrored)

        def copy():
            return pltpu.make_async_remote_copy(
                self.outs[k].at[pl.ds(first, number), pl.ds(*span)],
                self.pairs[k].at[pl.ds(first, number), pl.ds(*span)],
                self.pair_send.at[slot],
                self.pair_recv.at[slot],
                device_id=(self.me, 1 - self.core),
                device_id_type=MESH,
            )

        when(condition, lambda: copy().start())
        self.mirrored.append((condition, copy, group))

    def arrive(self, condition, k, slot, first, number, span, group):
        place = self.outs[k].at[pl.ds(first, number), pl.ds(*span)]

        def wait():
            pltpu.make_async_remote_copy(
                place,
                place,
                self.send_sem.at[k, slot],
                self.recv_sem.at[k, slot],
                device_id=self.to_x,
                device_id_type=MESH,
            ).wait_recv()

        when(condition, wait)
        self.mirror(condition, k, first, number, span, group)

    def members(self, step):
        if step == 0:
            return [(None, 0, 0)]
        return [(self.level >= step, step, -step), (self.level + step < LEVELS, 3 + step, step)]

    def slot_of(self, group, index):
        return 6 + 7 * group + index

    last = 6 + 28

    def own_copy(self, k):
        return pltpu.make_async_copy(self.ins[k], self.outs[k].at[self.me], self.local_sem.at[k])

    def start(self):
        whole_a, half_a, whole_b, half_b = self.spans
        last, me = self.last, self.me
        for k in self.everyone:
            self.own_copy(k).start()
            self.send(None, k, last, "own", me, 1, whole_b, self.to_x)
            self.send(None, k, last + 1, "own", me, 1, whole_b, self.to_y)
            self.send(self.has_up, k, 0, "own", me, 1, whole_a, self.up)
            self.send(self.has_down, k, 3, "own", me, 1, whole_a, self.down)
            self.send(None, k, self.slot_of(0, 0), "own", me, 1, whole_a, self.to_x)
            self.send(None, k, self.slot_of(1, 0), "own", me, 1, whole_a, self.to_y)

    def side_small(self):
        whole_a, half_a, whole_b, half_b = self.spans
        last = self.last
        for k in self.everyone:
            self.arrive(None, k, last, self.x_side, 1, whole_b, 0)
            self.send(None, k, last + 3, "out", self.x_side, 1, half_b[1], self.to_y)
            self.arrive(None, k, last + 1, self.y_side, 1, whole_b, 0)
            self.send(None, k, last + 2, "out", self.y_side, 1, half_b[0], self.to_x)
        for k in self.everyone:
            self.own_copy(k).wait()
            self.mirror(None, k, self.me, 1, (0, self.ins[k].shape[0]), 0)
            self.arrive(None, k, last + 2, self.diagonal, 1, half_b[0], 0)
            self.arrive(None, k, last + 3, self.diagonal, 1, half_b[1], 0)

    def start_planes(self):
        whole_b = self.spans[2]
        for k in self.everyone:
            self.send(self.has_up, k, self.last + 4, "out", PLANE * self.level, PLANE, whole_b, self.up)
            self.send(self.has_down, k, self.last + 7, "out", PLANE * self.level, PLANE, whole_b, self.down)

    def cross(self, step):
        whole_a, half_a = self.spans[:2]
        for k in self.everyone:
            for condition, index, distance in self.members(step):
                first = self.x_side + PLANE * distance
                self.arrive(condition, k, self.slot_of(0, index), first, 1, whole_a, distance)
                self.send(condition, k, self.slot_of(3, index), "out", first, 1, half_a[1], self.to_y)
                first = self.y_side + PLANE * distance
                self.arrive(condition, k, self.slot_of(1, index), first, 1, whole_a, distance)
                self.send(condition, k, self.slot_of(2, index), "out", first, 1, half_a[0], self.to_x)

    def halves(self, step):
        half_a = self.spans[1]
        for k in self.everyone:
            for condition, index, distance in self.members(step):
                first = self.diagonal + PLANE * distance
                self.arrive(condition, k, self.slot_of(2, index), first, 1, half_a[0], distance)
                self.arrive(condition, k, self.slot_of(3, index), first, 1, half_a[1], distance)

    def column(self, step):
        whole_a = self.spans[0]
        for k in self.everyone:
            for condition, index, distance in self.members(step):
                first = self.me + PLANE * distance
                rising = distance < 0
                self.arrive(condition, k, step - 1 if rising else 2 + step, first, 1, whole_a, distance)
                if step < LEVELS - 1:
                    onward = condition & (self.has_up if rising else self.has_down)
                    slot = step if rising else 3 + step
                    self.send(onward, k, slot, "out", first, 1, whole_a, self.up if rising else self.down)
                self.send(condition, k, self.slot_of(0, index), "out", first, 1, whole_a, self.to_x)
                self.send(condition, k, self.slot_of(1, index), "out", first, 1, whole_a, self.to_y)

    def planes(self, step):
        whole_b = self.spans[2]
        for k in self.everyone:
            for condition, index, distance in self.members(step):
                first = PLANE * (self.level + distance)
                rising = distance < 0
                self.arrive(condition, k, self.last + (3 if rising else 6) + step, first, PLANE, whole_b, distance)
                if step < LEVELS - 1:
                    onward = condition & (self.has_up if rising else self.has_down)
                    slot = self.last + (4 if rising else 7) + step
                    self.send(onward, k, slot, "out", first, PLANE, whole_b, self.up if rising else self.down)

    def paired_level(self, distance):
        for condition, copy, group in self.mirrored:
            if group == distance:
                when(condition, lambda copy=copy: copy().wait_recv())

    def end(self, levels_waited=False):
        for condition, copy in self.sent:
            when(condition, lambda copy=copy: copy().wait_send())
        for condition, copy, group in self.mirrored:
            when(condition, lambda copy=copy: copy().wait_send())
            if not levels_waited:
                when(condition, lambda copy=copy: copy().wait_recv())


GATHER_SLOTS = 6 + 28 + 10


def gather_semaphores(count, paired):
    dma = pltpu.SemaphoreType.DMA
    slots = (count, GATHER_SLOTS)
    pair_slots = (max(1, paired * (GATHER_SLOTS + 1)),)
    return [dma(slots), dma(slots), dma((count,)), dma(pair_slots), dma(pair_slots)]


def gather_blocks(arrays, with_pair, collective_id):
    count, blocks, paired = len(arrays), lax.axis_size("gx"), sum(with_pair)
    shapes = [jax.ShapeDtypeStruct((blocks, *a.shape), a.dtype) for a in arrays]
    shapes += [shape for shape, wanted in zip(shapes, with_pair) if wanted]
    return pl.pallas_call(
        functools.partial(gather_kernel, count, with_pair),
        out_shape=shapes,
        in_specs=[pl.BlockSpec(memory_space=pl.ANY)] * count,
        out_specs=[pl.BlockSpec(memory_space=pl.ANY)] * len(shapes),
        scratch_shapes=gather_semaphores(count, paired),
        compiler_params=pltpu.CompilerParams(collective_id=collective_id, has_side_effects=True),
    )(*arrays)


def dot_nn(left, right):
    return lax.dot_general(left, right, (((1,), (0,)), ((), ())), preferred_element_type=jnp.float32)


def dot_nt(left, right):
    return lax.dot_general(left, right, (((1,), (1,)), ((), ())), preferred_element_type=jnp.float32)


def experts_kernel(experts_all, *refs):
    rows_ref, grads_own, grads_pair, w_gate, w_up, w_down = refs[:6]
    weighted_out, grad_in_out, terms_out, gate_out, up_out, down_out = refs[6:12]
    held, grads, w_in, left_in, left_down, weighted_ref, grad_in_ref, terms_ref = refs[12:20]
    sums_in, sums_down, turned, grad_sem, w_sem, out_sem, sum_sem = refs[20:27]
    steps = gather_steps([rows_ref], [held.at[0]], [held.at[1]], refs[27:])
    level, core = steps.level, steps.core
    hidden, width = w_down.shape
    tiles = hidden // LANES
    rows = rows_ref.shape[0]
    visits = [
        level,
        jnp.where(level == 0, 1, level - 1),
        jnp.where(level == 0, 2, jnp.where(level == 3, 1, level + 1)),
        jnp.where(level < 2, 3, 0),
    ]

    def fetch(turn, half):
        return pltpu.make_async_copy(
            (grads_own, grads_pair)[half].at[pl.ds(PLANE * visits[turn], PLANE)],
            grads.at[turn % 2, half],
            grad_sem.at[turn % 2, half],
        )

    def fetch_start(turn):
        fetch(turn, 0).start()
        fetch(turn, 1).start()

    joins = [
        pltpu.make_async_copy(part, w_in.at[:, pl.ds(i * hidden, hidden)], w_sem.at[i])
        for i, part in enumerate((w_gate, w_up))
    ]
    lane = lax.broadcasted_iota(jnp.int32, (1, LANES), 1)
    expert = steps.me
    gate_pick = (((lane == expert) | (lane == experts_all + expert))).astype(jnp.float32)
    high_lane = (lane == 2 * experts_all * core + expert).astype(jnp.float32)
    low_lane = (lane == 2 * experts_all * core + experts_all + expert).astype(jnp.float32)
    group = 2 * rows

    def leave(turn):
        span = pl.ds(PLANE * visits[turn], PLANE)
        pairs = ((weighted_ref, weighted_out), (grad_in_ref, grad_in_out), (terms_ref, terms_out))
        return [
            pltpu.make_async_copy(here.at[:, span], there.at[:, span], out_sem.at[turn, i])
            for i, (here, there) in enumerate(pairs)
        ]

    def forward(turn, begin, end):
        first = PLANE * visits[turn]
        if begin == 0:
            fetch(turn, 0).wait()
            fetch(turn, 1).wait()

        def body(step, carry):
            half, pair = step // 2, step % 2
            at = first + 2 * pair
            lanes = held[half, pl.ds(at, 2), :, pl.ds(width, LANES)].reshape(group, LANES)
            gate_rows = jnp.sum(lanes.astype(jnp.float32) * gate_pick, axis=1, keepdims=True)
            grad_rows = grads[turn % 2, half, pl.ds(2 * pair, 2)].reshape(group, width)
            token_rows = held[half, pl.ds(at, 2), :, pl.ds(0, width)].reshape(group, width)
            grad_hidden = dot_nt(grad_rows, w_down[...])
            both = dot_nn(token_rows, w_in[...])
            terms = jnp.zeros((group, 1), jnp.float32)
            column = pl.multiple_of(step * group, group)
            for j in range(tiles):
                gate_in = both[:, j * LANES : (j + 1) * LANES]
                up_in = both[:, hidden + j * LANES : hidden + (j + 1) * LANES]
                back = grad_hidden[:, j * LANES : (j + 1) * LANES]
                gate_sigmoid = 1.0 / (1.0 + jnp.exp(-gate_in))
                gate_swish = gate_in * gate_sigmoid
                activated = gate_swish * up_in
                terms = terms + jnp.sum(activated * back, axis=1, keepdims=True)
                grad_act = gate_rows * back
                weighted = gate_rows * activated
                grad_gate = grad_act * up_in * gate_sigmoid * (1.0 + gate_in * (1.0 - gate_sigmoid))
                grad_up = grad_act * gate_swish
                for value, array, tile, left in (
                    (weighted, weighted_ref, j, left_down),
                    (grad_gate, grad_in_ref, j, left_in),
                    (grad_up, grad_in_ref, tiles + j, left_in),
                ):
                    span = pl.ds(tile * LANES, LANES)
                    array[half, pl.ds(at, 2), :, span] = value.astype(jnp.bfloat16).reshape(2, rows, LANES)
                    left[span, pl.ds(column, group)] = value.T.astype(jnp.bfloat16)
            high = terms.astype(jnp.bfloat16).astype(jnp.float32)
            spread = high * high_lane + (terms - high) * low_lane
            terms_ref[half, pl.ds(at, 2)] = spread.astype(jnp.bfloat16).reshape(2, rows, LANES)
            return carry

        lax.fori_loop(begin, end, body, 0)
        if end == 4:
            for copy in leave(turn):
                copy.start()

    wide = 256

    def weights(turn, begin, end):
        first = PLANE * visits[turn]

        def body(step, carry):
            span = pl.ds(pl.multiple_of(step * wide, wide), wide)
            token_rows = held[:, pl.ds(first, PLANE), :, span].reshape(2 * PLANE * rows, wide)
            grad_rows = grads[turn % 2, :, :, :, span].reshape(2 * PLANE * rows, wide)
            part_in = dot_nn(left_in[...], token_rows)
            part_down = dot_nn(left_down[...], grad_rows)
            if turn:
                part_in = sums_in[:, span] + part_in
                part_down = sums_down[:, span] + part_down
            sums_down[:, span] = part_down
            if turn < LEVELS - 1:
                sums_in[:, span] = part_in
            else:
                for i in range(2):
                    turned[i, span] = part_in[i * hidden : (i + 1) * hidden].T
                for copy in leave_sums(step):
                    copy.start()
            return carry

        lax.fori_loop(begin, end, body, 0)
        if end == width // wide and turn + 2 < LEVELS:
            fetch_start(turn + 2)

    def leave_sums(step):
        span = pl.ds(pl.multiple_of(step * wide, wide), wide)
        return [
            pltpu.make_async_copy(turned.at[0, span], gate_out.at[span], sum_sem.at[step, 0]),
            pltpu.make_async_copy(turned.at[1, span], up_out.at[span], sum_sem.at[step, 1]),
            pltpu.make_async_copy(sums_down.at[:, span], down_out.at[:, span], sum_sem.at[step, 2]),
        ]

    def level_ready(turn):
        if turn == 0:
            steps.paired_level(0)
            return
        for distance in range(-3, 4):
            if distance:
                wanted = visits[turn] == level + distance
                pl.when(wanted)(lambda distance=distance: steps.paired_level(distance))

    steps.start()
    fetch_start(0)
    for join in joins:
        join.start()
    fetch_start(1)
    steps.side_small()
    steps.column(1)
    steps.cross(0)
    for join in joins:
        join.wait()
    steps.column(2)
    steps.start_planes()
    steps.halves(0)
    level_ready(0)
    forward(0, 0, 2)
    steps.cross(1)
    forward(0, 2, 4)
    steps.column(3)
    weights(0, 0, 4)
    steps.planes(1)
    weights(0, 4, 8)
    steps.cross(2)
    steps.halves(1)
    level_ready(1)
    forward(1, 0, 2)
    steps.planes(2)
    forward(1, 2, 4)
    steps.cross(3)
    weights(1, 0, 4)
    weights(1, 4, 8)
    steps.halves(2)
    level_ready(2)
    forward(2, 0, 4)
    weights(2, 0, 8)
    steps.planes(3)
    steps.halves(3)
    level_ready(3)
    forward(3, 0, 4)
    weights(3, 0, 8)
    for turn in range(LEVELS):
        for copy in leave(turn):
            copy.wait()

    def last_sums(step, carry):
        for copy in leave_sums(step):
            copy.wait()
        return carry

    lax.fori_loop(0, width // wide, last_sums, 0)
    steps.end(levels_waited=True)


def experts_products(rows, grads_own, grads_pair, w_gate, w_up, w_down, experts_all, collective_id):
    blocks, low, count = lax.axis_size("gx"), jnp.bfloat16, rows.shape[0]
    hidden, width = w_down.shape
    everywhere = pl.BlockSpec(memory_space=pl.ANY)
    block_shape = (2, blocks, count)
    shapes = [
        jax.ShapeDtypeStruct((*block_shape, hidden), low),
        jax.ShapeDtypeStruct((*block_shape, 2 * hidden), low),
        jax.ShapeDtypeStruct((*block_shape, LANES), low),
        jax.ShapeDtypeStruct((width, hidden), jnp.float32),
        jax.ShapeDtypeStruct((width, hidden), jnp.float32),
        jax.ShapeDtypeStruct((hidden, width), jnp.float32),
    ]
    level_rows = 2 * PLANE * count
    dma = pltpu.SemaphoreType.DMA
    return pl.pallas_call(
        functools.partial(experts_kernel, experts_all),
        out_shape=shapes,
        in_specs=[everywhere] * 5 + [pl.BlockSpec(memory_space=pltpu.VMEM)],
        out_specs=[everywhere] * 6,
        scratch_shapes=[
            pltpu.VMEM((*block_shape, rows.shape[1]), low),
            pltpu.VMEM((2, 2, PLANE, count, width), low),
            pltpu.VMEM((width, 2 * hidden), low),
            pltpu.VMEM((2 * hidden, level_rows), low),
            pltpu.VMEM((hidden, level_rows), low),
            *[pltpu.VMEM(shape.shape, low) for shape in shapes[:3]],
            pltpu.VMEM((2 * hidden, width), jnp.float32),
            pltpu.VMEM((hidden, width), jnp.float32),
            pltpu.VMEM((2, width, hidden), jnp.float32),
            dma((2, 2)),
            dma((2,)),
            dma((LEVELS, 3)),
            dma((width // 256, 3)),
            *gather_semaphores(1, 1),
        ],
        compiler_params=pltpu.CompilerParams(
            collective_id=collective_id, has_side_effects=True, vmem_limit_bytes=63 * 1024 * 1024
        ),
    )(rows, grads_own, grads_pair, w_gate, w_up, w_down)


def scatter_kernel(plan, *refs):
    paired, factors, turned, count, gains = plan
    refs = list(refs)

    def take(number):
        taken = refs[:number]
        del refs[:number]
        return taken

    left = take(1)[0] if factors else None
    rights = take(factors)
    pieces = [take(count) for _ in range(1 + paired)]
    gain_ref = take(1)[0] if gains else None
    (out,) = take(1)
    gain_out = take(1)[0] if gains else None
    mine, half_y, half_x, full_x, full_y, slots_a, slots_b, side_b = take(8)
    send_sem, recv_sem, chain_send, chain_recv, load_sem = take(5)
    if paired:
        sibling, away, pair_send, pair_recv, ready_sem = take(5)
    if factors:
        right, right_sem = take(2)
    if gains:
        gain_slots, gain_send, gain_recv = take(3)
    me, core, level, x_side, y_side = neighbours()
    rows, width = mine.shape[1:]
    whole_a, half_a, whole_b, half_b = cut_rows(rows)
    far = me + 2 * PLANE - 4 * PLANE * (level // 2)
    greet(level, (x_side, y_side) + ((far,) if gains else ()), paired or gains, me, core)
    up, down = (me + PLANE, core), (me - PLANE, core)
    to_x, to_y = (x_side, core), (y_side, core)
    x_at, y_at, own_at = x_side % PLANE, y_side % PLANE, me % PLANE
    diagonal_at = (x_side + y_side - me) % PLANE
    forward = jnp.where(level < 2, 1, 0)
    order = [3 * forward, 2 * forward + (1 - forward), level + 1 - 2 * (level % 2), level]
    turns = range(LEVELS)
    sent = []

    def send(condition, source, target_ref, ssem, rsem, target):
        def copy():
            return pltpu.make_async_remote_copy(
                source, target_ref, ssem, rsem, device_id=target, device_id_type=MESH
            )

        when(condition, lambda: copy().start())
        sent.append((condition, copy))

    def arrive(condition, target_ref, rsem):
        def wait():
            pltpu.make_async_remote_copy(
                target_ref, target_ref, rsem, rsem, device_id=to_x, device_id_type=MESH
            ).wait_recv()

        when(condition, wait)

    def add(condition, height, target, *terms, step=16):
        def run():
            def body(i, carry):
                at = pl.multiple_of(i * step, step)
                total = target(at, step)[...].astype(jnp.float32)
                for term in terms:
                    total = total + term(at, step)[...].astype(jnp.float32)
                target(at, step)[...] = total.astype(jnp.bfloat16)
                return carry

            lax.fori_loop(0, height // step, body, 0)

        when(condition, run)

    def rows_of(ref, *index, start=0):
        return lambda at, step: ref.at[(*index, pl.ds(start + at, step))]

    def level_of(ref, turn):
        return ref.at[pl.ds(PLANE * order[turn], PLANE)]

    def load(half, turn):
        copies, lane = [], width - sum(piece.shape[2] for piece in pieces[half])
        for i, piece in enumerate(pieces[half]):
            place = (away if half else mine).at[pl.ds(PLANE * order[turn], PLANE), :, pl.ds(lane, piece.shape[2])]
            copies.append(pltpu.make_async_copy(level_of(piece, turn), place, load_sem.at[half, i, turn]))
            lane += piece.shape[2]
        return copies

    def right_copy(i):
        depth = rights[i].shape[1] if turned else rights[i].shape[0]
        place = right.at[:, pl.ds(i * depth, depth)] if turned else right
        return pltpu.make_async_copy(rights[i], place, right_sem.at[i])

    def hand(turn):
        return pltpu.make_async_remote_copy(
            level_of(away, turn),
            level_of(sibling, turn),
            pair_send.at[turn],
            pair_recv.at[turn],
            device_id=(me, 1 - core),
            device_id_type=MESH,
        )

    def produce(half, turn):
        first = PLANE * order[turn]
        wide = 256
        factor = left[half, pl.ds(first, PLANE)].reshape(PLANE * rows, left.shape[-1])

        def body(step, carry):
            span = pl.ds(pl.multiple_of(step * wide, wide), wide)
            value = dot_nt(factor, right[span]) if turned else dot_nn(factor, right[:, span])
            value = value.reshape(PLANE, rows, wide)
            if half == 0:
                value = value + sibling[pl.ds(first, PLANE), :, span].astype(jnp.float32)
            target = away if half else mine
            target[pl.ds(first, PLANE), :, span] = value.astype(jnp.bfloat16)
            return carry

        lax.fori_loop(0, (right.shape[0] if turned else right.shape[1]) // wide, body, 0)

    def hand_over(turn):
        if not paired:
            return
        if factors:
            produce(1, turn)
        for copy in load(1, turn):
            copy.wait()
        hand(turn).start()

    def settle(turn):
        for copy in load(0, turn):
            copy.wait()
        if not paired:
            return
        hand(turn).wait()
        if factors:
            produce(0, turn)
            lane = right.shape[0] if turned else right.shape[1]
        else:
            lane = 0
        if lane < width:
            first = PLANE * order[turn]
            span = pl.ds(lane, width - lane)
            for column in range(PLANE):
                mine[first + column, :, span] = (
                    mine[first + column, :, span].astype(jnp.float32)
                    + sibling[first + column, :, span].astype(jnp.float32)
                ).astype(jnp.bfloat16)

    sems = [[(send_sem.at[6 * turn + i], recv_sem.at[6 * turn + i]) for i in range(6)] for turn in turns]
    height = half_a[0][1]

    def scatter_first(turn):
        first = PLANE * order[turn]
        at, lower, upper = sems[turn], pl.ds(*half_a[0]), pl.ds(*half_a[1])
        send(None, mine.at[first + diagonal_at, lower], half_y.at[turn], *at[0], to_y)
        send(None, mine.at[first + diagonal_at, upper], half_x.at[turn], *at[1], to_x)
        send(None, mine.at[first + x_at, upper], full_x.at[turn, upper], *at[2], to_x)
        send(None, mine.at[first + y_at, lower], full_y.at[turn, lower], *at[3], to_y)

    def scatter_second(turn):
        first = PLANE * order[turn]
        at, lower, upper = sems[turn], pl.ds(*half_a[0]), pl.ds(*half_a[1])
        arrive(None, half_y.at[turn], at[0][1])
        add(None, height, rows_of(mine, first + x_at), rows_of(half_y, turn))
        send(None, mine.at[first + x_at, lower], full_x.at[turn, lower], *at[4], to_x)
        arrive(None, half_x.at[turn], at[1][1])
        add(None, height, rows_of(mine, first + y_at, start=height), rows_of(half_x, turn))
        send(None, mine.at[first + y_at, upper], full_y.at[turn, upper], *at[5], to_y)

    def chain(which, turn, block, slots, spread):
        to_level = order[turn]
        rising, falling = to_level > level, to_level < level
        begins = (rising & (level == 0)) | (falling & (level == LEVELS - 1))
        middle = (rising | falling) & jnp.logical_not(begins)
        arrive(middle, slots.at[to_level], chain_recv.at[which, to_level])
        spread(middle, to_level)
        outgoing = chain_send.at[which, to_level]
        send(rising, block, slots.at[to_level], outgoing, chain_recv.at[which, to_level], up)
        at = jnp.where(to_level == level - 1, LEVELS, to_level)
        send(falling, block, slots.at[at], outgoing, chain_recv.at[which, at], down)

    def add_small(condition, first, slot):
        for column in range(PLANE):
            add(
                condition,
                whole_b[1],
                rows_of(mine, first + column, start=whole_b[0]),
                rows_of(slots_b, slot, column),
            )

    def chain_small(turn):
        first = PLANE * order[turn]
        block = mine.at[pl.ds(first, PLANE), pl.ds(*whole_b)]
        chain(1, turn, block, slots_b, lambda condition, slot: add_small(condition, first, slot))

    def plane_arrives(turn):
        at, lower, upper = sems[turn], pl.ds(*half_a[0]), pl.ds(*half_a[1])
        arrive(None, full_x.at[turn, upper], at[2][1])
        arrive(None, full_y.at[turn, lower], at[3][1])
        arrive(None, full_x.at[turn, lower], at[4][1])
        arrive(None, full_y.at[turn, upper], at[5][1])

    def chain_large(turn):
        own = PLANE * order[turn] + own_at
        plane_arrives(turn)
        add(None, whole_a[1], rows_of(mine, own), rows_of(full_x, turn), rows_of(full_y, turn))
        chain(
            0,
            turn,
            mine.at[own, pl.ds(*whole_a)],
            slots_a,
            lambda condition, slot: add(condition, whole_a[1], rows_of(mine, own), rows_of(slots_a, slot)),
        )

    gain_partners = ((me, 1 - core), to_x, to_y, (me + PLANE - 2 * PLANE * (level % 2), core), (far, core))

    def gain_copy(turn):
        return pltpu.make_async_remote_copy(
            gain_slots.at[2 * turn],
            gain_slots.at[2 * turn + 1],
            gain_send.at[turn],
            gain_recv.at[turn],
            device_id=gain_partners[turn],
            device_id_type=MESH,
        )

    def gain_step(turn):
        if not gains:
            return
        if turn == 0:
            gain_slots[0] = gain_ref[...]
        else:
            gain_copy(turn - 1).wait_recv()
            gain_slots[2 * turn] = gain_slots[2 * turn - 2] + gain_slots[2 * turn - 1]
        if turn < len(gain_partners):
            gain_copy(turn).start()
        else:
            gain_out[...] = gain_slots[2 * turn]

    if factors:
        for i in range(factors):
            right_copy(i).start()
    for turn in turns:
        for half in range(1 + paired):
            for copy in load(half, turn):
                copy.start()
    if factors:
        for i in range(factors):
            right_copy(i).wait()
    gain_step(0)
    hand_over(0)
    if paired:
        hand_over(1)
    for turn in turns:
        settle(turn)
        scatter_first(turn)
        if turn < LEVELS - 1 and not paired:
            chain_small(turn)
        if turn + 2 < LEVELS:
            hand_over(turn + 2)
        if paired:
            if turn < LEVELS - 1:
                chain_small(turn)
            if turn >= 1:
                scatter_second(turn - 1)
            if turn >= 2:
                chain_large(turn - 2)
    if not paired:
        for turn in range(LEVELS - 1):
            scatter_second(turn)
            gain_step(turn + 1)
            if turn:
                chain_large(turn - 1)
    scatter_second(LEVELS - 1)
    gain_step(4)
    chain_large(LEVELS - 2)

    first = PLANE * level
    own = first + own_at
    arrivals = ((level > 0, level), (level < LEVELS - 1, LEVELS))
    for condition, slot in arrivals:
        arrive(condition, slots_b.at[slot], chain_recv.at[1, slot])
        add_small(condition, first, slot)
    side = [(send_sem.at[24 + i], recv_sem.at[24 + i]) for i in range(4)]
    short = half_b[0][1]
    spans = [pl.ds(0, short), pl.ds(short, short), pl.ds(2 * short, 2 * short), pl.ds(4 * short, 2 * short)]
    send(None, mine.at[first + diagonal_at, pl.ds(*half_b[0])], side_b.at[spans[0]], *side[0], to_y)
    send(None, mine.at[first + diagonal_at, pl.ds(*half_b[1])], side_b.at[spans[1]], *side[1], to_x)
    plane_arrives(LEVELS - 1)
    arrive(None, side_b.at[spans[0]], side[0][1])
    add(None, short, rows_of(mine, first + x_at, start=half_b[0][0]), rows_of(side_b))
    send(None, mine.at[first + x_at, pl.ds(*whole_b)], side_b.at[spans[2]], *side[2], to_x)
    arrive(None, side_b.at[spans[1]], side[1][1])
    add(None, short, rows_of(mine, first + y_at, start=half_b[1][0]), rows_of(side_b, start=short))
    send(None, mine.at[first + y_at, pl.ds(*whole_b)], side_b.at[spans[3]], *side[3], to_y)
    gain_step(5)
    base = core * rows if paired else 0
    step = 16

    def tail_a(i, carry):
        at = pl.multiple_of(i * step, step)
        span = pl.ds(at, step)
        total = mine[own, span].astype(jnp.float32)
        total = total + full_x[LEVELS - 1, span].astype(jnp.float32) + full_y[LEVELS - 1, span].astype(jnp.float32)
        out[pl.ds(pl.multiple_of(base + at, step), step)] = total
        return carry

    lax.fori_loop(0, whole_a[1] // step, tail_a, 0)
    for condition, slot in arrivals:
        arrive(condition, slots_a.at[slot], chain_recv.at[0, slot])

        def more(slot=slot):
            def body(i, carry):
                at = pl.multiple_of(i * step, step)
                span = pl.ds(pl.multiple_of(base + at, step), step)
                out[span] = out[span] + slots_a[slot, pl.ds(at, step)].astype(jnp.float32)
                return carry

            lax.fori_loop(0, whole_a[1] // step, body, 0)

        when(condition, more)
    arrive(None, side_b.at[spans[2]], side[2][1])
    arrive(None, side_b.at[spans[3]], side[3][1])

    def tail_b(i, carry):
        at = pl.multiple_of(i * step, step)
        total = mine[own, pl.ds(whole_b[0] + at, step)].astype(jnp.float32)
        total = total + side_b[pl.ds(2 * short + at, step)].astype(jnp.float32)
        total = total + side_b[pl.ds(4 * short + at, step)].astype(jnp.float32)
        out[pl.ds(pl.multiple_of(base + whole_b[0] + at, step), step)] = total
        return carry

    lax.fori_loop(0, whole_b[1] // step, tail_b, 0)
    if paired:

        def exchange(core_of_rows):
            span = pl.ds(pl.multiple_of(core_of_rows * rows, rows), rows)
            return pltpu.make_async_remote_copy(
                out.at[span],
                out.at[span],
                ready_sem.at[0],
                ready_sem.at[1],
                device_id=(me, 1 - core),
                device_id_type=MESH,
            )

        exchange(core).start()
        exchange(1 - core).wait_recv()
        exchange(core).wait_send()
    if gains:
        for turn in range(len(gain_partners)):
            gain_copy(turn).wait_send()
    for condition, copy in sent:
        when(condition, lambda copy=copy: copy().wait_send())


def scatter_sums(pieces, collective_id, away=(), product=None, gains=None):
    paired, low = bool(away) or product is not None, jnp.bfloat16
    operands, factors, turned, features = [], 0, False, 0
    if product:
        left, rights, turned = product
        features, factors = rights[0].shape[0 if turned else 1], len(rights)
        operands, (blocks, rows) = [left, *rights], left.shape[1:3]
    else:
        blocks, rows = pieces[0].shape[:2]
    width = features + sum(piece.shape[2] for piece in pieces)
    near, remote = 3 * rows // 4, rows // 4
    dma = pltpu.SemaphoreType.DMA
    scratch = [
        pltpu.VMEM((blocks, rows, width), low),
        pltpu.VMEM((LEVELS, near // 2, width), low),
        pltpu.VMEM((LEVELS, near // 2, width), low),
        pltpu.VMEM((LEVELS, near, width), low),
        pltpu.VMEM((LEVELS, near, width), low),
        pltpu.VMEM((LEVELS + 1, near, width), low),
        pltpu.VMEM((LEVELS + 1, PLANE, remote, width), low),
        pltpu.VMEM((3 * remote, width), low),
        *[dma((28,)), dma((28,)), dma((2, 5)), dma((2, 5)), dma((2, max(1, len(pieces)), LEVELS))],
    ]
    if paired:
        whole = pltpu.VMEM((blocks, rows, width), low)
        scratch += [whole, whole, dma((LEVELS,)), dma((LEVELS,)), dma((2,))]
    if factors:
        depth = left.shape[-1]
        scratch += [pltpu.VMEM((features, depth) if turned else (depth, features), low), dma((factors,))]
    vmem, everywhere = pl.BlockSpec(memory_space=pltpu.VMEM), pl.BlockSpec(memory_space=pl.ANY)
    operands += [*pieces, *away]
    in_specs = [everywhere] * len(operands)
    if factors:
        in_specs[0] = vmem
    shapes = [jax.ShapeDtypeStruct(((2 if paired else 1) * rows, width), jnp.float32)]
    if gains is not None:
        operands, in_specs = operands + [gains], in_specs + [vmem]
        shapes.append(jax.ShapeDtypeStruct(gains.shape, gains.dtype))
        scratch += [pltpu.VMEM((11, *gains.shape), gains.dtype), dma((5,)), dma((5,))]
    plan = (paired, factors, turned, len(pieces), gains is not None)
    return pl.pallas_call(
        functools.partial(scatter_kernel, plan),
        out_shape=shapes,
        in_specs=in_specs,
        out_specs=[vmem] * len(shapes),
        scratch_shapes=scratch,
        compiler_params=pltpu.CompilerParams(
            collective_id=collective_id, has_side_effects=True, vmem_limit_bytes=60 * 1024 * 1024
        ),
    )(*operands)


def kernels_fit():
    return lax.axis_size("gx") == LEVELS * PLANE and lax.axis_size("gy") == 2


def packed_gains(vectors):
    rows = jnp.concatenate([vector.reshape(-1, HEAD_DIM) for vector in vectors], axis=0)
    return jnp.pad(rows, ((0, -rows.shape[0] % 8), (0, 0)))


def unpacked_gains(rows, vectors):
    sums, at = [], 0
    for vector in vectors:
        length = vector.shape[0] // HEAD_DIM
        sums.append(rows[at : at + length].reshape(-1))
        at += length
    return sums


def two_parts(values):
    high = lax.reduce_precision(values, 8, 7)
    return high.astype(jnp.bfloat16), (values - high).astype(jnp.bfloat16)


def sparse_experts(normed_ffn, logits, route_hits, routes, cotangent, w_gate, w_up, w_down):
    sequence_length, model_width = normed_ffn.shape
    experts_all = logits.shape[1]
    devices_gx = lax.axis_size("gx")
    part_width = model_width // lax.axis_size("gy")
    capacity = 5 * sequence_length * TOP // (4 * experts_all)
    pairs_count = sequence_length * TOP
    hits_float = route_hits.astype(jnp.float32)
    chosen = jnp.sum(logits[:, None, :] * hits_float, axis=-1)
    gate_exps = jnp.exp(chosen)
    gate_values = gate_exps / jnp.sum(gate_exps, axis=1, keepdims=True)
    flat_hits = route_hits.reshape(pairs_count, experts_all).astype(jnp.int32)
    slot_rank = jnp.sum((jnp.cumsum(flat_hits, axis=0) - flat_hits) * flat_hits, axis=1)
    slot_dest = routes.reshape(-1) * capacity + slot_rank
    slot_pair = (
        jnp.full((experts_all * capacity,), pairs_count, jnp.int32)
        .at[slot_dest]
        .set(jnp.arange(pairs_count, dtype=jnp.int32))
    )
    slot_token = jnp.where(slot_pair < pairs_count, slot_pair // TOP, sequence_length)

    def to_experts(buffer):
        arrived = lax.all_to_all(buffer, "gx", split_axis=0, concat_axis=0, tiled=True)
        return arrived.reshape(devices_gx * capacity, model_width)

    def from_experts(partial_rows):
        share_rows = lax.psum_scatter(
            partial_rows.astype(jnp.bfloat16), "gy", scatter_dimension=1, tiled=True
        )
        returned = lax.all_to_all(
            share_rows.reshape(devices_gx, capacity, part_width),
            "gx",
            split_axis=0,
            concat_axis=0,
            tiled=True,
        )
        whole_rows = lax.all_gather(returned, "gy", axis=2, tiled=True)
        return whole_rows.reshape(devices_gx * capacity, model_width)

    send_rows = jnp.take(normed_ffn, slot_token, axis=0, mode="fill", fill_value=0)
    expert_in = to_experts(send_rows.reshape(devices_gx, capacity, model_width))
    gate_in = jnp.dot(expert_in, w_gate, preferred_element_type=jnp.float32)
    up_in = jnp.dot(expert_in, w_up, preferred_element_type=jnp.float32)
    gate_sigmoid = jax.nn.sigmoid(gate_in)
    gate_swish = gate_in * gate_sigmoid
    activated = (gate_swish * up_in).astype(jnp.bfloat16)
    expert_part = jnp.dot(activated, w_down, preferred_element_type=jnp.float32)
    expert_out = from_experts(expert_part)
    pair_rows = jnp.take(expert_out, slot_dest, axis=0).reshape(sequence_length, TOP, model_width)
    mixed_rows = jnp.einsum(
        "tk,tkd->td", gate_values, pair_rows, preferred_element_type=jnp.float32
    )
    grad_out_f = cotangent.astype(jnp.float32)
    grad_gates = jnp.einsum("td,tkd->tk", grad_out_f, pair_rows, preferred_element_type=jnp.float32)
    grad_chosen = gate_values * (
        grad_gates - jnp.sum(gate_values * grad_gates, axis=1, keepdims=True)
    )
    grad_logits = jnp.sum(grad_chosen[:, :, None] * hits_float, axis=1).astype(jnp.bfloat16)
    slot_gate = jnp.take(gate_values.reshape(-1), slot_pair, mode="fill", fill_value=0.0)
    grad_send = (
        jnp.take(grad_out_f, slot_token, axis=0, mode="fill", fill_value=0) * slot_gate[:, None]
    )
    grad_expert_out = to_experts(
        grad_send.astype(jnp.bfloat16).reshape(devices_gx, capacity, model_width)
    )
    grad_act = contract(grad_expert_out, w_down, 1, 1)
    down_term = contract(activated, grad_expert_out, 0, 0)
    grad_gate_in = (
        grad_act * up_in * gate_sigmoid * (1.0 + gate_in * (1.0 - gate_sigmoid))
    ).astype(jnp.bfloat16)
    grad_up_in = (grad_act * gate_swish).astype(jnp.bfloat16)
    gate_term = contract(expert_in, grad_gate_in, 0, 0)
    up_term = contract(expert_in, grad_up_in, 0, 0)
    grad_in_part = contract(grad_gate_in, w_gate, 1, 1) + contract(grad_up_in, w_up, 1, 1)
    grad_rows = from_experts(grad_in_part)
    grad_pairs = jnp.take(grad_rows, slot_dest, axis=0).reshape(sequence_length, TOP, model_width)
    grad_rows_sum = jnp.sum(grad_pairs.astype(jnp.float32), axis=1)
    return mixed_rows, grad_rows_sum, grad_logits, (gate_term[None], up_term[None], down_term[None])


def swap_cores(rows):
    return lax.ppermute(rows, "gy", [(0, 1), (1, 0)])


def own_half(rows):
    count = rows.shape[0] // lax.axis_size("gy")
    return lax.dynamic_slice_in_dim(rows, lax.axis_index("gy") * count, count, 0)


def dense_experts(normed_ffn, logits, route_hits, grads_own, grads_pair, w_gate, w_up, w_down):
    sequence_length, model_width = normed_ffn.shape
    experts_all = logits.shape[1]
    gate_exps = jnp.exp(jnp.where(jnp.any(route_hits, axis=1), logits, -1e30))
    gate_all = gate_exps / jnp.sum(gate_exps, axis=1, keepdims=True)
    gate_lanes = jnp.pad(jnp.concatenate(two_parts(gate_all), axis=1), ((0, 0), (0, LANES - 2 * experts_all)))
    row_lanes = jnp.concatenate([own_half(normed_ffn), own_half(gate_lanes)], axis=1)
    weighted, grad_in, terms, gate_term, up_term, down_term = experts_products(
        row_lanes, grads_own, grads_pair, w_gate, w_up, w_down, experts_all, 2
    )
    (back,) = scatter_sums([terms[0]], 3, [terms[1]], (grad_in, (w_gate, w_up), True))
    (mixed_rows,) = scatter_sums([], 4, [], (weighted, (w_down,), False))
    term_lanes = back[:, model_width : model_width + 4 * experts_all]
    grad_gates = jnp.sum(term_lanes.reshape(sequence_length, 4, experts_all), axis=1)
    grad_logits = (
        gate_all * (grad_gates - jnp.sum(gate_all * grad_gates, axis=1, keepdims=True))
    ).astype(jnp.bfloat16)
    return mixed_rows, back[:, :model_width], grad_logits, (gate_term[None], up_term[None], down_term[None])


def on_device(
    tokens_in,
    doc_ids,
    routes,
    q_weight,
    key_matrix,
    value_matrix,
    out_weight,
    router_weight,
    attn_gain,
    ffn_gain,
    query_norm_gain,
    k_gain,
    gate_weight,
    up_weight,
    down_weight,
    cotangent,
):
    sequence_length = tokens_in.shape[0]
    model_width = tokens_in.shape[1]
    devices_gx = lax.axis_size("gx")
    devices_gy = lax.axis_size("gy")
    part_width = model_width // devices_gy
    experts_all = router_weight.shape[1]
    query_group_count = QUERY_HEADS // KEY_VALUE_HEADS
    inv_root = 1.0 / math.sqrt(HEAD_DIM)
    router_lanes = jnp.pad(router_weight, ((0, 0), (0, LANES - experts_all)))
    rows_local = jnp.concatenate([q_weight, key_matrix, value_matrix, router_lanes, out_weight], axis=1)
    dense = kernels_fit() and experts_all <= 2 * TOP
    if dense:
        weights_all, grads_own, grads_pair = gather_blocks([rows_local, own_half(cotangent)], (0, 1), 1)
        weights_all = weights_all.reshape(-1, rows_local.shape[1])
    else:
        weights_all = lax.all_gather(rows_local, "gx", axis=0, tiled=True)
    q_width, kv_width = q_weight.shape[1], key_matrix.shape[1]
    qkv_width = q_width + 2 * kv_width
    qkv_full = weights_all[:, :qkv_width]
    router_full = weights_all[:, qkv_width : qkv_width + experts_all]
    o_full = weights_all[:, qkv_width + LANES :]
    heads_local = q_width // HEAD_DIM
    kv_local = kv_width // HEAD_DIM
    inputs_f = tokens_in.astype(jnp.float32)
    scale_one = root_mean_scale(inputs_f)
    unit_one = inputs_f * scale_one
    normalized_input = (unit_one * attn_gain).astype(jnp.bfloat16)
    qkv_rows = jnp.dot(normalized_input, qkv_full, preferred_element_type=jnp.float32)
    query_unrotated = qkv_rows[:, :q_width].reshape(sequence_length, heads_local, HEAD_DIM)
    key_unrotated = qkv_rows[:, q_width : q_width + kv_width].reshape(sequence_length, kv_local, HEAD_DIM)
    value_rows = (
        qkv_rows[:, q_width + kv_width :].astype(jnp.bfloat16).reshape(sequence_length, kv_local, HEAD_DIM)
    )
    cosine, sine_table = rotary_tables(sequence_length, HEAD_DIM)
    q_scale = root_mean_scale(query_unrotated)
    q_unit = query_unrotated * q_scale
    query_rows = (
        rotate(q_unit * query_norm_gain, cosine, sine_table)
        .astype(jnp.bfloat16)
        .reshape(sequence_length, kv_local, query_group_count, HEAD_DIM)
    )
    k_scale = root_mean_scale(key_unrotated)
    k_unit = key_unrotated * k_scale
    keys_rows = rotate(k_unit * k_gain, cosine, sine_table).astype(jnp.bfloat16)
    positions = jnp.arange(sequence_length)
    documents = doc_ids[0]
    allowed = (positions[None, :] <= positions[:, None]) & (
        documents[None, :] == documents[:, None]
    )

    def score_block():
        raw_scores = (
            jnp.einsum("qngd,knd->ngqk", query_rows, keys_rows, preferred_element_type=jnp.float32)
            * inv_root
        )
        return jnp.where(allowed, raw_scores, -1e30)

    scores = score_block()
    row_peak = jnp.max(scores, axis=-1, keepdims=True)
    attn_exps = jnp.exp(scores - row_peak)
    row_total = jnp.sum(attn_exps, axis=-1, keepdims=True)
    log_total = row_peak + jnp.log(row_total)
    probs_low = (attn_exps / row_total).astype(jnp.bfloat16)
    attended = jnp.einsum(
        "ngqk,knd->qngd", probs_low, value_rows, preferred_element_type=jnp.float32
    )
    attended = attended.reshape(sequence_length, heads_local * HEAD_DIM).astype(jnp.bfloat16)
    attn_part = contract(attended, o_full, 1, 1)
    attn_total = attn_part + swap_cores(attn_part)
    residual = inputs_f + attn_total
    scale_two = root_mean_scale(residual)
    unit_two = residual * scale_two
    normed_ffn = (unit_two * ffn_gain).astype(jnp.bfloat16)
    logits = jnp.dot(normed_ffn, router_full, preferred_element_type=jnp.float32)
    expert_iota = jnp.arange(experts_all, dtype=jnp.int32)
    route_hits = routes[:, :, None] == expert_iota
    if dense:
        mixed_rows, grad_rows_sum, grad_logits, expert_grads = dense_experts(
            normed_ffn, logits, route_hits, grads_own, grads_pair, gate_weight[0], up_weight[0], down_weight[0]
        )
    else:
        mixed_rows, grad_rows_sum, grad_logits, expert_grads = sparse_experts(
            normed_ffn, logits, route_hits, routes, cotangent, gate_weight[0], up_weight[0], down_weight[0]
        )
    output = (residual + mixed_rows).astype(jnp.bfloat16)
    grad_out_f = cotangent.astype(jnp.float32)
    router_term = contract(normed_ffn, grad_logits, 0, 0)
    grad_ffn_in = contract(grad_logits, router_full, 1, 1) + grad_rows_sum
    ffn_gain_term = jnp.sum(grad_ffn_in * unit_two, axis=0)
    grad_residual = grad_out_f + norm_back(grad_ffn_in * ffn_gain, unit_two, scale_two)
    grad_attn = grad_residual.astype(jnp.bfloat16)
    out_term = contract(grad_attn, attended, 0, 0)
    grad_attended = jnp.dot(grad_attn, o_full, preferred_element_type=jnp.float32).astype(
        jnp.bfloat16
    )
    grad_attended = grad_attended.reshape(sequence_length, kv_local, query_group_count, HEAD_DIM)
    probs_again = jnp.exp(score_block() - log_total)
    probs_again_low = probs_again.astype(jnp.bfloat16)
    grad_values = jnp.einsum(
        "ngqk,qngd->knd", probs_again_low, grad_attended, preferred_element_type=jnp.float32
    )
    grad_probs = jnp.einsum(
        "qngd,knd->ngqk", grad_attended, value_rows, preferred_element_type=jnp.float32
    )
    prob_inner = jnp.sum(probs_again * grad_probs, axis=-1, keepdims=True)
    grad_scores = (probs_again * (grad_probs - prob_inner)).astype(jnp.bfloat16)
    grad_queries = (
        jnp.einsum("ngqk,knd->qngd", grad_scores, keys_rows, preferred_element_type=jnp.float32)
        * inv_root
    )
    grad_keys = (
        jnp.einsum("ngqk,qngd->knd", grad_scores, query_rows, preferred_element_type=jnp.float32)
        * inv_root
    )
    grad_q_rot = rotate(
        grad_queries.reshape(sequence_length, heads_local, HEAD_DIM), cosine, -sine_table
    )
    grad_k_rot = rotate(grad_keys, cosine, -sine_table)
    q_gain_term = jnp.sum(grad_q_rot * q_unit, axis=(0, 1))
    k_gain_term = jnp.sum(grad_k_rot * k_unit, axis=(0, 1))
    grad_q_raw = (
        norm_back(grad_q_rot * query_norm_gain, q_unit, q_scale)
        .astype(jnp.bfloat16)
        .reshape(sequence_length, heads_local * HEAD_DIM)
    )
    grad_k_raw = (
        norm_back(grad_k_rot * k_gain, k_unit, k_scale)
        .astype(jnp.bfloat16)
        .reshape(sequence_length, kv_local * HEAD_DIM)
    )
    grad_v_raw = grad_values.astype(jnp.bfloat16).reshape(sequence_length, kv_local * HEAD_DIM)
    grad_qkv = jnp.concatenate([grad_q_raw, grad_k_raw, grad_v_raw], axis=1)
    qkv_term = contract(normalized_input, grad_qkv, 0, 0)
    grad_normed_part = contract(grad_qkv, qkv_full, 1, 1)
    grad_normed = grad_normed_part + swap_cores(grad_normed_part)
    attn_gain_term = jnp.sum(grad_normed * unit_one, axis=0)
    grad_input = (grad_residual + norm_back(grad_normed * attn_gain, unit_one, scale_one)).astype(
        jnp.bfloat16
    )
    own_mask = (jnp.arange(model_width) // part_width == lax.axis_index("gy")).astype(jnp.float32)
    gains = (attn_gain_term * own_mask, ffn_gain_term * own_mask, q_gain_term, k_gain_term)
    router_lanes = jnp.pad(router_term, ((0, 0), (0, LANES - experts_all)))
    if dense:
        pieces = [
            term.astype(jnp.bfloat16).reshape(devices_gx, -1, term.shape[1])
            for term in (qkv_term, router_lanes, out_term)
        ]
        sums, gain_rows = scatter_sums(pieces, 5, gains=packed_gains(gains))
        gains = unpacked_gains(gain_rows, gains)
    else:
        sums = jnp.concatenate(
            [
                lax.psum_scatter(term, "gx", scatter_dimension=0, tiled=True)
                for term in (qkv_term, router_lanes, out_term)
            ],
            axis=1,
        )
        gains = lax.psum(gains, ("gx", "gy"))
    gain_attn, gain_ffn, gain_query, gain_key = gains
    grad_q = sums[:, :q_width]
    grad_k = sums[:, q_width : q_width + kv_width]
    grad_v = sums[:, q_width + kv_width : qkv_width]
    grad_router = sums[:, qkv_width : qkv_width + experts_all]
    grad_out = sums[:, qkv_width + LANES :]
    return (
        output,
        grad_input,
        grad_q,
        grad_k,
        grad_v,
        grad_out,
        grad_router,
        gain_attn,
        gain_ffn,
        gain_query,
        gain_key,
        expert_grads[0],
        expert_grads[1],
        expert_grads[2],
    )


def solution(mesh):
    return jax.shard_map(
        on_device,
        mesh=mesh,
        in_specs=(
            P("gx", None),
            P("gx", None),
            P("gx", None),
            P("gx", "gy"),
            P("gx", "gy"),
            P("gx", "gy"),
            P("gx", "gy"),
            P("gx", None),
            P(),
            P(),
            P(),
            P(),
            P("gx", None, "gy"),
            P("gx", None, "gy"),
            P("gx", "gy", None),
            P("gx", None),
        ),
        out_specs=(
            P("gx", None),
            P("gx", None),
            P("gx", "gy"),
            P("gx", "gy"),
            P("gx", "gy"),
            P("gx", "gy"),
            P("gx", None),
            P(),
            P(),
            P(),
            P(),
            P("gx", None, "gy"),
            P("gx", None, "gy"),
            P("gx", "gy", None),
        ),
        check_vma=False,
    )
```

```python
import functools
import math

import jax
import jax.numpy as jnp
from jax import lax
from jax.experimental import pallas as pl
from jax.experimental.pallas import tpu as pltpu
from jax.sharding import PartitionSpec as P

QUERY_HEADS = 32
KEY_VALUE_HEADS = 4
HEAD_DIM = 128
LANES = 128
TOP = 8


EPSILON = 1e-06
THETA = 1000000.0


def root_mean_scale(values):
    return lax.rsqrt(jnp.mean(values * values, axis=-1, keepdims=True) + EPSILON)


def rotary_tables(sequence_length, head_width):
    half_width = head_width // 2
    frequencies = THETA ** (-(2.0 * jnp.arange(half_width, dtype=jnp.float32)) / head_width)
    angles = jnp.arange(sequence_length, dtype=jnp.float32)[:, None] * frequencies[None, :]
    return (jnp.cos(angles)[:, None, :], jnp.sin(angles)[:, None, :])


def norm_back(grad_normed, normed_unit, scale_rows):
    return scale_rows * (
        grad_normed - normed_unit * jnp.mean(grad_normed * normed_unit, axis=-1, keepdims=True)
    )


def contract(first_op, second_op, first_dim, second_dim):
    return lax.dot_general(
        first_op,
        second_op,
        (((first_dim,), (second_dim,)), ((), ())),
        preferred_element_type=jnp.float32,
    )


MESH = pl.DeviceIdType.MESH
LEVELS = 4
PLANE = 4


def cut_rows(rows):
    near, far = 3 * rows // 4, rows // 4
    return (
        (0, near),
        ((0, near // 2), (near // 2, near // 2)),
        (near, far),
        ((near, far // 2), (near + far // 2, far // 2)),
    )


def neighbours():
    me, core = lax.axis_index("gx"), lax.axis_index("gy")
    level = me // PLANE
    x_side = me + 1 - 2 * (me % 2)
    y_side = me + 2 - 4 * ((me // 2) % 2)
    return me, core, level, x_side, y_side


def greet(level, targets, with_core, me, core):
    barrier = pltpu.get_barrier_semaphore()

    def hello(device):
        pl.semaphore_signal(barrier, inc=1, device_id=device, device_id_type=MESH)

    for target in targets:
        hello((target, core))
    if with_core:
        hello((me, 1 - core))

    @pl.when(level > 0)
    def _():
        hello((me - PLANE, core))

    @pl.when(level < LEVELS - 1)
    def _():
        hello((me + PLANE, core))

    inner = jnp.where(level > 0, 1, 0) + jnp.where(level < LEVELS - 1, 1, 0)
    pl.semaphore_wait(barrier, len(targets) + int(with_core) + inner)


def when(condition, action):
    if condition is None:
        action()
    else:
        pl.when(condition)(action)


def gather_kernel(count, with_pair, *refs):
    paired = sum(with_pair)
    ins, outs, pairs = refs[:count], refs[count : 2 * count], list(refs[2 * count : 2 * count + paired])
    pairs = [pairs.pop(0) if wanted else None for wanted in with_pair]
    sems = refs[2 * count + paired :]
    steps = gather_steps(ins, outs, pairs, sems)
    for step in steps.order:
        step()
    steps.end()


class gather_steps:
    def __init__(self, ins, outs, pairs, sems):
        self.ins, self.outs, self.pairs = ins, outs, pairs
        self.send_sem, self.recv_sem, self.local_sem, self.pair_send, self.pair_recv = sems
        self.me, self.core, self.level, self.x_side, self.y_side = neighbours()
        self.diagonal = self.x_side + self.y_side - self.me
        self.spans = cut_rows(ins[0].shape[0])
        self.has_up, self.has_down = self.level < LEVELS - 1, self.level > 0
        self.up, self.down = (self.me + PLANE, self.core), (self.me - PLANE, self.core)
        self.to_x, self.to_y = (self.x_side, self.core), (self.y_side, self.core)
        self.sent, self.mirrored, self.everyone = [], [], range(len(ins))
        greet(self.level, (self.x_side, self.y_side), any(p is not None for p in pairs), self.me, self.core)
        self.order = [
            self.start,
            self.side_small,
            lambda: self.column(1),
            lambda: self.cross(0),
            lambda: self.column(2),
            self.start_planes,
            lambda: self.cross(1),
            lambda: self.column(3),
            lambda: self.planes(1),
            lambda: self.cross(2),
            lambda: self.planes(2),
            lambda: self.cross(3),
            lambda: self.planes(3),
            lambda: [self.halves(step) for step in range(LEVELS)],
        ]

    def send(self, condition, k, slot, source, first, number, span, target):
        def copy():
            there = self.outs[k].at[pl.ds(first, number), pl.ds(*span)]
            here = there
            if source == "own":
                here, there = self.ins[k].at[pl.ds(*span)], self.outs[k].at[first, pl.ds(*span)]
            return pltpu.make_async_remote_copy(
                here,
                there,
                self.send_sem.at[k, slot],
                self.recv_sem.at[k, slot],
                device_id=target,
                device_id_type=MESH,
            )

        when(condition, lambda: copy().start())
        self.sent.append((condition, copy))

    def mirror(self, condition, k, first, number, span, group):
        if self.pairs[k] is None:
            return
        slot = len(self.mirrored)

        def copy():
            return pltpu.make_async_remote_copy(
                self.outs[k].at[pl.ds(first, number), pl.ds(*span)],
                self.pairs[k].at[pl.ds(first, number), pl.ds(*span)],
                self.pair_send.at[slot],
                self.pair_recv.at[slot],
                device_id=(self.me, 1 - self.core),
                device_id_type=MESH,
            )

        when(condition, lambda: copy().start())
        self.mirrored.append((condition, copy, group))

    def arrive(self, condition, k, slot, first, number, span, group):
        place = self.outs[k].at[pl.ds(first, number), pl.ds(*span)]

        def wait():
            pltpu.make_async_remote_copy(
                place,
                place,
                self.send_sem.at[k, slot],
                self.recv_sem.at[k, slot],
                device_id=self.to_x,
                device_id_type=MESH,
            ).wait_recv()

        when(condition, wait)
        self.mirror(condition, k, first, number, span, group)

    def members(self, step):
        if step == 0:
            return [(None, 0, 0)]
        return [(self.level >= step, step, -step), (self.level + step < LEVELS, 3 + step, step)]

    def slot_of(self, group, index):
        return 6 + 7 * group + index

    last = 6 + 28

    def own_copy(self, k):
        return pltpu.make_async_copy(self.ins[k], self.outs[k].at[self.me], self.local_sem.at[k])

    def start(self):
        whole_a, half_a, whole_b, half_b = self.spans
        last, me = self.last, self.me
        for k in self.everyone:
            self.own_copy(k).start()
            self.send(None, k, last, "own", me, 1, whole_b, self.to_x)
            self.send(None, k, last + 1, "own", me, 1, whole_b, self.to_y)
            self.send(self.has_up, k, 0, "own", me, 1, whole_a, self.up)
            self.send(self.has_down, k, 3, "own", me, 1, whole_a, self.down)
            self.send(None, k, self.slot_of(0, 0), "own", me, 1, whole_a, self.to_x)
            self.send(None, k, self.slot_of(1, 0), "own", me, 1, whole_a, self.to_y)

    def side_small(self):
        whole_a, half_a, whole_b, half_b = self.spans
        last = self.last
        for k in self.everyone:
            self.arrive(None, k, last, self.x_side, 1, whole_b, 0)
            self.send(None, k, last + 3, "out", self.x_side, 1, half_b[1], self.to_y)
            self.arrive(None, k, last + 1, self.y_side, 1, whole_b, 0)
            self.send(None, k, last + 2, "out", self.y_side, 1, half_b[0], self.to_x)
        for k in self.everyone:
            self.own_copy(k).wait()
            self.mirror(None, k, self.me, 1, (0, self.ins[k].shape[0]), 0)
            self.arrive(None, k, last + 2, self.diagonal, 1, half_b[0], 0)
            self.arrive(None, k, last + 3, self.diagonal, 1, half_b[1], 0)

    def start_planes(self):
        whole_b = self.spans[2]
        for k in self.everyone:
            self.send(self.has_up, k, self.last + 4, "out", PLANE * self.level, PLANE, whole_b, self.up)
            self.send(self.has_down, k, self.last + 7, "out", PLANE * self.level, PLANE, whole_b, self.down)

    def cross(self, step):
        whole_a, half_a = self.spans[:2]
        for k in self.everyone:
            for condition, index, distance in self.members(step):
                first = self.x_side + PLANE * distance
                self.arrive(condition, k, self.slot_of(0, index), first, 1, whole_a, distance)
                self.send(condition, k, self.slot_of(3, index), "out", first, 1, half_a[1], self.to_y)
                first = self.y_side + PLANE * distance
                self.arrive(condition, k, self.slot_of(1, index), first, 1, whole_a, distance)
                self.send(condition, k, self.slot_of(2, index), "out", first, 1, half_a[0], self.to_x)

    def halves(self, step):
        half_a = self.spans[1]
        for k in self.everyone:
            for condition, index, distance in self.members(step):
                first = self.diagonal + PLANE * distance
                self.arrive(condition, k, self.slot_of(2, index), first, 1, half_a[0], distance)
                self.arrive(condition, k, self.slot_of(3, index), first, 1, half_a[1], distance)

    def column(self, step):
        whole_a = self.spans[0]
        for k in self.everyone:
            for condition, index, distance in self.members(step):
                first = self.me + PLANE * distance
                rising = distance < 0
                self.arrive(condition, k, step - 1 if rising else 2 + step, first, 1, whole_a, distance)
                if step < LEVELS - 1:
                    onward = condition & (self.has_up if rising else self.has_down)
                    slot = step if rising else 3 + step
                    self.send(onward, k, slot, "out", first, 1, whole_a, self.up if rising else self.down)
                self.send(condition, k, self.slot_of(0, index), "out", first, 1, whole_a, self.to_x)
                self.send(condition, k, self.slot_of(1, index), "out", first, 1, whole_a, self.to_y)

    def planes(self, step):
        whole_b = self.spans[2]
        for k in self.everyone:
            for condition, index, distance in self.members(step):
                first = PLANE * (self.level + distance)
                rising = distance < 0
                self.arrive(condition, k, self.last + (3 if rising else 6) + step, first, PLANE, whole_b, distance)
                if step < LEVELS - 1:
                    onward = condition & (self.has_up if rising else self.has_down)
                    slot = self.last + (4 if rising else 7) + step
                    self.send(onward, k, slot, "out", first, PLANE, whole_b, self.up if rising else self.down)

    def paired_level(self, distance):
        for condition, copy, group in self.mirrored:
            if group == distance:
                when(condition, lambda copy=copy: copy().wait_recv())

    def end(self, levels_waited=False):
        for condition, copy in self.sent:
            when(condition, lambda copy=copy: copy().wait_send())
        for condition, copy, group in self.mirrored:
            when(condition, lambda copy=copy: copy().wait_send())
            if not levels_waited:
                when(condition, lambda copy=copy: copy().wait_recv())


GATHER_SLOTS = 6 + 28 + 10


def gather_semaphores(count, paired):
    dma = pltpu.SemaphoreType.DMA
    slots = (count, GATHER_SLOTS)
    pair_slots = (max(1, paired * (GATHER_SLOTS + 1)),)
    return [dma(slots), dma(slots), dma((count,)), dma(pair_slots), dma(pair_slots)]


def gather_blocks(arrays, with_pair, collective_id):
    count, blocks, paired = len(arrays), lax.axis_size("gx"), sum(with_pair)
    shapes = [jax.ShapeDtypeStruct((blocks, *a.shape), a.dtype) for a in arrays]
    shapes += [shape for shape, wanted in zip(shapes, with_pair) if wanted]
    return pl.pallas_call(
        functools.partial(gather_kernel, count, with_pair),
        out_shape=shapes,
        in_specs=[pl.BlockSpec(memory_space=pl.ANY)] * count,
        out_specs=[pl.BlockSpec(memory_space=pl.ANY)] * len(shapes),
        scratch_shapes=gather_semaphores(count, paired),
        compiler_params=pltpu.CompilerParams(collective_id=collective_id, has_side_effects=True),
    )(*arrays)


def dot_nn(left, right):
    return lax.dot_general(left, right, (((1,), (0,)), ((), ())), preferred_element_type=jnp.float32)


def dot_nt(left, right):
    return lax.dot_general(left, right, (((1,), (1,)), ((), ())), preferred_element_type=jnp.float32)


def experts_kernel(experts_all, *refs):
    rows_ref, grad_rows_ref, w_gate, w_up, w_down = refs[:5]
    weighted_out, grad_in_out, terms_out, gate_out, up_out, down_out, grads_own, grads_pair = refs[5:13]
    held, grads, w_in, left_in, left_down, weighted_ref, grad_in_ref, terms_ref = refs[13:21]
    sums_in, sums_down, turned, grad_sem, w_sem, out_sem, sum_sem = refs[21:28]
    steps = gather_steps(
        [rows_ref, grad_rows_ref], [held.at[0], grads_own], [held.at[1], grads_pair], refs[28:]
    )
    level, core = steps.level, steps.core
    hidden, width = w_down.shape
    tiles = hidden // LANES
    rows = rows_ref.shape[0]
    visits = [
        level,
        jnp.where(level == 0, 1, level - 1),
        jnp.where(level == 0, 2, jnp.where(level == 3, 1, level + 1)),
        jnp.where(level < 2, 3, 0),
    ]

    def fetch(turn, half):
        return pltpu.make_async_copy(
            (grads_own, grads_pair)[half].at[pl.ds(PLANE * visits[turn], PLANE)],
            grads.at[turn % 2, half],
            grad_sem.at[turn % 2, half],
        )

    def fetch_start(turn):
        fetch(turn, 0).start()
        fetch(turn, 1).start()

    joins = [
        pltpu.make_async_copy(part, w_in.at[:, pl.ds(i * hidden, hidden)], w_sem.at[i])
        for i, part in enumerate((w_gate, w_up))
    ]
    lane = lax.broadcasted_iota(jnp.int32, (1, LANES), 1)
    expert = steps.me
    gate_pick = (((lane == expert) | (lane == experts_all + expert))).astype(jnp.float32)
    high_lane = (lane == 2 * experts_all * core + expert).astype(jnp.float32)
    low_lane = (lane == 2 * experts_all * core + experts_all + expert).astype(jnp.float32)
    group = 2 * rows

    def leave(turn):
        span = pl.ds(PLANE * visits[turn], PLANE)
        pairs = ((weighted_ref, weighted_out), (grad_in_ref, grad_in_out), (terms_ref, terms_out))
        return [
            pltpu.make_async_copy(here.at[:, span], there.at[:, span], out_sem.at[turn, i])
            for i, (here, there) in enumerate(pairs)
        ]

    def forward(turn, begin, end):
        first = PLANE * visits[turn]
        if begin == 0:
            fetch(turn, 0).wait()
            fetch(turn, 1).wait()

        def body(step, carry):
            half, pair = step // 2, step % 2
            at = first + 2 * pair
            lanes = held[half, pl.ds(at, 2), :, pl.ds(width, LANES)].reshape(group, LANES)
            gate_rows = jnp.sum(lanes.astype(jnp.float32) * gate_pick, axis=1, keepdims=True)
            grad_rows = grads[turn % 2, half, pl.ds(2 * pair, 2)].reshape(group, width)
            token_rows = held[half, pl.ds(at, 2), :, pl.ds(0, width)].reshape(group, width)
            grad_hidden = dot_nt(grad_rows, w_down[...])
            both = dot_nn(token_rows, w_in[...])
            terms = jnp.zeros((group, 1), jnp.float32)
            column = pl.multiple_of(step * group, group)
            for j in range(tiles):
                gate_in = both[:, j * LANES : (j + 1) * LANES]
                up_in = both[:, hidden + j * LANES : hidden + (j + 1) * LANES]
                back = grad_hidden[:, j * LANES : (j + 1) * LANES]
                gate_sigmoid = 1.0 / (1.0 + jnp.exp(-gate_in))
                gate_swish = gate_in * gate_sigmoid
                activated = gate_swish * up_in
                terms = terms + jnp.sum(activated * back, axis=1, keepdims=True)
                grad_act = gate_rows * back
                weighted = gate_rows * activated
                grad_gate = grad_act * up_in * gate_sigmoid * (1.0 + gate_in * (1.0 - gate_sigmoid))
                grad_up = grad_act * gate_swish
                for value, array, tile, left in (
                    (weighted, weighted_ref, j, left_down),
                    (grad_gate, grad_in_ref, j, left_in),
                    (grad_up, grad_in_ref, tiles + j, left_in),
                ):
                    span = pl.ds(tile * LANES, LANES)
                    array[half, pl.ds(at, 2), :, span] = value.astype(jnp.bfloat16).reshape(2, rows, LANES)
                    left[span, pl.ds(column, group)] = value.T.astype(jnp.bfloat16)
            high = terms.astype(jnp.bfloat16).astype(jnp.float32)
            spread = high * high_lane + (terms - high) * low_lane
            terms_ref[half, pl.ds(at, 2)] = spread.astype(jnp.bfloat16).reshape(2, rows, LANES)
            return carry

        lax.fori_loop(begin, end, body, 0)
        if end == 4:
            for copy in leave(turn):
                copy.start()

    wide = 256

    def weights(turn, begin, end):
        first = PLANE * visits[turn]

        def body(step, carry):
            span = pl.ds(pl.multiple_of(step * wide, wide), wide)
            token_rows = held[:, pl.ds(first, PLANE), :, span].reshape(2 * PLANE * rows, wide)
            grad_rows = grads[turn % 2, :, :, :, span].reshape(2 * PLANE * rows, wide)
            part_in = dot_nn(left_in[...], token_rows)
            part_down = dot_nn(left_down[...], grad_rows)
            if turn:
                part_in = sums_in[:, span] + part_in
                part_down = sums_down[:, span] + part_down
            sums_down[:, span] = part_down
            if turn < LEVELS - 1:
                sums_in[:, span] = part_in
            else:
                for i in range(2):
                    turned[i, span] = part_in[i * hidden : (i + 1) * hidden].T
                for copy in leave_sums(step):
                    copy.start()
            return carry

        lax.fori_loop(begin, end, body, 0)

    def leave_sums(step):
        span = pl.ds(pl.multiple_of(step * wide, wide), wide)
        return [
            pltpu.make_async_copy(turned.at[0, span], gate_out.at[span], sum_sem.at[step, 0]),
            pltpu.make_async_copy(turned.at[1, span], up_out.at[span], sum_sem.at[step, 1]),
            pltpu.make_async_copy(sums_down.at[:, span], down_out.at[:, span], sum_sem.at[step, 2]),
        ]

    def level_ready(turn):
        if turn == 0:
            steps.paired_level(0)
        for distance in range(-3, 4):
            if turn and distance:
                wanted = visits[turn] == level + distance
                pl.when(wanted)(lambda distance=distance: steps.paired_level(distance))
        fetch_start(turn)

    steps.start()
    for join in joins:
        join.start()
    steps.side_small()
    steps.column(1)
    steps.cross(0)
    for join in joins:
        join.wait()
    steps.column(2)
    steps.start_planes()
    steps.halves(0)
    steps.cross(1)
    level_ready(0)
    forward(0, 0, 4)
    steps.column(3)
    steps.planes(1)
    weights(0, 0, 4)
    steps.cross(2)
    steps.halves(1)
    level_ready(1)
    weights(0, 4, 8)
    forward(1, 0, 4)
    steps.planes(2)
    weights(1, 0, 4)
    steps.cross(3)
    steps.halves(2)
    level_ready(2)
    weights(1, 4, 8)
    forward(2, 0, 4)
    weights(2, 0, 8)
    steps.planes(3)
    steps.halves(3)
    level_ready(3)
    forward(3, 0, 4)
    weights(3, 0, 8)
    for turn in range(LEVELS):
        for copy in leave(turn):
            copy.wait()

    def last_sums(step, carry):
        for copy in leave_sums(step):
            copy.wait()
        return carry

    lax.fori_loop(0, width // wide, last_sums, 0)
    steps.end(levels_waited=True)


def experts_products(rows, grad_rows, w_gate, w_up, w_down, experts_all, collective_id):
    blocks, low, count = lax.axis_size("gx"), jnp.bfloat16, rows.shape[0]
    hidden, width = w_down.shape
    everywhere = pl.BlockSpec(memory_space=pl.ANY)
    block_shape = (2, blocks, count)
    shapes = [
        jax.ShapeDtypeStruct((*block_shape, hidden), low),
        jax.ShapeDtypeStruct((*block_shape, 2 * hidden), low),
        jax.ShapeDtypeStruct((*block_shape, LANES), low),
        jax.ShapeDtypeStruct((width, hidden), jnp.float32),
        jax.ShapeDtypeStruct((width, hidden), jnp.float32),
        jax.ShapeDtypeStruct((hidden, width), jnp.float32),
        *[jax.ShapeDtypeStruct((blocks, count, width), low)] * 2,
    ]
    level_rows = 2 * PLANE * count
    dma = pltpu.SemaphoreType.DMA
    return pl.pallas_call(
        functools.partial(experts_kernel, experts_all),
        out_shape=shapes,
        in_specs=[everywhere] * 4 + [pl.BlockSpec(memory_space=pltpu.VMEM)],
        out_specs=[everywhere] * 8,
        scratch_shapes=[
            pltpu.VMEM((*block_shape, rows.shape[1]), low),
            pltpu.VMEM((2, 2, PLANE, count, width), low),
            pltpu.VMEM((width, 2 * hidden), low),
            pltpu.VMEM((2 * hidden, level_rows), low),
            pltpu.VMEM((hidden, level_rows), low),
            *[pltpu.VMEM(shape.shape, low) for shape in shapes[:3]],
            pltpu.VMEM((2 * hidden, width), jnp.float32),
            pltpu.VMEM((hidden, width), jnp.float32),
            pltpu.VMEM((2, width, hidden), jnp.float32),
            dma((2, 2)),
            dma((2,)),
            dma((LEVELS, 3)),
            dma((width // 256, 3)),
            *gather_semaphores(2, 2),
        ],
        compiler_params=pltpu.CompilerParams(
            collective_id=collective_id, has_side_effects=True, vmem_limit_bytes=63 * 1024 * 1024
        ),
    )(rows, grad_rows, w_gate, w_up, w_down)[:6]


def scatter_kernel(plan, *refs):
    paired, factors, turned, count, gains = plan
    refs = list(refs)

    def take(number):
        taken = refs[:number]
        del refs[:number]
        return taken

    left = take(1)[0] if factors else None
    rights = take(factors)
    pieces = [take(count) for _ in range(1 + paired)]
    gain_ref = take(1)[0] if gains else None
    (out,) = take(1)
    gain_out = take(1)[0] if gains else None
    mine, half_y, half_x, full_x, full_y, slots_a, slots_b, side_b = take(8)
    send_sem, recv_sem, chain_send, chain_recv, load_sem = take(5)
    if paired:
        sibling, away, pair_send, pair_recv, ready_sem = take(5)
    if factors:
        right, right_sem = take(2)
    if gains:
        gain_slots, gain_send, gain_recv = take(3)
    me, core, level, x_side, y_side = neighbours()
    rows, width = mine.shape[1:]
    whole_a, half_a, whole_b, half_b = cut_rows(rows)
    far = me + 2 * PLANE - 4 * PLANE * (level // 2)
    greet(level, (x_side, y_side) + ((far,) if gains else ()), paired or gains, me, core)
    up, down = (me + PLANE, core), (me - PLANE, core)
    to_x, to_y = (x_side, core), (y_side, core)
    x_at, y_at, own_at = x_side % PLANE, y_side % PLANE, me % PLANE
    diagonal_at = (x_side + y_side - me) % PLANE
    forward = jnp.where(level < 2, 1, 0)
    order = [3 * forward, 2 * forward + (1 - forward), level + 1 - 2 * (level % 2), level]
    turns = range(LEVELS)
    sent = []

    def send(condition, source, target_ref, ssem, rsem, target):
        def copy():
            return pltpu.make_async_remote_copy(
                source, target_ref, ssem, rsem, device_id=target, device_id_type=MESH
            )

        when(condition, lambda: copy().start())
        sent.append((condition, copy))

    def arrive(condition, target_ref, rsem):
        def wait():
            pltpu.make_async_remote_copy(
                target_ref, target_ref, rsem, rsem, device_id=to_x, device_id_type=MESH
            ).wait_recv()

        when(condition, wait)

    def add(condition, height, target, *terms, step=16):
        def run():
            def body(i, carry):
                at = pl.multiple_of(i * step, step)
                total = target(at, step)[...].astype(jnp.float32)
                for term in terms:
                    total = total + term(at, step)[...].astype(jnp.float32)
                target(at, step)[...] = total.astype(jnp.bfloat16)
                return carry

            lax.fori_loop(0, height // step, body, 0)

        when(condition, run)

    def rows_of(ref, *index, start=0):
        return lambda at, step: ref.at[(*index, pl.ds(start + at, step))]

    def level_of(ref, turn):
        return ref.at[pl.ds(PLANE * order[turn], PLANE)]

    def load(half, turn):
        copies, lane = [], width - sum(piece.shape[2] for piece in pieces[half])
        for i, piece in enumerate(pieces[half]):
            place = (away if half else mine).at[pl.ds(PLANE * order[turn], PLANE), :, pl.ds(lane, piece.shape[2])]
            copies.append(pltpu.make_async_copy(level_of(piece, turn), place, load_sem.at[half, i, turn]))
            lane += piece.shape[2]
        return copies

    def right_copy(i):
        depth = rights[i].shape[1] if turned else rights[i].shape[0]
        place = right.at[:, pl.ds(i * depth, depth)] if turned else right
        return pltpu.make_async_copy(rights[i], place, right_sem.at[i])

    def hand(turn):
        return pltpu.make_async_remote_copy(
            level_of(away, turn),
            level_of(sibling, turn),
            pair_send.at[turn],
            pair_recv.at[turn],
            device_id=(me, 1 - core),
            device_id_type=MESH,
        )

    def produce(half, turn):
        first = PLANE * order[turn]
        wide = 256
        factor = left[half, pl.ds(first, PLANE)].reshape(PLANE * rows, left.shape[-1])

        def body(step, carry):
            span = pl.ds(pl.multiple_of(step * wide, wide), wide)
            value = dot_nt(factor, right[span]) if turned else dot_nn(factor, right[:, span])
            value = value.reshape(PLANE, rows, wide)
            if half == 0:
                value = value + sibling[pl.ds(first, PLANE), :, span].astype(jnp.float32)
            target = away if half else mine
            target[pl.ds(first, PLANE), :, span] = value.astype(jnp.bfloat16)
            return carry

        lax.fori_loop(0, (right.shape[0] if turned else right.shape[1]) // wide, body, 0)

    def hand_over(turn):
        if not paired:
            return
        if factors:
            produce(1, turn)
        for copy in load(1, turn):
            copy.wait()
        hand(turn).start()

    def settle(turn):
        for copy in load(0, turn):
            copy.wait()
        if not paired:
            return
        hand(turn).wait()
        if factors:
            produce(0, turn)
            lane = right.shape[0] if turned else right.shape[1]
        else:
            lane = 0
        if lane < width:
            first = PLANE * order[turn]
            span = pl.ds(lane, width - lane)
            for column in range(PLANE):
                mine[first + column, :, span] = (
                    mine[first + column, :, span].astype(jnp.float32)
                    + sibling[first + column, :, span].astype(jnp.float32)
                ).astype(jnp.bfloat16)

    sems = [[(send_sem.at[6 * turn + i], recv_sem.at[6 * turn + i]) for i in range(6)] for turn in turns]
    height = half_a[0][1]

    def scatter_first(turn):
        first = PLANE * order[turn]
        at, lower, upper = sems[turn], pl.ds(*half_a[0]), pl.ds(*half_a[1])
        send(None, mine.at[first + diagonal_at, lower], half_y.at[turn], *at[0], to_y)
        send(None, mine.at[first + diagonal_at, upper], half_x.at[turn], *at[1], to_x)
        send(None, mine.at[first + x_at, upper], full_x.at[turn, upper], *at[2], to_x)
        send(None, mine.at[first + y_at, lower], full_y.at[turn, lower], *at[3], to_y)

    def scatter_second(turn):
        first = PLANE * order[turn]
        at, lower, upper = sems[turn], pl.ds(*half_a[0]), pl.ds(*half_a[1])
        arrive(None, half_y.at[turn], at[0][1])
        add(None, height, rows_of(mine, first + x_at), rows_of(half_y, turn))
        send(None, mine.at[first + x_at, lower], full_x.at[turn, lower], *at[4], to_x)
        arrive(None, half_x.at[turn], at[1][1])
        add(None, height, rows_of(mine, first + y_at, start=height), rows_of(half_x, turn))
        send(None, mine.at[first + y_at, upper], full_y.at[turn, upper], *at[5], to_y)

    def chain(which, turn, block, slots, spread):
        to_level = order[turn]
        rising, falling = to_level > level, to_level < level
        begins = (rising & (level == 0)) | (falling & (level == LEVELS - 1))
        middle = (rising | falling) & jnp.logical_not(begins)
        arrive(middle, slots.at[to_level], chain_recv.at[which, to_level])
        spread(middle, to_level)
        outgoing = chain_send.at[which, to_level]
        send(rising, block, slots.at[to_level], outgoing, chain_recv.at[which, to_level], up)
        at = jnp.where(to_level == level - 1, LEVELS, to_level)
        send(falling, block, slots.at[at], outgoing, chain_recv.at[which, at], down)

    def add_small(condition, first, slot):
        for column in range(PLANE):
            add(
                condition,
                whole_b[1],
                rows_of(mine, first + column, start=whole_b[0]),
                rows_of(slots_b, slot, column),
            )

    def chain_small(turn):
        first = PLANE * order[turn]
        block = mine.at[pl.ds(first, PLANE), pl.ds(*whole_b)]
        chain(1, turn, block, slots_b, lambda condition, slot: add_small(condition, first, slot))

    def plane_arrives(turn):
        at, lower, upper = sems[turn], pl.ds(*half_a[0]), pl.ds(*half_a[1])
        arrive(None, full_x.at[turn, upper], at[2][1])
        arrive(None, full_y.at[turn, lower], at[3][1])
        arrive(None, full_x.at[turn, lower], at[4][1])
        arrive(None, full_y.at[turn, upper], at[5][1])

    def chain_large(turn):
        own = PLANE * order[turn] + own_at
        plane_arrives(turn)
        add(None, whole_a[1], rows_of(mine, own), rows_of(full_x, turn), rows_of(full_y, turn))
        chain(
            0,
            turn,
            mine.at[own, pl.ds(*whole_a)],
            slots_a,
            lambda condition, slot: add(condition, whole_a[1], rows_of(mine, own), rows_of(slots_a, slot)),
        )

    gain_partners = ((me, 1 - core), to_x, to_y, (me + PLANE - 2 * PLANE * (level % 2), core), (far, core))

    def gain_copy(turn):
        return pltpu.make_async_remote_copy(
            gain_slots.at[2 * turn],
            gain_slots.at[2 * turn + 1],
            gain_send.at[turn],
            gain_recv.at[turn],
            device_id=gain_partners[turn],
            device_id_type=MESH,
        )

    def gain_step(turn):
        if not gains:
            return
        if turn == 0:
            gain_slots[0] = gain_ref[...]
        else:
            gain_copy(turn - 1).wait_recv()
            gain_slots[2 * turn] = gain_slots[2 * turn - 2] + gain_slots[2 * turn - 1]
        if turn < len(gain_partners):
            gain_copy(turn).start()
        else:
            gain_out[...] = gain_slots[2 * turn]

    if factors:
        for i in range(factors):
            right_copy(i).start()
    for turn in turns:
        for half in range(1 + paired):
            for copy in load(half, turn):
                copy.start()
    if factors:
        for i in range(factors):
            right_copy(i).wait()
    gain_step(0)
    hand_over(0)
    if paired:
        hand_over(1)
    for turn in turns:
        settle(turn)
        scatter_first(turn)
        if turn < LEVELS - 1 and not paired:
            chain_small(turn)
        if turn + 2 < LEVELS:
            hand_over(turn + 2)
        if paired:
            if turn < LEVELS - 1:
                chain_small(turn)
            if turn >= 1:
                scatter_second(turn - 1)
            if turn >= 2:
                chain_large(turn - 2)
    if not paired:
        for turn in range(LEVELS - 1):
            scatter_second(turn)
            gain_step(turn + 1)
            if turn:
                chain_large(turn - 1)
    scatter_second(LEVELS - 1)
    gain_step(4)
    chain_large(LEVELS - 2)

    first = PLANE * level
    own = first + own_at
    arrivals = ((level > 0, level), (level < LEVELS - 1, LEVELS))
    for condition, slot in arrivals:
        arrive(condition, slots_b.at[slot], chain_recv.at[1, slot])
        add_small(condition, first, slot)
    side = [(send_sem.at[24 + i], recv_sem.at[24 + i]) for i in range(4)]
    short = half_b[0][1]
    spans = [pl.ds(0, short), pl.ds(short, short), pl.ds(2 * short, 2 * short), pl.ds(4 * short, 2 * short)]
    send(None, mine.at[first + diagonal_at, pl.ds(*half_b[0])], side_b.at[spans[0]], *side[0], to_y)
    send(None, mine.at[first + diagonal_at, pl.ds(*half_b[1])], side_b.at[spans[1]], *side[1], to_x)
    plane_arrives(LEVELS - 1)
    arrive(None, side_b.at[spans[0]], side[0][1])
    add(None, short, rows_of(mine, first + x_at, start=half_b[0][0]), rows_of(side_b))
    send(None, mine.at[first + x_at, pl.ds(*whole_b)], side_b.at[spans[2]], *side[2], to_x)
    arrive(None, side_b.at[spans[1]], side[1][1])
    add(None, short, rows_of(mine, first + y_at, start=half_b[1][0]), rows_of(side_b, start=short))
    send(None, mine.at[first + y_at, pl.ds(*whole_b)], side_b.at[spans[3]], *side[3], to_y)
    gain_step(5)
    base = core * rows if paired else 0
    step = 16

    def tail_a(i, carry):
        at = pl.multiple_of(i * step, step)
        span = pl.ds(at, step)
        total = mine[own, span].astype(jnp.float32)
        total = total + full_x[LEVELS - 1, span].astype(jnp.float32) + full_y[LEVELS - 1, span].astype(jnp.float32)
        out[pl.ds(pl.multiple_of(base + at, step), step)] = total
        return carry

    lax.fori_loop(0, whole_a[1] // step, tail_a, 0)
    for condition, slot in arrivals:
        arrive(condition, slots_a.at[slot], chain_recv.at[0, slot])

        def more(slot=slot):
            def body(i, carry):
                at = pl.multiple_of(i * step, step)
                span = pl.ds(pl.multiple_of(base + at, step), step)
                out[span] = out[span] + slots_a[slot, pl.ds(at, step)].astype(jnp.float32)
                return carry

            lax.fori_loop(0, whole_a[1] // step, body, 0)

        when(condition, more)
    arrive(None, side_b.at[spans[2]], side[2][1])
    arrive(None, side_b.at[spans[3]], side[3][1])

    def tail_b(i, carry):
        at = pl.multiple_of(i * step, step)
        total = mine[own, pl.ds(whole_b[0] + at, step)].astype(jnp.float32)
        total = total + side_b[pl.ds(2 * short + at, step)].astype(jnp.float32)
        total = total + side_b[pl.ds(4 * short + at, step)].astype(jnp.float32)
        out[pl.ds(pl.multiple_of(base + whole_b[0] + at, step), step)] = total
        return carry

    lax.fori_loop(0, whole_b[1] // step, tail_b, 0)
    if paired:

        def exchange(core_of_rows):
            span = pl.ds(pl.multiple_of(core_of_rows * rows, rows), rows)
            return pltpu.make_async_remote_copy(
                out.at[span],
                out.at[span],
                ready_sem.at[0],
                ready_sem.at[1],
                device_id=(me, 1 - core),
                device_id_type=MESH,
            )

        exchange(core).start()
        exchange(1 - core).wait_recv()
        exchange(core).wait_send()
    if gains:
        for turn in range(len(gain_partners)):
            gain_copy(turn).wait_send()
    for condition, copy in sent:
        when(condition, lambda copy=copy: copy().wait_send())


def scatter_sums(pieces, collective_id, away=(), product=None, gains=None):
    paired, low = bool(away) or product is not None, jnp.bfloat16
    operands, factors, turned, features = [], 0, False, 0
    if product:
        left, rights, turned = product
        features, factors = rights[0].shape[0 if turned else 1], len(rights)
        operands, (blocks, rows) = [left, *rights], left.shape[1:3]
    else:
        blocks, rows = pieces[0].shape[:2]
    width = features + sum(piece.shape[2] for piece in pieces)
    near, remote = 3 * rows // 4, rows // 4
    dma = pltpu.SemaphoreType.DMA
    scratch = [
        pltpu.VMEM((blocks, rows, width), low),
        pltpu.VMEM((LEVELS, near // 2, width), low),
        pltpu.VMEM((LEVELS, near // 2, width), low),
        pltpu.VMEM((LEVELS, near, width), low),
        pltpu.VMEM((LEVELS, near, width), low),
        pltpu.VMEM((LEVELS + 1, near, width), low),
        pltpu.VMEM((LEVELS + 1, PLANE, remote, width), low),
        pltpu.VMEM((3 * remote, width), low),
        *[dma((28,)), dma((28,)), dma((2, 5)), dma((2, 5)), dma((2, max(1, len(pieces)), LEVELS))],
    ]
    if paired:
        whole = pltpu.VMEM((blocks, rows, width), low)
        scratch += [whole, whole, dma((LEVELS,)), dma((LEVELS,)), dma((2,))]
    if factors:
        depth = left.shape[-1]
        scratch += [pltpu.VMEM((features, depth) if turned else (depth, features), low), dma((factors,))]
    vmem, everywhere = pl.BlockSpec(memory_space=pltpu.VMEM), pl.BlockSpec(memory_space=pl.ANY)
    operands += [*pieces, *away]
    in_specs = [everywhere] * len(operands)
    if factors:
        in_specs[0] = vmem
    shapes = [jax.ShapeDtypeStruct(((2 if paired else 1) * rows, width), jnp.float32)]
    if gains is not None:
        operands, in_specs = operands + [gains], in_specs + [vmem]
        shapes.append(jax.ShapeDtypeStruct(gains.shape, gains.dtype))
        scratch += [pltpu.VMEM((11, *gains.shape), gains.dtype), dma((5,)), dma((5,))]
    plan = (paired, factors, turned, len(pieces), gains is not None)
    return pl.pallas_call(
        functools.partial(scatter_kernel, plan),
        out_shape=shapes,
        in_specs=in_specs,
        out_specs=[vmem] * len(shapes),
        scratch_shapes=scratch,
        compiler_params=pltpu.CompilerParams(
            collective_id=collective_id, has_side_effects=True, vmem_limit_bytes=60 * 1024 * 1024
        ),
    )(*operands)


def kernels_fit():
    return lax.axis_size("gx") == LEVELS * PLANE and lax.axis_size("gy") == 2


def packed_gains(vectors):
    rows = jnp.concatenate([vector.reshape(-1, HEAD_DIM) for vector in vectors], axis=0)
    return jnp.pad(rows, ((0, -rows.shape[0] % 8), (0, 0)))


def unpacked_gains(rows, vectors):
    sums, at = [], 0
    for vector in vectors:
        length = vector.shape[0] // HEAD_DIM
        sums.append(rows[at : at + length].reshape(-1))
        at += length
    return sums


def two_parts(values):
    high = lax.reduce_precision(values, 8, 7)
    return high.astype(jnp.bfloat16), (values - high).astype(jnp.bfloat16)


def sparse_experts(normed_ffn, logits, route_hits, routes, cotangent, w_gate, w_up, w_down):
    sequence_length, model_width = normed_ffn.shape
    experts_all = logits.shape[1]
    devices_gx = lax.axis_size("gx")
    part_width = model_width // lax.axis_size("gy")
    capacity = 5 * sequence_length * TOP // (4 * experts_all)
    pairs_count = sequence_length * TOP
    hits_float = route_hits.astype(jnp.float32)
    chosen = jnp.sum(logits[:, None, :] * hits_float, axis=-1)
    gate_exps = jnp.exp(chosen)
    gate_values = gate_exps / jnp.sum(gate_exps, axis=1, keepdims=True)
    flat_hits = route_hits.reshape(pairs_count, experts_all).astype(jnp.int32)
    slot_rank = jnp.sum((jnp.cumsum(flat_hits, axis=0) - flat_hits) * flat_hits, axis=1)
    slot_dest = routes.reshape(-1) * capacity + slot_rank
    slot_pair = (
        jnp.full((experts_all * capacity,), pairs_count, jnp.int32)
        .at[slot_dest]
        .set(jnp.arange(pairs_count, dtype=jnp.int32))
    )
    slot_token = jnp.where(slot_pair < pairs_count, slot_pair // TOP, sequence_length)

    def to_experts(buffer):
        arrived = lax.all_to_all(buffer, "gx", split_axis=0, concat_axis=0, tiled=True)
        return arrived.reshape(devices_gx * capacity, model_width)

    def from_experts(partial_rows):
        share_rows = lax.psum_scatter(
            partial_rows.astype(jnp.bfloat16), "gy", scatter_dimension=1, tiled=True
        )
        returned = lax.all_to_all(
            share_rows.reshape(devices_gx, capacity, part_width),
            "gx",
            split_axis=0,
            concat_axis=0,
            tiled=True,
        )
        whole_rows = lax.all_gather(returned, "gy", axis=2, tiled=True)
        return whole_rows.reshape(devices_gx * capacity, model_width)

    send_rows = jnp.take(normed_ffn, slot_token, axis=0, mode="fill", fill_value=0)
    expert_in = to_experts(send_rows.reshape(devices_gx, capacity, model_width))
    gate_in = jnp.dot(expert_in, w_gate, preferred_element_type=jnp.float32)
    up_in = jnp.dot(expert_in, w_up, preferred_element_type=jnp.float32)
    gate_sigmoid = jax.nn.sigmoid(gate_in)
    gate_swish = gate_in * gate_sigmoid
    activated = (gate_swish * up_in).astype(jnp.bfloat16)
    expert_part = jnp.dot(activated, w_down, preferred_element_type=jnp.float32)
    expert_out = from_experts(expert_part)
    pair_rows = jnp.take(expert_out, slot_dest, axis=0).reshape(sequence_length, TOP, model_width)
    mixed_rows = jnp.einsum(
        "tk,tkd->td", gate_values, pair_rows, preferred_element_type=jnp.float32
    )
    grad_out_f = cotangent.astype(jnp.float32)
    grad_gates = jnp.einsum("td,tkd->tk", grad_out_f, pair_rows, preferred_element_type=jnp.float32)
    grad_chosen = gate_values * (
        grad_gates - jnp.sum(gate_values * grad_gates, axis=1, keepdims=True)
    )
    grad_logits = jnp.sum(grad_chosen[:, :, None] * hits_float, axis=1).astype(jnp.bfloat16)
    slot_gate = jnp.take(gate_values.reshape(-1), slot_pair, mode="fill", fill_value=0.0)
    grad_send = (
        jnp.take(grad_out_f, slot_token, axis=0, mode="fill", fill_value=0) * slot_gate[:, None]
    )
    grad_expert_out = to_experts(
        grad_send.astype(jnp.bfloat16).reshape(devices_gx, capacity, model_width)
    )
    grad_act = contract(grad_expert_out, w_down, 1, 1)
    down_term = contract(activated, grad_expert_out, 0, 0)
    grad_gate_in = (
        grad_act * up_in * gate_sigmoid * (1.0 + gate_in * (1.0 - gate_sigmoid))
    ).astype(jnp.bfloat16)
    grad_up_in = (grad_act * gate_swish).astype(jnp.bfloat16)
    gate_term = contract(expert_in, grad_gate_in, 0, 0)
    up_term = contract(expert_in, grad_up_in, 0, 0)
    grad_in_part = contract(grad_gate_in, w_gate, 1, 1) + contract(grad_up_in, w_up, 1, 1)
    grad_rows = from_experts(grad_in_part)
    grad_pairs = jnp.take(grad_rows, slot_dest, axis=0).reshape(sequence_length, TOP, model_width)
    grad_rows_sum = jnp.sum(grad_pairs.astype(jnp.float32), axis=1)
    return mixed_rows, grad_rows_sum, grad_logits, (gate_term[None], up_term[None], down_term[None])


def swap_cores(rows):
    return lax.ppermute(rows, "gy", [(0, 1), (1, 0)])


def own_half(rows):
    count = rows.shape[0] // lax.axis_size("gy")
    return lax.dynamic_slice_in_dim(rows, lax.axis_index("gy") * count, count, 0)


def dense_experts(normed_ffn, logits, route_hits, cotangent, w_gate, w_up, w_down):
    sequence_length, model_width = normed_ffn.shape
    experts_all = logits.shape[1]
    gate_exps = jnp.exp(jnp.where(jnp.any(route_hits, axis=1), logits, -1e30))
    gate_all = gate_exps / jnp.sum(gate_exps, axis=1, keepdims=True)
    gate_lanes = jnp.pad(jnp.concatenate(two_parts(gate_all), axis=1), ((0, 0), (0, LANES - 2 * experts_all)))
    row_lanes = jnp.concatenate([own_half(normed_ffn), own_half(gate_lanes)], axis=1)
    weighted, grad_in, terms, gate_term, up_term, down_term = experts_products(
        row_lanes, own_half(cotangent), w_gate, w_up, w_down, experts_all, 2
    )
    (back,) = scatter_sums([terms[0]], 3, [terms[1]], (grad_in, (w_gate, w_up), True))
    (mixed_rows,) = scatter_sums([], 4, [], (weighted, (w_down,), False))
    term_lanes = back[:, model_width : model_width + 4 * experts_all]
    grad_gates = jnp.sum(term_lanes.reshape(sequence_length, 4, experts_all), axis=1)
    grad_logits = (
        gate_all * (grad_gates - jnp.sum(gate_all * grad_gates, axis=1, keepdims=True))
    ).astype(jnp.bfloat16)
    return mixed_rows, back[:, :model_width], grad_logits, (gate_term[None], up_term[None], down_term[None])


def turn_lanes(values, cosine, sine_table):
    return values * cosine + pltpu.roll(values, HEAD_DIM // 2, 1) * sine_table


def unit_rows(values):
    scale = lax.rsqrt(jnp.mean(values * values, axis=1, keepdims=True) + EPSILON)
    return values * scale, scale


def allowed_pairs(docs_column, docs_row):
    shape = (docs_column.shape[0], docs_row.shape[1])
    keys_at, queries_at = lax.broadcasted_iota(jnp.int32, shape, 0), lax.broadcasted_iota(jnp.int32, shape, 1)
    return (keys_at <= queries_at) & (docs_column == docs_row)


def head_span(head):
    return pl.ds(pl.multiple_of(head * HEAD_DIM, HEAD_DIM), HEAD_DIM)


def attend_kernel(
    q_heads, kv_heads, raw_ref, cosine_ref, sine_ref, docs_column, docs_row, q_gain, k_gain,
    attended_ref, query_ref, key_ref, value_ref, totals_ref,
):
    cosine, sine_table = cosine_ref[...], sine_ref[...]
    allowed = allowed_pairs(docs_column[...], docs_row[...])
    group, inv_root = q_heads // kv_heads, 1.0 / math.sqrt(HEAD_DIM)
    for kv in range(kv_heads):
        unit, _ = unit_rows(raw_ref[:, head_span(q_heads + kv)])
        key_rows = turn_lanes(unit * k_gain[...], cosine, sine_table).astype(jnp.bfloat16)
        value_rows = raw_ref[:, head_span(q_heads + kv_heads + kv)]
        key_ref[:, head_span(kv)] = key_rows
        value_ref[:, head_span(kv)] = value_rows.astype(jnp.bfloat16)
        value_columns = value_rows.T.astype(jnp.bfloat16)

        def body(index, carry, kv=kv, key_rows=key_rows, value_columns=value_columns):
            head = kv * group + index
            unit, _ = unit_rows(raw_ref[:, head_span(head)])
            query_rows = turn_lanes(unit * q_gain[...], cosine, sine_table).astype(jnp.bfloat16)
            query_ref[:, head_span(head)] = query_rows
            scores = jnp.where(allowed, dot_nt(key_rows, query_rows) * inv_root, -1e30)
            peak = jnp.max(scores, axis=0, keepdims=True)
            exps = jnp.exp(scores - peak)
            total = jnp.sum(exps, axis=0, keepdims=True)
            totals_ref[pl.ds(head, 1), :] = peak + jnp.log(total)
            probs = (exps / total).astype(jnp.bfloat16)
            attended_ref[:, head_span(head)] = dot_nn(value_columns, probs).T.astype(jnp.bfloat16)
            return carry

        lax.fori_loop(0, group, body, 0, unroll=2)


def attend_back_kernel(
    q_heads, kv_heads, raw_ref, cosine_ref, sine_ref, docs_column, docs_row, q_gain, k_gain,
    query_ref, key_ref, value_ref, totals_ref, grad_ref, grad_raw_ref, gains_ref, sums_ref,
):
    cosine, sine_table = cosine_ref[...], sine_ref[...]
    allowed = allowed_pairs(docs_column[...], docs_row[...])
    group, inv_root = q_heads // kv_heads, 1.0 / math.sqrt(HEAD_DIM)
    gains_ref[...] = jnp.zeros_like(gains_ref)

    def back_to_raw(grad, head, gain, gain_row):
        grad = turn_lanes(grad, cosine, -sine_table)
        unit, scale = unit_rows(raw_ref[:, head_span(head)])
        gains_ref[pl.ds(gain_row, 1), :] += jnp.sum(grad * unit, axis=0, keepdims=True)
        grad = grad * gain
        grad = scale * (grad - unit * jnp.mean(grad * unit, axis=1, keepdims=True))
        grad_raw_ref[:, head_span(head)] = grad.astype(jnp.bfloat16)

    for kv in range(kv_heads):
        key_rows, value_rows = key_ref[:, head_span(kv)], value_ref[:, head_span(kv)]
        key_columns = key_rows.astype(jnp.float32).T.astype(jnp.bfloat16)
        sums_ref[...] = jnp.zeros_like(sums_ref)

        def body(index, carry, kv=kv, key_rows=key_rows, value_rows=value_rows, key_columns=key_columns):
            head = kv * group + index
            query_rows, grad_rows = query_ref[:, head_span(head)], grad_ref[:, head_span(head)]
            scores = jnp.where(allowed, dot_nt(key_rows, query_rows) * inv_root, -1e30)
            probs = jnp.exp(scores - totals_ref[pl.ds(head, 1), :])
            sums_ref[0] += dot_nn(probs.astype(jnp.bfloat16), grad_rows)
            grad_probs = dot_nt(value_rows, grad_rows)
            inner = jnp.sum(probs * grad_probs, axis=0, keepdims=True)
            grad_scores = (probs * (grad_probs - inner)).astype(jnp.bfloat16)
            sums_ref[1] += dot_nn(grad_scores, query_rows)
            grad_queries = dot_nn(key_columns, grad_scores).T * inv_root
            back_to_raw(grad_queries, head, q_gain[...], 0)
            return carry

        lax.fori_loop(0, group, body, 0, unroll=2)
        back_to_raw(sums_ref[1] * inv_root, q_heads + kv, k_gain[...], 1)
        grad_raw_ref[:, head_span(q_heads + kv_heads + kv)] = sums_ref[0].astype(jnp.bfloat16)


def attention_shared(qkv_rows, doc_ids, query_norm_gain, k_gain):
    length = qkv_rows.shape[0]
    cosine, sine_table = rotary_tables(length, HEAD_DIM)
    cosine, sine_table = cosine[:, 0], sine_table[:, 0]
    return (
        qkv_rows,
        jnp.concatenate([cosine, cosine], axis=1),
        jnp.concatenate([-sine_table, sine_table], axis=1),
        doc_ids.reshape(length, 1),
        doc_ids.reshape(1, length),
        query_norm_gain.reshape(1, HEAD_DIM),
        k_gain.reshape(1, HEAD_DIM),
    )


def attend(shared, q_heads, kv_heads):
    length, low, shape = shared[0].shape[0], jnp.bfloat16, jax.ShapeDtypeStruct
    return pl.pallas_call(
        functools.partial(attend_kernel, q_heads, kv_heads),
        out_shape=[
            shape((length, q_heads * HEAD_DIM), low),
            shape((length, q_heads * HEAD_DIM), low),
            shape((length, kv_heads * HEAD_DIM), low),
            shape((length, kv_heads * HEAD_DIM), low),
            shape((q_heads, length), jnp.float32),
        ],
        compiler_params=pltpu.CompilerParams(vmem_limit_bytes=48 * 1024 * 1024),
    )(*shared)


def attend_back(shared, kept, grad_attended, q_heads, kv_heads):
    length, shape = shared[0].shape[0], jax.ShapeDtypeStruct
    return pl.pallas_call(
        functools.partial(attend_back_kernel, q_heads, kv_heads),
        out_shape=[shape(shared[0].shape, jnp.bfloat16), shape((8, HEAD_DIM), jnp.float32)],
        scratch_shapes=[pltpu.VMEM((2, length, HEAD_DIM), jnp.float32)],
        compiler_params=pltpu.CompilerParams(vmem_limit_bytes=48 * 1024 * 1024),
    )(*shared, *kept, grad_attended)


def on_device(
    tokens_in,
    doc_ids,
    routes,
    q_weight,
    key_matrix,
    value_matrix,
    out_weight,
    router_weight,
    attn_gain,
    ffn_gain,
    query_norm_gain,
    k_gain,
    gate_weight,
    up_weight,
    down_weight,
    cotangent,
):
    sequence_length = tokens_in.shape[0]
    model_width = tokens_in.shape[1]
    devices_gx = lax.axis_size("gx")
    devices_gy = lax.axis_size("gy")
    part_width = model_width // devices_gy
    experts_all = router_weight.shape[1]
    router_lanes = jnp.pad(router_weight, ((0, 0), (0, LANES - experts_all)))
    rows_local = jnp.concatenate([q_weight, key_matrix, value_matrix, router_lanes, out_weight], axis=1)
    dense = kernels_fit() and experts_all <= 2 * TOP
    if dense:
        (weights_all,) = gather_blocks([rows_local], (0,), 1)
        weights_all = weights_all.reshape(-1, rows_local.shape[1])
    else:
        weights_all = lax.all_gather(rows_local, "gx", axis=0, tiled=True)
    q_width, kv_width = q_weight.shape[1], key_matrix.shape[1]
    qkv_width = q_width + 2 * kv_width
    qkv_full = weights_all[:, :qkv_width]
    router_full = weights_all[:, qkv_width : qkv_width + experts_all]
    o_full = weights_all[:, qkv_width + LANES :]
    heads_local = q_width // HEAD_DIM
    kv_local = kv_width // HEAD_DIM
    inputs_f = tokens_in.astype(jnp.float32)
    scale_one = root_mean_scale(inputs_f)
    unit_one = inputs_f * scale_one
    normalized_input = (unit_one * attn_gain).astype(jnp.bfloat16)
    qkv_rows = jnp.dot(normalized_input, qkv_full, preferred_element_type=jnp.float32)
    shared = attention_shared(qkv_rows, doc_ids, query_norm_gain, k_gain)
    attended, *kept = attend(shared, heads_local, kv_local)
    attn_part = contract(attended, o_full, 1, 1)
    attn_total = attn_part + swap_cores(attn_part)
    residual = inputs_f + attn_total
    scale_two = root_mean_scale(residual)
    unit_two = residual * scale_two
    normed_ffn = (unit_two * ffn_gain).astype(jnp.bfloat16)
    logits = jnp.dot(normed_ffn, router_full, preferred_element_type=jnp.float32)
    expert_iota = jnp.arange(experts_all, dtype=jnp.int32)
    route_hits = routes[:, :, None] == expert_iota
    if dense:
        mixed_rows, grad_rows_sum, grad_logits, expert_grads = dense_experts(
            normed_ffn, logits, route_hits, cotangent, gate_weight[0], up_weight[0], down_weight[0]
        )
    else:
        mixed_rows, grad_rows_sum, grad_logits, expert_grads = sparse_experts(
            normed_ffn, logits, route_hits, routes, cotangent, gate_weight[0], up_weight[0], down_weight[0]
        )
    output = (residual + mixed_rows).astype(jnp.bfloat16)
    grad_out_f = cotangent.astype(jnp.float32)
    router_term = contract(normed_ffn, grad_logits, 0, 0)
    grad_ffn_in = contract(grad_logits, router_full, 1, 1) + grad_rows_sum
    ffn_gain_term = jnp.sum(grad_ffn_in * unit_two, axis=0)
    grad_residual = grad_out_f + norm_back(grad_ffn_in * ffn_gain, unit_two, scale_two)
    grad_attn = grad_residual.astype(jnp.bfloat16)
    out_term = contract(grad_attn, attended, 0, 0)
    grad_attended = jnp.dot(grad_attn, o_full, preferred_element_type=jnp.float32).astype(
        jnp.bfloat16
    )
    grad_qkv, head_gains = attend_back(shared, kept, grad_attended, heads_local, kv_local)
    q_gain_term, k_gain_term = head_gains[0], head_gains[1]
    qkv_term = contract(normalized_input, grad_qkv, 0, 0)
    grad_normed_part = contract(grad_qkv, qkv_full, 1, 1)
    grad_normed = grad_normed_part + swap_cores(grad_normed_part)
    attn_gain_term = jnp.sum(grad_normed * unit_one, axis=0)
    grad_input = (grad_residual + norm_back(grad_normed * attn_gain, unit_one, scale_one)).astype(
        jnp.bfloat16
    )
    own_mask = (jnp.arange(model_width) // part_width == lax.axis_index("gy")).astype(jnp.float32)
    gains = (attn_gain_term * own_mask, ffn_gain_term * own_mask, q_gain_term, k_gain_term)
    router_lanes = jnp.pad(router_term, ((0, 0), (0, LANES - experts_all)))
    if dense:
        pieces = [
            term.astype(jnp.bfloat16).reshape(devices_gx, -1, term.shape[1])
            for term in (qkv_term, router_lanes, out_term)
        ]
        sums, gain_rows = scatter_sums(pieces, 5, gains=packed_gains(gains))
        gains = unpacked_gains(gain_rows, gains)
    else:
        sums = jnp.concatenate(
            [
                lax.psum_scatter(term, "gx", scatter_dimension=0, tiled=True)
                for term in (qkv_term, router_lanes, out_term)
            ],
            axis=1,
        )
        gains = lax.psum(gains, ("gx", "gy"))
    gain_attn, gain_ffn, gain_query, gain_key = gains
    grad_q = sums[:, :q_width]
    grad_k = sums[:, q_width : q_width + kv_width]
    grad_v = sums[:, q_width + kv_width : qkv_width]
    grad_router = sums[:, qkv_width : qkv_width + experts_all]
    grad_out = sums[:, qkv_width + LANES :]
    return (
        output,
        grad_input,
        grad_q,
        grad_k,
        grad_v,
        grad_out,
        grad_router,
        gain_attn,
        gain_ffn,
        gain_query,
        gain_key,
        expert_grads[0],
        expert_grads[1],
        expert_grads[2],
    )


def solution(mesh):
    return jax.shard_map(
        on_device,
        mesh=mesh,
        in_specs=(
            P("gx", None),
            P("gx", None),
            P("gx", None),
            P("gx", "gy"),
            P("gx", "gy"),
            P("gx", "gy"),
            P("gx", "gy"),
            P("gx", None),
            P(),
            P(),
            P(),
            P(),
            P("gx", None, "gy"),
            P("gx", None, "gy"),
            P("gx", "gy", None),
            P("gx", None),
        ),
        out_specs=(
            P("gx", None),
            P("gx", None),
            P("gx", "gy"),
            P("gx", "gy"),
            P("gx", "gy"),
            P("gx", "gy"),
            P("gx", None),
            P(),
            P(),
            P(),
            P(),
            P("gx", None, "gy"),
            P("gx", None, "gy"),
            P("gx", "gy", None),
        ),
        check_vma=False,
    )
```

```python
import functools
import math

import jax
import jax.numpy as jnp
from jax import lax
from jax.experimental import pallas as pl
from jax.experimental.pallas import tpu as pltpu
from jax.sharding import PartitionSpec as P

QUERY_HEADS = 32
KEY_VALUE_HEADS = 4
HEAD_DIM = 128
LANES = 128
TOP = 8


EPSILON = 1e-06
THETA = 1000000.0


def root_mean_scale(values):
    return lax.rsqrt(jnp.mean(values * values, axis=-1, keepdims=True) + EPSILON)


def rotary_tables(sequence_length, head_width):
    half_width = head_width // 2
    frequencies = THETA ** (-(2.0 * jnp.arange(half_width, dtype=jnp.float32)) / head_width)
    angles = jnp.arange(sequence_length, dtype=jnp.float32)[:, None] * frequencies[None, :]
    return (jnp.cos(angles)[:, None, :], jnp.sin(angles)[:, None, :])


def norm_back(grad_normed, normed_unit, scale_rows):
    return scale_rows * (
        grad_normed - normed_unit * jnp.mean(grad_normed * normed_unit, axis=-1, keepdims=True)
    )


def contract(first_op, second_op, first_dim, second_dim):
    return lax.dot_general(
        first_op,
        second_op,
        (((first_dim,), (second_dim,)), ((), ())),
        preferred_element_type=jnp.float32,
    )


MESH = pl.DeviceIdType.MESH
LEVELS = 4
PLANE = 4


def cut_rows(rows):
    near, far = 3 * rows // 4, rows // 4
    return (
        (0, near),
        ((0, near // 2), (near // 2, near // 2)),
        (near, far),
        ((near, far // 2), (near + far // 2, far // 2)),
    )


def neighbours():
    me, core = lax.axis_index("gx"), lax.axis_index("gy")
    level = me // PLANE
    x_side = me + 1 - 2 * (me % 2)
    y_side = me + 2 - 4 * ((me // 2) % 2)
    return me, core, level, x_side, y_side


def greet(level, targets, with_core, me, core):
    barrier = pltpu.get_barrier_semaphore()

    def hello(device):
        pl.semaphore_signal(barrier, inc=1, device_id=device, device_id_type=MESH)

    for target in targets:
        hello((target, core))
    if with_core:
        hello((me, 1 - core))

    @pl.when(level > 0)
    def _():
        hello((me - PLANE, core))

    @pl.when(level < LEVELS - 1)
    def _():
        hello((me + PLANE, core))

    inner = jnp.where(level > 0, 1, 0) + jnp.where(level < LEVELS - 1, 1, 0)
    pl.semaphore_wait(barrier, len(targets) + int(with_core) + inner)


def when(condition, action):
    if condition is None:
        action()
    else:
        pl.when(condition)(action)


def gather_kernel(count, with_pair, *refs):
    paired = sum(with_pair)
    ins, outs, pairs = refs[:count], refs[count : 2 * count], list(refs[2 * count : 2 * count + paired])
    pairs = [pairs.pop(0) if wanted else None for wanted in with_pair]
    sems = refs[2 * count + paired :]
    steps = gather_steps(ins, outs, pairs, sems)
    for step in steps.order:
        step()
    steps.end()


class gather_steps:
    def __init__(self, ins, outs, pairs, sems):
        self.ins, self.outs, self.pairs = ins, outs, pairs
        self.send_sem, self.recv_sem, self.local_sem, self.pair_send, self.pair_recv = sems
        self.me, self.core, self.level, self.x_side, self.y_side = neighbours()
        self.diagonal = self.x_side + self.y_side - self.me
        self.spans = cut_rows(ins[0].shape[0])
        self.has_up, self.has_down = self.level < LEVELS - 1, self.level > 0
        self.up, self.down = (self.me + PLANE, self.core), (self.me - PLANE, self.core)
        self.to_x, self.to_y = (self.x_side, self.core), (self.y_side, self.core)
        self.sent, self.mirrored, self.everyone = [], [], range(len(ins))
        greet(self.level, (self.x_side, self.y_side), any(p is not None for p in pairs), self.me, self.core)
        self.order = [
            self.start,
            self.side_small,
            lambda: self.column(1),
            lambda: self.cross(0),
            lambda: self.column(2),
            self.start_planes,
            lambda: self.cross(1),
            lambda: self.column(3),
            lambda: self.planes(1),
            lambda: self.cross(2),
            lambda: self.planes(2),
            lambda: self.cross(3),
            lambda: self.planes(3),
            lambda: [self.halves(step) for step in range(LEVELS)],
        ]

    def send(self, condition, k, slot, source, first, number, span, target):
        def copy():
            there = self.outs[k].at[pl.ds(first, number), pl.ds(*span)]
            here = there
            if source == "own":
                here, there = self.ins[k].at[pl.ds(*span)], self.outs[k].at[first, pl.ds(*span)]
            return pltpu.make_async_remote_copy(
                here,
                there,
                self.send_sem.at[k, slot],
                self.recv_sem.at[k, slot],
                device_id=target,
                device_id_type=MESH,
            )

        when(condition, lambda: copy().start())
        self.sent.append((condition, copy))

    def mirror(self, condition, k, first, number, span, group):
        if self.pairs[k] is None:
            return
        slot = len(self.mirrored)

        def copy():
            return pltpu.make_async_remote_copy(
                self.outs[k].at[pl.ds(first, number), pl.ds(*span)],
                self.pairs[k].at[pl.ds(first, number), pl.ds(*span)],
                self.pair_send.at[slot],
                self.pair_recv.at[slot],
                device_id=(self.me, 1 - self.core),
                device_id_type=MESH,
            )

        when(condition, lambda: copy().start())
        self.mirrored.append((condition, copy, group))

    def arrive(self, condition, k, slot, first, number, span, group):
        place = self.outs[k].at[pl.ds(first, number), pl.ds(*span)]

        def wait():
            pltpu.make_async_remote_copy(
                place,
                place,
                self.send_sem.at[k, slot],
                self.recv_sem.at[k, slot],
                device_id=self.to_x,
                device_id_type=MESH,
            ).wait_recv()

        when(condition, wait)
        self.mirror(condition, k, first, number, span, group)

    def members(self, step):
        if step == 0:
            return [(None, 0, 0)]
        return [(self.level >= step, step, -step), (self.level + step < LEVELS, 3 + step, step)]

    def slot_of(self, group, index):
        return 6 + 7 * group + index

    last = 6 + 28

    def own_copy(self, k):
        return pltpu.make_async_copy(self.ins[k], self.outs[k].at[self.me], self.local_sem.at[k])

    def start(self):
        whole_a, half_a, whole_b, half_b = self.spans
        last, me = self.last, self.me
        for k in self.everyone:
            self.own_copy(k).start()
            self.send(None, k, last, "own", me, 1, whole_b, self.to_x)
            self.send(None, k, last + 1, "own", me, 1, whole_b, self.to_y)
            self.send(self.has_up, k, 0, "own", me, 1, whole_a, self.up)
            self.send(self.has_down, k, 3, "own", me, 1, whole_a, self.down)
            self.send(None, k, self.slot_of(0, 0), "own", me, 1, whole_a, self.to_x)
            self.send(None, k, self.slot_of(1, 0), "own", me, 1, whole_a, self.to_y)

    def side_small(self):
        whole_a, half_a, whole_b, half_b = self.spans
        last = self.last
        for k in self.everyone:
            self.arrive(None, k, last, self.x_side, 1, whole_b, 0)
            self.send(None, k, last + 3, "out", self.x_side, 1, half_b[1], self.to_y)
            self.arrive(None, k, last + 1, self.y_side, 1, whole_b, 0)
            self.send(None, k, last + 2, "out", self.y_side, 1, half_b[0], self.to_x)
        for k in self.everyone:
            self.own_copy(k).wait()
            self.mirror(None, k, self.me, 1, (0, self.ins[k].shape[0]), 0)
            self.arrive(None, k, last + 2, self.diagonal, 1, half_b[0], 0)
            self.arrive(None, k, last + 3, self.diagonal, 1, half_b[1], 0)

    def start_planes(self):
        whole_b = self.spans[2]
        for k in self.everyone:
            self.send(self.has_up, k, self.last + 4, "out", PLANE * self.level, PLANE, whole_b, self.up)
            self.send(self.has_down, k, self.last + 7, "out", PLANE * self.level, PLANE, whole_b, self.down)

    def cross(self, step):
        whole_a, half_a = self.spans[:2]
        for k in self.everyone:
            for condition, index, distance in self.members(step):
                first = self.x_side + PLANE * distance
                self.arrive(condition, k, self.slot_of(0, index), first, 1, whole_a, distance)
                self.send(condition, k, self.slot_of(3, index), "out", first, 1, half_a[1], self.to_y)
                first = self.y_side + PLANE * distance
                self.arrive(condition, k, self.slot_of(1, index), first, 1, whole_a, distance)
                self.send(condition, k, self.slot_of(2, index), "out", first, 1, half_a[0], self.to_x)

    def halves(self, step):
        half_a = self.spans[1]
        for k in self.everyone:
            for condition, index, distance in self.members(step):
                first = self.diagonal + PLANE * distance
                self.arrive(condition, k, self.slot_of(2, index), first, 1, half_a[0], distance)
                self.arrive(condition, k, self.slot_of(3, index), first, 1, half_a[1], distance)

    def column(self, step):
        whole_a = self.spans[0]
        for k in self.everyone:
            for condition, index, distance in self.members(step):
                first = self.me + PLANE * distance
                rising = distance < 0
                self.arrive(condition, k, step - 1 if rising else 2 + step, first, 1, whole_a, distance)
                if step < LEVELS - 1:
                    onward = condition & (self.has_up if rising else self.has_down)
                    slot = step if rising else 3 + step
                    self.send(onward, k, slot, "out", first, 1, whole_a, self.up if rising else self.down)
                self.send(condition, k, self.slot_of(0, index), "out", first, 1, whole_a, self.to_x)
                self.send(condition, k, self.slot_of(1, index), "out", first, 1, whole_a, self.to_y)

    def planes(self, step):
        whole_b = self.spans[2]
        for k in self.everyone:
            for condition, index, distance in self.members(step):
                first = PLANE * (self.level + distance)
                rising = distance < 0
                self.arrive(condition, k, self.last + (3 if rising else 6) + step, first, PLANE, whole_b, distance)
                if step < LEVELS - 1:
                    onward = condition & (self.has_up if rising else self.has_down)
                    slot = self.last + (4 if rising else 7) + step
                    self.send(onward, k, slot, "out", first, PLANE, whole_b, self.up if rising else self.down)

    def paired_level(self, distance):
        for condition, copy, group in self.mirrored:
            if group == distance:
                when(condition, lambda copy=copy: copy().wait_recv())

    def end(self, levels_waited=False):
        for condition, copy in self.sent:
            when(condition, lambda copy=copy: copy().wait_send())
        for condition, copy, group in self.mirrored:
            when(condition, lambda copy=copy: copy().wait_send())
            if not levels_waited:
                when(condition, lambda copy=copy: copy().wait_recv())


GATHER_SLOTS = 6 + 28 + 10


def gather_semaphores(count, paired):
    dma = pltpu.SemaphoreType.DMA
    slots = (count, GATHER_SLOTS)
    pair_slots = (max(1, paired * (GATHER_SLOTS + 1)),)
    return [dma(slots), dma(slots), dma((count,)), dma(pair_slots), dma(pair_slots)]


def gather_blocks(arrays, with_pair, collective_id):
    count, blocks, paired = len(arrays), lax.axis_size("gx"), sum(with_pair)
    shapes = [jax.ShapeDtypeStruct((blocks, *a.shape), a.dtype) for a in arrays]
    shapes += [shape for shape, wanted in zip(shapes, with_pair) if wanted]
    return pl.pallas_call(
        functools.partial(gather_kernel, count, with_pair),
        out_shape=shapes,
        in_specs=[pl.BlockSpec(memory_space=pl.ANY)] * count,
        out_specs=[pl.BlockSpec(memory_space=pl.ANY)] * len(shapes),
        scratch_shapes=gather_semaphores(count, paired),
        compiler_params=pltpu.CompilerParams(collective_id=collective_id, has_side_effects=True),
    )(*arrays)


def dot_nn(left, right):
    return lax.dot_general(left, right, (((1,), (0,)), ((), ())), preferred_element_type=jnp.float32)


def dot_nt(left, right):
    return lax.dot_general(left, right, (((1,), (1,)), ((), ())), preferred_element_type=jnp.float32)


def experts_kernel(experts_all, *refs):
    rows_ref, grad_rows_ref, w_gate, w_up, w_down = refs[:5]
    weighted_out, grad_in_out, terms_out, gate_out, up_out, down_out, grads_own, grads_pair = refs[5:13]
    held, grads, w_in, left_in, left_down, weighted_ref, grad_in_ref, terms_ref = refs[13:21]
    sums_in, sums_down, turned, grad_sem, w_sem, out_sem, sum_sem = refs[21:28]
    steps = gather_steps(
        [rows_ref, grad_rows_ref], [held.at[0], grads_own], [held.at[1], grads_pair], refs[28:]
    )
    level, core = steps.level, steps.core
    hidden, width = w_down.shape
    tiles = hidden // LANES
    rows = rows_ref.shape[0]
    visits = [
        level,
        jnp.where(level == 0, 1, level - 1),
        jnp.where(level == 0, 2, jnp.where(level == 3, 1, level + 1)),
        jnp.where(level < 2, 3, 0),
    ]

    def fetch(turn, half):
        return pltpu.make_async_copy(
            (grads_own, grads_pair)[half].at[pl.ds(PLANE * visits[turn], PLANE)],
            grads.at[turn % 2, half],
            grad_sem.at[turn % 2, half],
        )

    def fetch_start(turn):
        fetch(turn, 0).start()
        fetch(turn, 1).start()

    joins = [
        pltpu.make_async_copy(part, w_in.at[:, pl.ds(i * hidden, hidden)], w_sem.at[i])
        for i, part in enumerate((w_gate, w_up))
    ]
    lane = lax.broadcasted_iota(jnp.int32, (1, LANES), 1)
    expert = steps.me
    gate_pick = (((lane == expert) | (lane == experts_all + expert))).astype(jnp.float32)
    high_lane = (lane == 2 * experts_all * core + expert).astype(jnp.float32)
    low_lane = (lane == 2 * experts_all * core + experts_all + expert).astype(jnp.float32)
    group = 2 * rows

    def leave(turn):
        span = pl.ds(PLANE * visits[turn], PLANE)
        pairs = ((weighted_ref, weighted_out), (grad_in_ref, grad_in_out), (terms_ref, terms_out))
        return [
            pltpu.make_async_copy(here.at[:, span], there.at[:, span], out_sem.at[turn, i])
            for i, (here, there) in enumerate(pairs)
        ]

    def forward(turn, begin, end):
        first = PLANE * visits[turn]
        if begin == 0:
            fetch(turn, 0).wait()
            fetch(turn, 1).wait()

        def body(step, carry):
            half, pair = step // 2, step % 2
            at = first + 2 * pair
            lanes = held[half, pl.ds(at, 2), :, pl.ds(width, LANES)].reshape(group, LANES)
            gate_rows = jnp.sum(lanes.astype(jnp.float32) * gate_pick, axis=1, keepdims=True)
            grad_rows = grads[turn % 2, half, pl.ds(2 * pair, 2)].reshape(group, width)
            token_rows = held[half, pl.ds(at, 2), :, pl.ds(0, width)].reshape(group, width)
            grad_hidden = dot_nt(grad_rows, w_down[...])
            both = dot_nn(token_rows, w_in[...])
            terms = jnp.zeros((group, 1), jnp.float32)
            column = pl.multiple_of(step * group, group)
            for j in range(tiles):
                gate_in = both[:, j * LANES : (j + 1) * LANES]
                up_in = both[:, hidden + j * LANES : hidden + (j + 1) * LANES]
                back = grad_hidden[:, j * LANES : (j + 1) * LANES]
                gate_sigmoid = 1.0 / (1.0 + jnp.exp(-gate_in))
                gate_swish = gate_in * gate_sigmoid
                activated = gate_swish * up_in
                terms = terms + jnp.sum(activated * back, axis=1, keepdims=True)
                grad_act = gate_rows * back
                weighted = gate_rows * activated
                grad_gate = grad_act * up_in * gate_sigmoid * (1.0 + gate_in * (1.0 - gate_sigmoid))
                grad_up = grad_act * gate_swish
                for value, array, tile, left in (
                    (weighted, weighted_ref, j, left_down),
                    (grad_gate, grad_in_ref, j, left_in),
                    (grad_up, grad_in_ref, tiles + j, left_in),
                ):
                    span = pl.ds(tile * LANES, LANES)
                    array[half, pl.ds(at, 2), :, span] = value.astype(jnp.bfloat16).reshape(2, rows, LANES)
                    left[span, pl.ds(column, group)] = value.T.astype(jnp.bfloat16)
            high = terms.astype(jnp.bfloat16).astype(jnp.float32)
            spread = high * high_lane + (terms - high) * low_lane
            terms_ref[half, pl.ds(at, 2)] = spread.astype(jnp.bfloat16).reshape(2, rows, LANES)
            return carry

        lax.fori_loop(begin, end, body, 0)
        if end == 4:
            for copy in leave(turn):
                copy.start()

    wide = 256

    def weights(turn, begin, end):
        first = PLANE * visits[turn]

        def body(step, carry):
            span = pl.ds(pl.multiple_of(step * wide, wide), wide)
            token_rows = held[:, pl.ds(first, PLANE), :, span].reshape(2 * PLANE * rows, wide)
            grad_rows = grads[turn % 2, :, :, :, span].reshape(2 * PLANE * rows, wide)
            part_in = dot_nn(left_in[...], token_rows)
            part_down = dot_nn(left_down[...], grad_rows)
            if turn:
                part_in = sums_in[:, span] + part_in
                part_down = sums_down[:, span] + part_down
            sums_down[:, span] = part_down
            if turn < LEVELS - 1:
                sums_in[:, span] = part_in
            else:
                for i in range(2):
                    turned[i, span] = part_in[i * hidden : (i + 1) * hidden].T
                for copy in leave_sums(step):
                    copy.start()
            return carry

        lax.fori_loop(begin, end, body, 0)

    def leave_sums(step):
        span = pl.ds(pl.multiple_of(step * wide, wide), wide)
        return [
            pltpu.make_async_copy(turned.at[0, span], gate_out.at[span], sum_sem.at[step, 0]),
            pltpu.make_async_copy(turned.at[1, span], up_out.at[span], sum_sem.at[step, 1]),
            pltpu.make_async_copy(sums_down.at[:, span], down_out.at[:, span], sum_sem.at[step, 2]),
        ]

    def level_ready(turn):
        if turn == 0:
            steps.paired_level(0)
        for distance in range(-3, 4):
            if turn and distance:
                wanted = visits[turn] == level + distance
                pl.when(wanted)(lambda distance=distance: steps.paired_level(distance))
        fetch_start(turn)

    steps.start()
    for join in joins:
        join.start()
    steps.side_small()
    steps.column(1)
    steps.cross(0)
    for join in joins:
        join.wait()
    steps.column(2)
    steps.start_planes()
    steps.halves(0)
    steps.cross(1)
    level_ready(0)
    forward(0, 0, 4)
    steps.column(3)
    steps.planes(1)
    weights(0, 0, 4)
    steps.cross(2)
    steps.halves(1)
    level_ready(1)
    weights(0, 4, 8)
    forward(1, 0, 4)
    steps.planes(2)
    weights(1, 0, 4)
    steps.cross(3)
    steps.halves(2)
    level_ready(2)
    weights(1, 4, 8)
    forward(2, 0, 4)
    weights(2, 0, 8)
    steps.planes(3)
    steps.halves(3)
    level_ready(3)
    forward(3, 0, 4)
    weights(3, 0, 8)
    for turn in range(LEVELS):
        for copy in leave(turn):
            copy.wait()

    def last_sums(step, carry):
        for copy in leave_sums(step):
            copy.wait()
        return carry

    lax.fori_loop(0, width // wide, last_sums, 0)
    steps.end(levels_waited=True)


def experts_products(rows, grad_rows, w_gate, w_up, w_down, experts_all, collective_id):
    blocks, low, count = lax.axis_size("gx"), jnp.bfloat16, rows.shape[0]
    hidden, width = w_down.shape
    everywhere = pl.BlockSpec(memory_space=pl.ANY)
    block_shape = (2, blocks, count)
    shapes = [
        jax.ShapeDtypeStruct((*block_shape, hidden), low),
        jax.ShapeDtypeStruct((*block_shape, 2 * hidden), low),
        jax.ShapeDtypeStruct((*block_shape, LANES), low),
        jax.ShapeDtypeStruct((width, hidden), jnp.float32),
        jax.ShapeDtypeStruct((width, hidden), jnp.float32),
        jax.ShapeDtypeStruct((hidden, width), jnp.float32),
        *[jax.ShapeDtypeStruct((blocks, count, width), low)] * 2,
    ]
    level_rows = 2 * PLANE * count
    dma = pltpu.SemaphoreType.DMA
    return pl.pallas_call(
        functools.partial(experts_kernel, experts_all),
        out_shape=shapes,
        in_specs=[everywhere] * 4 + [pl.BlockSpec(memory_space=pltpu.VMEM)],
        out_specs=[everywhere] * 8,
        scratch_shapes=[
            pltpu.VMEM((*block_shape, rows.shape[1]), low),
            pltpu.VMEM((2, 2, PLANE, count, width), low),
            pltpu.VMEM((width, 2 * hidden), low),
            pltpu.VMEM((2 * hidden, level_rows), low),
            pltpu.VMEM((hidden, level_rows), low),
            *[pltpu.VMEM(shape.shape, low) for shape in shapes[:3]],
            pltpu.VMEM((2 * hidden, width), jnp.float32),
            pltpu.VMEM((hidden, width), jnp.float32),
            pltpu.VMEM((2, width, hidden), jnp.float32),
            dma((2, 2)),
            dma((2,)),
            dma((LEVELS, 3)),
            dma((width // 256, 3)),
            *gather_semaphores(2, 2),
        ],
        compiler_params=pltpu.CompilerParams(
            collective_id=collective_id, has_side_effects=True, vmem_limit_bytes=63 * 1024 * 1024
        ),
    )(rows, grad_rows, w_gate, w_up, w_down)[:6]


class scatter_moves:
    def __init__(self, held, out):
        self.mine, self.half_y, self.half_x, self.full_x, self.full_y, self.slots_a, self.slots_b, self.side_b = held[:8]
        self.send_sem, self.recv_sem, self.chain_send, self.chain_recv = held[8:12]
        self.out = out
        self.me, self.core, level, x_side, y_side = neighbours()
        self.level = level
        self.up, self.down = (self.me + PLANE, self.core), (self.me - PLANE, self.core)
        self.to_x, self.to_y = (x_side, self.core), (y_side, self.core)
        self.x_at, self.y_at, self.own_at = x_side % PLANE, y_side % PLANE, self.me % PLANE
        self.diagonal_at = (x_side + y_side - self.me) % PLANE
        forward = jnp.where(level < 2, 1, 0)
        self.order = [3 * forward, 2 * forward + (1 - forward), level + 1 - 2 * (level % 2), level]
        self.rows, self.width = self.mine.shape[1:]
        self.spans = cut_rows(self.rows)
        self.sent = []

    def send(self, condition, source, target_ref, ssem, rsem, target):
        def copy():
            return pltpu.make_async_remote_copy(
                source, target_ref, ssem, rsem, device_id=target, device_id_type=MESH
            )

        when(condition, lambda: copy().start())
        self.sent.append((condition, copy))

    def arrive(self, condition, target_ref, rsem):
        def wait():
            pltpu.make_async_remote_copy(
                target_ref, target_ref, rsem, rsem, device_id=self.to_x, device_id_type=MESH
            ).wait_recv()

        when(condition, wait)

    def add(self, condition, height, target, *terms, step=16):
        def run():
            def body(i, carry):
                at = pl.multiple_of(i * step, step)
                total = target(at, step)[...].astype(jnp.float32)
                for term in terms:
                    total = total + term(at, step)[...].astype(jnp.float32)
                target(at, step)[...] = total.astype(jnp.bfloat16)
                return carry

            lax.fori_loop(0, height // step, body, 0)

        when(condition, run)

    def rows_of(self, ref, *index, start=0):
        return lambda at, step: ref.at[(*index, pl.ds(start + at, step))]

    def turn_sems(self, turn):
        return [(self.send_sem.at[6 * turn + i], self.recv_sem.at[6 * turn + i]) for i in range(6)]

    def half_spans(self):
        half_a = self.spans[1]
        return half_a[0][1], pl.ds(*half_a[0]), pl.ds(*half_a[1])

    def first(self, turn):
        base, at = PLANE * self.order[turn], self.turn_sems(turn)
        _, lower, upper = self.half_spans()
        mine, to_x, to_y = self.mine, self.to_x, self.to_y
        self.send(None, mine.at[base + self.diagonal_at, lower], self.half_y.at[turn], *at[0], to_y)
        self.send(None, mine.at[base + self.diagonal_at, upper], self.half_x.at[turn], *at[1], to_x)
        self.send(None, mine.at[base + self.x_at, upper], self.full_x.at[turn, upper], *at[2], to_x)
        self.send(None, mine.at[base + self.y_at, lower], self.full_y.at[turn, lower], *at[3], to_y)

    def second(self, turn):
        base, at = PLANE * self.order[turn], self.turn_sems(turn)
        height, lower, upper = self.half_spans()
        mine, rows_of = self.mine, self.rows_of
        self.arrive(None, self.half_y.at[turn], at[0][1])
        self.add(None, height, rows_of(mine, base + self.x_at), rows_of(self.half_y, turn))
        self.send(None, mine.at[base + self.x_at, lower], self.full_x.at[turn, lower], *at[4], self.to_x)
        self.arrive(None, self.half_x.at[turn], at[1][1])
        self.add(None, height, rows_of(mine, base + self.y_at, start=height), rows_of(self.half_x, turn))
        self.send(None, mine.at[base + self.y_at, upper], self.full_y.at[turn, upper], *at[5], self.to_y)

    def chain(self, which, turn, block, slots, spread):
        to_level, level = self.order[turn], self.level
        rising, falling = to_level > level, to_level < level
        begins = (rising & (level == 0)) | (falling & (level == LEVELS - 1))
        middle = (rising | falling) & jnp.logical_not(begins)
        self.arrive(middle, slots.at[to_level], self.chain_recv.at[which, to_level])
        spread(middle, to_level)
        outgoing = self.chain_send.at[which, to_level]
        self.send(rising, block, slots.at[to_level], outgoing, self.chain_recv.at[which, to_level], self.up)
        at = jnp.where(to_level == level - 1, LEVELS, to_level)
        self.send(falling, block, slots.at[at], outgoing, self.chain_recv.at[which, at], self.down)

    def add_small(self, condition, base, slot):
        start, number = self.spans[2]
        for column in range(PLANE):
            self.add(
                condition,
                number,
                self.rows_of(self.mine, base + column, start=start),
                self.rows_of(self.slots_b, slot, column),
            )

    def chain_small(self, turn):
        if turn == LEVELS - 1:
            return
        base = PLANE * self.order[turn]
        block = self.mine.at[pl.ds(base, PLANE), pl.ds(*self.spans[2])]
        self.chain(1, turn, block, self.slots_b, lambda condition, slot: self.add_small(condition, base, slot))

    def plane_arrives(self, turn):
        at = self.turn_sems(turn)
        _, lower, upper = self.half_spans()
        self.arrive(None, self.full_x.at[turn, upper], at[2][1])
        self.arrive(None, self.full_y.at[turn, lower], at[3][1])
        self.arrive(None, self.full_x.at[turn, lower], at[4][1])
        self.arrive(None, self.full_y.at[turn, upper], at[5][1])

    def chain_large(self, turn):
        if turn == LEVELS - 1:
            return
        own, number = PLANE * self.order[turn] + self.own_at, self.spans[0][1]
        rows_of, mine = self.rows_of, self.mine
        self.plane_arrives(turn)
        self.add(None, number, rows_of(mine, own), rows_of(self.full_x, turn), rows_of(self.full_y, turn))
        self.chain(
            0,
            turn,
            mine.at[own, pl.ds(*self.spans[0])],
            self.slots_a,
            lambda condition, slot: self.add(condition, number, rows_of(mine, own), rows_of(self.slots_a, slot)),
        )

    def side(self):
        short = self.spans[3][0][1]
        spans = [pl.ds(0, short), pl.ds(short, short), pl.ds(2 * short, 2 * short), pl.ds(4 * short, 2 * short)]
        return [(self.side_b.at[span], self.send_sem.at[24 + i], self.recv_sem.at[24 + i]) for i, span in enumerate(spans)]

    def arrivals(self):
        return ((self.level > 0, self.level), (self.level < LEVELS - 1, LEVELS))

    def end_small(self):
        base, mine, half_b = PLANE * self.level, self.mine, self.spans[3]
        for condition, slot in self.arrivals():
            self.arrive(condition, self.slots_b.at[slot], self.chain_recv.at[1, slot])
            self.add_small(condition, base, slot)
        side = self.side()
        self.send(None, mine.at[base + self.diagonal_at, pl.ds(*half_b[0])], *side[0], self.to_y)
        self.send(None, mine.at[base + self.diagonal_at, pl.ds(*half_b[1])], *side[1], self.to_x)

    def end_sides(self):
        base, mine, rows_of = PLANE * self.level, self.mine, self.rows_of
        whole_b, half_b = self.spans[2:]
        side, short = self.side(), half_b[0][1]
        self.plane_arrives(LEVELS - 1)
        self.arrive(None, side[0][0], side[0][2])
        self.add(None, short, rows_of(mine, base + self.x_at, start=half_b[0][0]), rows_of(self.side_b))
        self.send(None, mine.at[base + self.x_at, pl.ds(*whole_b)], *side[2], self.to_x)
        self.arrive(None, side[1][0], side[1][2])
        self.add(None, short, rows_of(mine, base + self.y_at, start=half_b[1][0]), rows_of(self.side_b, start=short))
        self.send(None, mine.at[base + self.y_at, pl.ds(*whole_b)], *side[3], self.to_y)

    def end_sums(self, base):
        whole_a, half_a, whole_b, half_b = self.spans
        own, out, mine, step = PLANE * self.level + self.own_at, self.out, self.mine, 16
        full_x, full_y, slots_a, side_b = self.full_x, self.full_y, self.slots_a, self.side_b

        def place(at):
            return pl.ds(pl.multiple_of(base + at, step), step)

        def tail_a(i, carry):
            at = pl.multiple_of(i * step, step)
            span, turn = pl.ds(at, step), LEVELS - 1
            total = mine[own, span].astype(jnp.float32)
            total = total + full_x[turn, span].astype(jnp.float32) + full_y[turn, span].astype(jnp.float32)
            out[place(at)] = total
            return carry

        lax.fori_loop(0, whole_a[1] // step, tail_a, 0)
        for condition, slot in self.arrivals():
            self.arrive(condition, slots_a.at[slot], self.chain_recv.at[0, slot])

            def more(slot=slot):
                def body(i, carry):
                    at = pl.multiple_of(i * step, step)
                    out[place(at)] = out[place(at)] + slots_a[slot, pl.ds(at, step)].astype(jnp.float32)
                    return carry

                lax.fori_loop(0, whole_a[1] // step, body, 0)

            when(condition, more)
        side, short = self.side(), half_b[0][1]
        self.arrive(None, side[2][0], side[2][2])
        self.arrive(None, side[3][0], side[3][2])

        def tail_b(i, carry):
            at = pl.multiple_of(i * step, step)
            total = mine[own, pl.ds(whole_b[0] + at, step)].astype(jnp.float32)
            total = total + side_b[pl.ds(2 * short + at, step)].astype(jnp.float32)
            total = total + side_b[pl.ds(4 * short + at, step)].astype(jnp.float32)
            out[place(whole_b[0] + at)] = total
            return carry

        lax.fori_loop(0, whole_b[1] // step, tail_b, 0)

    def end_waits(self):
        for condition, copy in self.sent:
            when(condition, lambda copy=copy: copy().wait_send())


def scatter_places(blocks, rows, width):
    near, far, low, dma = 3 * rows // 4, rows // 4, jnp.bfloat16, pltpu.SemaphoreType.DMA
    shapes = [
        (blocks, rows, width),
        (LEVELS, near // 2, width),
        (LEVELS, near // 2, width),
        (LEVELS, near, width),
        (LEVELS, near, width),
        (LEVELS + 1, near, width),
        (LEVELS + 1, PLANE, far, width),
        (3 * far, width),
    ]
    return [pltpu.VMEM(shape, low) for shape in shapes] + [dma((28,)), dma((28,)), dma((2, 5)), dma((2, 5))]


PLACES = 12


def scatter_kernel(count, *refs):
    pieces, gain_ref, out, gain_out = refs[:count], *refs[count : count + 3]
    held, (load_sem, gain_slots, gain_send, gain_recv) = refs[count + 3 : -4], refs[-4:]
    moves = scatter_moves(held, out)
    me, core, level = moves.me, moves.core, moves.level
    far = me + 2 * PLANE - 4 * PLANE * (level // 2)
    greet(level, (moves.to_x[0], moves.to_y[0], far), True, me, core)
    partners = ((me, 1 - core), moves.to_x, moves.to_y, (me + PLANE - 2 * PLANE * (level % 2), core), (far, core))

    def gain_copy(turn):
        return pltpu.make_async_remote_copy(
            gain_slots.at[2 * turn],
            gain_slots.at[2 * turn + 1],
            gain_send.at[turn],
            gain_recv.at[turn],
            device_id=partners[turn],
            device_id_type=MESH,
        )

    def gain_step(turn):
        if turn == 0:
            gain_slots[0] = gain_ref[...]
        else:
            gain_copy(turn - 1).wait_recv()
            gain_slots[2 * turn] = gain_slots[2 * turn - 2] + gain_slots[2 * turn - 1]
        if turn < len(partners):
            gain_copy(turn).start()
        else:
            gain_out[...] = gain_slots[2 * turn]

    def load(turn):
        copies, lane = [], 0
        span = pl.ds(PLANE * moves.order[turn], PLANE)
        for i, piece in enumerate(pieces):
            place = moves.mine.at[span, :, pl.ds(lane, piece.shape[2])]
            copies.append(pltpu.make_async_copy(piece.at[span], place, load_sem.at[i, turn]))
            lane += piece.shape[2]
        return copies

    for turn in range(LEVELS):
        for copy in load(turn):
            copy.start()
    gain_step(0)
    for turn in range(LEVELS):
        for copy in load(turn):
            copy.wait()
        moves.first(turn)
        moves.chain_small(turn)
    for turn in range(LEVELS - 1):
        moves.second(turn)
        gain_step(turn + 1)
        if turn:
            moves.chain_large(turn - 1)
    moves.second(LEVELS - 1)
    gain_step(4)
    moves.chain_large(LEVELS - 2)
    moves.end_small()
    moves.end_sides()
    gain_step(5)
    moves.end_sums(0)
    for turn in range(len(partners)):
        gain_copy(turn).wait_send()
    moves.end_waits()


def scatter_sums(pieces, gains, collective_id):
    blocks, rows = pieces[0].shape[:2]
    width = sum(piece.shape[2] for piece in pieces)
    dma = pltpu.SemaphoreType.DMA
    vmem, everywhere = pl.BlockSpec(memory_space=pltpu.VMEM), pl.BlockSpec(memory_space=pl.ANY)
    return pl.pallas_call(
        functools.partial(scatter_kernel, len(pieces)),
        out_shape=[
            jax.ShapeDtypeStruct((rows, width), jnp.float32),
            jax.ShapeDtypeStruct(gains.shape, gains.dtype),
        ],
        in_specs=[everywhere] * len(pieces) + [vmem],
        out_specs=[vmem] * 2,
        scratch_shapes=[
            *scatter_places(blocks, rows, width),
            dma((len(pieces), LEVELS)),
            pltpu.VMEM((11, *gains.shape), gains.dtype),
            dma((5,)),
            dma((5,)),
        ],
        compiler_params=pltpu.CompilerParams(
            collective_id=collective_id, has_side_effects=True, vmem_limit_bytes=60 * 1024 * 1024
        ),
    )(*pieces, gains)


def return_kernel(grad_in, weighted, terms, w_gate, w_up, w_down, back_out, mixed_out, *refs):
    streams = [
        scatter_moves(refs[:PLACES], back_out),
        scatter_moves(refs[PLACES : 2 * PLACES], mixed_out),
    ]
    sibling, away, left, right_in, right_down = refs[2 * PLACES : 2 * PLACES + 5]
    pair_send, pair_recv, left_sem, right_sem, term_sem, ready_sem, credit = refs[2 * PLACES + 5 :]
    me, core, order, rows = streams[0].me, streams[0].core, streams[0].order, streams[0].rows
    greet(streams[0].level, (streams[0].to_x[0], streams[0].to_y[0]), True, me, core)
    hidden, features = w_down.shape
    depths, lefts = (2 * hidden, hidden), (grad_in, weighted)
    turns, wide = 2 * LEVELS, 256
    rights = [
        pltpu.make_async_copy(w_gate, right_in.at[:, pl.ds(0, hidden)], right_sem.at[0]),
        pltpu.make_async_copy(w_up, right_in.at[:, pl.ds(hidden, hidden)], right_sem.at[1]),
        pltpu.make_async_copy(w_down, right_down, right_sem.at[2]),
    ]

    def level_span(turn):
        return pl.ds(PLANE * order[turn % LEVELS], PLANE)

    def left_copy(turn):
        stream = turn // LEVELS
        return pltpu.make_async_copy(
            lefts[stream].at[:, level_span(turn)],
            left.at[turn % 2, :, :, :, pl.ds(0, depths[stream])],
            left_sem.at[turn % 2],
        )

    def term_copy(turn, half):
        lanes = pl.ds(features, LANES)
        place = away.at[turn % 2, :, :, lanes] if half else streams[0].mine.at[level_span(turn), :, lanes]
        return pltpu.make_async_copy(terms.at[half, level_span(turn)], place, term_sem.at[half])

    def width_of(turn):
        return streams[turn // LEVELS].width

    def hand(turn):
        lanes = pl.ds(0, width_of(turn))
        return pltpu.make_async_remote_copy(
            away.at[turn % 2, :, :, lanes],
            sibling.at[turn % 2, :, :, lanes],
            pair_send.at[turn],
            pair_recv.at[turn],
            device_id=(me, 1 - core),
            device_id_type=MESH,
        )

    def product(turn, half, store):
        stream, slot = turn // LEVELS, turn % 2
        factor = left[slot, half, :, :, pl.ds(0, depths[stream])].reshape(PLANE * rows, depths[stream])

        def body(step, carry):
            span = pl.ds(pl.multiple_of(step * wide, wide), wide)
            value = dot_nt(factor, right_in[span]) if stream == 0 else dot_nn(factor, right_down[:, span])
            store(span, value.reshape(PLANE, rows, wide))
            return carry

        lax.fori_loop(0, features // wide, body, 0)

    def hand_over(turn):
        left_copy(turn).wait()
        if turn + 1 < turns:
            left_copy(turn + 1).start()
        if turn < LEVELS:
            term_copy(turn, 1).start()
            term_copy(turn, 0).start()

        def store(span, value):
            away[turn % 2, :, :, span] = value.astype(jnp.bfloat16)

        product(turn, 1, store)
        if turn < LEVELS:
            term_copy(turn, 1).wait()
            term_copy(turn, 0).wait()
        if turn >= 2:
            pl.semaphore_wait(credit, 1)
        hand(turn).start()

    def settle(turn):
        hand(turn).wait()
        mine, slot = streams[turn // LEVELS].mine, turn % 2

        def store(span, value):
            value = value + sibling[slot, :, :, span].astype(jnp.float32)
            mine[level_span(turn), :, span] = value.astype(jnp.bfloat16)

        product(turn, 0, store)
        if turn < LEVELS:
            lanes = pl.ds(features, LANES)
            value = mine[level_span(turn), :, lanes].astype(jnp.float32)
            value = value + sibling[slot, :, :, lanes].astype(jnp.float32)
            mine[level_span(turn), :, lanes] = value.astype(jnp.bfloat16)
        if turn + 2 < turns:
            pl.semaphore_signal(credit, inc=1, device_id=(me, 1 - core), device_id_type=MESH)

    def exchange(stream, core_of_rows):
        out = streams[stream].out
        span = pl.ds(pl.multiple_of(core_of_rows * rows, rows), rows)
        return pltpu.make_async_remote_copy(
            out.at[span],
            out.at[span],
            ready_sem.at[stream, 0],
            ready_sem.at[stream, 1],
            device_id=(me, 1 - core),
            device_id_type=MESH,
        )

    def end(stream):
        streams[stream].end_sums(core * rows)
        exchange(stream, core).start()

    left_copy(0).start()
    for copy in rights:
        copy.start()
    for copy in rights:
        copy.wait()
    hand_over(0)
    for turn in range(turns + 2):
        if turn < turns:
            stream = streams[turn // LEVELS]
            settle(turn)
            stream.first(turn % LEVELS)
            if turn + 1 < turns:
                hand_over(turn + 1)
            stream.chain_small(turn % LEVELS)
        if 1 <= turn <= turns:
            streams[(turn - 1) // LEVELS].second((turn - 1) % LEVELS)
        if turn >= 2:
            streams[(turn - 2) // LEVELS].chain_large((turn - 2) % LEVELS)
        if turn == LEVELS + 1:
            streams[0].end_small()
        if turn == LEVELS + 2:
            streams[0].end_sides()
        if turn == LEVELS + 3:
            end(0)
    streams[1].end_small()
    streams[1].end_sides()
    end(1)
    for stream in range(2):
        exchange(stream, 1 - core).wait_recv()
        exchange(stream, core).wait_send()
        streams[stream].end_waits()


def return_sums(grad_in, weighted, terms, w_gate, w_up, w_down, collective_id):
    low, dma = jnp.bfloat16, pltpu.SemaphoreType.DMA
    blocks, rows, depth = grad_in.shape[1:]
    hidden, features = w_down.shape
    wide = features + LANES
    vmem, everywhere = pl.BlockSpec(memory_space=pltpu.VMEM), pl.BlockSpec(memory_space=pl.ANY)
    slots = pltpu.VMEM((2, PLANE, rows, wide), low)
    return pl.pallas_call(
        return_kernel,
        out_shape=[
            jax.ShapeDtypeStruct((2 * rows, wide), jnp.float32),
            jax.ShapeDtypeStruct((2 * rows, features), jnp.float32),
        ],
        in_specs=[everywhere] * 6,
        out_specs=[vmem] * 2,
        scratch_shapes=[
            *scatter_places(blocks, rows, wide),
            *scatter_places(blocks, rows, features),
            slots,
            slots,
            pltpu.VMEM((2, 2, PLANE, rows, depth), low),
            pltpu.VMEM((features, depth), low),
            pltpu.VMEM((hidden, features), low),
            dma((2 * LEVELS,)),
            dma((2 * LEVELS,)),
            dma((2,)),
            dma((3,)),
            dma((2,)),
            dma((2, 2)),
            pltpu.SemaphoreType.REGULAR,
        ],
        compiler_params=pltpu.CompilerParams(
            collective_id=collective_id, has_side_effects=True, vmem_limit_bytes=63 * 1024 * 1024
        ),
    )(grad_in, weighted, terms, w_gate, w_up, w_down)


def kernels_fit():
    return lax.axis_size("gx") == LEVELS * PLANE and lax.axis_size("gy") == 2


def packed_gains(vectors):
    rows = jnp.concatenate([vector.reshape(-1, HEAD_DIM) for vector in vectors], axis=0)
    return jnp.pad(rows, ((0, -rows.shape[0] % 8), (0, 0)))


def unpacked_gains(rows, vectors):
    sums, at = [], 0
    for vector in vectors:
        length = vector.shape[0] // HEAD_DIM
        sums.append(rows[at : at + length].reshape(-1))
        at += length
    return sums


def two_parts(values):
    high = lax.reduce_precision(values, 8, 7)
    return high.astype(jnp.bfloat16), (values - high).astype(jnp.bfloat16)


def sparse_experts(normed_ffn, logits, route_hits, routes, cotangent, w_gate, w_up, w_down):
    sequence_length, model_width = normed_ffn.shape
    experts_all = logits.shape[1]
    devices_gx = lax.axis_size("gx")
    part_width = model_width // lax.axis_size("gy")
    capacity = 5 * sequence_length * TOP // (4 * experts_all)
    pairs_count = sequence_length * TOP
    hits_float = route_hits.astype(jnp.float32)
    chosen = jnp.sum(logits[:, None, :] * hits_float, axis=-1)
    gate_exps = jnp.exp(chosen)
    gate_values = gate_exps / jnp.sum(gate_exps, axis=1, keepdims=True)
    flat_hits = route_hits.reshape(pairs_count, experts_all).astype(jnp.int32)
    slot_rank = jnp.sum((jnp.cumsum(flat_hits, axis=0) - flat_hits) * flat_hits, axis=1)
    slot_dest = routes.reshape(-1) * capacity + slot_rank
    slot_pair = (
        jnp.full((experts_all * capacity,), pairs_count, jnp.int32)
        .at[slot_dest]
        .set(jnp.arange(pairs_count, dtype=jnp.int32))
    )
    slot_token = jnp.where(slot_pair < pairs_count, slot_pair // TOP, sequence_length)

    def to_experts(buffer):
        arrived = lax.all_to_all(buffer, "gx", split_axis=0, concat_axis=0, tiled=True)
        return arrived.reshape(devices_gx * capacity, model_width)

    def from_experts(partial_rows):
        share_rows = lax.psum_scatter(
            partial_rows.astype(jnp.bfloat16), "gy", scatter_dimension=1, tiled=True
        )
        returned = lax.all_to_all(
            share_rows.reshape(devices_gx, capacity, part_width),
            "gx",
            split_axis=0,
            concat_axis=0,
            tiled=True,
        )
        whole_rows = lax.all_gather(returned, "gy", axis=2, tiled=True)
        return whole_rows.reshape(devices_gx * capacity, model_width)

    send_rows = jnp.take(normed_ffn, slot_token, axis=0, mode="fill", fill_value=0)
    expert_in = to_experts(send_rows.reshape(devices_gx, capacity, model_width))
    gate_in = jnp.dot(expert_in, w_gate, preferred_element_type=jnp.float32)
    up_in = jnp.dot(expert_in, w_up, preferred_element_type=jnp.float32)
    gate_sigmoid = jax.nn.sigmoid(gate_in)
    gate_swish = gate_in * gate_sigmoid
    activated = (gate_swish * up_in).astype(jnp.bfloat16)
    expert_part = jnp.dot(activated, w_down, preferred_element_type=jnp.float32)
    expert_out = from_experts(expert_part)
    pair_rows = jnp.take(expert_out, slot_dest, axis=0).reshape(sequence_length, TOP, model_width)
    mixed_rows = jnp.einsum(
        "tk,tkd->td", gate_values, pair_rows, preferred_element_type=jnp.float32
    )
    grad_out_f = cotangent.astype(jnp.float32)
    grad_gates = jnp.einsum("td,tkd->tk", grad_out_f, pair_rows, preferred_element_type=jnp.float32)
    grad_chosen = gate_values * (
        grad_gates - jnp.sum(gate_values * grad_gates, axis=1, keepdims=True)
    )
    grad_logits = jnp.sum(grad_chosen[:, :, None] * hits_float, axis=1).astype(jnp.bfloat16)
    slot_gate = jnp.take(gate_values.reshape(-1), slot_pair, mode="fill", fill_value=0.0)
    grad_send = (
        jnp.take(grad_out_f, slot_token, axis=0, mode="fill", fill_value=0) * slot_gate[:, None]
    )
    grad_expert_out = to_experts(
        grad_send.astype(jnp.bfloat16).reshape(devices_gx, capacity, model_width)
    )
    grad_act = contract(grad_expert_out, w_down, 1, 1)
    down_term = contract(activated, grad_expert_out, 0, 0)
    grad_gate_in = (
        grad_act * up_in * gate_sigmoid * (1.0 + gate_in * (1.0 - gate_sigmoid))
    ).astype(jnp.bfloat16)
    grad_up_in = (grad_act * gate_swish).astype(jnp.bfloat16)
    gate_term = contract(expert_in, grad_gate_in, 0, 0)
    up_term = contract(expert_in, grad_up_in, 0, 0)
    grad_in_part = contract(grad_gate_in, w_gate, 1, 1) + contract(grad_up_in, w_up, 1, 1)
    grad_rows = from_experts(grad_in_part)
    grad_pairs = jnp.take(grad_rows, slot_dest, axis=0).reshape(sequence_length, TOP, model_width)
    grad_rows_sum = jnp.sum(grad_pairs.astype(jnp.float32), axis=1)
    return mixed_rows, grad_rows_sum, grad_logits, (gate_term[None], up_term[None], down_term[None])


def swap_cores(rows):
    return lax.ppermute(rows, "gy", [(0, 1), (1, 0)])


def own_half(rows):
    count = rows.shape[0] // lax.axis_size("gy")
    return lax.dynamic_slice_in_dim(rows, lax.axis_index("gy") * count, count, 0)


def dense_experts(normed_ffn, logits, route_hits, cotangent, w_gate, w_up, w_down):
    sequence_length, model_width = normed_ffn.shape
    experts_all = logits.shape[1]
    gate_exps = jnp.exp(jnp.where(jnp.any(route_hits, axis=1), logits, -1e30))
    gate_all = gate_exps / jnp.sum(gate_exps, axis=1, keepdims=True)
    gate_lanes = jnp.pad(jnp.concatenate(two_parts(gate_all), axis=1), ((0, 0), (0, LANES - 2 * experts_all)))
    row_lanes = jnp.concatenate([own_half(normed_ffn), own_half(gate_lanes)], axis=1)
    weighted, grad_in, terms, gate_term, up_term, down_term = experts_products(
        row_lanes, own_half(cotangent), w_gate, w_up, w_down, experts_all, 2
    )
    back, mixed_rows = return_sums(grad_in, weighted, terms, w_gate, w_up, w_down, 3)
    term_lanes = back[:, model_width : model_width + 4 * experts_all]
    grad_gates = jnp.sum(term_lanes.reshape(sequence_length, 4, experts_all), axis=1)
    grad_logits = (
        gate_all * (grad_gates - jnp.sum(gate_all * grad_gates, axis=1, keepdims=True))
    ).astype(jnp.bfloat16)
    return mixed_rows, back[:, :model_width], grad_logits, (gate_term[None], up_term[None], down_term[None])


def turn_lanes(values, cosine, sine_table):
    return values * cosine + pltpu.roll(values, HEAD_DIM // 2, 1) * sine_table


def unit_rows(values):
    scale = lax.rsqrt(jnp.mean(values * values, axis=1, keepdims=True) + EPSILON)
    return values * scale, scale


def allowed_pairs(docs_column, docs_row):
    shape = (docs_column.shape[0], docs_row.shape[1])
    keys_at, queries_at = lax.broadcasted_iota(jnp.int32, shape, 0), lax.broadcasted_iota(jnp.int32, shape, 1)
    return (keys_at <= queries_at) & (docs_column == docs_row)


def head_span(head):
    return pl.ds(pl.multiple_of(head * HEAD_DIM, HEAD_DIM), HEAD_DIM)


def attend_kernel(
    q_heads, kv_heads, raw_ref, cosine_ref, sine_ref, docs_column, docs_row, q_gain, k_gain,
    attended_ref, query_ref, key_ref, value_ref, totals_ref,
):
    cosine, sine_table = cosine_ref[...], sine_ref[...]
    allowed = allowed_pairs(docs_column[...], docs_row[...])
    group, inv_root = q_heads // kv_heads, 1.0 / math.sqrt(HEAD_DIM)
    for kv in range(kv_heads):
        unit, _ = unit_rows(raw_ref[:, head_span(q_heads + kv)])
        key_rows = turn_lanes(unit * k_gain[...], cosine, sine_table).astype(jnp.bfloat16)
        value_rows = raw_ref[:, head_span(q_heads + kv_heads + kv)]
        key_ref[:, head_span(kv)] = key_rows
        value_ref[:, head_span(kv)] = value_rows.astype(jnp.bfloat16)
        value_columns = value_rows.T.astype(jnp.bfloat16)

        def body(index, carry, kv=kv, key_rows=key_rows, value_columns=value_columns):
            head = kv * group + index
            unit, _ = unit_rows(raw_ref[:, head_span(head)])
            query_rows = turn_lanes(unit * q_gain[...], cosine, sine_table).astype(jnp.bfloat16)
            query_ref[:, head_span(head)] = query_rows
            scores = jnp.where(allowed, dot_nt(key_rows, query_rows) * inv_root, -1e30)
            peak = jnp.max(scores, axis=0, keepdims=True)
            exps = jnp.exp(scores - peak)
            total = jnp.sum(exps, axis=0, keepdims=True)
            totals_ref[pl.ds(head, 1), :] = peak + jnp.log(total)
            probs = (exps / total).astype(jnp.bfloat16)
            attended_ref[:, head_span(head)] = dot_nn(value_columns, probs).T.astype(jnp.bfloat16)
            return carry

        lax.fori_loop(0, group, body, 0, unroll=2)


def attend_back_kernel(
    q_heads, kv_heads, raw_ref, cosine_ref, sine_ref, docs_column, docs_row, q_gain, k_gain,
    query_ref, key_ref, value_ref, totals_ref, grad_ref, grad_raw_ref, gains_ref, sums_ref,
):
    cosine, sine_table = cosine_ref[...], sine_ref[...]
    allowed = allowed_pairs(docs_column[...], docs_row[...])
    group, inv_root = q_heads // kv_heads, 1.0 / math.sqrt(HEAD_DIM)
    gains_ref[...] = jnp.zeros_like(gains_ref)

    def back_to_raw(grad, head, gain, gain_row):
        grad = turn_lanes(grad, cosine, -sine_table)
        unit, scale = unit_rows(raw_ref[:, head_span(head)])
        gains_ref[pl.ds(gain_row, 1), :] += jnp.sum(grad * unit, axis=0, keepdims=True)
        grad = grad * gain
        grad = scale * (grad - unit * jnp.mean(grad * unit, axis=1, keepdims=True))
        grad_raw_ref[:, head_span(head)] = grad.astype(jnp.bfloat16)

    for kv in range(kv_heads):
        key_rows, value_rows = key_ref[:, head_span(kv)], value_ref[:, head_span(kv)]
        key_columns = key_rows.astype(jnp.float32).T.astype(jnp.bfloat16)
        sums_ref[...] = jnp.zeros_like(sums_ref)

        def body(index, carry, kv=kv, key_rows=key_rows, value_rows=value_rows, key_columns=key_columns):
            head = kv * group + index
            query_rows, grad_rows = query_ref[:, head_span(head)], grad_ref[:, head_span(head)]
            scores = jnp.where(allowed, dot_nt(key_rows, query_rows) * inv_root, -1e30)
            probs = jnp.exp(scores - totals_ref[pl.ds(head, 1), :])
            sums_ref[0] += dot_nn(probs.astype(jnp.bfloat16), grad_rows)
            grad_probs = dot_nt(value_rows, grad_rows)
            inner = jnp.sum(probs * grad_probs, axis=0, keepdims=True)
            grad_scores = (probs * (grad_probs - inner)).astype(jnp.bfloat16)
            sums_ref[1] += dot_nn(grad_scores, query_rows)
            grad_queries = dot_nn(key_columns, grad_scores).T * inv_root
            back_to_raw(grad_queries, head, q_gain[...], 0)
            return carry

        lax.fori_loop(0, group, body, 0, unroll=2)
        back_to_raw(sums_ref[1] * inv_root, q_heads + kv, k_gain[...], 1)
        grad_raw_ref[:, head_span(q_heads + kv_heads + kv)] = sums_ref[0].astype(jnp.bfloat16)


def attention_shared(qkv_rows, doc_ids, query_norm_gain, k_gain):
    length = qkv_rows.shape[0]
    cosine, sine_table = rotary_tables(length, HEAD_DIM)
    cosine, sine_table = cosine[:, 0], sine_table[:, 0]
    return (
        qkv_rows,
        jnp.concatenate([cosine, cosine], axis=1),
        jnp.concatenate([-sine_table, sine_table], axis=1),
        doc_ids.reshape(length, 1),
        doc_ids.reshape(1, length),
        query_norm_gain.reshape(1, HEAD_DIM),
        k_gain.reshape(1, HEAD_DIM),
    )


def attend(shared, q_heads, kv_heads):
    length, low, shape = shared[0].shape[0], jnp.bfloat16, jax.ShapeDtypeStruct
    return pl.pallas_call(
        functools.partial(attend_kernel, q_heads, kv_heads),
        out_shape=[
            shape((length, q_heads * HEAD_DIM), low),
            shape((length, q_heads * HEAD_DIM), low),
            shape((length, kv_heads * HEAD_DIM), low),
            shape((length, kv_heads * HEAD_DIM), low),
            shape((q_heads, length), jnp.float32),
        ],
        compiler_params=pltpu.CompilerParams(vmem_limit_bytes=48 * 1024 * 1024),
    )(*shared)


def attend_back(shared, kept, grad_attended, q_heads, kv_heads):
    length, shape = shared[0].shape[0], jax.ShapeDtypeStruct
    return pl.pallas_call(
        functools.partial(attend_back_kernel, q_heads, kv_heads),
        out_shape=[shape(shared[0].shape, jnp.bfloat16), shape((8, HEAD_DIM), jnp.float32)],
        scratch_shapes=[pltpu.VMEM((2, length, HEAD_DIM), jnp.float32)],
        compiler_params=pltpu.CompilerParams(vmem_limit_bytes=48 * 1024 * 1024),
    )(*shared, *kept, grad_attended)


def on_device(
    tokens_in,
    doc_ids,
    routes,
    q_weight,
    key_matrix,
    value_matrix,
    out_weight,
    router_weight,
    attn_gain,
    ffn_gain,
    query_norm_gain,
    k_gain,
    gate_weight,
    up_weight,
    down_weight,
    cotangent,
):
    sequence_length = tokens_in.shape[0]
    model_width = tokens_in.shape[1]
    devices_gx = lax.axis_size("gx")
    devices_gy = lax.axis_size("gy")
    part_width = model_width // devices_gy
    experts_all = router_weight.shape[1]
    router_lanes = jnp.pad(router_weight, ((0, 0), (0, LANES - experts_all)))
    rows_local = jnp.concatenate([q_weight, key_matrix, value_matrix, router_lanes, out_weight], axis=1)
    dense = kernels_fit() and experts_all <= 2 * TOP
    if dense:
        (weights_all,) = gather_blocks([rows_local], (0,), 1)
        weights_all = weights_all.reshape(-1, rows_local.shape[1])
    else:
        weights_all = lax.all_gather(rows_local, "gx", axis=0, tiled=True)
    q_width, kv_width = q_weight.shape[1], key_matrix.shape[1]
    qkv_width = q_width + 2 * kv_width
    qkv_full = weights_all[:, :qkv_width]
    router_full = weights_all[:, qkv_width : qkv_width + experts_all]
    o_full = weights_all[:, qkv_width + LANES :]
    heads_local = q_width // HEAD_DIM
    kv_local = kv_width // HEAD_DIM
    inputs_f = tokens_in.astype(jnp.float32)
    scale_one = root_mean_scale(inputs_f)
    unit_one = inputs_f * scale_one
    normalized_input = (unit_one * attn_gain).astype(jnp.bfloat16)
    qkv_rows = jnp.dot(normalized_input, qkv_full, preferred_element_type=jnp.float32)
    shared = attention_shared(qkv_rows, doc_ids, query_norm_gain, k_gain)
    attended, *kept = attend(shared, heads_local, kv_local)
    attn_part = contract(attended, o_full, 1, 1)
    attn_total = attn_part + swap_cores(attn_part)
    residual = inputs_f + attn_total
    scale_two = root_mean_scale(residual)
    unit_two = residual * scale_two
    normed_ffn = (unit_two * ffn_gain).astype(jnp.bfloat16)
    logits = jnp.dot(normed_ffn, router_full, preferred_element_type=jnp.float32)
    expert_iota = jnp.arange(experts_all, dtype=jnp.int32)
    route_hits = routes[:, :, None] == expert_iota
    if dense:
        mixed_rows, grad_rows_sum, grad_logits, expert_grads = dense_experts(
            normed_ffn, logits, route_hits, cotangent, gate_weight[0], up_weight[0], down_weight[0]
        )
    else:
        mixed_rows, grad_rows_sum, grad_logits, expert_grads = sparse_experts(
            normed_ffn, logits, route_hits, routes, cotangent, gate_weight[0], up_weight[0], down_weight[0]
        )
    output = (residual + mixed_rows).astype(jnp.bfloat16)
    grad_out_f = cotangent.astype(jnp.float32)
    router_term = contract(normed_ffn, grad_logits, 0, 0)
    grad_ffn_in = contract(grad_logits, router_full, 1, 1) + grad_rows_sum
    ffn_gain_term = jnp.sum(grad_ffn_in * unit_two, axis=0)
    grad_residual = grad_out_f + norm_back(grad_ffn_in * ffn_gain, unit_two, scale_two)
    grad_attn = grad_residual.astype(jnp.bfloat16)
    out_term = contract(grad_attn, attended, 0, 0)
    grad_attended = jnp.dot(grad_attn, o_full, preferred_element_type=jnp.float32).astype(
        jnp.bfloat16
    )
    grad_qkv, head_gains = attend_back(shared, kept, grad_attended, heads_local, kv_local)
    q_gain_term, k_gain_term = head_gains[0], head_gains[1]
    qkv_term = contract(normalized_input, grad_qkv, 0, 0)
    grad_normed_part = contract(grad_qkv, qkv_full, 1, 1)
    grad_normed = grad_normed_part + swap_cores(grad_normed_part)
    attn_gain_term = jnp.sum(grad_normed * unit_one, axis=0)
    grad_input = (grad_residual + norm_back(grad_normed * attn_gain, unit_one, scale_one)).astype(
        jnp.bfloat16
    )
    own_mask = (jnp.arange(model_width) // part_width == lax.axis_index("gy")).astype(jnp.float32)
    gains = (attn_gain_term * own_mask, ffn_gain_term * own_mask, q_gain_term, k_gain_term)
    router_lanes = jnp.pad(router_term, ((0, 0), (0, LANES - experts_all)))
    if dense:
        pieces = [
            term.astype(jnp.bfloat16).reshape(devices_gx, -1, term.shape[1])
            for term in (qkv_term, router_lanes, out_term)
        ]
        sums, gain_rows = scatter_sums(pieces, packed_gains(gains), 4)
        gains = unpacked_gains(gain_rows, gains)
    else:
        sums = jnp.concatenate(
            [
                lax.psum_scatter(term, "gx", scatter_dimension=0, tiled=True)
                for term in (qkv_term, router_lanes, out_term)
            ],
            axis=1,
        )
        gains = lax.psum(gains, ("gx", "gy"))
    gain_attn, gain_ffn, gain_query, gain_key = gains
    grad_q = sums[:, :q_width]
    grad_k = sums[:, q_width : q_width + kv_width]
    grad_v = sums[:, q_width + kv_width : qkv_width]
    grad_router = sums[:, qkv_width : qkv_width + experts_all]
    grad_out = sums[:, qkv_width + LANES :]
    return (
        output,
        grad_input,
        grad_q,
        grad_k,
        grad_v,
        grad_out,
        grad_router,
        gain_attn,
        gain_ffn,
        gain_query,
        gain_key,
        expert_grads[0],
        expert_grads[1],
        expert_grads[2],
    )


def solution(mesh):
    return jax.shard_map(
        on_device,
        mesh=mesh,
        in_specs=(
            P("gx", None),
            P("gx", None),
            P("gx", None),
            P("gx", "gy"),
            P("gx", "gy"),
            P("gx", "gy"),
            P("gx", "gy"),
            P("gx", None),
            P(),
            P(),
            P(),
            P(),
            P("gx", None, "gy"),
            P("gx", None, "gy"),
            P("gx", "gy", None),
            P("gx", None),
        ),
        out_specs=(
            P("gx", None),
            P("gx", None),
            P("gx", "gy"),
            P("gx", "gy"),
            P("gx", "gy"),
            P("gx", "gy"),
            P("gx", None),
            P(),
            P(),
            P(),
            P(),
            P("gx", None, "gy"),
            P("gx", None, "gy"),
            P("gx", "gy", None),
        ),
        check_vma=False,
    )
```

```python
import functools
import math

import jax
import jax.numpy as jnp
from jax import lax
from jax.experimental import pallas as pl
from jax.experimental.pallas import tpu as pltpu
from jax.sharding import PartitionSpec as P

QUERY_HEADS = 32
KEY_VALUE_HEADS = 4
HEAD_DIM = 128
LANES = 128
TOP = 8


EPSILON = 1e-06
THETA = 1000000.0


def root_mean_scale(values):
    return lax.rsqrt(jnp.mean(values * values, axis=-1, keepdims=True) + EPSILON)


def rotary_tables(sequence_length, head_width):
    half_width = head_width // 2
    frequencies = THETA ** (-(2.0 * jnp.arange(half_width, dtype=jnp.float32)) / head_width)
    angles = jnp.arange(sequence_length, dtype=jnp.float32)[:, None] * frequencies[None, :]
    return (jnp.cos(angles)[:, None, :], jnp.sin(angles)[:, None, :])


def norm_back(grad_normed, normed_unit, scale_rows):
    return scale_rows * (
        grad_normed - normed_unit * jnp.mean(grad_normed * normed_unit, axis=-1, keepdims=True)
    )


def contract(first_op, second_op, first_dim, second_dim):
    return lax.dot_general(
        first_op,
        second_op,
        (((first_dim,), (second_dim,)), ((), ())),
        preferred_element_type=jnp.float32,
    )


MESH = pl.DeviceIdType.MESH
LEVELS = 4
PLANE = 4


def cut_rows(rows):
    near, far = 3 * rows // 4, rows // 4
    return (
        (0, near),
        ((0, near // 2), (near // 2, near // 2)),
        (near, far),
        ((near, far // 2), (near + far // 2, far // 2)),
    )


def neighbours():
    me, core = lax.axis_index("gx"), lax.axis_index("gy")
    level = me // PLANE
    x_side = me + 1 - 2 * (me % 2)
    y_side = me + 2 - 4 * ((me // 2) % 2)
    return me, core, level, x_side, y_side


def greet(level, targets, with_core, me, core):
    barrier = pltpu.get_barrier_semaphore()

    def hello(device):
        pl.semaphore_signal(barrier, inc=1, device_id=device, device_id_type=MESH)

    for target in targets:
        hello((target, core))
    if with_core:
        hello((me, 1 - core))

    @pl.when(level > 0)
    def _():
        hello((me - PLANE, core))

    @pl.when(level < LEVELS - 1)
    def _():
        hello((me + PLANE, core))

    inner = jnp.where(level > 0, 1, 0) + jnp.where(level < LEVELS - 1, 1, 0)
    pl.semaphore_wait(barrier, len(targets) + int(with_core) + inner)


def when(condition, action):
    if condition is None:
        action()
    else:
        pl.when(condition)(action)


def gather_kernel(count, with_pair, *refs):
    paired = sum(with_pair)
    ins, outs, pairs = refs[:count], refs[count : 2 * count], list(refs[2 * count : 2 * count + paired])
    pairs = [pairs.pop(0) if wanted else None for wanted in with_pair]
    sems = refs[2 * count + paired :]
    steps = gather_steps(ins, outs, pairs, sems)
    for step in steps.order:
        step()
    steps.end()


class gather_steps:
    def __init__(self, ins, outs, pairs, sems):
        self.ins, self.outs, self.pairs = ins, outs, pairs
        self.send_sem, self.recv_sem, self.local_sem, self.pair_send, self.pair_recv = sems
        self.me, self.core, self.level, self.x_side, self.y_side = neighbours()
        self.diagonal = self.x_side + self.y_side - self.me
        self.spans = cut_rows(ins[0].shape[0])
        self.has_up, self.has_down = self.level < LEVELS - 1, self.level > 0
        self.up, self.down = (self.me + PLANE, self.core), (self.me - PLANE, self.core)
        self.to_x, self.to_y = (self.x_side, self.core), (self.y_side, self.core)
        self.sent, self.mirrored, self.everyone = [], [], range(len(ins))
        greet(self.level, (self.x_side, self.y_side), any(p is not None for p in pairs), self.me, self.core)
        self.order = [
            self.start,
            self.side_small,
            lambda: self.column(1),
            lambda: self.cross(0),
            lambda: self.column(2),
            self.start_planes,
            lambda: self.cross(1),
            lambda: self.column(3),
            lambda: self.planes(1),
            lambda: self.cross(2),
            lambda: self.planes(2),
            lambda: self.cross(3),
            lambda: self.planes(3),
            lambda: [self.halves(step) for step in range(LEVELS)],
        ]

    def send(self, condition, k, slot, source, first, number, span, target):
        def copy():
            there = self.outs[k].at[pl.ds(first, number), pl.ds(*span)]
            here = there
            if source == "own":
                here, there = self.ins[k].at[pl.ds(*span)], self.outs[k].at[first, pl.ds(*span)]
            return pltpu.make_async_remote_copy(
                here,
                there,
                self.send_sem.at[k, slot],
                self.recv_sem.at[k, slot],
                device_id=target,
                device_id_type=MESH,
            )

        when(condition, lambda: copy().start())
        self.sent.append((condition, copy))

    def mirror(self, condition, k, first, number, span, group):
        if self.pairs[k] is None:
            return
        slot = len(self.mirrored)

        def copy():
            return pltpu.make_async_remote_copy(
                self.outs[k].at[pl.ds(first, number), pl.ds(*span)],
                self.pairs[k].at[pl.ds(first, number), pl.ds(*span)],
                self.pair_send.at[slot],
                self.pair_recv.at[slot],
                device_id=(self.me, 1 - self.core),
                device_id_type=MESH,
            )

        when(condition, lambda: copy().start())
        self.mirrored.append((condition, copy, group))

    def arrive(self, condition, k, slot, first, number, span, group):
        place = self.outs[k].at[pl.ds(first, number), pl.ds(*span)]

        def wait():
            pltpu.make_async_remote_copy(
                place,
                place,
                self.send_sem.at[k, slot],
                self.recv_sem.at[k, slot],
                device_id=self.to_x,
                device_id_type=MESH,
            ).wait_recv()

        when(condition, wait)
        self.mirror(condition, k, first, number, span, group)

    def members(self, step):
        if step == 0:
            return [(None, 0, 0)]
        return [(self.level >= step, step, -step), (self.level + step < LEVELS, 3 + step, step)]

    def slot_of(self, group, index):
        return 6 + 7 * group + index

    last = 6 + 28

    def own_copy(self, k):
        return pltpu.make_async_copy(self.ins[k], self.outs[k].at[self.me], self.local_sem.at[k])

    def start(self):
        whole_a, half_a, whole_b, half_b = self.spans
        last, me = self.last, self.me
        for k in self.everyone:
            self.own_copy(k).start()
            self.send(None, k, last, "own", me, 1, whole_b, self.to_x)
            self.send(None, k, last + 1, "own", me, 1, whole_b, self.to_y)
            self.send(self.has_up, k, 0, "own", me, 1, whole_a, self.up)
            self.send(self.has_down, k, 3, "own", me, 1, whole_a, self.down)
            self.send(None, k, self.slot_of(0, 0), "own", me, 1, whole_a, self.to_x)
            self.send(None, k, self.slot_of(1, 0), "own", me, 1, whole_a, self.to_y)

    def side_small(self):
        whole_a, half_a, whole_b, half_b = self.spans
        last = self.last
        for k in self.everyone:
            self.arrive(None, k, last, self.x_side, 1, whole_b, 0)
            self.send(None, k, last + 3, "out", self.x_side, 1, half_b[1], self.to_y)
            self.arrive(None, k, last + 1, self.y_side, 1, whole_b, 0)
            self.send(None, k, last + 2, "out", self.y_side, 1, half_b[0], self.to_x)
        for k in self.everyone:
            self.own_copy(k).wait()
            self.mirror(None, k, self.me, 1, (0, self.ins[k].shape[0]), 0)
            self.arrive(None, k, last + 2, self.diagonal, 1, half_b[0], 0)
            self.arrive(None, k, last + 3, self.diagonal, 1, half_b[1], 0)

    def start_planes(self):
        whole_b = self.spans[2]
        for k in self.everyone:
            self.send(self.has_up, k, self.last + 4, "out", PLANE * self.level, PLANE, whole_b, self.up)
            self.send(self.has_down, k, self.last + 7, "out", PLANE * self.level, PLANE, whole_b, self.down)

    def cross(self, step):
        whole_a, half_a = self.spans[:2]
        for k in self.everyone:
            for condition, index, distance in self.members(step):
                first = self.x_side + PLANE * distance
                self.arrive(condition, k, self.slot_of(0, index), first, 1, whole_a, distance)
                self.send(condition, k, self.slot_of(3, index), "out", first, 1, half_a[1], self.to_y)
                first = self.y_side + PLANE * distance
                self.arrive(condition, k, self.slot_of(1, index), first, 1, whole_a, distance)
                self.send(condition, k, self.slot_of(2, index), "out", first, 1, half_a[0], self.to_x)

    def halves(self, step):
        half_a = self.spans[1]
        for k in self.everyone:
            for condition, index, distance in self.members(step):
                first = self.diagonal + PLANE * distance
                self.arrive(condition, k, self.slot_of(2, index), first, 1, half_a[0], distance)
                self.arrive(condition, k, self.slot_of(3, index), first, 1, half_a[1], distance)

    def column(self, step):
        whole_a = self.spans[0]
        for k in self.everyone:
            for condition, index, distance in self.members(step):
                first = self.me + PLANE * distance
                rising = distance < 0
                self.arrive(condition, k, step - 1 if rising else 2 + step, first, 1, whole_a, distance)
                if step < LEVELS - 1:
                    onward = condition & (self.has_up if rising else self.has_down)
                    slot = step if rising else 3 + step
                    self.send(onward, k, slot, "out", first, 1, whole_a, self.up if rising else self.down)
                self.send(condition, k, self.slot_of(0, index), "out", first, 1, whole_a, self.to_x)
                self.send(condition, k, self.slot_of(1, index), "out", first, 1, whole_a, self.to_y)

    def planes(self, step):
        whole_b = self.spans[2]
        for k in self.everyone:
            for condition, index, distance in self.members(step):
                first = PLANE * (self.level + distance)
                rising = distance < 0
                self.arrive(condition, k, self.last + (3 if rising else 6) + step, first, PLANE, whole_b, distance)
                if step < LEVELS - 1:
                    onward = condition & (self.has_up if rising else self.has_down)
                    slot = self.last + (4 if rising else 7) + step
                    self.send(onward, k, slot, "out", first, PLANE, whole_b, self.up if rising else self.down)

    def paired_level(self, distance):
        for condition, copy, group in self.mirrored:
            if group == distance:
                when(condition, lambda copy=copy: copy().wait_recv())

    def end(self, levels_waited=False):
        for condition, copy in self.sent:
            when(condition, lambda copy=copy: copy().wait_send())
        for condition, copy, group in self.mirrored:
            when(condition, lambda copy=copy: copy().wait_send())
            if not levels_waited:
                when(condition, lambda copy=copy: copy().wait_recv())


GATHER_SLOTS = 6 + 28 + 10


def gather_semaphores(count, paired):
    dma = pltpu.SemaphoreType.DMA
    slots = (count, GATHER_SLOTS)
    pair_slots = (max(1, paired * (GATHER_SLOTS + 1)),)
    return [dma(slots), dma(slots), dma((count,)), dma(pair_slots), dma(pair_slots)]


def gather_blocks(arrays, with_pair, collective_id):
    count, blocks, paired = len(arrays), lax.axis_size("gx"), sum(with_pair)
    shapes = [jax.ShapeDtypeStruct((blocks, *a.shape), a.dtype) for a in arrays]
    shapes += [shape for shape, wanted in zip(shapes, with_pair) if wanted]
    return pl.pallas_call(
        functools.partial(gather_kernel, count, with_pair),
        out_shape=shapes,
        in_specs=[pl.BlockSpec(memory_space=pl.ANY)] * count,
        out_specs=[pl.BlockSpec(memory_space=pl.ANY)] * len(shapes),
        scratch_shapes=gather_semaphores(count, paired),
        compiler_params=pltpu.CompilerParams(collective_id=collective_id, has_side_effects=True),
    )(*arrays)


def dot_nn(left, right):
    return lax.dot_general(left, right, (((1,), (0,)), ((), ())), preferred_element_type=jnp.float32)


def dot_nt(left, right):
    return lax.dot_general(left, right, (((1,), (1,)), ((), ())), preferred_element_type=jnp.float32)


def experts_kernel(experts_all, *refs):
    rows_ref, grad_rows_ref, w_gate, w_up, w_down = refs[:5]
    weighted_out, grad_in_out, terms_out, gate_out, up_out, down_out, grads_own, grads_pair = refs[5:13]
    held, grads, w_in, left_in, left_down, weighted_ref, grad_in_ref, terms_ref = refs[13:21]
    sums_in, sums_down, turned, grad_sem, w_sem, out_sem, sum_sem = refs[21:28]
    steps = gather_steps(
        [rows_ref, grad_rows_ref], [held.at[0], grads_own], [held.at[1], grads_pair], refs[28:]
    )
    level, core = steps.level, steps.core
    hidden, width = w_down.shape
    tiles = hidden // LANES
    rows = rows_ref.shape[0]
    visits = [
        level,
        jnp.where(level == 0, 1, level - 1),
        jnp.where(level == 0, 2, jnp.where(level == 3, 1, level + 1)),
        jnp.where(level < 2, 3, 0),
    ]

    def fetch(turn, half):
        return pltpu.make_async_copy(
            (grads_own, grads_pair)[half].at[pl.ds(PLANE * visits[turn], PLANE)],
            grads.at[turn % 2, half],
            grad_sem.at[turn % 2, half],
        )

    def fetch_start(turn):
        fetch(turn, 0).start()
        fetch(turn, 1).start()

    joins = [
        pltpu.make_async_copy(part, w_in.at[:, pl.ds(i * hidden, hidden)], w_sem.at[i])
        for i, part in enumerate((w_gate, w_up))
    ]
    lane = lax.broadcasted_iota(jnp.int32, (1, LANES), 1)
    expert = steps.me
    gate_pick = (((lane == expert) | (lane == experts_all + expert))).astype(jnp.float32)
    high_lane = (lane == 2 * experts_all * core + expert).astype(jnp.float32)
    low_lane = (lane == 2 * experts_all * core + experts_all + expert).astype(jnp.float32)
    group = 2 * rows

    def leave(turn):
        span = pl.ds(PLANE * visits[turn], PLANE)
        pairs = ((weighted_ref, weighted_out), (grad_in_ref, grad_in_out), (terms_ref, terms_out))
        return [
            pltpu.make_async_copy(here.at[:, span], there.at[:, span], out_sem.at[turn, i])
            for i, (here, there) in enumerate(pairs)
        ]

    def forward(turn, begin, end):
        first = PLANE * visits[turn]
        if begin == 0:
            fetch(turn, 0).wait()
            fetch(turn, 1).wait()

        def body(step, carry):
            half, pair = step // 2, step % 2
            at = first + 2 * pair
            lanes = held[half, pl.ds(at, 2), :, pl.ds(width, LANES)].reshape(group, LANES)
            gate_rows = jnp.sum(lanes.astype(jnp.float32) * gate_pick, axis=1, keepdims=True)
            grad_rows = grads[turn % 2, half, pl.ds(2 * pair, 2)].reshape(group, width)
            token_rows = held[half, pl.ds(at, 2), :, pl.ds(0, width)].reshape(group, width)
            grad_hidden = dot_nt(grad_rows, w_down[...])
            both = dot_nn(token_rows, w_in[...])
            terms = jnp.zeros((group, 1), jnp.float32)
            column = pl.multiple_of(step * group, group)
            for j in range(tiles):
                gate_in = both[:, j * LANES : (j + 1) * LANES]
                up_in = both[:, hidden + j * LANES : hidden + (j + 1) * LANES]
                back = grad_hidden[:, j * LANES : (j + 1) * LANES]
                gate_sigmoid = 1.0 / (1.0 + jnp.exp(-gate_in))
                gate_swish = gate_in * gate_sigmoid
                activated = gate_swish * up_in
                terms = terms + jnp.sum(activated * back, axis=1, keepdims=True)
                grad_act = gate_rows * back
                weighted = gate_rows * activated
                grad_gate = grad_act * up_in * gate_sigmoid * (1.0 + gate_in * (1.0 - gate_sigmoid))
                grad_up = grad_act * gate_swish
                for value, array, tile, left in (
                    (weighted, weighted_ref, j, left_down),
                    (grad_gate, grad_in_ref, j, left_in),
                    (grad_up, grad_in_ref, tiles + j, left_in),
                ):
                    span = pl.ds(tile * LANES, LANES)
                    array[half, pl.ds(at, 2), :, span] = value.astype(jnp.bfloat16).reshape(2, rows, LANES)
                    left[span, pl.ds(column, group)] = value.T.astype(jnp.bfloat16)
            high = terms.astype(jnp.bfloat16).astype(jnp.float32)
            spread = high * high_lane + (terms - high) * low_lane
            terms_ref[half, pl.ds(at, 2)] = spread.astype(jnp.bfloat16).reshape(2, rows, LANES)
            return carry

        lax.fori_loop(begin, end, body, 0)
        if end == 4:
            for copy in leave(turn):
                copy.start()

    wide = 256

    def weights(turn, begin, end):
        first = PLANE * visits[turn]

        def body(step, carry):
            span = pl.ds(pl.multiple_of(step * wide, wide), wide)
            token_rows = held[:, pl.ds(first, PLANE), :, span].reshape(2 * PLANE * rows, wide)
            grad_rows = grads[turn % 2, :, :, :, span].reshape(2 * PLANE * rows, wide)
            part_in = dot_nn(left_in[...], token_rows)
            part_down = dot_nn(left_down[...], grad_rows)
            if turn:
                part_in = sums_in[:, span] + part_in
                part_down = sums_down[:, span] + part_down
            sums_down[:, span] = part_down
            if turn < LEVELS - 1:
                sums_in[:, span] = part_in
            else:
                for i in range(2):
                    turned[i, span] = part_in[i * hidden : (i + 1) * hidden].T
                for copy in leave_sums(step):
                    copy.start()
            return carry

        lax.fori_loop(begin, end, body, 0)

    def leave_sums(step):
        span = pl.ds(pl.multiple_of(step * wide, wide), wide)
        return [
            pltpu.make_async_copy(turned.at[0, span], gate_out.at[span], sum_sem.at[step, 0]),
            pltpu.make_async_copy(turned.at[1, span], up_out.at[span], sum_sem.at[step, 1]),
            pltpu.make_async_copy(sums_down.at[:, span], down_out.at[:, span], sum_sem.at[step, 2]),
        ]

    def level_ready(turn):
        if turn == 0:
            steps.paired_level(0)
        for distance in range(-3, 4):
            if turn and distance:
                wanted = visits[turn] == level + distance
                pl.when(wanted)(lambda distance=distance: steps.paired_level(distance))
        fetch_start(turn)

    steps.start()
    for join in joins:
        join.start()
    steps.side_small()
    steps.column(1)
    steps.cross(0)
    for join in joins:
        join.wait()
    steps.column(2)
    steps.start_planes()
    steps.halves(0)
    steps.cross(1)
    level_ready(0)
    forward(0, 0, 4)
    steps.column(3)
    steps.planes(1)
    weights(0, 0, 4)
    steps.cross(2)
    steps.halves(1)
    level_ready(1)
    weights(0, 4, 8)
    forward(1, 0, 4)
    steps.planes(2)
    weights(1, 0, 4)
    steps.cross(3)
    steps.halves(2)
    level_ready(2)
    weights(1, 4, 8)
    forward(2, 0, 4)
    weights(2, 0, 8)
    steps.planes(3)
    steps.halves(3)
    level_ready(3)
    forward(3, 0, 4)
    weights(3, 0, 8)
    for turn in range(LEVELS):
        for copy in leave(turn):
            copy.wait()

    def last_sums(step, carry):
        for copy in leave_sums(step):
            copy.wait()
        return carry

    lax.fori_loop(0, width // wide, last_sums, 0)
    steps.end(levels_waited=True)


def experts_products(rows, grad_rows, w_gate, w_up, w_down, experts_all, collective_id):
    blocks, low, count = lax.axis_size("gx"), jnp.bfloat16, rows.shape[0]
    hidden, width = w_down.shape
    everywhere = pl.BlockSpec(memory_space=pl.ANY)
    block_shape = (2, blocks, count)
    shapes = [
        jax.ShapeDtypeStruct((*block_shape, hidden), low),
        jax.ShapeDtypeStruct((*block_shape, 2 * hidden), low),
        jax.ShapeDtypeStruct((*block_shape, LANES), low),
        jax.ShapeDtypeStruct((width, hidden), jnp.float32),
        jax.ShapeDtypeStruct((width, hidden), jnp.float32),
        jax.ShapeDtypeStruct((hidden, width), jnp.float32),
        *[jax.ShapeDtypeStruct((blocks, count, width), low)] * 2,
    ]
    level_rows = 2 * PLANE * count
    dma = pltpu.SemaphoreType.DMA
    return pl.pallas_call(
        functools.partial(experts_kernel, experts_all),
        out_shape=shapes,
        in_specs=[everywhere] * 4 + [pl.BlockSpec(memory_space=pltpu.VMEM)],
        out_specs=[everywhere] * 8,
        scratch_shapes=[
            pltpu.VMEM((*block_shape, rows.shape[1]), low),
            pltpu.VMEM((2, 2, PLANE, count, width), low),
            pltpu.VMEM((width, 2 * hidden), low),
            pltpu.VMEM((2 * hidden, level_rows), low),
            pltpu.VMEM((hidden, level_rows), low),
            *[pltpu.VMEM(shape.shape, low) for shape in shapes[:3]],
            pltpu.VMEM((2 * hidden, width), jnp.float32),
            pltpu.VMEM((hidden, width), jnp.float32),
            pltpu.VMEM((2, width, hidden), jnp.float32),
            dma((2, 2)),
            dma((2,)),
            dma((LEVELS, 3)),
            dma((width // 256, 3)),
            *gather_semaphores(2, 2),
        ],
        compiler_params=pltpu.CompilerParams(
            collective_id=collective_id, has_side_effects=True, vmem_limit_bytes=63 * 1024 * 1024
        ),
    )(rows, grad_rows, w_gate, w_up, w_down)[:6]


class scatter_moves:
    def __init__(self, held, out):
        self.mine, self.half_y, self.half_x, self.full_x, self.full_y, self.slots_a, self.slots_b, self.side_b = held[:8]
        self.send_sem, self.recv_sem, self.chain_send, self.chain_recv = held[8:12]
        self.out = out
        self.me, self.core, level, x_side, y_side = neighbours()
        self.level = level
        self.up, self.down = (self.me + PLANE, self.core), (self.me - PLANE, self.core)
        self.to_x, self.to_y = (x_side, self.core), (y_side, self.core)
        self.x_at, self.y_at, self.own_at = x_side % PLANE, y_side % PLANE, self.me % PLANE
        self.diagonal_at = (x_side + y_side - self.me) % PLANE
        forward = jnp.where(level < 2, 1, 0)
        self.order = [3 * forward, 2 * forward + (1 - forward), level + 1 - 2 * (level % 2), level]
        self.rows, self.width = self.mine.shape[1:]
        self.spans = cut_rows(self.rows)
        self.sent = []

    def send(self, condition, source, target_ref, ssem, rsem, target):
        def copy():
            return pltpu.make_async_remote_copy(
                source, target_ref, ssem, rsem, device_id=target, device_id_type=MESH
            )

        when(condition, lambda: copy().start())
        self.sent.append((condition, copy))

    def arrive(self, condition, target_ref, rsem):
        def wait():
            pltpu.make_async_remote_copy(
                target_ref, target_ref, rsem, rsem, device_id=self.to_x, device_id_type=MESH
            ).wait_recv()

        when(condition, wait)

    def add(self, condition, height, target, *terms, step=16):
        def run():
            def body(i, carry):
                at = pl.multiple_of(i * step, step)
                total = target(at, step)[...].astype(jnp.float32)
                for term in terms:
                    total = total + term(at, step)[...].astype(jnp.float32)
                target(at, step)[...] = total.astype(jnp.bfloat16)
                return carry

            lax.fori_loop(0, height // step, body, 0)

        when(condition, run)

    def rows_of(self, ref, *index, start=0):
        return lambda at, step: ref.at[(*index, pl.ds(start + at, step))]

    def turn_sems(self, turn):
        return [(self.send_sem.at[6 * turn + i], self.recv_sem.at[6 * turn + i]) for i in range(6)]

    def half_spans(self):
        half_a = self.spans[1]
        return half_a[0][1], pl.ds(*half_a[0]), pl.ds(*half_a[1])

    def first(self, turn):
        base, at = PLANE * self.order[turn], self.turn_sems(turn)
        _, lower, upper = self.half_spans()
        mine, to_x, to_y = self.mine, self.to_x, self.to_y
        self.send(None, mine.at[base + self.diagonal_at, lower], self.half_y.at[turn], *at[0], to_y)
        self.send(None, mine.at[base + self.diagonal_at, upper], self.half_x.at[turn], *at[1], to_x)
        self.send(None, mine.at[base + self.x_at, upper], self.full_x.at[turn, upper], *at[2], to_x)
        self.send(None, mine.at[base + self.y_at, lower], self.full_y.at[turn, lower], *at[3], to_y)

    def second(self, turn):
        base, at = PLANE * self.order[turn], self.turn_sems(turn)
        height, lower, upper = self.half_spans()
        mine, rows_of = self.mine, self.rows_of
        self.arrive(None, self.half_y.at[turn], at[0][1])
        self.add(None, height, rows_of(mine, base + self.x_at), rows_of(self.half_y, turn))
        self.send(None, mine.at[base + self.x_at, lower], self.full_x.at[turn, lower], *at[4], self.to_x)
        self.arrive(None, self.half_x.at[turn], at[1][1])
        self.add(None, height, rows_of(mine, base + self.y_at, start=height), rows_of(self.half_x, turn))
        self.send(None, mine.at[base + self.y_at, upper], self.full_y.at[turn, upper], *at[5], self.to_y)

    def chain(self, which, turn, block, slots, spread):
        to_level, level = self.order[turn], self.level
        rising, falling = to_level > level, to_level < level
        begins = (rising & (level == 0)) | (falling & (level == LEVELS - 1))
        middle = (rising | falling) & jnp.logical_not(begins)
        self.arrive(middle, slots.at[to_level], self.chain_recv.at[which, to_level])
        spread(middle, to_level)
        outgoing = self.chain_send.at[which, to_level]
        self.send(rising, block, slots.at[to_level], outgoing, self.chain_recv.at[which, to_level], self.up)
        at = jnp.where(to_level == level - 1, LEVELS, to_level)
        self.send(falling, block, slots.at[at], outgoing, self.chain_recv.at[which, at], self.down)

    def add_small(self, condition, base, slot):
        start, number = self.spans[2]
        for column in range(PLANE):
            self.add(
                condition,
                number,
                self.rows_of(self.mine, base + column, start=start),
                self.rows_of(self.slots_b, slot, column),
            )

    def chain_small(self, turn):
        if turn == LEVELS - 1:
            return
        base = PLANE * self.order[turn]
        block = self.mine.at[pl.ds(base, PLANE), pl.ds(*self.spans[2])]
        self.chain(1, turn, block, self.slots_b, lambda condition, slot: self.add_small(condition, base, slot))

    def plane_arrives(self, turn):
        at = self.turn_sems(turn)
        _, lower, upper = self.half_spans()
        self.arrive(None, self.full_x.at[turn, upper], at[2][1])
        self.arrive(None, self.full_y.at[turn, lower], at[3][1])
        self.arrive(None, self.full_x.at[turn, lower], at[4][1])
        self.arrive(None, self.full_y.at[turn, upper], at[5][1])

    def chain_large(self, turn):
        if turn == LEVELS - 1:
            return
        own, number = PLANE * self.order[turn] + self.own_at, self.spans[0][1]
        rows_of, mine = self.rows_of, self.mine
        self.plane_arrives(turn)
        self.add(None, number, rows_of(mine, own), rows_of(self.full_x, turn), rows_of(self.full_y, turn))
        self.chain(
            0,
            turn,
            mine.at[own, pl.ds(*self.spans[0])],
            self.slots_a,
            lambda condition, slot: self.add(condition, number, rows_of(mine, own), rows_of(self.slots_a, slot)),
        )

    def side(self):
        short = self.spans[3][0][1]
        spans = [pl.ds(0, short), pl.ds(short, short), pl.ds(2 * short, 2 * short), pl.ds(4 * short, 2 * short)]
        return [(self.side_b.at[span], self.send_sem.at[24 + i], self.recv_sem.at[24 + i]) for i, span in enumerate(spans)]

    def arrivals(self):
        return ((self.level > 0, self.level), (self.level < LEVELS - 1, LEVELS))

    def end_small(self):
        base, mine, half_b = PLANE * self.level, self.mine, self.spans[3]
        for condition, slot in self.arrivals():
            self.arrive(condition, self.slots_b.at[slot], self.chain_recv.at[1, slot])
            self.add_small(condition, base, slot)
        side = self.side()
        self.send(None, mine.at[base + self.diagonal_at, pl.ds(*half_b[0])], *side[0], self.to_y)
        self.send(None, mine.at[base + self.diagonal_at, pl.ds(*half_b[1])], *side[1], self.to_x)

    def end_sides(self):
        base, mine, rows_of = PLANE * self.level, self.mine, self.rows_of
        whole_b, half_b = self.spans[2:]
        side, short = self.side(), half_b[0][1]
        self.plane_arrives(LEVELS - 1)
        self.arrive(None, side[0][0], side[0][2])
        self.add(None, short, rows_of(mine, base + self.x_at, start=half_b[0][0]), rows_of(self.side_b))
        self.send(None, mine.at[base + self.x_at, pl.ds(*whole_b)], *side[2], self.to_x)
        self.arrive(None, side[1][0], side[1][2])
        self.add(None, short, rows_of(mine, base + self.y_at, start=half_b[1][0]), rows_of(self.side_b, start=short))
        self.send(None, mine.at[base + self.y_at, pl.ds(*whole_b)], *side[3], self.to_y)

    def end_sums(self, base):
        whole_a, half_a, whole_b, half_b = self.spans
        own, out, mine, step = PLANE * self.level + self.own_at, self.out, self.mine, 16
        full_x, full_y, slots_a, side_b = self.full_x, self.full_y, self.slots_a, self.side_b

        def place(at):
            return pl.ds(pl.multiple_of(base + at, step), step)

        def tail_a(i, carry):
            at = pl.multiple_of(i * step, step)
            span, turn = pl.ds(at, step), LEVELS - 1
            total = mine[own, span].astype(jnp.float32)
            total = total + full_x[turn, span].astype(jnp.float32) + full_y[turn, span].astype(jnp.float32)
            out[place(at)] = total
            return carry

        lax.fori_loop(0, whole_a[1] // step, tail_a, 0)
        for condition, slot in self.arrivals():
            self.arrive(condition, slots_a.at[slot], self.chain_recv.at[0, slot])

            def more(slot=slot):
                def body(i, carry):
                    at = pl.multiple_of(i * step, step)
                    out[place(at)] = out[place(at)] + slots_a[slot, pl.ds(at, step)].astype(jnp.float32)
                    return carry

                lax.fori_loop(0, whole_a[1] // step, body, 0)

            when(condition, more)
        side, short = self.side(), half_b[0][1]
        self.arrive(None, side[2][0], side[2][2])
        self.arrive(None, side[3][0], side[3][2])

        def tail_b(i, carry):
            at = pl.multiple_of(i * step, step)
            total = mine[own, pl.ds(whole_b[0] + at, step)].astype(jnp.float32)
            total = total + side_b[pl.ds(2 * short + at, step)].astype(jnp.float32)
            total = total + side_b[pl.ds(4 * short + at, step)].astype(jnp.float32)
            out[place(whole_b[0] + at)] = total
            return carry

        lax.fori_loop(0, whole_b[1] // step, tail_b, 0)

    def end_waits(self):
        for condition, copy in self.sent:
            when(condition, lambda copy=copy: copy().wait_send())


def scatter_places(blocks, rows, width):
    near, far, low, dma = 3 * rows // 4, rows // 4, jnp.bfloat16, pltpu.SemaphoreType.DMA
    shapes = [
        (blocks, rows, width),
        (LEVELS, near // 2, width),
        (LEVELS, near // 2, width),
        (LEVELS, near, width),
        (LEVELS, near, width),
        (LEVELS + 1, near, width),
        (LEVELS + 1, PLANE, far, width),
        (3 * far, width),
    ]
    return [pltpu.VMEM(shape, low) for shape in shapes] + [dma((28,)), dma((28,)), dma((2, 5)), dma((2, 5))]


PLACES = 12


def scatter_kernel(*refs):
    normed, grad_qkv, router_term, grad_attn, attended, gain_ref, out, gain_out = refs[:8]
    held, (load_sem, gain_slots, gain_send, gain_recv) = refs[8:-4], refs[-4:]
    moves = scatter_moves(held, out)
    me, core, level = moves.me, moves.core, moves.level
    far = me + 2 * PLANE - 4 * PLANE * (level // 2)
    greet(level, (moves.to_x[0], moves.to_y[0], far), True, me, core)
    partners = ((me, 1 - core), moves.to_x, moves.to_y, (me + PLANE - 2 * PLANE * (level % 2), core), (far, core))

    def gain_copy(turn):
        return pltpu.make_async_remote_copy(
            gain_slots.at[2 * turn],
            gain_slots.at[2 * turn + 1],
            gain_send.at[turn],
            gain_recv.at[turn],
            device_id=partners[turn],
            device_id_type=MESH,
        )

    def gain_step(turn):
        if turn == 0:
            gain_slots[0] = gain_ref[...]
        else:
            gain_copy(turn - 1).wait_recv()
            gain_slots[2 * turn] = gain_slots[2 * turn - 2] + gain_slots[2 * turn - 1]
        if turn < len(partners):
            gain_copy(turn).start()
        else:
            gain_out[...] = gain_slots[2 * turn]

    router_lane = grad_qkv.shape[1]

    def load(turn):
        span = pl.ds(PLANE * moves.order[turn], PLANE)
        place = moves.mine.at[span, :, pl.ds(router_lane, LANES)]
        return pltpu.make_async_copy(router_term.at[span], place, load_sem.at[turn])

    def products(turn):
        level_rows, wide = PLANE * moves.rows, 256
        span = pl.ds(PLANE * moves.order[turn], PLANE)
        features = pl.ds(pl.multiple_of(moves.order[turn] * level_rows, level_rows), level_rows)
        for left, right, lane in ((normed, grad_qkv, 0), (grad_attn, attended, router_lane + LANES)):
            left_rows = left[:, features].astype(jnp.float32).T.astype(jnp.bfloat16)

            def body(step, carry, left_rows=left_rows, right=right, lane=lane):
                at = pl.multiple_of(step * wide, wide)
                value = dot_nn(left_rows, right[:, pl.ds(at, wide)]).astype(jnp.bfloat16)
                lanes = pl.ds(pl.multiple_of(lane + at, LANES), wide)
                moves.mine[span, :, lanes] = value.reshape(PLANE, moves.rows, wide)
                return carry

            lax.fori_loop(0, right.shape[1] // wide, body, 0)

    for turn in range(LEVELS):
        load(turn).start()
    gain_step(0)
    for turn in range(LEVELS):
        products(turn)
        load(turn).wait()
        moves.first(turn)
        moves.chain_small(turn)
    for turn in range(LEVELS - 1):
        moves.second(turn)
        gain_step(turn + 1)
        if turn:
            moves.chain_large(turn - 1)
    moves.second(LEVELS - 1)
    gain_step(4)
    moves.chain_large(LEVELS - 2)
    moves.end_small()
    moves.end_sides()
    gain_step(5)
    moves.end_sums(0)
    for turn in range(len(partners)):
        gain_copy(turn).wait_send()
    moves.end_waits()


def scatter_sums(normed, grad_qkv, router_term, grad_attn, attended, gains, collective_id):
    blocks, rows, _ = router_term.shape
    width = grad_qkv.shape[1] + LANES + attended.shape[1]
    dma = pltpu.SemaphoreType.DMA
    vmem, everywhere = pl.BlockSpec(memory_space=pltpu.VMEM), pl.BlockSpec(memory_space=pl.ANY)
    return pl.pallas_call(
        scatter_kernel,
        out_shape=[
            jax.ShapeDtypeStruct((rows, width), jnp.float32),
            jax.ShapeDtypeStruct(gains.shape, gains.dtype),
        ],
        in_specs=[vmem, vmem, everywhere, vmem, vmem, vmem],
        out_specs=[vmem] * 2,
        scratch_shapes=[
            *scatter_places(blocks, rows, width),
            dma((LEVELS,)),
            pltpu.VMEM((11, *gains.shape), gains.dtype),
            dma((5,)),
            dma((5,)),
        ],
        compiler_params=pltpu.CompilerParams(
            collective_id=collective_id, has_side_effects=True, vmem_limit_bytes=60 * 1024 * 1024
        ),
    )(normed, grad_qkv, router_term, grad_attn, attended, gains)


def return_kernel(grad_in, weighted, terms, w_gate, w_up, w_down, back_out, mixed_out, *refs):
    streams = [
        scatter_moves(refs[:PLACES], back_out),
        scatter_moves(refs[PLACES : 2 * PLACES], mixed_out),
    ]
    sibling, away, left, right_in, right_down = refs[2 * PLACES : 2 * PLACES + 5]
    pair_send, pair_recv, left_sem, right_sem, term_sem, ready_sem, credit = refs[2 * PLACES + 5 :]
    me, core, order, rows = streams[0].me, streams[0].core, streams[0].order, streams[0].rows
    greet(streams[0].level, (streams[0].to_x[0], streams[0].to_y[0]), True, me, core)
    hidden, features = w_down.shape
    depths, lefts = (2 * hidden, hidden), (grad_in, weighted)
    turns, wide = 2 * LEVELS, 256
    rights = [
        pltpu.make_async_copy(w_gate, right_in.at[:, pl.ds(0, hidden)], right_sem.at[0]),
        pltpu.make_async_copy(w_up, right_in.at[:, pl.ds(hidden, hidden)], right_sem.at[1]),
        pltpu.make_async_copy(w_down, right_down, right_sem.at[2]),
    ]

    def level_span(turn):
        return pl.ds(PLANE * order[turn % LEVELS], PLANE)

    def left_copy(turn):
        stream = turn // LEVELS
        return pltpu.make_async_copy(
            lefts[stream].at[:, level_span(turn)],
            left.at[turn % 2, :, :, :, pl.ds(0, depths[stream])],
            left_sem.at[turn % 2],
        )

    def term_copy(turn, half):
        lanes = pl.ds(features, LANES)
        place = away.at[turn % 2, :, :, lanes] if half else streams[0].mine.at[level_span(turn), :, lanes]
        return pltpu.make_async_copy(terms.at[half, level_span(turn)], place, term_sem.at[half])

    def width_of(turn):
        return streams[turn // LEVELS].width

    def hand(turn):
        lanes = pl.ds(0, width_of(turn))
        return pltpu.make_async_remote_copy(
            away.at[turn % 2, :, :, lanes],
            sibling.at[turn % 2, :, :, lanes],
            pair_send.at[turn],
            pair_recv.at[turn],
            device_id=(me, 1 - core),
            device_id_type=MESH,
        )

    def product(turn, half, store):
        stream, slot = turn // LEVELS, turn % 2
        factor = left[slot, half, :, :, pl.ds(0, depths[stream])].reshape(PLANE * rows, depths[stream])

        def body(step, carry):
            span = pl.ds(pl.multiple_of(step * wide, wide), wide)
            value = dot_nt(factor, right_in[span]) if stream == 0 else dot_nn(factor, right_down[:, span])
            store(span, value.reshape(PLANE, rows, wide))
            return carry

        lax.fori_loop(0, features // wide, body, 0)

    def hand_over(turn):
        left_copy(turn).wait()
        if turn + 1 < turns:
            left_copy(turn + 1).start()
        if turn < LEVELS:
            term_copy(turn, 1).start()
            term_copy(turn, 0).start()

        def store(span, value):
            away[turn % 2, :, :, span] = value.astype(jnp.bfloat16)

        product(turn, 1, store)
        if turn < LEVELS:
            term_copy(turn, 1).wait()
            term_copy(turn, 0).wait()
        if turn >= 2:
            pl.semaphore_wait(credit, 1)
        hand(turn).start()

    def settle(turn):
        hand(turn).wait()
        mine, slot = streams[turn // LEVELS].mine, turn % 2

        def store(span, value):
            value = value + sibling[slot, :, :, span].astype(jnp.float32)
            mine[level_span(turn), :, span] = value.astype(jnp.bfloat16)

        product(turn, 0, store)
        if turn < LEVELS:
            lanes = pl.ds(features, LANES)
            value = mine[level_span(turn), :, lanes].astype(jnp.float32)
            value = value + sibling[slot, :, :, lanes].astype(jnp.float32)
            mine[level_span(turn), :, lanes] = value.astype(jnp.bfloat16)
        if turn + 2 < turns:
            pl.semaphore_signal(credit, inc=1, device_id=(me, 1 - core), device_id_type=MESH)

    def exchange(stream, core_of_rows):
        out = streams[stream].out
        span = pl.ds(pl.multiple_of(core_of_rows * rows, rows), rows)
        return pltpu.make_async_remote_copy(
            out.at[span],
            out.at[span],
            ready_sem.at[stream, 0],
            ready_sem.at[stream, 1],
            device_id=(me, 1 - core),
            device_id_type=MESH,
        )

    def end(stream):
        streams[stream].end_sums(core * rows)
        exchange(stream, core).start()

    left_copy(0).start()
    for copy in rights:
        copy.start()
    for copy in rights:
        copy.wait()
    hand_over(0)
    for turn in range(turns + 2):
        if turn < turns:
            stream = streams[turn // LEVELS]
            settle(turn)
            stream.first(turn % LEVELS)
            if turn + 1 < turns:
                hand_over(turn + 1)
            stream.chain_small(turn % LEVELS)
        if 1 <= turn <= turns:
            streams[(turn - 1) // LEVELS].second((turn - 1) % LEVELS)
        if turn >= 2:
            streams[(turn - 2) // LEVELS].chain_large((turn - 2) % LEVELS)
        if turn == LEVELS + 1:
            streams[0].end_small()
        if turn == LEVELS + 2:
            streams[0].end_sides()
        if turn == LEVELS + 3:
            end(0)
    streams[1].end_small()
    streams[1].end_sides()
    end(1)
    for stream in range(2):
        exchange(stream, 1 - core).wait_recv()
        exchange(stream, core).wait_send()
        streams[stream].end_waits()


def return_sums(grad_in, weighted, terms, w_gate, w_up, w_down, collective_id):
    low, dma = jnp.bfloat16, pltpu.SemaphoreType.DMA
    blocks, rows, depth = grad_in.shape[1:]
    hidden, features = w_down.shape
    wide = features + LANES
    vmem, everywhere = pl.BlockSpec(memory_space=pltpu.VMEM), pl.BlockSpec(memory_space=pl.ANY)
    slots = pltpu.VMEM((2, PLANE, rows, wide), low)
    return pl.pallas_call(
        return_kernel,
        out_shape=[
            jax.ShapeDtypeStruct((2 * rows, wide), jnp.float32),
            jax.ShapeDtypeStruct((2 * rows, features), jnp.float32),
        ],
        in_specs=[everywhere] * 6,
        out_specs=[vmem] * 2,
        scratch_shapes=[
            *scatter_places(blocks, rows, wide),
            *scatter_places(blocks, rows, features),
            slots,
            slots,
            pltpu.VMEM((2, 2, PLANE, rows, depth), low),
            pltpu.VMEM((features, depth), low),
            pltpu.VMEM((hidden, features), low),
            dma((2 * LEVELS,)),
            dma((2 * LEVELS,)),
            dma((2,)),
            dma((3,)),
            dma((2,)),
            dma((2, 2)),
            pltpu.SemaphoreType.REGULAR,
        ],
        compiler_params=pltpu.CompilerParams(
            collective_id=collective_id, has_side_effects=True, vmem_limit_bytes=63 * 1024 * 1024
        ),
    )(grad_in, weighted, terms, w_gate, w_up, w_down)


def kernels_fit():
    return lax.axis_size("gx") == LEVELS * PLANE and lax.axis_size("gy") == 2


def packed_gains(vectors):
    rows = jnp.concatenate([vector.reshape(-1, HEAD_DIM) for vector in vectors], axis=0)
    return jnp.pad(rows, ((0, -rows.shape[0] % 8), (0, 0)))


def unpacked_gains(rows, vectors):
    sums, at = [], 0
    for vector in vectors:
        length = vector.shape[0] // HEAD_DIM
        sums.append(rows[at : at + length].reshape(-1))
        at += length
    return sums


def two_parts(values):
    high = lax.reduce_precision(values, 8, 7)
    return high.astype(jnp.bfloat16), (values - high).astype(jnp.bfloat16)


def sparse_experts(normed_ffn, logits, route_hits, routes, cotangent, w_gate, w_up, w_down):
    sequence_length, model_width = normed_ffn.shape
    experts_all = logits.shape[1]
    devices_gx = lax.axis_size("gx")
    part_width = model_width // lax.axis_size("gy")
    capacity = 5 * sequence_length * TOP // (4 * experts_all)
    pairs_count = sequence_length * TOP
    hits_float = route_hits.astype(jnp.float32)
    chosen = jnp.sum(logits[:, None, :] * hits_float, axis=-1)
    gate_exps = jnp.exp(chosen)
    gate_values = gate_exps / jnp.sum(gate_exps, axis=1, keepdims=True)
    flat_hits = route_hits.reshape(pairs_count, experts_all).astype(jnp.int32)
    slot_rank = jnp.sum((jnp.cumsum(flat_hits, axis=0) - flat_hits) * flat_hits, axis=1)
    slot_dest = routes.reshape(-1) * capacity + slot_rank
    slot_pair = (
        jnp.full((experts_all * capacity,), pairs_count, jnp.int32)
        .at[slot_dest]
        .set(jnp.arange(pairs_count, dtype=jnp.int32))
    )
    slot_token = jnp.where(slot_pair < pairs_count, slot_pair // TOP, sequence_length)

    def to_experts(buffer):
        arrived = lax.all_to_all(buffer, "gx", split_axis=0, concat_axis=0, tiled=True)
        return arrived.reshape(devices_gx * capacity, model_width)

    def from_experts(partial_rows):
        share_rows = lax.psum_scatter(
            partial_rows.astype(jnp.bfloat16), "gy", scatter_dimension=1, tiled=True
        )
        returned = lax.all_to_all(
            share_rows.reshape(devices_gx, capacity, part_width),
            "gx",
            split_axis=0,
            concat_axis=0,
            tiled=True,
        )
        whole_rows = lax.all_gather(returned, "gy", axis=2, tiled=True)
        return whole_rows.reshape(devices_gx * capacity, model_width)

    send_rows = jnp.take(normed_ffn, slot_token, axis=0, mode="fill", fill_value=0)
    expert_in = to_experts(send_rows.reshape(devices_gx, capacity, model_width))
    gate_in = jnp.dot(expert_in, w_gate, preferred_element_type=jnp.float32)
    up_in = jnp.dot(expert_in, w_up, preferred_element_type=jnp.float32)
    gate_sigmoid = jax.nn.sigmoid(gate_in)
    gate_swish = gate_in * gate_sigmoid
    activated = (gate_swish * up_in).astype(jnp.bfloat16)
    expert_part = jnp.dot(activated, w_down, preferred_element_type=jnp.float32)
    expert_out = from_experts(expert_part)
    pair_rows = jnp.take(expert_out, slot_dest, axis=0).reshape(sequence_length, TOP, model_width)
    mixed_rows = jnp.einsum(
        "tk,tkd->td", gate_values, pair_rows, preferred_element_type=jnp.float32
    )
    grad_out_f = cotangent.astype(jnp.float32)
    grad_gates = jnp.einsum("td,tkd->tk", grad_out_f, pair_rows, preferred_element_type=jnp.float32)
    grad_chosen = gate_values * (
        grad_gates - jnp.sum(gate_values * grad_gates, axis=1, keepdims=True)
    )
    grad_logits = jnp.sum(grad_chosen[:, :, None] * hits_float, axis=1).astype(jnp.bfloat16)
    slot_gate = jnp.take(gate_values.reshape(-1), slot_pair, mode="fill", fill_value=0.0)
    grad_send = (
        jnp.take(grad_out_f, slot_token, axis=0, mode="fill", fill_value=0) * slot_gate[:, None]
    )
    grad_expert_out = to_experts(
        grad_send.astype(jnp.bfloat16).reshape(devices_gx, capacity, model_width)
    )
    grad_act = contract(grad_expert_out, w_down, 1, 1)
    down_term = contract(activated, grad_expert_out, 0, 0)
    grad_gate_in = (
        grad_act * up_in * gate_sigmoid * (1.0 + gate_in * (1.0 - gate_sigmoid))
    ).astype(jnp.bfloat16)
    grad_up_in = (grad_act * gate_swish).astype(jnp.bfloat16)
    gate_term = contract(expert_in, grad_gate_in, 0, 0)
    up_term = contract(expert_in, grad_up_in, 0, 0)
    grad_in_part = contract(grad_gate_in, w_gate, 1, 1) + contract(grad_up_in, w_up, 1, 1)
    grad_rows = from_experts(grad_in_part)
    grad_pairs = jnp.take(grad_rows, slot_dest, axis=0).reshape(sequence_length, TOP, model_width)
    grad_rows_sum = jnp.sum(grad_pairs.astype(jnp.float32), axis=1)
    return mixed_rows, grad_rows_sum, grad_logits, (gate_term[None], up_term[None], down_term[None])


def swap_cores(rows):
    return lax.ppermute(rows, "gy", [(0, 1), (1, 0)])


def own_half(rows):
    count = rows.shape[0] // lax.axis_size("gy")
    return lax.dynamic_slice_in_dim(rows, lax.axis_index("gy") * count, count, 0)


def dense_experts(normed_ffn, logits, route_hits, cotangent, w_gate, w_up, w_down):
    sequence_length, model_width = normed_ffn.shape
    experts_all = logits.shape[1]
    gate_exps = jnp.exp(jnp.where(jnp.any(route_hits, axis=1), logits, -1e30))
    gate_all = gate_exps / jnp.sum(gate_exps, axis=1, keepdims=True)
    gate_lanes = jnp.pad(jnp.concatenate(two_parts(gate_all), axis=1), ((0, 0), (0, LANES - 2 * experts_all)))
    row_lanes = jnp.concatenate([own_half(normed_ffn), own_half(gate_lanes)], axis=1)
    weighted, grad_in, terms, gate_term, up_term, down_term = experts_products(
        row_lanes, own_half(cotangent), w_gate, w_up, w_down, experts_all, 2
    )
    back, mixed_rows = return_sums(grad_in, weighted, terms, w_gate, w_up, w_down, 3)
    term_lanes = back[:, model_width : model_width + 4 * experts_all]
    grad_gates = jnp.sum(term_lanes.reshape(sequence_length, 4, experts_all), axis=1)
    grad_logits = (
        gate_all * (grad_gates - jnp.sum(gate_all * grad_gates, axis=1, keepdims=True))
    ).astype(jnp.bfloat16)
    return mixed_rows, back[:, :model_width], grad_logits, (gate_term[None], up_term[None], down_term[None])


def turn_lanes(values, cosine, sine_table):
    return values * cosine + pltpu.roll(values, HEAD_DIM // 2, 1) * sine_table


def unit_rows(values):
    scale = lax.rsqrt(jnp.mean(values * values, axis=1, keepdims=True) + EPSILON)
    return values * scale, scale


def allowed_pairs(docs_column, docs_row):
    shape = (docs_column.shape[0], docs_row.shape[1])
    keys_at, queries_at = lax.broadcasted_iota(jnp.int32, shape, 0), lax.broadcasted_iota(jnp.int32, shape, 1)
    return (keys_at <= queries_at) & (docs_column == docs_row)


def head_span(head):
    return pl.ds(pl.multiple_of(head * HEAD_DIM, HEAD_DIM), HEAD_DIM)


def attend_kernel(
    q_heads, kv_heads, raw_ref, cosine_ref, sine_ref, docs_column, docs_row, q_gain, k_gain,
    attended_ref, query_ref, key_ref, value_ref, totals_ref,
):
    cosine, sine_table = cosine_ref[...], sine_ref[...]
    allowed = allowed_pairs(docs_column[...], docs_row[...])
    group, inv_root = q_heads // kv_heads, 1.0 / math.sqrt(HEAD_DIM)
    for kv in range(kv_heads):
        unit, _ = unit_rows(raw_ref[:, head_span(q_heads + kv)])
        key_rows = turn_lanes(unit * k_gain[...], cosine, sine_table).astype(jnp.bfloat16)
        value_rows = raw_ref[:, head_span(q_heads + kv_heads + kv)]
        key_ref[:, head_span(kv)] = key_rows
        value_ref[:, head_span(kv)] = value_rows.astype(jnp.bfloat16)
        value_columns = value_rows.T.astype(jnp.bfloat16)

        def body(index, carry, kv=kv, key_rows=key_rows, value_columns=value_columns):
            head = kv * group + index
            unit, _ = unit_rows(raw_ref[:, head_span(head)])
            query_rows = turn_lanes(unit * q_gain[...], cosine, sine_table).astype(jnp.bfloat16)
            query_ref[:, head_span(head)] = query_rows
            scores = jnp.where(allowed, dot_nt(key_rows, query_rows) * inv_root, -1e30)
            peak = jnp.max(scores, axis=0, keepdims=True)
            exps = jnp.exp(scores - peak)
            total = jnp.sum(exps, axis=0, keepdims=True)
            totals_ref[pl.ds(head, 1), :] = peak + jnp.log(total)
            probs = (exps / total).astype(jnp.bfloat16)
            attended_ref[:, head_span(head)] = dot_nn(value_columns, probs).T.astype(jnp.bfloat16)
            return carry

        lax.fori_loop(0, group, body, 0, unroll=2)


def attend_back_kernel(
    q_heads, kv_heads, raw_ref, cosine_ref, sine_ref, docs_column, docs_row, q_gain, k_gain,
    query_ref, key_ref, value_ref, totals_ref, grad_ref, grad_raw_ref, gains_ref, sums_ref,
):
    cosine, sine_table = cosine_ref[...], sine_ref[...]
    allowed = allowed_pairs(docs_column[...], docs_row[...])
    group, inv_root = q_heads // kv_heads, 1.0 / math.sqrt(HEAD_DIM)
    gains_ref[...] = jnp.zeros_like(gains_ref)

    def back_to_raw(grad, head, gain, gain_row):
        grad = turn_lanes(grad, cosine, -sine_table)
        unit, scale = unit_rows(raw_ref[:, head_span(head)])
        gains_ref[pl.ds(gain_row, 1), :] += jnp.sum(grad * unit, axis=0, keepdims=True)
        grad = grad * gain
        grad = scale * (grad - unit * jnp.mean(grad * unit, axis=1, keepdims=True))
        grad_raw_ref[:, head_span(head)] = grad.astype(jnp.bfloat16)

    for kv in range(kv_heads):
        key_rows, value_rows = key_ref[:, head_span(kv)], value_ref[:, head_span(kv)]
        key_columns = key_rows.astype(jnp.float32).T.astype(jnp.bfloat16)
        sums_ref[...] = jnp.zeros_like(sums_ref)

        def body(index, carry, kv=kv, key_rows=key_rows, value_rows=value_rows, key_columns=key_columns):
            head = kv * group + index
            query_rows, grad_rows = query_ref[:, head_span(head)], grad_ref[:, head_span(head)]
            scores = jnp.where(allowed, dot_nt(key_rows, query_rows) * inv_root, -1e30)
            probs = jnp.exp(scores - totals_ref[pl.ds(head, 1), :])
            sums_ref[0] += dot_nn(probs.astype(jnp.bfloat16), grad_rows)
            grad_probs = dot_nt(value_rows, grad_rows)
            inner = jnp.sum(probs * grad_probs, axis=0, keepdims=True)
            grad_scores = (probs * (grad_probs - inner)).astype(jnp.bfloat16)
            sums_ref[1] += dot_nn(grad_scores, query_rows)
            grad_queries = dot_nn(key_columns, grad_scores).T * inv_root
            back_to_raw(grad_queries, head, q_gain[...], 0)
            return carry

        lax.fori_loop(0, group, body, 0, unroll=2)
        back_to_raw(sums_ref[1] * inv_root, q_heads + kv, k_gain[...], 1)
        grad_raw_ref[:, head_span(q_heads + kv_heads + kv)] = sums_ref[0].astype(jnp.bfloat16)


def attention_shared(qkv_rows, doc_ids, query_norm_gain, k_gain):
    length = qkv_rows.shape[0]
    cosine, sine_table = rotary_tables(length, HEAD_DIM)
    cosine, sine_table = cosine[:, 0], sine_table[:, 0]
    return (
        qkv_rows,
        jnp.concatenate([cosine, cosine], axis=1),
        jnp.concatenate([-sine_table, sine_table], axis=1),
        doc_ids.reshape(length, 1),
        doc_ids.reshape(1, length),
        query_norm_gain.reshape(1, HEAD_DIM),
        k_gain.reshape(1, HEAD_DIM),
    )


def attend(shared, q_heads, kv_heads):
    length, low, shape = shared[0].shape[0], jnp.bfloat16, jax.ShapeDtypeStruct
    return pl.pallas_call(
        functools.partial(attend_kernel, q_heads, kv_heads),
        out_shape=[
            shape((length, q_heads * HEAD_DIM), low),
            shape((length, q_heads * HEAD_DIM), low),
            shape((length, kv_heads * HEAD_DIM), low),
            shape((length, kv_heads * HEAD_DIM), low),
            shape((q_heads, length), jnp.float32),
        ],
        compiler_params=pltpu.CompilerParams(vmem_limit_bytes=48 * 1024 * 1024),
    )(*shared)


def attend_back(shared, kept, grad_attended, q_heads, kv_heads):
    length, shape = shared[0].shape[0], jax.ShapeDtypeStruct
    return pl.pallas_call(
        functools.partial(attend_back_kernel, q_heads, kv_heads),
        out_shape=[shape(shared[0].shape, jnp.bfloat16), shape((8, HEAD_DIM), jnp.float32)],
        scratch_shapes=[pltpu.VMEM((2, length, HEAD_DIM), jnp.float32)],
        compiler_params=pltpu.CompilerParams(vmem_limit_bytes=48 * 1024 * 1024),
    )(*shared, *kept, grad_attended)


def on_device(
    tokens_in,
    doc_ids,
    routes,
    q_weight,
    key_matrix,
    value_matrix,
    out_weight,
    router_weight,
    attn_gain,
    ffn_gain,
    query_norm_gain,
    k_gain,
    gate_weight,
    up_weight,
    down_weight,
    cotangent,
):
    sequence_length = tokens_in.shape[0]
    model_width = tokens_in.shape[1]
    devices_gx = lax.axis_size("gx")
    devices_gy = lax.axis_size("gy")
    part_width = model_width // devices_gy
    experts_all = router_weight.shape[1]
    router_lanes = jnp.pad(router_weight, ((0, 0), (0, LANES - experts_all)))
    rows_local = jnp.concatenate([q_weight, key_matrix, value_matrix, router_lanes, out_weight], axis=1)
    dense = kernels_fit() and experts_all <= 2 * TOP
    if dense:
        (weights_all,) = gather_blocks([rows_local], (0,), 1)
        weights_all = weights_all.reshape(-1, rows_local.shape[1])
    else:
        weights_all = lax.all_gather(rows_local, "gx", axis=0, tiled=True)
    q_width, kv_width = q_weight.shape[1], key_matrix.shape[1]
    qkv_width = q_width + 2 * kv_width
    qkv_full = weights_all[:, :qkv_width]
    router_full = weights_all[:, qkv_width : qkv_width + experts_all]
    o_full = weights_all[:, qkv_width + LANES :]
    heads_local = q_width // HEAD_DIM
    kv_local = kv_width // HEAD_DIM
    inputs_f = tokens_in.astype(jnp.float32)
    scale_one = root_mean_scale(inputs_f)
    unit_one = inputs_f * scale_one
    normalized_input = (unit_one * attn_gain).astype(jnp.bfloat16)
    qkv_rows = jnp.dot(normalized_input, qkv_full, preferred_element_type=jnp.float32)
    shared = attention_shared(qkv_rows, doc_ids, query_norm_gain, k_gain)
    attended, *kept = attend(shared, heads_local, kv_local)
    attn_part = contract(attended, o_full, 1, 1)
    attn_total = attn_part + swap_cores(attn_part)
    residual = inputs_f + attn_total
    scale_two = root_mean_scale(residual)
    unit_two = residual * scale_two
    normed_ffn = (unit_two * ffn_gain).astype(jnp.bfloat16)
    logits = jnp.dot(normed_ffn, router_full, preferred_element_type=jnp.float32)
    expert_iota = jnp.arange(experts_all, dtype=jnp.int32)
    route_hits = routes[:, :, None] == expert_iota
    if dense:
        mixed_rows, grad_rows_sum, grad_logits, expert_grads = dense_experts(
            normed_ffn, logits, route_hits, cotangent, gate_weight[0], up_weight[0], down_weight[0]
        )
    else:
        mixed_rows, grad_rows_sum, grad_logits, expert_grads = sparse_experts(
            normed_ffn, logits, route_hits, routes, cotangent, gate_weight[0], up_weight[0], down_weight[0]
        )
    output = (residual + mixed_rows).astype(jnp.bfloat16)
    grad_out_f = cotangent.astype(jnp.float32)
    router_term = contract(normed_ffn, grad_logits, 0, 0)
    grad_ffn_in = contract(grad_logits, router_full, 1, 1) + grad_rows_sum
    ffn_gain_term = jnp.sum(grad_ffn_in * unit_two, axis=0)
    grad_residual = grad_out_f + norm_back(grad_ffn_in * ffn_gain, unit_two, scale_two)
    grad_attn = grad_residual.astype(jnp.bfloat16)
    grad_attended = jnp.dot(grad_attn, o_full, preferred_element_type=jnp.float32).astype(
        jnp.bfloat16
    )
    grad_qkv, head_gains = attend_back(shared, kept, grad_attended, heads_local, kv_local)
    q_gain_term, k_gain_term = head_gains[0], head_gains[1]
    grad_normed_part = contract(grad_qkv, qkv_full, 1, 1)
    grad_normed = grad_normed_part + swap_cores(grad_normed_part)
    attn_gain_term = jnp.sum(grad_normed * unit_one, axis=0)
    grad_input = (grad_residual + norm_back(grad_normed * attn_gain, unit_one, scale_one)).astype(
        jnp.bfloat16
    )
    own_mask = (jnp.arange(model_width) // part_width == lax.axis_index("gy")).astype(jnp.float32)
    gains = (attn_gain_term * own_mask, ffn_gain_term * own_mask, q_gain_term, k_gain_term)
    router_lanes = jnp.pad(router_term, ((0, 0), (0, LANES - experts_all)))
    if dense:
        router_blocks = router_lanes.astype(jnp.bfloat16).reshape(devices_gx, -1, LANES)
        sums, gain_rows = scatter_sums(
            normalized_input, grad_qkv, router_blocks, grad_attn, attended, packed_gains(gains), 4
        )
        gains = unpacked_gains(gain_rows, gains)
    else:
        sums = jnp.concatenate(
            [
                lax.psum_scatter(term, "gx", scatter_dimension=0, tiled=True)
                for term in (
                    contract(normalized_input, grad_qkv, 0, 0),
                    router_lanes,
                    contract(grad_attn, attended, 0, 0),
                )
            ],
            axis=1,
        )
        gains = lax.psum(gains, ("gx", "gy"))
    gain_attn, gain_ffn, gain_query, gain_key = gains
    grad_q = sums[:, :q_width]
    grad_k = sums[:, q_width : q_width + kv_width]
    grad_v = sums[:, q_width + kv_width : qkv_width]
    grad_router = sums[:, qkv_width : qkv_width + experts_all]
    grad_out = sums[:, qkv_width + LANES :]
    return (
        output,
        grad_input,
        grad_q,
        grad_k,
        grad_v,
        grad_out,
        grad_router,
        gain_attn,
        gain_ffn,
        gain_query,
        gain_key,
        expert_grads[0],
        expert_grads[1],
        expert_grads[2],
    )


def solution(mesh):
    return jax.shard_map(
        on_device,
        mesh=mesh,
        in_specs=(
            P("gx", None),
            P("gx", None),
            P("gx", None),
            P("gx", "gy"),
            P("gx", "gy"),
            P("gx", "gy"),
            P("gx", "gy"),
            P("gx", None),
            P(),
            P(),
            P(),
            P(),
            P("gx", None, "gy"),
            P("gx", None, "gy"),
            P("gx", "gy", None),
            P("gx", None),
        ),
        out_specs=(
            P("gx", None),
            P("gx", None),
            P("gx", "gy"),
            P("gx", "gy"),
            P("gx", "gy"),
            P("gx", "gy"),
            P("gx", None),
            P(),
            P(),
            P(),
            P(),
            P("gx", None, "gy"),
            P("gx", None, "gy"),
            P("gx", "gy", None),
        ),
        check_vma=False,
    )
```

```python
import functools
import math

import jax
import jax.numpy as jnp
from jax import lax
from jax.experimental import pallas as pl
from jax.experimental.pallas import tpu as pltpu
from jax.sharding import PartitionSpec as P

QUERY_HEADS = 32
KEY_VALUE_HEADS = 4
HEAD_DIM = 128
LANES = 128
TOP = 8


EPSILON = 1e-06
THETA = 1000000.0


def root_mean_scale(values):
    return lax.rsqrt(jnp.mean(values * values, axis=-1, keepdims=True) + EPSILON)


def rotary_tables(sequence_length, head_width):
    half_width = head_width // 2
    frequencies = THETA ** (-(2.0 * jnp.arange(half_width, dtype=jnp.float32)) / head_width)
    angles = jnp.arange(sequence_length, dtype=jnp.float32)[:, None] * frequencies[None, :]
    return (jnp.cos(angles)[:, None, :], jnp.sin(angles)[:, None, :])


def norm_back(grad_normed, normed_unit, scale_rows):
    return scale_rows * (
        grad_normed - normed_unit * jnp.mean(grad_normed * normed_unit, axis=-1, keepdims=True)
    )


def contract(first_op, second_op, first_dim, second_dim):
    return lax.dot_general(
        first_op,
        second_op,
        (((first_dim,), (second_dim,)), ((), ())),
        preferred_element_type=jnp.float32,
    )


MESH = pl.DeviceIdType.MESH
LEVELS = 4
PLANE = 4


def cut_rows(rows):
    near, far = 3 * rows // 4, rows // 4
    return (
        (0, near),
        ((0, near // 2), (near // 2, near // 2)),
        (near, far),
        ((near, far // 2), (near + far // 2, far // 2)),
    )


def neighbours():
    me, core = lax.axis_index("gx"), lax.axis_index("gy")
    level = me // PLANE
    x_side = me + 1 - 2 * (me % 2)
    y_side = me + 2 - 4 * ((me // 2) % 2)
    return me, core, level, x_side, y_side


def greet(level, targets, with_core, me, core):
    barrier = pltpu.get_barrier_semaphore()

    def hello(device):
        pl.semaphore_signal(barrier, inc=1, device_id=device, device_id_type=MESH)

    for target in targets:
        hello((target, core))
    if with_core:
        hello((me, 1 - core))

    @pl.when(level > 0)
    def _():
        hello((me - PLANE, core))

    @pl.when(level < LEVELS - 1)
    def _():
        hello((me + PLANE, core))

    inner = jnp.where(level > 0, 1, 0) + jnp.where(level < LEVELS - 1, 1, 0)
    pl.semaphore_wait(barrier, len(targets) + int(with_core) + inner)


def when(condition, action):
    if condition is None:
        action()
    else:
        pl.when(condition)(action)


def gather_kernel(count, with_pair, *refs):
    paired = sum(with_pair)
    ins, outs, pairs = refs[:count], refs[count : 2 * count], list(refs[2 * count : 2 * count + paired])
    pairs = [pairs.pop(0) if wanted else None for wanted in with_pair]
    sems = refs[2 * count + paired :]
    steps = gather_steps(ins, outs, pairs, sems)
    for step in steps.order:
        step()
    steps.end()


class gather_steps:
    def __init__(self, ins, outs, pairs, sems):
        self.ins, self.outs, self.pairs = ins, outs, pairs
        self.send_sem, self.recv_sem, self.local_sem, self.pair_send, self.pair_recv = sems
        self.me, self.core, self.level, self.x_side, self.y_side = neighbours()
        self.diagonal = self.x_side + self.y_side - self.me
        self.spans = cut_rows(ins[0].shape[0])
        self.has_up, self.has_down = self.level < LEVELS - 1, self.level > 0
        self.up, self.down = (self.me + PLANE, self.core), (self.me - PLANE, self.core)
        self.to_x, self.to_y = (self.x_side, self.core), (self.y_side, self.core)
        self.sent, self.mirrored, self.everyone = [], [], range(len(ins))
        for k in self.everyone:
            self.own_copy(k).start()
        greet(self.level, (self.x_side, self.y_side), any(p is not None for p in pairs), self.me, self.core)
        self.order = [
            self.start,
            self.side_small,
            lambda: self.column(1),
            lambda: self.cross(0),
            lambda: self.column(2),
            self.start_planes,
            lambda: self.cross(1),
            lambda: self.column(3),
            lambda: self.planes(1),
            lambda: self.cross(2),
            lambda: self.planes(2),
            lambda: self.cross(3),
            lambda: self.planes(3),
            lambda: [self.halves(step) for step in range(LEVELS)],
        ]

    def send(self, condition, k, slot, source, first, number, span, target):
        def copy():
            there = self.outs[k].at[pl.ds(first, number), pl.ds(*span)]
            here = there
            if source == "own":
                here, there = self.ins[k].at[pl.ds(*span)], self.outs[k].at[first, pl.ds(*span)]
            return pltpu.make_async_remote_copy(
                here,
                there,
                self.send_sem.at[k, slot],
                self.recv_sem.at[k, slot],
                device_id=target,
                device_id_type=MESH,
            )

        when(condition, lambda: copy().start())
        self.sent.append((condition, copy))

    def mirror(self, condition, k, first, number, span, group):
        if self.pairs[k] is None:
            return
        slot = len(self.mirrored)

        def copy():
            return pltpu.make_async_remote_copy(
                self.outs[k].at[pl.ds(first, number), pl.ds(*span)],
                self.pairs[k].at[pl.ds(first, number), pl.ds(*span)],
                self.pair_send.at[slot],
                self.pair_recv.at[slot],
                device_id=(self.me, 1 - self.core),
                device_id_type=MESH,
            )

        when(condition, lambda: copy().start())
        self.mirrored.append((condition, copy, group))

    def arrive(self, condition, k, slot, first, number, span, group):
        place = self.outs[k].at[pl.ds(first, number), pl.ds(*span)]

        def wait():
            pltpu.make_async_remote_copy(
                place,
                place,
                self.send_sem.at[k, slot],
                self.recv_sem.at[k, slot],
                device_id=self.to_x,
                device_id_type=MESH,
            ).wait_recv()

        when(condition, wait)
        self.mirror(condition, k, first, number, span, group)

    def members(self, step):
        if step == 0:
            return [(None, 0, 0)]
        return [(self.level >= step, step, -step), (self.level + step < LEVELS, 3 + step, step)]

    def slot_of(self, group, index):
        return 6 + 7 * group + index

    last = 6 + 28

    def own_copy(self, k):
        return pltpu.make_async_copy(self.ins[k], self.outs[k].at[self.me], self.local_sem.at[k])

    def start(self):
        whole_a, half_a, whole_b, half_b = self.spans
        last, me = self.last, self.me
        for k in self.everyone:
            self.send(None, k, last, "own", me, 1, whole_b, self.to_x)
            self.send(None, k, last + 1, "own", me, 1, whole_b, self.to_y)
            self.send(self.has_up, k, 0, "own", me, 1, whole_a, self.up)
            self.send(self.has_down, k, 3, "own", me, 1, whole_a, self.down)
            self.send(None, k, self.slot_of(0, 0), "own", me, 1, whole_a, self.to_x)
            self.send(None, k, self.slot_of(1, 0), "own", me, 1, whole_a, self.to_y)

    def side_small(self):
        whole_a, half_a, whole_b, half_b = self.spans
        last = self.last
        for k in self.everyone:
            self.arrive(None, k, last, self.x_side, 1, whole_b, 0)
            self.send(None, k, last + 3, "out", self.x_side, 1, half_b[1], self.to_y)
            self.arrive(None, k, last + 1, self.y_side, 1, whole_b, 0)
            self.send(None, k, last + 2, "out", self.y_side, 1, half_b[0], self.to_x)
        for k in self.everyone:
            self.own_copy(k).wait()
            self.mirror(None, k, self.me, 1, (0, self.ins[k].shape[0]), 0)
            self.arrive(None, k, last + 2, self.diagonal, 1, half_b[0], 0)
            self.arrive(None, k, last + 3, self.diagonal, 1, half_b[1], 0)

    def start_planes(self):
        whole_b = self.spans[2]
        for k in self.everyone:
            self.send(self.has_up, k, self.last + 4, "out", PLANE * self.level, PLANE, whole_b, self.up)
            self.send(self.has_down, k, self.last + 7, "out", PLANE * self.level, PLANE, whole_b, self.down)

    def cross(self, step):
        whole_a, half_a = self.spans[:2]
        for k in self.everyone:
            for condition, index, distance in self.members(step):
                first = self.x_side + PLANE * distance
                self.arrive(condition, k, self.slot_of(0, index), first, 1, whole_a, distance)
                self.send(condition, k, self.slot_of(3, index), "out", first, 1, half_a[1], self.to_y)
                first = self.y_side + PLANE * distance
                self.arrive(condition, k, self.slot_of(1, index), first, 1, whole_a, distance)
                self.send(condition, k, self.slot_of(2, index), "out", first, 1, half_a[0], self.to_x)

    def halves(self, step):
        half_a = self.spans[1]
        for k in self.everyone:
            for condition, index, distance in self.members(step):
                first = self.diagonal + PLANE * distance
                self.arrive(condition, k, self.slot_of(2, index), first, 1, half_a[0], distance)
                self.arrive(condition, k, self.slot_of(3, index), first, 1, half_a[1], distance)

    def column(self, step):
        whole_a = self.spans[0]
        for k in self.everyone:
            for condition, index, distance in self.members(step):
                first = self.me + PLANE * distance
                rising = distance < 0
                self.arrive(condition, k, step - 1 if rising else 2 + step, first, 1, whole_a, distance)
                if step < LEVELS - 1:
                    onward = condition & (self.has_up if rising else self.has_down)
                    slot = step if rising else 3 + step
                    self.send(onward, k, slot, "out", first, 1, whole_a, self.up if rising else self.down)
                self.send(condition, k, self.slot_of(0, index), "out", first, 1, whole_a, self.to_x)
                self.send(condition, k, self.slot_of(1, index), "out", first, 1, whole_a, self.to_y)

    def planes(self, step):
        whole_b = self.spans[2]
        for k in self.everyone:
            for condition, index, distance in self.members(step):
                first = PLANE * (self.level + distance)
                rising = distance < 0
                self.arrive(condition, k, self.last + (3 if rising else 6) + step, first, PLANE, whole_b, distance)
                if step < LEVELS - 1:
                    onward = condition & (self.has_up if rising else self.has_down)
                    slot = self.last + (4 if rising else 7) + step
                    self.send(onward, k, slot, "out", first, PLANE, whole_b, self.up if rising else self.down)

    def paired_level(self, distance):
        for condition, copy, group in self.mirrored:
            if group == distance:
                when(condition, lambda copy=copy: copy().wait_recv())

    def end(self, levels_waited=False):
        for condition, copy in self.sent:
            when(condition, lambda copy=copy: copy().wait_send())
        for condition, copy, group in self.mirrored:
            when(condition, lambda copy=copy: copy().wait_send())
            if not levels_waited:
                when(condition, lambda copy=copy: copy().wait_recv())


GATHER_SLOTS = 6 + 28 + 10


def gather_semaphores(count, paired):
    dma = pltpu.SemaphoreType.DMA
    slots = (count, GATHER_SLOTS)
    pair_slots = (max(1, paired * (GATHER_SLOTS + 1)),)
    return [dma(slots), dma(slots), dma((count,)), dma(pair_slots), dma(pair_slots)]


def gather_blocks(arrays, with_pair, collective_id):
    count, blocks, paired = len(arrays), lax.axis_size("gx"), sum(with_pair)
    shapes = [jax.ShapeDtypeStruct((blocks, *a.shape), a.dtype) for a in arrays]
    shapes += [shape for shape, wanted in zip(shapes, with_pair) if wanted]
    return pl.pallas_call(
        functools.partial(gather_kernel, count, with_pair),
        out_shape=shapes,
        in_specs=[pl.BlockSpec(memory_space=pl.ANY)] * count,
        out_specs=[pl.BlockSpec(memory_space=pl.ANY)] * len(shapes),
        scratch_shapes=gather_semaphores(count, paired),
        compiler_params=pltpu.CompilerParams(collective_id=collective_id, has_side_effects=True),
    )(*arrays)


def dot_nn(left, right):
    return lax.dot_general(left, right, (((1,), (0,)), ((), ())), preferred_element_type=jnp.float32)


def dot_nt(left, right):
    return lax.dot_general(left, right, (((1,), (1,)), ((), ())), preferred_element_type=jnp.float32)


def experts_kernel(experts_all, *refs):
    rows_ref, grad_rows_ref, w_gate, w_up, w_down = refs[:5]
    weighted_out, grad_in_out, terms_out, gate_out, up_out, down_out, grads_own, grads_pair = refs[5:13]
    held, grads, w_in, left_in, left_down, weighted_ref, grad_in_ref, terms_ref = refs[13:21]
    sums_in, sums_down, turned, grad_sem, w_sem, out_sem, sum_sem = refs[21:28]
    hidden, width = w_down.shape
    joins = [
        pltpu.make_async_copy(part, w_in.at[:, pl.ds(i * hidden, hidden)], w_sem.at[i])
        for i, part in enumerate((w_gate, w_up))
    ]
    for join in joins:
        join.start()
    steps = gather_steps(
        [rows_ref, grad_rows_ref], [held.at[0], grads_own], [held.at[1], grads_pair], refs[28:]
    )
    level, core = steps.level, steps.core
    tiles = hidden // LANES
    rows = rows_ref.shape[0]
    visits = [
        level,
        jnp.where(level == 0, 1, level - 1),
        jnp.where(level == 0, 2, jnp.where(level == 3, 1, level + 1)),
        jnp.where(level < 2, 3, 0),
    ]

    def fetch(turn, half):
        return pltpu.make_async_copy(
            (grads_own, grads_pair)[half].at[pl.ds(PLANE * visits[turn], PLANE)],
            grads.at[turn % 2, half],
            grad_sem.at[turn % 2, half],
        )

    def fetch_start(turn):
        fetch(turn, 0).start()
        fetch(turn, 1).start()

    lane = lax.broadcasted_iota(jnp.int32, (1, LANES), 1)
    expert = steps.me
    gate_pick = (((lane == expert) | (lane == experts_all + expert))).astype(jnp.float32)
    high_lane = (lane == 2 * experts_all * core + expert).astype(jnp.float32)
    low_lane = (lane == 2 * experts_all * core + experts_all + expert).astype(jnp.float32)
    group = 2 * rows

    def leave(turn):
        span = pl.ds(PLANE * visits[turn], PLANE)
        pairs = ((weighted_ref, weighted_out), (grad_in_ref, grad_in_out), (terms_ref, terms_out))
        return [
            pltpu.make_async_copy(here.at[:, span], there.at[:, span], out_sem.at[turn, i])
            for i, (here, there) in enumerate(pairs)
        ]

    def forward(turn, begin, end):
        first = PLANE * visits[turn]
        if begin == 0:
            fetch(turn, 0).wait()
            fetch(turn, 1).wait()

        def body(step, carry):
            half, pair = step // 2, step % 2
            at = first + 2 * pair
            lanes = held[half, pl.ds(at, 2), :, pl.ds(width, LANES)].reshape(group, LANES)
            gate_rows = jnp.sum(lanes.astype(jnp.float32) * gate_pick, axis=1, keepdims=True)
            grad_rows = grads[turn % 2, half, pl.ds(2 * pair, 2)].reshape(group, width)
            token_rows = held[half, pl.ds(at, 2), :, pl.ds(0, width)].reshape(group, width)
            grad_hidden = dot_nt(grad_rows, w_down[...])
            both = dot_nn(token_rows, w_in[...])
            terms = jnp.zeros((group, 1), jnp.float32)
            column = pl.multiple_of(step * group, group)
            for j in range(tiles):
                gate_in = both[:, j * LANES : (j + 1) * LANES]
                up_in = both[:, hidden + j * LANES : hidden + (j + 1) * LANES]
                back = grad_hidden[:, j * LANES : (j + 1) * LANES]
                gate_sigmoid = 1.0 / (1.0 + jnp.exp(-gate_in))
                gate_swish = gate_in * gate_sigmoid
                activated = gate_swish * up_in
                terms = terms + jnp.sum(activated * back, axis=1, keepdims=True)
                grad_act = gate_rows * back
                weighted = gate_rows * activated
                grad_gate = grad_act * up_in * gate_sigmoid * (1.0 + gate_in * (1.0 - gate_sigmoid))
                grad_up = grad_act * gate_swish
                for value, array, tile, left in (
                    (weighted, weighted_ref, j, left_down),
                    (grad_gate, grad_in_ref, j, left_in),
                    (grad_up, grad_in_ref, tiles + j, left_in),
                ):
                    span = pl.ds(tile * LANES, LANES)
                    array[half, pl.ds(at, 2), :, span] = value.astype(jnp.bfloat16).reshape(2, rows, LANES)
                    left[span, pl.ds(column, group)] = value.T.astype(jnp.bfloat16)
            high = terms.astype(jnp.bfloat16).astype(jnp.float32)
            spread = high * high_lane + (terms - high) * low_lane
            terms_ref[half, pl.ds(at, 2)] = spread.astype(jnp.bfloat16).reshape(2, rows, LANES)
            return carry

        lax.fori_loop(begin, end, body, 0)
        if end == 4:
            for copy in leave(turn):
                copy.start()

    wide = 256

    def weights(turn, begin, end):
        first = PLANE * visits[turn]

        def body(step, carry):
            span = pl.ds(pl.multiple_of(step * wide, wide), wide)
            token_rows = held[:, pl.ds(first, PLANE), :, span].reshape(2 * PLANE * rows, wide)
            grad_rows = grads[turn % 2, :, :, :, span].reshape(2 * PLANE * rows, wide)
            part_in = dot_nn(left_in[...], token_rows)
            part_down = dot_nn(left_down[...], grad_rows)
            if turn:
                part_in = sums_in[:, span] + part_in
                part_down = sums_down[:, span] + part_down
            sums_down[:, span] = part_down
            if turn < LEVELS - 1:
                sums_in[:, span] = part_in
            else:
                for i in range(2):
                    turned[i, span] = part_in[i * hidden : (i + 1) * hidden].T
                for copy in leave_sums(step):
                    copy.start()
            return carry

        lax.fori_loop(begin, end, body, 0)

    def leave_sums(step):
        span = pl.ds(pl.multiple_of(step * wide, wide), wide)
        return [
            pltpu.make_async_copy(turned.at[0, span], gate_out.at[span], sum_sem.at[step, 0]),
            pltpu.make_async_copy(turned.at[1, span], up_out.at[span], sum_sem.at[step, 1]),
            pltpu.make_async_copy(sums_down.at[:, span], down_out.at[:, span], sum_sem.at[step, 2]),
        ]

    def level_ready(turn):
        if turn == 0:
            steps.paired_level(0)
        for distance in range(-3, 4):
            if turn and distance:
                wanted = visits[turn] == level + distance
                pl.when(wanted)(lambda distance=distance: steps.paired_level(distance))
        fetch_start(turn)

    steps.start()
    steps.side_small()
    steps.column(1)
    steps.cross(0)
    for join in joins:
        join.wait()
    steps.column(2)
    steps.start_planes()
    steps.halves(0)
    steps.cross(1)
    level_ready(0)
    forward(0, 0, 4)
    steps.column(3)
    steps.planes(1)
    weights(0, 0, 4)
    steps.cross(2)
    steps.halves(1)
    level_ready(1)
    weights(0, 4, 8)
    forward(1, 0, 4)
    steps.planes(2)
    weights(1, 0, 4)
    steps.cross(3)
    steps.halves(2)
    level_ready(2)
    weights(1, 4, 8)
    forward(2, 0, 4)
    weights(2, 0, 8)
    steps.planes(3)
    steps.halves(3)
    level_ready(3)
    forward(3, 0, 4)
    weights(3, 0, 8)
    for turn in range(LEVELS):
        for copy in leave(turn):
            copy.wait()

    def last_sums(step, carry):
        for copy in leave_sums(step):
            copy.wait()
        return carry

    lax.fori_loop(0, width // wide, last_sums, 0)
    steps.end(levels_waited=True)


def experts_products(rows, grad_rows, w_gate, w_up, w_down, experts_all, collective_id):
    blocks, low, count = lax.axis_size("gx"), jnp.bfloat16, rows.shape[0]
    hidden, width = w_down.shape
    everywhere = pl.BlockSpec(memory_space=pl.ANY)
    block_shape = (2, blocks, count)
    shapes = [
        jax.ShapeDtypeStruct((*block_shape, hidden), low),
        jax.ShapeDtypeStruct((*block_shape, 2 * hidden), low),
        jax.ShapeDtypeStruct((*block_shape, LANES), low),
        jax.ShapeDtypeStruct((width, hidden), jnp.float32),
        jax.ShapeDtypeStruct((width, hidden), jnp.float32),
        jax.ShapeDtypeStruct((hidden, width), jnp.float32),
        *[jax.ShapeDtypeStruct((blocks, count, width), low)] * 2,
    ]
    level_rows = 2 * PLANE * count
    dma = pltpu.SemaphoreType.DMA
    return pl.pallas_call(
        functools.partial(experts_kernel, experts_all),
        out_shape=shapes,
        in_specs=[everywhere] * 4 + [pl.BlockSpec(memory_space=pltpu.VMEM)],
        out_specs=[everywhere] * 8,
        scratch_shapes=[
            pltpu.VMEM((*block_shape, rows.shape[1]), low),
            pltpu.VMEM((2, 2, PLANE, count, width), low),
            pltpu.VMEM((width, 2 * hidden), low),
            pltpu.VMEM((2 * hidden, level_rows), low),
            pltpu.VMEM((hidden, level_rows), low),
            *[pltpu.VMEM(shape.shape, low) for shape in shapes[:3]],
            pltpu.VMEM((2 * hidden, width), jnp.float32),
            pltpu.VMEM((hidden, width), jnp.float32),
            pltpu.VMEM((2, width, hidden), jnp.float32),
            dma((2, 2)),
            dma((2,)),
            dma((LEVELS, 3)),
            dma((width // 256, 3)),
            *gather_semaphores(2, 2),
        ],
        compiler_params=pltpu.CompilerParams(
            collective_id=collective_id, has_side_effects=True, vmem_limit_bytes=63 * 1024 * 1024
        ),
    )(rows, grad_rows, w_gate, w_up, w_down)[:6]


class scatter_moves:
    def __init__(self, held, out):
        self.mine, self.half_y, self.half_x, self.full_x, self.full_y, self.slots_a, self.slots_b, self.side_b = held[:8]
        self.send_sem, self.recv_sem, self.chain_send, self.chain_recv = held[8:12]
        self.out = out
        self.me, self.core, level, x_side, y_side = neighbours()
        self.level = level
        self.up, self.down = (self.me + PLANE, self.core), (self.me - PLANE, self.core)
        self.to_x, self.to_y = (x_side, self.core), (y_side, self.core)
        self.x_at, self.y_at, self.own_at = x_side % PLANE, y_side % PLANE, self.me % PLANE
        self.diagonal_at = (x_side + y_side - self.me) % PLANE
        forward = jnp.where(level < 2, 1, 0)
        self.order = [3 * forward, 2 * forward + (1 - forward), level + 1 - 2 * (level % 2), level]
        self.rows, self.width = self.mine.shape[1:]
        self.spans = cut_rows(self.rows)
        self.sent = []

    def send(self, condition, source, target_ref, ssem, rsem, target):
        def copy():
            return pltpu.make_async_remote_copy(
                source, target_ref, ssem, rsem, device_id=target, device_id_type=MESH
            )

        when(condition, lambda: copy().start())
        self.sent.append((condition, copy))

    def arrive(self, condition, target_ref, rsem):
        def wait():
            pltpu.make_async_remote_copy(
                target_ref, target_ref, rsem, rsem, device_id=self.to_x, device_id_type=MESH
            ).wait_recv()

        when(condition, wait)

    def add(self, condition, height, target, *terms, step=16):
        def run():
            def body(i, carry):
                at = pl.multiple_of(i * step, step)
                total = target(at, step)[...].astype(jnp.float32)
                for term in terms:
                    total = total + term(at, step)[...].astype(jnp.float32)
                target(at, step)[...] = total.astype(jnp.bfloat16)
                return carry

            lax.fori_loop(0, height // step, body, 0)

        when(condition, run)

    def rows_of(self, ref, *index, start=0):
        return lambda at, step: ref.at[(*index, pl.ds(start + at, step))]

    def turn_sems(self, turn):
        return [(self.send_sem.at[6 * turn + i], self.recv_sem.at[6 * turn + i]) for i in range(6)]

    def half_spans(self):
        half_a = self.spans[1]
        return half_a[0][1], pl.ds(*half_a[0]), pl.ds(*half_a[1])

    def first(self, turn):
        base, at = PLANE * self.order[turn], self.turn_sems(turn)
        _, lower, upper = self.half_spans()
        mine, to_x, to_y = self.mine, self.to_x, self.to_y
        self.send(None, mine.at[base + self.diagonal_at, lower], self.half_y.at[turn], *at[0], to_y)
        self.send(None, mine.at[base + self.diagonal_at, upper], self.half_x.at[turn], *at[1], to_x)
        self.send(None, mine.at[base + self.x_at, upper], self.full_x.at[turn, upper], *at[2], to_x)
        self.send(None, mine.at[base + self.y_at, lower], self.full_y.at[turn, lower], *at[3], to_y)

    def second(self, turn):
        base, at = PLANE * self.order[turn], self.turn_sems(turn)
        height, lower, upper = self.half_spans()
        mine, rows_of = self.mine, self.rows_of
        self.arrive(None, self.half_y.at[turn], at[0][1])
        self.add(None, height, rows_of(mine, base + self.x_at), rows_of(self.half_y, turn))
        self.send(None, mine.at[base + self.x_at, lower], self.full_x.at[turn, lower], *at[4], self.to_x)
        self.arrive(None, self.half_x.at[turn], at[1][1])
        self.add(None, height, rows_of(mine, base + self.y_at, start=height), rows_of(self.half_x, turn))
        self.send(None, mine.at[base + self.y_at, upper], self.full_y.at[turn, upper], *at[5], self.to_y)

    def chain(self, which, turn, block, slots, spread):
        to_level, level = self.order[turn], self.level
        rising, falling = to_level > level, to_level < level
        begins = (rising & (level == 0)) | (falling & (level == LEVELS - 1))
        middle = (rising | falling) & jnp.logical_not(begins)
        self.arrive(middle, slots.at[to_level], self.chain_recv.at[which, to_level])
        spread(middle, to_level)
        outgoing = self.chain_send.at[which, to_level]
        self.send(rising, block, slots.at[to_level], outgoing, self.chain_recv.at[which, to_level], self.up)
        at = jnp.where(to_level == level - 1, LEVELS, to_level)
        self.send(falling, block, slots.at[at], outgoing, self.chain_recv.at[which, at], self.down)

    def add_small(self, condition, base, slot):
        start, number = self.spans[2]
        for column in range(PLANE):
            self.add(
                condition,
                number,
                self.rows_of(self.mine, base + column, start=start),
                self.rows_of(self.slots_b, slot, column),
            )

    def chain_small(self, turn):
        if turn == LEVELS - 1:
            return
        base = PLANE * self.order[turn]
        block = self.mine.at[pl.ds(base, PLANE), pl.ds(*self.spans[2])]
        self.chain(1, turn, block, self.slots_b, lambda condition, slot: self.add_small(condition, base, slot))

    def plane_arrives(self, turn):
        at = self.turn_sems(turn)
        _, lower, upper = self.half_spans()
        self.arrive(None, self.full_x.at[turn, upper], at[2][1])
        self.arrive(None, self.full_y.at[turn, lower], at[3][1])
        self.arrive(None, self.full_x.at[turn, lower], at[4][1])
        self.arrive(None, self.full_y.at[turn, upper], at[5][1])

    def chain_large(self, turn):
        if turn == LEVELS - 1:
            return
        own, number = PLANE * self.order[turn] + self.own_at, self.spans[0][1]
        rows_of, mine = self.rows_of, self.mine
        self.plane_arrives(turn)
        self.add(None, number, rows_of(mine, own), rows_of(self.full_x, turn), rows_of(self.full_y, turn))
        self.chain(
            0,
            turn,
            mine.at[own, pl.ds(*self.spans[0])],
            self.slots_a,
            lambda condition, slot: self.add(condition, number, rows_of(mine, own), rows_of(self.slots_a, slot)),
        )

    def side(self):
        short = self.spans[3][0][1]
        spans = [pl.ds(0, short), pl.ds(short, short), pl.ds(2 * short, 2 * short), pl.ds(4 * short, 2 * short)]
        return [(self.side_b.at[span], self.send_sem.at[24 + i], self.recv_sem.at[24 + i]) for i, span in enumerate(spans)]

    def arrivals(self):
        return ((self.level > 0, self.level), (self.level < LEVELS - 1, LEVELS))

    def end_small(self):
        base, mine, half_b = PLANE * self.level, self.mine, self.spans[3]
        for condition, slot in self.arrivals():
            self.arrive(condition, self.slots_b.at[slot], self.chain_recv.at[1, slot])
            self.add_small(condition, base, slot)
        side = self.side()
        self.send(None, mine.at[base + self.diagonal_at, pl.ds(*half_b[0])], *side[0], self.to_y)
        self.send(None, mine.at[base + self.diagonal_at, pl.ds(*half_b[1])], *side[1], self.to_x)

    def end_sides(self):
        base, mine, rows_of = PLANE * self.level, self.mine, self.rows_of
        whole_b, half_b = self.spans[2:]
        side, short = self.side(), half_b[0][1]
        self.plane_arrives(LEVELS - 1)
        self.arrive(None, side[0][0], side[0][2])
        self.add(None, short, rows_of(mine, base + self.x_at, start=half_b[0][0]), rows_of(self.side_b))
        self.send(None, mine.at[base + self.x_at, pl.ds(*whole_b)], *side[2], self.to_x)
        self.arrive(None, side[1][0], side[1][2])
        self.add(None, short, rows_of(mine, base + self.y_at, start=half_b[1][0]), rows_of(self.side_b, start=short))
        self.send(None, mine.at[base + self.y_at, pl.ds(*whole_b)], *side[3], self.to_y)

    def end_sums(self, base):
        whole_a, half_a, whole_b, half_b = self.spans
        own, out, mine, step = PLANE * self.level + self.own_at, self.out, self.mine, 16
        full_x, full_y, slots_a, side_b = self.full_x, self.full_y, self.slots_a, self.side_b

        def place(at):
            return pl.ds(pl.multiple_of(base + at, step), step)

        def tail_a(i, carry):
            at = pl.multiple_of(i * step, step)
            span, turn = pl.ds(at, step), LEVELS - 1
            total = mine[own, span].astype(jnp.float32)
            total = total + full_x[turn, span].astype(jnp.float32) + full_y[turn, span].astype(jnp.float32)
            out[place(at)] = total
            return carry

        lax.fori_loop(0, whole_a[1] // step, tail_a, 0)
        for condition, slot in self.arrivals():
            self.arrive(condition, slots_a.at[slot], self.chain_recv.at[0, slot])

            def more(slot=slot):
                def body(i, carry):
                    at = pl.multiple_of(i * step, step)
                    out[place(at)] = out[place(at)] + slots_a[slot, pl.ds(at, step)].astype(jnp.float32)
                    return carry

                lax.fori_loop(0, whole_a[1] // step, body, 0)

            when(condition, more)
        side, short = self.side(), half_b[0][1]
        self.arrive(None, side[2][0], side[2][2])
        self.arrive(None, side[3][0], side[3][2])

        def tail_b(i, carry):
            at = pl.multiple_of(i * step, step)
            total = mine[own, pl.ds(whole_b[0] + at, step)].astype(jnp.float32)
            total = total + side_b[pl.ds(2 * short + at, step)].astype(jnp.float32)
            total = total + side_b[pl.ds(4 * short + at, step)].astype(jnp.float32)
            out[place(whole_b[0] + at)] = total
            return carry

        lax.fori_loop(0, whole_b[1] // step, tail_b, 0)

    def end_waits(self):
        for condition, copy in self.sent:
            when(condition, lambda copy=copy: copy().wait_send())


def scatter_places(blocks, rows, width):
    near, far, low, dma = 3 * rows // 4, rows // 4, jnp.bfloat16, pltpu.SemaphoreType.DMA
    shapes = [
        (blocks, rows, width),
        (LEVELS, near // 2, width),
        (LEVELS, near // 2, width),
        (LEVELS, near, width),
        (LEVELS, near, width),
        (LEVELS + 1, near, width),
        (LEVELS + 1, PLANE, far, width),
        (3 * far, width),
    ]
    return [pltpu.VMEM(shape, low) for shape in shapes] + [dma((28,)), dma((28,)), dma((2, 5)), dma((2, 5))]


PLACES = 12


def scatter_kernel(*refs):
    normed, grad_qkv, router_term, grad_attn, attended, gain_ref = refs[:6]
    tokens, grad_residual, grad_normed, attn_gain = refs[6:10]
    pieces_out, (gain_out, grad_input) = refs[10:15], refs[15:17]
    held, (out, load_sem, leave_sem, gain_slots, gain_send, gain_recv) = refs[17:-6], refs[-6:]
    moves = scatter_moves(held, out)
    me, core, level = moves.me, moves.core, moves.level
    far = me + 2 * PLANE - 4 * PLANE * (level // 2)
    partners = ((me, 1 - core), moves.to_x, moves.to_y, (me + PLANE - 2 * PLANE * (level % 2), core), (far, core))

    def gain_copy(turn):
        return pltpu.make_async_remote_copy(
            gain_slots.at[2 * turn],
            gain_slots.at[2 * turn + 1],
            gain_send.at[turn],
            gain_recv.at[turn],
            device_id=partners[turn],
            device_id_type=MESH,
        )

    def gain_step(turn):
        if turn == 0:
            gain_slots[0] = gain_ref[...]
        else:
            gain_copy(turn - 1).wait_recv()
            gain_slots[2 * turn] = gain_slots[2 * turn - 2] + gain_slots[2 * turn - 1]
        if turn < len(partners):
            gain_copy(turn).start()
        else:
            gain_out[...] = gain_slots[2 * turn]

    router_lane = grad_qkv.shape[1]

    def load(turn):
        span = pl.ds(PLANE * moves.order[turn], PLANE)
        place = moves.mine.at[span, :, pl.ds(router_lane, LANES)]
        return pltpu.make_async_copy(router_term.at[span], place, load_sem.at[turn])

    def products(turn):
        level_rows, wide = PLANE * moves.rows, 256
        span = pl.ds(PLANE * moves.order[turn], PLANE)
        features = pl.ds(pl.multiple_of(moves.order[turn] * level_rows, level_rows), level_rows)
        for left, right, lane in ((normed, grad_qkv, 0), (grad_attn, attended, router_lane + LANES)):
            left_rows = left[:, features].astype(jnp.float32).T.astype(jnp.bfloat16)

            def body(step, carry, left_rows=left_rows, right=right, lane=lane):
                at = pl.multiple_of(step * wide, wide)
                value = dot_nn(left_rows, right[:, pl.ds(at, wide)]).astype(jnp.bfloat16)
                lanes = pl.ds(pl.multiple_of(lane + at, LANES), wide)
                moves.mine[span, :, lanes] = value.reshape(PLANE, moves.rows, wide)
                return carry

            lax.fori_loop(0, right.shape[1] // wide, body, 0)

    def input_rows():
        step = 16

        def body(i, carry):
            span = pl.ds(pl.multiple_of(i * step, step), step)
            unit, scale = unit_rows(tokens[span].astype(jnp.float32))
            grad = grad_normed[span] * attn_gain[...]
            grad = scale * (grad - unit * jnp.mean(grad * unit, axis=1, keepdims=True))
            grad_input[span] = (grad_residual[span] + grad).astype(jnp.bfloat16)
            return carry

        lax.fori_loop(0, tokens.shape[0] // step, body, 0)

    def leave():
        copies, lane = [], 0
        for i, piece in enumerate(pieces_out):
            width = piece.shape[1]
            copies.append(pltpu.make_async_copy(out.at[:, pl.ds(lane, width)], piece, leave_sem.at[i]))
            lane += width
        return copies

    for turn in range(LEVELS):
        load(turn).start()
    products(0)
    greet(level, (moves.to_x[0], moves.to_y[0], far), True, me, core)
    gain_step(0)
    for turn in range(LEVELS):
        if turn:
            products(turn)
        load(turn).wait()
        moves.first(turn)
        moves.chain_small(turn)
    input_rows()
    for turn in range(LEVELS - 1):
        moves.second(turn)
        gain_step(turn + 1)
        if turn:
            moves.chain_large(turn - 1)
    moves.second(LEVELS - 1)
    gain_step(4)
    moves.chain_large(LEVELS - 2)
    moves.end_small()
    moves.end_sides()
    gain_step(5)
    moves.end_sums(0)
    for copy in leave():
        copy.start()
    for turn in range(len(partners)):
        gain_copy(turn).wait_send()
    moves.end_waits()
    for copy in leave():
        copy.wait()


def scatter_sums(factors, gains, lasts, kv_width, collective_id):
    _, grad_qkv, router_term, _, attended = factors
    blocks, rows, _ = router_term.shape
    widths = (grad_qkv.shape[1] - 2 * kv_width, kv_width, kv_width, LANES, attended.shape[1])
    dma, tokens = pltpu.SemaphoreType.DMA, lasts[0]
    vmem, everywhere = pl.BlockSpec(memory_space=pltpu.VMEM), pl.BlockSpec(memory_space=pl.ANY)
    return pl.pallas_call(
        scatter_kernel,
        out_shape=[
            *[jax.ShapeDtypeStruct((rows, width), jnp.float32) for width in widths],
            jax.ShapeDtypeStruct(gains.shape, gains.dtype),
            jax.ShapeDtypeStruct(tokens.shape, tokens.dtype),
        ],
        in_specs=[vmem, vmem, everywhere, vmem, vmem, vmem, vmem, vmem, vmem, vmem],
        out_specs=[everywhere] * 5 + [vmem] * 2,
        scratch_shapes=[
            *scatter_places(blocks, rows, sum(widths)),
            pltpu.VMEM((rows, sum(widths)), jnp.float32),
            dma((LEVELS,)),
            dma((5,)),
            pltpu.VMEM((11, *gains.shape), gains.dtype),
            dma((5,)),
            dma((5,)),
        ],
        compiler_params=pltpu.CompilerParams(
            collective_id=collective_id, has_side_effects=True, vmem_limit_bytes=63 * 1024 * 1024
        ),
    )(*factors, gains, *lasts)


def return_kernel(grad_in, weighted, terms, w_gate, w_up, w_down, back_out, mixed_out, *refs):
    streams = [
        scatter_moves(refs[:PLACES], back_out),
        scatter_moves(refs[PLACES : 2 * PLACES], mixed_out),
    ]
    sibling, away, left, right_in, right_down = refs[2 * PLACES : 2 * PLACES + 5]
    pair_send, pair_recv, left_sem, right_sem, term_sem, ready_sem, credit = refs[2 * PLACES + 5 :]
    me, core, order, rows = streams[0].me, streams[0].core, streams[0].order, streams[0].rows
    hidden, features = w_down.shape
    depths, lefts = (2 * hidden, hidden), (grad_in, weighted)
    turns, wide = 2 * LEVELS, 256
    rights = [
        pltpu.make_async_copy(w_gate, right_in.at[:, pl.ds(0, hidden)], right_sem.at[0]),
        pltpu.make_async_copy(w_up, right_in.at[:, pl.ds(hidden, hidden)], right_sem.at[1]),
        pltpu.make_async_copy(w_down, right_down, right_sem.at[2]),
    ]

    def level_span(turn):
        return pl.ds(PLANE * order[turn % LEVELS], PLANE)

    def left_copy(turn):
        stream = turn // LEVELS
        return pltpu.make_async_copy(
            lefts[stream].at[:, level_span(turn)],
            left.at[turn % 2, :, :, :, pl.ds(0, depths[stream])],
            left_sem.at[turn % 2],
        )

    def term_copy(turn, half):
        lanes = pl.ds(features, LANES)
        place = away.at[turn % 2, :, :, lanes] if half else streams[0].mine.at[level_span(turn), :, lanes]
        return pltpu.make_async_copy(terms.at[half, level_span(turn)], place, term_sem.at[half])

    def width_of(turn):
        return streams[turn // LEVELS].width

    def hand(turn):
        lanes = pl.ds(0, width_of(turn))
        return pltpu.make_async_remote_copy(
            away.at[turn % 2, :, :, lanes],
            sibling.at[turn % 2, :, :, lanes],
            pair_send.at[turn],
            pair_recv.at[turn],
            device_id=(me, 1 - core),
            device_id_type=MESH,
        )

    def product(turn, half, store):
        stream, slot = turn // LEVELS, turn % 2
        factor = left[slot, half, :, :, pl.ds(0, depths[stream])].reshape(PLANE * rows, depths[stream])

        def body(step, carry):
            span = pl.ds(pl.multiple_of(step * wide, wide), wide)
            value = dot_nt(factor, right_in[span]) if stream == 0 else dot_nn(factor, right_down[:, span])
            store(span, value.reshape(PLANE, rows, wide))
            return carry

        lax.fori_loop(0, features // wide, body, 0)

    def hand_over(turn):
        left_copy(turn).wait()
        if turn + 1 < turns:
            left_copy(turn + 1).start()
        if turn < LEVELS:
            term_copy(turn, 1).start()
            term_copy(turn, 0).start()

        def store(span, value):
            away[turn % 2, :, :, span] = value.astype(jnp.bfloat16)

        product(turn, 1, store)
        if turn < LEVELS:
            term_copy(turn, 1).wait()
            term_copy(turn, 0).wait()
        if turn == 0:
            greet(streams[0].level, (streams[0].to_x[0], streams[0].to_y[0]), True, me, core)
        if turn >= 2:
            pl.semaphore_wait(credit, 1)
        hand(turn).start()

    def settle(turn):
        hand(turn).wait()
        mine, slot = streams[turn // LEVELS].mine, turn % 2

        def store(span, value):
            value = value + sibling[slot, :, :, span].astype(jnp.float32)
            mine[level_span(turn), :, span] = value.astype(jnp.bfloat16)

        product(turn, 0, store)
        if turn < LEVELS:
            lanes = pl.ds(features, LANES)
            value = mine[level_span(turn), :, lanes].astype(jnp.float32)
            value = value + sibling[slot, :, :, lanes].astype(jnp.float32)
            mine[level_span(turn), :, lanes] = value.astype(jnp.bfloat16)
        if turn + 2 < turns:
            pl.semaphore_signal(credit, inc=1, device_id=(me, 1 - core), device_id_type=MESH)

    def exchange(stream, core_of_rows):
        out = streams[stream].out
        span = pl.ds(pl.multiple_of(core_of_rows * rows, rows), rows)
        return pltpu.make_async_remote_copy(
            out.at[span],
            out.at[span],
            ready_sem.at[stream, 0],
            ready_sem.at[stream, 1],
            device_id=(me, 1 - core),
            device_id_type=MESH,
        )

    def end(stream):
        streams[stream].end_sums(core * rows)
        exchange(stream, core).start()

    left_copy(0).start()
    for copy in rights:
        copy.start()
    for copy in rights:
        copy.wait()
    hand_over(0)
    for turn in range(turns + 2):
        if turn < turns:
            stream = streams[turn // LEVELS]
            settle(turn)
            stream.first(turn % LEVELS)
            if turn + 1 < turns:
                hand_over(turn + 1)
            stream.chain_small(turn % LEVELS)
        if 1 <= turn <= turns:
            streams[(turn - 1) // LEVELS].second((turn - 1) % LEVELS)
        if turn >= 2:
            streams[(turn - 2) // LEVELS].chain_large((turn - 2) % LEVELS)
        if turn == LEVELS + 1:
            streams[0].end_small()
        if turn == LEVELS + 2:
            streams[0].end_sides()
        if turn == LEVELS + 3:
            end(0)
    streams[1].end_small()
    streams[1].end_sides()
    end(1)
    for stream in range(2):
        exchange(stream, 1 - core).wait_recv()
        exchange(stream, core).wait_send()
        streams[stream].end_waits()


def return_sums(grad_in, weighted, terms, w_gate, w_up, w_down, collective_id):
    low, dma = jnp.bfloat16, pltpu.SemaphoreType.DMA
    blocks, rows, depth = grad_in.shape[1:]
    hidden, features = w_down.shape
    wide = features + LANES
    vmem, everywhere = pl.BlockSpec(memory_space=pltpu.VMEM), pl.BlockSpec(memory_space=pl.ANY)
    slots = pltpu.VMEM((2, PLANE, rows, wide), low)
    return pl.pallas_call(
        return_kernel,
        out_shape=[
            jax.ShapeDtypeStruct((2 * rows, wide), jnp.float32),
            jax.ShapeDtypeStruct((2 * rows, features), jnp.float32),
        ],
        in_specs=[everywhere] * 6,
        out_specs=[vmem] * 2,
        scratch_shapes=[
            *scatter_places(blocks, rows, wide),
            *scatter_places(blocks, rows, features),
            slots,
            slots,
            pltpu.VMEM((2, 2, PLANE, rows, depth), low),
            pltpu.VMEM((features, depth), low),
            pltpu.VMEM((hidden, features), low),
            dma((2 * LEVELS,)),
            dma((2 * LEVELS,)),
            dma((2,)),
            dma((3,)),
            dma((2,)),
            dma((2, 2)),
            pltpu.SemaphoreType.REGULAR,
        ],
        compiler_params=pltpu.CompilerParams(
            collective_id=collective_id, has_side_effects=True, vmem_limit_bytes=63 * 1024 * 1024
        ),
    )(grad_in, weighted, terms, w_gate, w_up, w_down)


def kernels_fit():
    return lax.axis_size("gx") == LEVELS * PLANE and lax.axis_size("gy") == 2


def packed_gains(vectors):
    rows = jnp.concatenate([vector.reshape(-1, HEAD_DIM) for vector in vectors], axis=0)
    return jnp.pad(rows, ((0, -rows.shape[0] % 8), (0, 0)))


def unpacked_gains(rows, vectors):
    sums, at = [], 0
    for vector in vectors:
        length = vector.shape[0] // HEAD_DIM
        sums.append(rows[at : at + length].reshape(-1))
        at += length
    return sums


def two_parts(values):
    high = lax.reduce_precision(values, 8, 7)
    return high.astype(jnp.bfloat16), (values - high).astype(jnp.bfloat16)


def sparse_experts(normed_ffn, logits, route_hits, routes, cotangent, w_gate, w_up, w_down):
    sequence_length, model_width = normed_ffn.shape
    experts_all = logits.shape[1]
    devices_gx = lax.axis_size("gx")
    part_width = model_width // lax.axis_size("gy")
    capacity = 5 * sequence_length * TOP // (4 * experts_all)
    pairs_count = sequence_length * TOP
    hits_float = route_hits.astype(jnp.float32)
    chosen = jnp.sum(logits[:, None, :] * hits_float, axis=-1)
    gate_exps = jnp.exp(chosen)
    gate_values = gate_exps / jnp.sum(gate_exps, axis=1, keepdims=True)
    flat_hits = route_hits.reshape(pairs_count, experts_all).astype(jnp.int32)
    slot_rank = jnp.sum((jnp.cumsum(flat_hits, axis=0) - flat_hits) * flat_hits, axis=1)
    slot_dest = routes.reshape(-1) * capacity + slot_rank
    slot_pair = (
        jnp.full((experts_all * capacity,), pairs_count, jnp.int32)
        .at[slot_dest]
        .set(jnp.arange(pairs_count, dtype=jnp.int32))
    )
    slot_token = jnp.where(slot_pair < pairs_count, slot_pair // TOP, sequence_length)

    def to_experts(buffer):
        arrived = lax.all_to_all(buffer, "gx", split_axis=0, concat_axis=0, tiled=True)
        return arrived.reshape(devices_gx * capacity, model_width)

    def from_experts(partial_rows):
        share_rows = lax.psum_scatter(
            partial_rows.astype(jnp.bfloat16), "gy", scatter_dimension=1, tiled=True
        )
        returned = lax.all_to_all(
            share_rows.reshape(devices_gx, capacity, part_width),
            "gx",
            split_axis=0,
            concat_axis=0,
            tiled=True,
        )
        whole_rows = lax.all_gather(returned, "gy", axis=2, tiled=True)
        return whole_rows.reshape(devices_gx * capacity, model_width)

    send_rows = jnp.take(normed_ffn, slot_token, axis=0, mode="fill", fill_value=0)
    expert_in = to_experts(send_rows.reshape(devices_gx, capacity, model_width))
    gate_in = jnp.dot(expert_in, w_gate, preferred_element_type=jnp.float32)
    up_in = jnp.dot(expert_in, w_up, preferred_element_type=jnp.float32)
    gate_sigmoid = jax.nn.sigmoid(gate_in)
    gate_swish = gate_in * gate_sigmoid
    activated = (gate_swish * up_in).astype(jnp.bfloat16)
    expert_part = jnp.dot(activated, w_down, preferred_element_type=jnp.float32)
    expert_out = from_experts(expert_part)
    pair_rows = jnp.take(expert_out, slot_dest, axis=0).reshape(sequence_length, TOP, model_width)
    mixed_rows = jnp.einsum(
        "tk,tkd->td", gate_values, pair_rows, preferred_element_type=jnp.float32
    )
    grad_out_f = cotangent.astype(jnp.float32)
    grad_gates = jnp.einsum("td,tkd->tk", grad_out_f, pair_rows, preferred_element_type=jnp.float32)
    grad_chosen = gate_values * (
        grad_gates - jnp.sum(gate_values * grad_gates, axis=1, keepdims=True)
    )
    grad_logits = jnp.sum(grad_chosen[:, :, None] * hits_float, axis=1).astype(jnp.bfloat16)
    slot_gate = jnp.take(gate_values.reshape(-1), slot_pair, mode="fill", fill_value=0.0)
    grad_send = (
        jnp.take(grad_out_f, slot_token, axis=0, mode="fill", fill_value=0) * slot_gate[:, None]
    )
    grad_expert_out = to_experts(
        grad_send.astype(jnp.bfloat16).reshape(devices_gx, capacity, model_width)
    )
    grad_act = contract(grad_expert_out, w_down, 1, 1)
    down_term = contract(activated, grad_expert_out, 0, 0)
    grad_gate_in = (
        grad_act * up_in * gate_sigmoid * (1.0 + gate_in * (1.0 - gate_sigmoid))
    ).astype(jnp.bfloat16)
    grad_up_in = (grad_act * gate_swish).astype(jnp.bfloat16)
    gate_term = contract(expert_in, grad_gate_in, 0, 0)
    up_term = contract(expert_in, grad_up_in, 0, 0)
    grad_in_part = contract(grad_gate_in, w_gate, 1, 1) + contract(grad_up_in, w_up, 1, 1)
    grad_rows = from_experts(grad_in_part)
    grad_pairs = jnp.take(grad_rows, slot_dest, axis=0).reshape(sequence_length, TOP, model_width)
    grad_rows_sum = jnp.sum(grad_pairs.astype(jnp.float32), axis=1)
    return mixed_rows, grad_rows_sum, grad_logits, (gate_term[None], up_term[None], down_term[None])


def swap_cores(rows):
    return lax.ppermute(rows, "gy", [(0, 1), (1, 0)])


def own_half(rows):
    count = rows.shape[0] // lax.axis_size("gy")
    return lax.dynamic_slice_in_dim(rows, lax.axis_index("gy") * count, count, 0)


def dense_experts(normed_ffn, logits, route_hits, cotangent, w_gate, w_up, w_down):
    sequence_length, model_width = normed_ffn.shape
    experts_all = logits.shape[1]
    gate_exps = jnp.exp(jnp.where(jnp.any(route_hits, axis=1), logits, -1e30))
    gate_all = gate_exps / jnp.sum(gate_exps, axis=1, keepdims=True)
    gate_lanes = jnp.pad(jnp.concatenate(two_parts(gate_all), axis=1), ((0, 0), (0, LANES - 2 * experts_all)))
    row_lanes = jnp.concatenate([own_half(normed_ffn), own_half(gate_lanes)], axis=1)
    weighted, grad_in, terms, gate_term, up_term, down_term = experts_products(
        row_lanes, own_half(cotangent), w_gate, w_up, w_down, experts_all, 2
    )
    back, mixed_rows = return_sums(grad_in, weighted, terms, w_gate, w_up, w_down, 3)
    term_lanes = back[:, model_width : model_width + 4 * experts_all]
    grad_gates = jnp.sum(term_lanes.reshape(sequence_length, 4, experts_all), axis=1)
    grad_logits = (
        gate_all * (grad_gates - jnp.sum(gate_all * grad_gates, axis=1, keepdims=True))
    ).astype(jnp.bfloat16)
    return mixed_rows, back[:, :model_width], grad_logits, (gate_term[None], up_term[None], down_term[None])


def turn_lanes(values, cosine, sine_table):
    return values * cosine + pltpu.roll(values, HEAD_DIM // 2, 1) * sine_table


def unit_rows(values):
    scale = lax.rsqrt(jnp.mean(values * values, axis=1, keepdims=True) + EPSILON)
    return values * scale, scale


def allowed_pairs(docs_column, docs_row):
    shape = (docs_column.shape[0], docs_row.shape[1])
    keys_at, queries_at = lax.broadcasted_iota(jnp.int32, shape, 0), lax.broadcasted_iota(jnp.int32, shape, 1)
    return (keys_at <= queries_at) & (docs_column == docs_row)


def head_span(head):
    return pl.ds(pl.multiple_of(head * HEAD_DIM, HEAD_DIM), HEAD_DIM)


def weight_copies(w_ref, w_in, w_out, w_sem, wide, last_first):
    groups = list(range(w_in.shape[1] // wide))
    if last_first:
        groups = groups[-1:] + groups[:-1]
    into = [
        (n, pltpu.make_async_copy(w_ref.at[:, pl.ds(n * wide, wide)], w_in.at[:, pl.ds(n * wide, wide)], w_sem.at[n]))
        for n in groups
    ]
    start = w_in.shape[1] + LANES
    out = [
        pltpu.make_async_copy(
            w_ref.at[:, pl.ds(start + n * wide, wide)],
            w_out.at[:, pl.ds(n * wide, wide)],
            w_sem.at[len(groups) + n],
        )
        for n in range(w_out.shape[1] // wide)
    ]
    return into, out


def dot_groups(target, left, right, begin, count, transposed, wide=256):
    def body(i, carry):
        span = pl.ds(pl.multiple_of(begin + i * wide, wide), wide)
        value = dot_nt(left[...], right[span]) if transposed else dot_nn(left[...], right[:, span])
        target[:, span] = value.astype(target.dtype)
        return carry

    lax.fori_loop(0, count // wide, body, 0)


GROUP = 512


def attend_kernel(
    q_heads, kv_heads, normed_ref, w_ref, cosine_ref, sine_ref, docs_column, docs_row, q_gain, k_gain,
    raw_ref, attended_ref, query_ref, key_ref, value_ref, totals_ref, part_ref, w_in, w_out, w_sem,
):
    into, out = weight_copies(w_ref, w_in, w_out, w_sem, GROUP, True)
    for _, copy in into:
        copy.start()
    for copy in out:
        copy.start()
    for n, copy in into:
        copy.wait()
        dot_groups(raw_ref, normed_ref, w_in, n * GROUP, GROUP, False)
    cosine, sine_table = cosine_ref[...], sine_ref[...]
    allowed = allowed_pairs(docs_column[...], docs_row[...])
    group, inv_root = q_heads // kv_heads, 1.0 / math.sqrt(HEAD_DIM)
    for kv in range(kv_heads):
        unit, _ = unit_rows(raw_ref[:, head_span(q_heads + kv)])
        key_rows = turn_lanes(unit * k_gain[...], cosine, sine_table).astype(jnp.bfloat16)
        value_rows = raw_ref[:, head_span(q_heads + kv_heads + kv)]
        key_ref[:, head_span(kv)] = key_rows
        value_ref[:, head_span(kv)] = value_rows.astype(jnp.bfloat16)
        value_columns = value_rows.T.astype(jnp.bfloat16)

        def body(index, carry, kv=kv, key_rows=key_rows, value_columns=value_columns):
            head = kv * group + index
            unit, _ = unit_rows(raw_ref[:, head_span(head)])
            query_rows = turn_lanes(unit * q_gain[...], cosine, sine_table).astype(jnp.bfloat16)
            query_ref[:, head_span(head)] = query_rows
            scores = jnp.where(allowed, dot_nt(key_rows, query_rows) * inv_root, -1e30)
            peak = jnp.max(scores, axis=0, keepdims=True)
            exps = jnp.exp(scores - peak)
            total = jnp.sum(exps, axis=0, keepdims=True)
            totals_ref[pl.ds(head, 1), :] = peak + jnp.log(total)
            probs = (exps / total).astype(jnp.bfloat16)
            attended_ref[:, head_span(head)] = dot_nn(value_columns, probs).T.astype(jnp.bfloat16)
            return carry

        lax.fori_loop(0, group, body, 0, unroll=2)
    for copy in out:
        copy.wait()
    dot_groups(part_ref, attended_ref, w_out, 0, w_out.shape[0], True)


def attend_back_kernel(
    q_heads, kv_heads, grad_attn_ref, w_ref, cosine_ref, sine_ref, docs_column, docs_row, q_gain, k_gain,
    raw_ref, query_ref, key_ref, value_ref, totals_ref,
    grad_raw_ref, gains_ref, part_ref, grad_ref, sums_ref, w_in, w_out, w_sem,
):
    into, out = weight_copies(w_ref, w_in, w_out, w_sem, GROUP, False)
    for copy in out:
        copy.start()
    for _, copy in into:
        copy.start()
    for n, copy in enumerate(out):
        copy.wait()
        dot_groups(grad_ref, grad_attn_ref, w_out, n * GROUP, GROUP, False)
    cosine, sine_table = cosine_ref[...], sine_ref[...]
    allowed = allowed_pairs(docs_column[...], docs_row[...])
    group, inv_root = q_heads // kv_heads, 1.0 / math.sqrt(HEAD_DIM)
    gains_ref[...] = jnp.zeros_like(gains_ref)

    def back_to_raw(grad, head, gain, gain_row):
        grad = turn_lanes(grad, cosine, -sine_table)
        unit, scale = unit_rows(raw_ref[:, head_span(head)])
        gains_ref[pl.ds(gain_row, 1), :] += jnp.sum(grad * unit, axis=0, keepdims=True)
        grad = grad * gain
        grad = scale * (grad - unit * jnp.mean(grad * unit, axis=1, keepdims=True))
        grad_raw_ref[:, head_span(head)] = grad.astype(jnp.bfloat16)

    for kv in range(kv_heads):
        key_rows, value_rows = key_ref[:, head_span(kv)], value_ref[:, head_span(kv)]
        key_columns = key_rows.astype(jnp.float32).T.astype(jnp.bfloat16)
        sums_ref[...] = jnp.zeros_like(sums_ref)

        def body(index, carry, kv=kv, key_rows=key_rows, value_rows=value_rows, key_columns=key_columns):
            head = kv * group + index
            query_rows, grad_rows = query_ref[:, head_span(head)], grad_ref[:, head_span(head)]
            scores = jnp.where(allowed, dot_nt(key_rows, query_rows) * inv_root, -1e30)
            probs = jnp.exp(scores - totals_ref[pl.ds(head, 1), :])
            sums_ref[0] += dot_nn(probs.astype(jnp.bfloat16), grad_rows)
            grad_probs = dot_nt(value_rows, grad_rows)
            inner = jnp.sum(probs * grad_probs, axis=0, keepdims=True)
            grad_scores = (probs * (grad_probs - inner)).astype(jnp.bfloat16)
            sums_ref[1] += dot_nn(grad_scores, query_rows)
            grad_queries = dot_nn(key_columns, grad_scores).T * inv_root
            back_to_raw(grad_queries, head, q_gain[...], 0)
            return carry

        lax.fori_loop(0, group, body, 0, unroll=2)
        back_to_raw(sums_ref[1] * inv_root, q_heads + kv, k_gain[...], 1)
        grad_raw_ref[:, head_span(q_heads + kv_heads + kv)] = sums_ref[0].astype(jnp.bfloat16)
    for _, copy in into:
        copy.wait()
    dot_groups(part_ref, grad_raw_ref, w_in, 0, w_in.shape[0], True)


def attention_shared(weights_all, doc_ids, query_norm_gain, k_gain):
    length = doc_ids.shape[1]
    cosine, sine_table = rotary_tables(length, HEAD_DIM)
    cosine, sine_table = cosine[:, 0], sine_table[:, 0]
    return (
        weights_all,
        jnp.concatenate([cosine, cosine], axis=1),
        jnp.concatenate([-sine_table, sine_table], axis=1),
        doc_ids.reshape(length, 1),
        doc_ids.reshape(1, length),
        query_norm_gain.reshape(1, HEAD_DIM),
        k_gain.reshape(1, HEAD_DIM),
    )


def attention_specs(q_heads, kv_heads, features, inputs):
    vmem, everywhere = pl.BlockSpec(memory_space=pltpu.VMEM), pl.BlockSpec(memory_space=pl.ANY)
    wide, out_wide = (q_heads + 2 * kv_heads) * HEAD_DIM, q_heads * HEAD_DIM
    scratch = [
        pltpu.VMEM((features, wide), jnp.bfloat16),
        pltpu.VMEM((features, out_wide), jnp.bfloat16),
        pltpu.SemaphoreType.DMA(((wide + out_wide) // GROUP,)),
    ]
    return [vmem, everywhere] + [vmem] * (inputs - 2), scratch


def attend(normed, shared, q_heads, kv_heads):
    (length, features), low, shape = normed.shape, jnp.bfloat16, jax.ShapeDtypeStruct
    in_specs, scratch = attention_specs(q_heads, kv_heads, features, 1 + len(shared))
    return pl.pallas_call(
        functools.partial(attend_kernel, q_heads, kv_heads),
        out_shape=[
            shape((length, (q_heads + 2 * kv_heads) * HEAD_DIM), jnp.float32),
            shape((length, q_heads * HEAD_DIM), low),
            shape((length, q_heads * HEAD_DIM), low),
            shape((length, kv_heads * HEAD_DIM), low),
            shape((length, kv_heads * HEAD_DIM), low),
            shape((q_heads, length), jnp.float32),
            shape((length, features), jnp.float32),
        ],
        in_specs=in_specs,
        scratch_shapes=scratch,
        compiler_params=pltpu.CompilerParams(vmem_limit_bytes=48 * 1024 * 1024),
    )(normed, *shared)


def attend_back(grad_attn, shared, kept, q_heads, kv_heads):
    (length, features), shape = grad_attn.shape, jax.ShapeDtypeStruct
    in_specs, scratch = attention_specs(q_heads, kv_heads, features, 1 + len(shared) + len(kept))
    return pl.pallas_call(
        functools.partial(attend_back_kernel, q_heads, kv_heads),
        out_shape=[
            shape((length, (q_heads + 2 * kv_heads) * HEAD_DIM), jnp.bfloat16),
            shape((8, HEAD_DIM), jnp.float32),
            shape((length, features), jnp.float32),
        ],
        in_specs=in_specs,
        scratch_shapes=[
            pltpu.VMEM((length, q_heads * HEAD_DIM), jnp.bfloat16),
            pltpu.VMEM((2, length, HEAD_DIM), jnp.float32),
            *scratch,
        ],
        compiler_params=pltpu.CompilerParams(vmem_limit_bytes=48 * 1024 * 1024),
    )(grad_attn, *shared, *kept)


def on_device(
    tokens_in,
    doc_ids,
    routes,
    q_weight,
    key_matrix,
    value_matrix,
    out_weight,
    router_weight,
    attn_gain,
    ffn_gain,
    query_norm_gain,
    k_gain,
    gate_weight,
    up_weight,
    down_weight,
    cotangent,
):
    sequence_length = tokens_in.shape[0]
    model_width = tokens_in.shape[1]
    devices_gx = lax.axis_size("gx")
    devices_gy = lax.axis_size("gy")
    part_width = model_width // devices_gy
    experts_all = router_weight.shape[1]
    router_lanes = jnp.pad(router_weight, ((0, 0), (0, LANES - experts_all)))
    rows_local = jnp.concatenate([q_weight, key_matrix, value_matrix, router_lanes, out_weight], axis=1)
    dense = kernels_fit() and experts_all <= 2 * TOP
    if dense:
        (weights_all,) = gather_blocks([rows_local], (0,), 1)
        weights_all = weights_all.reshape(-1, rows_local.shape[1])
    else:
        weights_all = lax.all_gather(rows_local, "gx", axis=0, tiled=True)
    q_width, kv_width = q_weight.shape[1], key_matrix.shape[1]
    qkv_width = q_width + 2 * kv_width
    router_full = weights_all[:, qkv_width : qkv_width + experts_all]
    heads_local = q_width // HEAD_DIM
    kv_local = kv_width // HEAD_DIM
    inputs_f = tokens_in.astype(jnp.float32)
    scale_one = root_mean_scale(inputs_f)
    unit_one = inputs_f * scale_one
    normalized_input = (unit_one * attn_gain).astype(jnp.bfloat16)
    shared = attention_shared(weights_all, doc_ids, query_norm_gain, k_gain)
    raw_rows, attended, *kept, attn_part = attend(normalized_input, shared, heads_local, kv_local)
    attn_total = attn_part + swap_cores(attn_part)
    residual = inputs_f + attn_total
    scale_two = root_mean_scale(residual)
    unit_two = residual * scale_two
    normed_ffn = (unit_two * ffn_gain).astype(jnp.bfloat16)
    logits = jnp.dot(normed_ffn, router_full, preferred_element_type=jnp.float32)
    expert_iota = jnp.arange(experts_all, dtype=jnp.int32)
    route_hits = routes[:, :, None] == expert_iota
    if dense:
        mixed_rows, grad_rows_sum, grad_logits, expert_grads = dense_experts(
            normed_ffn, logits, route_hits, cotangent, gate_weight[0], up_weight[0], down_weight[0]
        )
    else:
        mixed_rows, grad_rows_sum, grad_logits, expert_grads = sparse_experts(
            normed_ffn, logits, route_hits, routes, cotangent, gate_weight[0], up_weight[0], down_weight[0]
        )
    output = (residual + mixed_rows).astype(jnp.bfloat16)
    grad_out_f = cotangent.astype(jnp.float32)
    router_term = contract(normed_ffn, grad_logits, 0, 0)
    grad_ffn_in = contract(grad_logits, router_full, 1, 1) + grad_rows_sum
    ffn_gain_term = jnp.sum(grad_ffn_in * unit_two, axis=0)
    grad_residual = grad_out_f + norm_back(grad_ffn_in * ffn_gain, unit_two, scale_two)
    grad_attn = grad_residual.astype(jnp.bfloat16)
    grad_qkv, head_gains, grad_normed_part = attend_back(
        grad_attn, shared, (raw_rows, *kept), heads_local, kv_local
    )
    q_gain_term, k_gain_term = head_gains[0], head_gains[1]
    grad_normed = grad_normed_part + swap_cores(grad_normed_part)
    attn_gain_term = jnp.sum(grad_normed * unit_one, axis=0)
    own_mask = (jnp.arange(model_width) // part_width == lax.axis_index("gy")).astype(jnp.float32)
    gains = (attn_gain_term * own_mask, ffn_gain_term * own_mask, q_gain_term, k_gain_term)
    router_lanes = jnp.pad(router_term, ((0, 0), (0, LANES - experts_all)))
    if dense:
        router_blocks = router_lanes.astype(jnp.bfloat16).reshape(devices_gx, -1, LANES)
        factors = (normalized_input, grad_qkv, router_blocks, grad_attn, attended)
        lasts = (tokens_in, grad_residual, grad_normed, attn_gain.reshape(1, model_width))
        grad_q, grad_k, grad_v, grad_router, grad_out, gain_rows, grad_input = scatter_sums(
            factors, packed_gains(gains), lasts, kv_width, 4
        )
        gains = unpacked_gains(gain_rows, gains)
    else:
        sums = jnp.concatenate(
            [
                lax.psum_scatter(term, "gx", scatter_dimension=0, tiled=True)
                for term in (
                    contract(normalized_input, grad_qkv, 0, 0),
                    router_lanes,
                    contract(grad_attn, attended, 0, 0),
                )
            ],
            axis=1,
        )
        gains = lax.psum(gains, ("gx", "gy"))
        grad_q = sums[:, :q_width]
        grad_k = sums[:, q_width : q_width + kv_width]
        grad_v = sums[:, q_width + kv_width : qkv_width]
        grad_router = sums[:, qkv_width : qkv_width + LANES]
        grad_out = sums[:, qkv_width + LANES :]
        grad_input = grad_residual + norm_back(grad_normed * attn_gain, unit_one, scale_one)
        grad_input = grad_input.astype(jnp.bfloat16)
    gain_attn, gain_ffn, gain_query, gain_key = gains
    grad_router = grad_router[:, :experts_all]
    return (
        output,
        grad_input,
        grad_q,
        grad_k,
        grad_v,
        grad_out,
        grad_router,
        gain_attn,
        gain_ffn,
        gain_query,
        gain_key,
        expert_grads[0],
        expert_grads[1],
        expert_grads[2],
    )


def solution(mesh):
    return jax.shard_map(
        on_device,
        mesh=mesh,
        in_specs=(
            P("gx", None),
            P("gx", None),
            P("gx", None),
            P("gx", "gy"),
            P("gx", "gy"),
            P("gx", "gy"),
            P("gx", "gy"),
            P("gx", None),
            P(),
            P(),
            P(),
            P(),
            P("gx", None, "gy"),
            P("gx", None, "gy"),
            P("gx", "gy", None),
            P("gx", None),
        ),
        out_specs=(
            P("gx", None),
            P("gx", None),
            P("gx", "gy"),
            P("gx", "gy"),
            P("gx", "gy"),
            P("gx", "gy"),
            P("gx", None),
            P(),
            P(),
            P(),
            P(),
            P("gx", None, "gy"),
            P("gx", None, "gy"),
            P("gx", "gy", None),
        ),
        check_vma=False,
    )
```

```python
import functools
import math

import jax
import jax.numpy as jnp
from jax import lax
from jax.experimental import pallas as pl
from jax.experimental.pallas import tpu as pltpu
from jax.sharding import PartitionSpec as P

QUERY_HEADS = 32
KEY_VALUE_HEADS = 4
HEAD_DIM = 128
LANES = 128
TOP = 8


EPSILON = 1e-06
THETA = 1000000.0


def root_mean_scale(values):
    return lax.rsqrt(jnp.mean(values * values, axis=-1, keepdims=True) + EPSILON)


def rotary_tables(sequence_length, head_width):
    half_width = head_width // 2
    frequencies = THETA ** (-(2.0 * jnp.arange(half_width, dtype=jnp.float32)) / head_width)
    angles = jnp.arange(sequence_length, dtype=jnp.float32)[:, None] * frequencies[None, :]
    return (jnp.cos(angles)[:, None, :], jnp.sin(angles)[:, None, :])


def norm_back(grad_normed, normed_unit, scale_rows):
    return scale_rows * (
        grad_normed - normed_unit * jnp.mean(grad_normed * normed_unit, axis=-1, keepdims=True)
    )


def contract(first_op, second_op, first_dim, second_dim):
    return lax.dot_general(
        first_op,
        second_op,
        (((first_dim,), (second_dim,)), ((), ())),
        preferred_element_type=jnp.float32,
    )


MESH = pl.DeviceIdType.MESH
LEVELS = 4
PLANE = 4


def cut_rows(rows):
    near, far = 3 * rows // 4, rows // 4
    return (
        (0, near),
        ((0, near // 2), (near // 2, near // 2)),
        (near, far),
        ((near, far // 2), (near + far // 2, far // 2)),
    )


def neighbours():
    me, core = lax.axis_index("gx"), lax.axis_index("gy")
    level = me // PLANE
    x_side = me + 1 - 2 * (me % 2)
    y_side = me + 2 - 4 * ((me // 2) % 2)
    return me, core, level, x_side, y_side


def greet(level, targets, with_core, me, core):
    barrier = pltpu.get_barrier_semaphore()

    def hello(device):
        pl.semaphore_signal(barrier, inc=1, device_id=device, device_id_type=MESH)

    for target in targets:
        hello((target, core))
    if with_core:
        hello((me, 1 - core))

    @pl.when(level > 0)
    def _():
        hello((me - PLANE, core))

    @pl.when(level < LEVELS - 1)
    def _():
        hello((me + PLANE, core))

    inner = jnp.where(level > 0, 1, 0) + jnp.where(level < LEVELS - 1, 1, 0)
    pl.semaphore_wait(barrier, len(targets) + int(with_core) + inner)


def when(condition, action):
    if condition is None:
        action()
    else:
        pl.when(condition)(action)


def gather_kernel(count, with_pair, *refs):
    paired = sum(with_pair)
    ins, outs, pairs = refs[:count], refs[count : 2 * count], list(refs[2 * count : 2 * count + paired])
    pairs = [pairs.pop(0) if wanted else None for wanted in with_pair]
    sems = refs[2 * count + paired :]
    steps = gather_steps(ins, outs, pairs, sems)
    for step in steps.order:
        step()
    steps.end()


class gather_steps:
    def __init__(self, ins, outs, pairs, sems):
        self.ins, self.outs, self.pairs = ins, outs, pairs
        self.send_sem, self.recv_sem, self.local_sem, self.pair_send, self.pair_recv = sems
        self.me, self.core, self.level, self.x_side, self.y_side = neighbours()
        self.diagonal = self.x_side + self.y_side - self.me
        self.spans = cut_rows(ins[0].shape[0])
        self.has_up, self.has_down = self.level < LEVELS - 1, self.level > 0
        self.up, self.down = (self.me + PLANE, self.core), (self.me - PLANE, self.core)
        self.to_x, self.to_y = (self.x_side, self.core), (self.y_side, self.core)
        self.sent, self.mirrored, self.everyone = [], [], range(len(ins))
        for k in self.everyone:
            self.own_copy(k).start()
        greet(self.level, (self.x_side, self.y_side), any(p is not None for p in pairs), self.me, self.core)
        self.order = [
            self.start,
            self.side_small,
            lambda: self.column(1),
            lambda: self.cross(0),
            lambda: self.column(2),
            self.start_planes,
            lambda: self.cross(1),
            lambda: self.column(3),
            lambda: self.planes(1),
            lambda: self.cross(2),
            lambda: self.planes(2),
            lambda: self.cross(3),
            lambda: self.planes(3),
            lambda: [self.halves(step) for step in range(LEVELS)],
        ]

    def send(self, condition, k, slot, source, first, number, span, target):
        def copy():
            there = self.outs[k].at[pl.ds(first, number), pl.ds(*span)]
            here = there
            if source == "own":
                here, there = self.ins[k].at[pl.ds(*span)], self.outs[k].at[first, pl.ds(*span)]
            return pltpu.make_async_remote_copy(
                here,
                there,
                self.send_sem.at[k, slot],
                self.recv_sem.at[k, slot],
                device_id=target,
                device_id_type=MESH,
            )

        when(condition, lambda: copy().start())
        self.sent.append((condition, copy))

    def mirror(self, condition, k, first, number, span, group):
        if self.pairs[k] is None:
            return
        slot = len(self.mirrored)

        def copy():
            return pltpu.make_async_remote_copy(
                self.outs[k].at[pl.ds(first, number), pl.ds(*span)],
                self.pairs[k].at[pl.ds(first, number), pl.ds(*span)],
                self.pair_send.at[slot],
                self.pair_recv.at[slot],
                device_id=(self.me, 1 - self.core),
                device_id_type=MESH,
            )

        when(condition, lambda: copy().start())
        self.mirrored.append((condition, copy, group))

    def arrive(self, condition, k, slot, first, number, span, group):
        place = self.outs[k].at[pl.ds(first, number), pl.ds(*span)]

        def wait():
            pltpu.make_async_remote_copy(
                place,
                place,
                self.send_sem.at[k, slot],
                self.recv_sem.at[k, slot],
                device_id=self.to_x,
                device_id_type=MESH,
            ).wait_recv()

        when(condition, wait)
        self.mirror(condition, k, first, number, span, group)

    def members(self, step):
        if step == 0:
            return [(None, 0, 0)]
        return [(self.level >= step, step, -step), (self.level + step < LEVELS, 3 + step, step)]

    def slot_of(self, group, index):
        return 6 + 7 * group + index

    last = 6 + 28

    def own_copy(self, k):
        return pltpu.make_async_copy(self.ins[k], self.outs[k].at[self.me], self.local_sem.at[k])

    def start(self):
        whole_a, half_a, whole_b, half_b = self.spans
        last, me = self.last, self.me
        for k in self.everyone:
            self.send(None, k, last, "own", me, 1, whole_b, self.to_x)
            self.send(None, k, last + 1, "own", me, 1, whole_b, self.to_y)
            self.send(self.has_up, k, 0, "own", me, 1, whole_a, self.up)
            self.send(self.has_down, k, 3, "own", me, 1, whole_a, self.down)
            self.send(None, k, self.slot_of(0, 0), "own", me, 1, whole_a, self.to_x)
            self.send(None, k, self.slot_of(1, 0), "own", me, 1, whole_a, self.to_y)

    def side_small(self):
        whole_a, half_a, whole_b, half_b = self.spans
        last = self.last
        for k in self.everyone:
            self.arrive(None, k, last, self.x_side, 1, whole_b, (0, 1))
            self.send(None, k, last + 3, "out", self.x_side, 1, half_b[1], self.to_y)
            self.arrive(None, k, last + 1, self.y_side, 1, whole_b, (0, 1))
            self.send(None, k, last + 2, "out", self.y_side, 1, half_b[0], self.to_x)
        for k in self.everyone:
            self.own_copy(k).wait()
            self.mirror(None, k, self.me, 1, (0, self.ins[k].shape[0]), (0, 0))
            self.arrive(None, k, last + 2, self.diagonal, 1, half_b[0], (0, 1))
            self.arrive(None, k, last + 3, self.diagonal, 1, half_b[1], (0, 1))

    def start_planes(self):
        whole_b = self.spans[2]
        for k in self.everyone:
            self.send(self.has_up, k, self.last + 4, "out", PLANE * self.level, PLANE, whole_b, self.up)
            self.send(self.has_down, k, self.last + 7, "out", PLANE * self.level, PLANE, whole_b, self.down)

    def cross(self, step):
        whole_a, half_a = self.spans[:2]
        for k in self.everyone:
            for condition, index, distance in self.members(step):
                first = self.x_side + PLANE * distance
                self.arrive(condition, k, self.slot_of(0, index), first, 1, whole_a, (distance, 0))
                self.send(condition, k, self.slot_of(3, index), "out", first, 1, half_a[1], self.to_y)
                first = self.y_side + PLANE * distance
                self.arrive(condition, k, self.slot_of(1, index), first, 1, whole_a, (distance, 0))
                self.send(condition, k, self.slot_of(2, index), "out", first, 1, half_a[0], self.to_x)

    def halves(self, step):
        half_a = self.spans[1]
        for k in self.everyone:
            for condition, index, distance in self.members(step):
                first = self.diagonal + PLANE * distance
                self.arrive(condition, k, self.slot_of(2, index), first, 1, half_a[0], (distance, 0))
                self.arrive(condition, k, self.slot_of(3, index), first, 1, half_a[1], (distance, 0))

    def column(self, step):
        whole_a = self.spans[0]
        for k in self.everyone:
            for condition, index, distance in self.members(step):
                first = self.me + PLANE * distance
                rising = distance < 0
                self.arrive(condition, k, step - 1 if rising else 2 + step, first, 1, whole_a, (distance, 0))
                if step < LEVELS - 1:
                    onward = condition & (self.has_up if rising else self.has_down)
                    slot = step if rising else 3 + step
                    self.send(onward, k, slot, "out", first, 1, whole_a, self.up if rising else self.down)
                self.send(condition, k, self.slot_of(0, index), "out", first, 1, whole_a, self.to_x)
                self.send(condition, k, self.slot_of(1, index), "out", first, 1, whole_a, self.to_y)

    def planes(self, step):
        whole_b = self.spans[2]
        for k in self.everyone:
            for condition, index, distance in self.members(step):
                first = PLANE * (self.level + distance)
                rising = distance < 0
                slot = self.last + (3 if rising else 6) + step
                self.arrive(condition, k, slot, first, PLANE, whole_b, (distance, 1))
                if step < LEVELS - 1:
                    onward = condition & (self.has_up if rising else self.has_down)
                    slot = self.last + (4 if rising else 7) + step
                    self.send(onward, k, slot, "out", first, PLANE, whole_b, self.up if rising else self.down)

    def paired_level(self, distance, parts):
        for condition, copy, group in self.mirrored:
            if group[0] == distance and group[1] in parts:
                when(condition, lambda copy=copy: copy().wait_recv())

    def end(self, levels_waited=False):
        for condition, copy in self.sent:
            when(condition, lambda copy=copy: copy().wait_send())
        for condition, copy, group in self.mirrored:
            when(condition, lambda copy=copy: copy().wait_send())
            if not levels_waited:
                when(condition, lambda copy=copy: copy().wait_recv())


GATHER_SLOTS = 6 + 28 + 10


def gather_semaphores(count, paired):
    dma = pltpu.SemaphoreType.DMA
    slots = (count, GATHER_SLOTS)
    pair_slots = (max(1, paired * (GATHER_SLOTS + 1)),)
    return [dma(slots), dma(slots), dma((count,)), dma(pair_slots), dma(pair_slots)]


def gather_blocks(arrays, with_pair, collective_id):
    count, blocks, paired = len(arrays), lax.axis_size("gx"), sum(with_pair)
    shapes = [jax.ShapeDtypeStruct((blocks, *a.shape), a.dtype) for a in arrays]
    shapes += [shape for shape, wanted in zip(shapes, with_pair) if wanted]
    return pl.pallas_call(
        functools.partial(gather_kernel, count, with_pair),
        out_shape=shapes,
        in_specs=[pl.BlockSpec(memory_space=pl.ANY)] * count,
        out_specs=[pl.BlockSpec(memory_space=pl.ANY)] * len(shapes),
        scratch_shapes=gather_semaphores(count, paired),
        compiler_params=pltpu.CompilerParams(collective_id=collective_id, has_side_effects=True),
    )(*arrays)


def dot_nn(left, right):
    return lax.dot_general(left, right, (((1,), (0,)), ((), ())), preferred_element_type=jnp.float32)


def dot_nt(left, right):
    return lax.dot_general(left, right, (((1,), (1,)), ((), ())), preferred_element_type=jnp.float32)


def experts_kernel(experts_all, *refs):
    rows_ref, grad_rows_ref, w_gate, w_up, w_down = refs[:5]
    weighted_out, grad_in_out, terms_out, gate_out, up_out, down_out, grads_own, grads_pair = refs[5:13]
    held, grads, w_in, left_in, left_down, weighted_ref, grad_in_ref, terms_ref = refs[13:21]
    sums_in, sums_down, turned, down_low, grad_sem, part_sem, w_sem, out_sem, sum_sem = refs[21:30]
    hidden, width = w_down.shape
    joins = [
        pltpu.make_async_copy(part, w_in.at[:, pl.ds(i * hidden, hidden)], w_sem.at[i])
        for i, part in enumerate((w_gate, w_up))
    ]
    for join in joins:
        join.start()
    rows = rows_ref.shape[0]
    grad_half = grad_rows_ref.at[pl.ds(pl.multiple_of(lax.axis_index("gy") * rows, rows), rows)]
    steps = gather_steps([rows_ref, grad_half], [held.at[0], grads_own], [held.at[1], grads_pair], refs[30:])
    level, core = steps.level, steps.core
    tiles = hidden // LANES
    visits = [
        level,
        jnp.where(level == 0, 1, level - 1),
        jnp.where(level == 0, 2, jnp.where(level == 3, 1, level + 1)),
        jnp.where(level < 2, 3, 0),
    ]

    def fetch(turn, half):
        return pltpu.make_async_copy(
            (grads_own, grads_pair)[half].at[pl.ds(PLANE * visits[turn], PLANE)],
            grads.at[turn % 2, half],
            grad_sem.at[turn % 2, half],
        )

    part_rows = {None: (0, rows), 0: steps.spans[0], 1: steps.spans[2]}

    def fetch_part(part, half):
        span = pl.ds(*part_rows[part])
        return pltpu.make_async_copy(
            (grads_own, grads_pair)[half].at[pl.ds(PLANE * visits[-1], PLANE), span],
            grads.at[(LEVELS - 1) % 2, half, :, span],
            part_sem.at[part, half],
        )

    def fetches(turn, part):
        return [fetch(turn, half) if part is None else fetch_part(part, half) for half in range(2)]

    lane = lax.broadcasted_iota(jnp.int32, (1, LANES), 1)
    expert = steps.me
    gate_pick = (((lane == expert) | (lane == experts_all + expert))).astype(jnp.float32)
    high_lane = (lane == 2 * experts_all * core + expert).astype(jnp.float32)
    low_lane = (lane == 2 * experts_all * core + experts_all + expert).astype(jnp.float32)

    def leave(turn):
        span = pl.ds(PLANE * visits[turn], PLANE)
        pairs = ((weighted_ref, weighted_out), (grad_in_ref, grad_in_out), (terms_ref, terms_out))
        return [
            pltpu.make_async_copy(here.at[:, span], there.at[:, span], out_sem.at[turn, i])
            for i, (here, there) in enumerate(pairs)
        ]

    def forward(turn, begin=0, end=4, part=None):
        first, (row, number) = PLANE * visits[turn], part_rows[part]
        together = 2 if part is None else PLANE
        group, per_half, span_rows = together * number, PLANE // together, pl.ds(row, number)
        if begin == 0:
            for copy in fetches(turn, part):
                copy.wait()

        def body(step, carry):
            half, pair = step // per_half, step % per_half
            at = first + together * pair
            blocks = pl.ds(at, together)
            lanes = held[half, blocks, span_rows, pl.ds(width, LANES)].reshape(group, LANES)
            gate_rows = jnp.sum(lanes.astype(jnp.float32) * gate_pick, axis=1, keepdims=True)
            grad_rows = grads[turn % 2, half, pl.ds(together * pair, together), span_rows].reshape(group, width)
            token_rows = held[half, blocks, span_rows, pl.ds(0, width)].reshape(group, width)
            grad_hidden = dot_nt(grad_rows, w_down[...])
            both = dot_nn(token_rows, w_in[...])
            terms = jnp.zeros((group, 1), jnp.float32)
            column = pl.multiple_of(2 * PLANE * row + step * group, LANES)
            for j in range(tiles):
                gate_in = both[:, j * LANES : (j + 1) * LANES]
                up_in = both[:, hidden + j * LANES : hidden + (j + 1) * LANES]
                back = grad_hidden[:, j * LANES : (j + 1) * LANES]
                gate_sigmoid = 1.0 / (1.0 + jnp.exp(-gate_in))
                gate_swish = gate_in * gate_sigmoid
                activated = gate_swish * up_in
                terms = terms + jnp.sum(activated * back, axis=1, keepdims=True)
                grad_act = gate_rows * back
                weighted = gate_rows * activated
                grad_gate = grad_act * up_in * gate_sigmoid * (1.0 + gate_in * (1.0 - gate_sigmoid))
                grad_up = grad_act * gate_swish
                for value, array, tile, left in (
                    (weighted, weighted_ref, j, left_down),
                    (grad_gate, grad_in_ref, j, left_in),
                    (grad_up, grad_in_ref, tiles + j, left_in),
                ):
                    span = pl.ds(tile * LANES, LANES)
                    low = value.astype(jnp.bfloat16).reshape(together, number, LANES)
                    array[half, blocks, span_rows, span] = low
                    left[span, pl.ds(column, group)] = value.T.astype(jnp.bfloat16)
            high = terms.astype(jnp.bfloat16).astype(jnp.float32)
            spread = high * high_lane + (terms - high) * low_lane
            terms_ref[half, blocks, span_rows] = spread.astype(jnp.bfloat16).reshape(together, number, LANES)
            return carry

        lax.fori_loop(begin, min(end, 2 * per_half), body, 0)
        if end == 4 and part != 0:
            for copy in leave(turn):
                copy.start()

    wide = 256

    def weights(turn, begin=0, end=8, part=None):
        first, (row, number) = PLANE * visits[turn], part_rows[part]
        span_rows, depth = pl.ds(row, number), 2 * PLANE * number
        columns = pl.ds(2 * PLANE * row, depth)

        def body(step, carry):
            span = pl.ds(pl.multiple_of(step * wide, wide), wide)
            token_rows = held[:, pl.ds(first, PLANE), span_rows, span].reshape(depth, wide)
            grad_rows = grads[turn % 2, :, :, span_rows, span].reshape(depth, wide)
            part_in = dot_nn(left_in[:, columns], token_rows)
            part_down = dot_nn(left_down[:, columns], grad_rows)
            if turn:
                part_in = sums_in[:, span] + part_in
                part_down = sums_down[:, span] + part_down
            if part != 1:
                sums_in[:, span] = part_in
                sums_down[:, span] = part_down
            else:
                for i in range(2):
                    turned[i, span] = part_in[i * hidden : (i + 1) * hidden].T.astype(jnp.bfloat16)
                down_low[:, span] = part_down.astype(jnp.bfloat16)
                for copy in leave_sums(step):
                    copy.start()
            return carry

        lax.fori_loop(begin, end, body, 0)

    def leave_sums(step):
        span = pl.ds(pl.multiple_of(step * wide, wide), wide)
        return [
            pltpu.make_async_copy(turned.at[0, span], gate_out.at[span], sum_sem.at[step, 0]),
            pltpu.make_async_copy(turned.at[1, span], up_out.at[span], sum_sem.at[step, 1]),
            pltpu.make_async_copy(down_low.at[:, span], down_out.at[:, span], sum_sem.at[step, 2]),
        ]

    def level_ready(turn, part=None):
        parts = (0, 1) if part is None else (part,)
        if turn == 0:
            steps.paired_level(0, parts)
        for distance in range(-3, 4):
            if turn and distance:
                wanted = visits[turn] == level + distance
                pl.when(wanted)(lambda distance=distance: steps.paired_level(distance, parts))
        for copy in fetches(turn, part):
            copy.start()

    steps.start()
    steps.side_small()
    steps.column(1)
    steps.cross(0)
    for join in joins:
        join.wait()
    steps.column(2)
    steps.start_planes()
    steps.halves(0)
    steps.cross(1)
    level_ready(0)
    forward(0, 0, 4)
    steps.column(3)
    steps.planes(1)
    weights(0, 0, 4)
    steps.cross(2)
    steps.halves(1)
    level_ready(1)
    weights(0, 4, 8)
    forward(1, 0, 4)
    steps.planes(2)
    weights(1, 0, 4)
    steps.cross(3)
    steps.halves(2)
    level_ready(2)
    weights(1, 4, 8)
    forward(2, 0, 4)
    steps.halves(3)
    level_ready(3, 0)
    weights(2, 0, 8)
    forward(3, part=0)
    weights(3, part=0)
    steps.planes(3)
    level_ready(3, 1)
    forward(3, part=1)
    weights(3, part=1)
    for turn in range(LEVELS):
        for copy in leave(turn):
            copy.wait()

    def last_sums(step, carry):
        for copy in leave_sums(step):
            copy.wait()
        return carry

    lax.fori_loop(0, width // wide, last_sums, 0)
    steps.end(levels_waited=True)


def experts_products(rows, grad_rows, w_gate, w_up, w_down, experts_all, collective_id):
    blocks, low, count = lax.axis_size("gx"), jnp.bfloat16, rows.shape[0]
    hidden, width = w_down.shape
    everywhere = pl.BlockSpec(memory_space=pl.ANY)
    block_shape = (2, blocks, count)
    shapes = [
        jax.ShapeDtypeStruct((*block_shape, hidden), low),
        jax.ShapeDtypeStruct((*block_shape, 2 * hidden), low),
        jax.ShapeDtypeStruct((*block_shape, LANES), low),
        jax.ShapeDtypeStruct((width, hidden), low),
        jax.ShapeDtypeStruct((width, hidden), low),
        jax.ShapeDtypeStruct((hidden, width), low),
        *[jax.ShapeDtypeStruct((blocks, count, width), low)] * 2,
    ]
    level_rows = 2 * PLANE * count
    dma = pltpu.SemaphoreType.DMA
    return pl.pallas_call(
        functools.partial(experts_kernel, experts_all),
        out_shape=shapes,
        in_specs=[everywhere] * 4 + [pl.BlockSpec(memory_space=pltpu.VMEM)],
        out_specs=[everywhere] * 8,
        scratch_shapes=[
            pltpu.VMEM((*block_shape, rows.shape[1]), low),
            pltpu.VMEM((2, 2, PLANE, count, width), low),
            pltpu.VMEM((width, 2 * hidden), low),
            pltpu.VMEM((2 * hidden, level_rows), low),
            pltpu.VMEM((hidden, level_rows), low),
            *[pltpu.VMEM(shape.shape, low) for shape in shapes[:3]],
            pltpu.VMEM((2 * hidden, width), jnp.float32),
            pltpu.VMEM((hidden, width), jnp.float32),
            pltpu.VMEM((2, width, hidden), low),
            pltpu.VMEM((hidden, width), low),
            dma((2, 2)),
            dma((2, 2)),
            dma((2,)),
            dma((LEVELS, 3)),
            dma((width // 256, 3)),
            *gather_semaphores(2, 2),
        ],
        compiler_params=pltpu.CompilerParams(
            collective_id=collective_id, has_side_effects=True, vmem_limit_bytes=63 * 1024 * 1024
        ),
    )(rows, grad_rows, w_gate, w_up, w_down)[:6]


class scatter_moves:
    def __init__(self, held, out):
        self.mine, self.half_y, self.half_x, self.full_x, self.full_y, self.slots_a, self.slots_b, self.side_b = held[:8]
        self.send_sem, self.recv_sem, self.chain_send, self.chain_recv = held[8:12]
        self.out = out
        self.me, self.core, level, x_side, y_side = neighbours()
        self.level = level
        self.up, self.down = (self.me + PLANE, self.core), (self.me - PLANE, self.core)
        self.to_x, self.to_y = (x_side, self.core), (y_side, self.core)
        self.x_at, self.y_at, self.own_at = x_side % PLANE, y_side % PLANE, self.me % PLANE
        self.diagonal_at = (x_side + y_side - self.me) % PLANE
        forward = jnp.where(level < 2, 1, 0)
        self.order = [3 * forward, 2 * forward + (1 - forward), level + 1 - 2 * (level % 2), level]
        self.rows, self.width = self.mine.shape[1:]
        self.spans = cut_rows(self.rows)
        self.sent = []

    def send(self, condition, source, target_ref, ssem, rsem, target):
        def copy():
            return pltpu.make_async_remote_copy(
                source, target_ref, ssem, rsem, device_id=target, device_id_type=MESH
            )

        when(condition, lambda: copy().start())
        self.sent.append((condition, copy))

    def arrive(self, condition, target_ref, rsem):
        def wait():
            pltpu.make_async_remote_copy(
                target_ref, target_ref, rsem, rsem, device_id=self.to_x, device_id_type=MESH
            ).wait_recv()

        when(condition, wait)

    def add(self, condition, height, target, *terms, step=16):
        def run():
            def body(i, carry):
                at = pl.multiple_of(i * step, step)
                total = target(at, step)[...].astype(jnp.float32)
                for term in terms:
                    total = total + term(at, step)[...].astype(jnp.float32)
                target(at, step)[...] = total.astype(jnp.bfloat16)
                return carry

            lax.fori_loop(0, height // step, body, 0)

        when(condition, run)

    def rows_of(self, ref, *index, start=0):
        return lambda at, step: ref.at[(*index, pl.ds(start + at, step))]

    def turn_sems(self, turn):
        return [(self.send_sem.at[6 * turn + i], self.recv_sem.at[6 * turn + i]) for i in range(6)]

    def half_spans(self):
        half_a = self.spans[1]
        return half_a[0][1], pl.ds(*half_a[0]), pl.ds(*half_a[1])

    def first(self, turn):
        base, at = PLANE * self.order[turn], self.turn_sems(turn)
        _, lower, upper = self.half_spans()
        mine, to_x, to_y = self.mine, self.to_x, self.to_y
        self.send(None, mine.at[base + self.diagonal_at, lower], self.half_y.at[turn], *at[0], to_y)
        self.send(None, mine.at[base + self.diagonal_at, upper], self.half_x.at[turn], *at[1], to_x)
        self.send(None, mine.at[base + self.x_at, upper], self.full_x.at[turn, upper], *at[2], to_x)
        self.send(None, mine.at[base + self.y_at, lower], self.full_y.at[turn, lower], *at[3], to_y)

    def second(self, turn):
        base, at = PLANE * self.order[turn], self.turn_sems(turn)
        height, lower, upper = self.half_spans()
        mine, rows_of = self.mine, self.rows_of
        self.arrive(None, self.half_y.at[turn], at[0][1])
        self.add(None, height, rows_of(mine, base + self.x_at), rows_of(self.half_y, turn))
        self.send(None, mine.at[base + self.x_at, lower], self.full_x.at[turn, lower], *at[4], self.to_x)
        self.arrive(None, self.half_x.at[turn], at[1][1])
        self.add(None, height, rows_of(mine, base + self.y_at, start=height), rows_of(self.half_x, turn))
        self.send(None, mine.at[base + self.y_at, upper], self.full_y.at[turn, upper], *at[5], self.to_y)

    def chain(self, which, turn, block, slots, spread):
        to_level, level = self.order[turn], self.level
        rising, falling = to_level > level, to_level < level
        begins = (rising & (level == 0)) | (falling & (level == LEVELS - 1))
        middle = (rising | falling) & jnp.logical_not(begins)
        self.arrive(middle, slots.at[to_level], self.chain_recv.at[which, to_level])
        spread(middle, to_level)
        outgoing = self.chain_send.at[which, to_level]
        self.send(rising, block, slots.at[to_level], outgoing, self.chain_recv.at[which, to_level], self.up)
        at = jnp.where(to_level == level - 1, LEVELS, to_level)
        self.send(falling, block, slots.at[at], outgoing, self.chain_recv.at[which, at], self.down)

    def add_small(self, condition, base, slot):
        start, number = self.spans[2]
        for column in range(PLANE):
            self.add(
                condition,
                number,
                self.rows_of(self.mine, base + column, start=start),
                self.rows_of(self.slots_b, slot, column),
            )

    def chain_small(self, turn):
        if turn == LEVELS - 1:
            return
        base = PLANE * self.order[turn]
        block = self.mine.at[pl.ds(base, PLANE), pl.ds(*self.spans[2])]
        self.chain(1, turn, block, self.slots_b, lambda condition, slot: self.add_small(condition, base, slot))

    def plane_arrives(self, turn):
        at = self.turn_sems(turn)
        _, lower, upper = self.half_spans()
        self.arrive(None, self.full_x.at[turn, upper], at[2][1])
        self.arrive(None, self.full_y.at[turn, lower], at[3][1])
        self.arrive(None, self.full_x.at[turn, lower], at[4][1])
        self.arrive(None, self.full_y.at[turn, upper], at[5][1])

    def chain_large(self, turn):
        if turn == LEVELS - 1:
            return
        own, number = PLANE * self.order[turn] + self.own_at, self.spans[0][1]
        rows_of, mine = self.rows_of, self.mine
        self.plane_arrives(turn)
        self.add(None, number, rows_of(mine, own), rows_of(self.full_x, turn), rows_of(self.full_y, turn))
        self.chain(
            0,
            turn,
            mine.at[own, pl.ds(*self.spans[0])],
            self.slots_a,
            lambda condition, slot: self.add(condition, number, rows_of(mine, own), rows_of(self.slots_a, slot)),
        )

    def side(self):
        short = self.spans[3][0][1]
        spans = [pl.ds(0, short), pl.ds(short, short), pl.ds(2 * short, 2 * short), pl.ds(4 * short, 2 * short)]
        return [(self.side_b.at[span], self.send_sem.at[24 + i], self.recv_sem.at[24 + i]) for i, span in enumerate(spans)]

    def arrivals(self):
        return ((self.level > 0, self.level), (self.level < LEVELS - 1, LEVELS))

    def end_small(self):
        base, mine, half_b = PLANE * self.level, self.mine, self.spans[3]
        for condition, slot in self.arrivals():
            self.arrive(condition, self.slots_b.at[slot], self.chain_recv.at[1, slot])
            self.add_small(condition, base, slot)
        side = self.side()
        self.send(None, mine.at[base + self.diagonal_at, pl.ds(*half_b[0])], *side[0], self.to_y)
        self.send(None, mine.at[base + self.diagonal_at, pl.ds(*half_b[1])], *side[1], self.to_x)

    def end_sides(self):
        base, mine, rows_of = PLANE * self.level, self.mine, self.rows_of
        whole_b, half_b = self.spans[2:]
        side, short = self.side(), half_b[0][1]
        self.plane_arrives(LEVELS - 1)
        self.arrive(None, side[0][0], side[0][2])
        self.add(None, short, rows_of(mine, base + self.x_at, start=half_b[0][0]), rows_of(self.side_b))
        self.send(None, mine.at[base + self.x_at, pl.ds(*whole_b)], *side[2], self.to_x)
        self.arrive(None, side[1][0], side[1][2])
        self.add(None, short, rows_of(mine, base + self.y_at, start=half_b[1][0]), rows_of(self.side_b, start=short))
        self.send(None, mine.at[base + self.y_at, pl.ds(*whole_b)], *side[3], self.to_y)

    def end_sums(self, base):
        whole_a, half_a, whole_b, half_b = self.spans
        own, out, mine, step = PLANE * self.level + self.own_at, self.out, self.mine, 16
        full_x, full_y, slots_a, side_b = self.full_x, self.full_y, self.slots_a, self.side_b

        def place(at):
            return pl.ds(pl.multiple_of(base + at, step), step)

        def tail_a(i, carry):
            at = pl.multiple_of(i * step, step)
            span, turn = pl.ds(at, step), LEVELS - 1
            total = mine[own, span].astype(jnp.float32)
            total = total + full_x[turn, span].astype(jnp.float32) + full_y[turn, span].astype(jnp.float32)
            out[place(at)] = total
            return carry

        lax.fori_loop(0, whole_a[1] // step, tail_a, 0)
        for condition, slot in self.arrivals():
            self.arrive(condition, slots_a.at[slot], self.chain_recv.at[0, slot])

            def more(slot=slot):
                def body(i, carry):
                    at = pl.multiple_of(i * step, step)
                    out[place(at)] = out[place(at)] + slots_a[slot, pl.ds(at, step)].astype(jnp.float32)
                    return carry

                lax.fori_loop(0, whole_a[1] // step, body, 0)

            when(condition, more)
        side, short = self.side(), half_b[0][1]
        self.arrive(None, side[2][0], side[2][2])
        self.arrive(None, side[3][0], side[3][2])

        def tail_b(i, carry):
            at = pl.multiple_of(i * step, step)
            total = mine[own, pl.ds(whole_b[0] + at, step)].astype(jnp.float32)
            total = total + side_b[pl.ds(2 * short + at, step)].astype(jnp.float32)
            total = total + side_b[pl.ds(4 * short + at, step)].astype(jnp.float32)
            out[place(whole_b[0] + at)] = total
            return carry

        lax.fori_loop(0, whole_b[1] // step, tail_b, 0)

    def end_waits(self):
        for condition, copy in self.sent:
            when(condition, lambda copy=copy: copy().wait_send())


def scatter_places(blocks, rows, width):
    near, far, low, dma = 3 * rows // 4, rows // 4, jnp.bfloat16, pltpu.SemaphoreType.DMA
    shapes = [
        (blocks, rows, width),
        (LEVELS, near // 2, width),
        (LEVELS, near // 2, width),
        (LEVELS, near, width),
        (LEVELS, near, width),
        (LEVELS + 1, near, width),
        (LEVELS + 1, PLANE, far, width),
        (3 * far, width),
    ]
    return [pltpu.VMEM(shape, low) for shape in shapes] + [dma((28,)), dma((28,)), dma((2, 5)), dma((2, 5))]


PLACES = 12


def scatter_kernel(*refs):
    normed, grad_qkv, router_term, grad_attn, attended, gain_ref = refs[:6]
    tokens, grad_residual, grad_normed, attn_gain = refs[6:10]
    pieces_out, (gain_out, grad_input) = refs[10:15], refs[15:17]
    held, (out, load_sem, leave_sem, gain_slots, gain_send, gain_recv) = refs[17:-6], refs[-6:]
    moves = scatter_moves(held, out)
    me, core, level = moves.me, moves.core, moves.level
    far = me + 2 * PLANE - 4 * PLANE * (level // 2)
    partners = ((me, 1 - core), moves.to_x, moves.to_y, (me + PLANE - 2 * PLANE * (level % 2), core), (far, core))

    def gain_copy(turn):
        return pltpu.make_async_remote_copy(
            gain_slots.at[2 * turn],
            gain_slots.at[2 * turn + 1],
            gain_send.at[turn],
            gain_recv.at[turn],
            device_id=partners[turn],
            device_id_type=MESH,
        )

    def gain_step(turn):
        if turn == 0:
            gain_slots[0] = gain_ref[...]
        else:
            gain_copy(turn - 1).wait_recv()
            gain_slots[2 * turn] = gain_slots[2 * turn - 2] + gain_slots[2 * turn - 1]
        if turn < len(partners):
            gain_copy(turn).start()
        else:
            gain_out[...] = gain_slots[2 * turn]

    router_lane = grad_qkv.shape[1]

    def load(turn):
        span = pl.ds(PLANE * moves.order[turn], PLANE)
        place = moves.mine.at[span, :, pl.ds(router_lane, LANES)]
        return pltpu.make_async_copy(router_term.at[span], place, load_sem.at[turn])

    def products(turn):
        level_rows, wide = PLANE * moves.rows, 256
        span = pl.ds(PLANE * moves.order[turn], PLANE)
        features = pl.ds(pl.multiple_of(moves.order[turn] * level_rows, level_rows), level_rows)
        for left, right, lane in ((normed, grad_qkv, 0), (grad_attn, attended, router_lane + LANES)):
            left_rows = left[:, features].astype(jnp.float32).T.astype(jnp.bfloat16)

            def body(step, carry, left_rows=left_rows, right=right, lane=lane):
                at = pl.multiple_of(step * wide, wide)
                value = dot_nn(left_rows, right[:, pl.ds(at, wide)]).astype(jnp.bfloat16)
                lanes = pl.ds(pl.multiple_of(lane + at, LANES), wide)
                moves.mine[span, :, lanes] = value.reshape(PLANE, moves.rows, wide)
                return carry

            lax.fori_loop(0, right.shape[1] // wide, body, 0)

    def input_rows():
        step = 16

        def body(i, carry):
            span = pl.ds(pl.multiple_of(i * step, step), step)
            unit, scale = unit_rows(tokens[span].astype(jnp.float32))
            grad = grad_normed[span] * attn_gain[...]
            grad = scale * (grad - unit * jnp.mean(grad * unit, axis=1, keepdims=True))
            grad_input[span] = (grad_residual[span] + grad).astype(jnp.bfloat16)
            return carry

        lax.fori_loop(0, tokens.shape[0] // step, body, 0)

    def leave():
        copies, lane = [], 0
        for i, piece in enumerate(pieces_out):
            width = piece.shape[1]
            copies.append(pltpu.make_async_copy(out.at[:, pl.ds(lane, width)], piece, leave_sem.at[i]))
            lane += width
        return copies

    for turn in range(LEVELS):
        load(turn).start()
    products(0)
    greet(level, (moves.to_x[0], moves.to_y[0], far), True, me, core)
    gain_step(0)
    for turn in range(LEVELS):
        if turn:
            products(turn)
        load(turn).wait()
        moves.first(turn)
        moves.chain_small(turn)
    input_rows()
    for turn in range(LEVELS - 1):
        moves.second(turn)
        gain_step(turn + 1)
        if turn:
            moves.chain_large(turn - 1)
    moves.second(LEVELS - 1)
    gain_step(4)
    moves.chain_large(LEVELS - 2)
    moves.end_small()
    moves.end_sides()
    gain_step(5)
    moves.end_sums(0)
    for copy in leave():
        copy.start()
    for turn in range(len(partners)):
        gain_copy(turn).wait_send()
    moves.end_waits()
    for copy in leave():
        copy.wait()


def scatter_sums(factors, gains, lasts, kv_width, collective_id):
    _, grad_qkv, router_term, _, attended = factors
    blocks, rows, _ = router_term.shape
    widths = (grad_qkv.shape[1] - 2 * kv_width, kv_width, kv_width, LANES, attended.shape[1])
    dma, tokens = pltpu.SemaphoreType.DMA, lasts[0]
    vmem, everywhere = pl.BlockSpec(memory_space=pltpu.VMEM), pl.BlockSpec(memory_space=pl.ANY)
    return pl.pallas_call(
        scatter_kernel,
        out_shape=[
            *[jax.ShapeDtypeStruct((rows, width), jnp.float32) for width in widths],
            jax.ShapeDtypeStruct(gains.shape, gains.dtype),
            jax.ShapeDtypeStruct(tokens.shape, tokens.dtype),
        ],
        in_specs=[vmem, vmem, everywhere, vmem, vmem, vmem, vmem, vmem, vmem, vmem],
        out_specs=[everywhere] * 5 + [vmem] * 2,
        scratch_shapes=[
            *scatter_places(blocks, rows, sum(widths)),
            pltpu.VMEM((rows, sum(widths)), jnp.float32),
            dma((LEVELS,)),
            dma((5,)),
            pltpu.VMEM((11, *gains.shape), gains.dtype),
            dma((5,)),
            dma((5,)),
        ],
        compiler_params=pltpu.CompilerParams(
            collective_id=collective_id, has_side_effects=True, vmem_limit_bytes=63 * 1024 * 1024
        ),
    )(*factors, gains, *lasts)


def return_kernel(grad_in, weighted, terms, w_gate, w_up, w_down, back_out, mixed_out, *refs):
    streams = [
        scatter_moves(refs[:PLACES], back_out),
        scatter_moves(refs[PLACES : 2 * PLACES], mixed_out),
    ]
    sibling, away, left, right_in, right_down = refs[2 * PLACES : 2 * PLACES + 5]
    pair_send, pair_recv, left_sem, right_sem, term_sem, ready_sem, credit = refs[2 * PLACES + 5 :]
    me, core, order, rows = streams[0].me, streams[0].core, streams[0].order, streams[0].rows
    hidden, features = w_down.shape
    depths, lefts = (2 * hidden, hidden), (grad_in, weighted)
    turns, wide = 2 * LEVELS, 256
    rights = [
        pltpu.make_async_copy(w_gate, right_in.at[:, pl.ds(0, hidden)], right_sem.at[0]),
        pltpu.make_async_copy(w_up, right_in.at[:, pl.ds(hidden, hidden)], right_sem.at[1]),
        pltpu.make_async_copy(w_down, right_down, right_sem.at[2]),
    ]

    def level_span(turn):
        return pl.ds(PLANE * order[turn % LEVELS], PLANE)

    def left_copy(turn):
        stream = turn // LEVELS
        return pltpu.make_async_copy(
            lefts[stream].at[:, level_span(turn)],
            left.at[turn % 2, :, :, :, pl.ds(0, depths[stream])],
            left_sem.at[turn % 2],
        )

    def term_copy(turn, half):
        lanes = pl.ds(features, LANES)
        place = away.at[turn % 2, :, :, lanes] if half else streams[0].mine.at[level_span(turn), :, lanes]
        return pltpu.make_async_copy(terms.at[half, level_span(turn)], place, term_sem.at[half])

    def width_of(turn):
        return streams[turn // LEVELS].width

    def hand(turn):
        lanes = pl.ds(0, width_of(turn))
        return pltpu.make_async_remote_copy(
            away.at[turn % 2, :, :, lanes],
            sibling.at[turn % 2, :, :, lanes],
            pair_send.at[turn],
            pair_recv.at[turn],
            device_id=(me, 1 - core),
            device_id_type=MESH,
        )

    def product(turn, half, store):
        stream, slot = turn // LEVELS, turn % 2
        factor = left[slot, half, :, :, pl.ds(0, depths[stream])].reshape(PLANE * rows, depths[stream])

        def body(step, carry):
            span = pl.ds(pl.multiple_of(step * wide, wide), wide)
            value = dot_nt(factor, right_in[span]) if stream == 0 else dot_nn(factor, right_down[:, span])
            store(span, value.reshape(PLANE, rows, wide))
            return carry

        lax.fori_loop(0, features // wide, body, 0)

    def hand_over(turn):
        left_copy(turn).wait()
        if turn + 1 < turns:
            left_copy(turn + 1).start()
        if turn < LEVELS:
            term_copy(turn, 1).start()
            term_copy(turn, 0).start()

        def store(span, value):
            away[turn % 2, :, :, span] = value.astype(jnp.bfloat16)

        product(turn, 1, store)
        if turn < LEVELS:
            term_copy(turn, 1).wait()
            term_copy(turn, 0).wait()
        if turn == 0:
            greet(streams[0].level, (streams[0].to_x[0], streams[0].to_y[0]), True, me, core)
        if turn >= 2:
            pl.semaphore_wait(credit, 1)
        hand(turn).start()

    def settle(turn):
        hand(turn).wait()
        mine, slot = streams[turn // LEVELS].mine, turn % 2

        def store(span, value):
            value = value + sibling[slot, :, :, span].astype(jnp.float32)
            mine[level_span(turn), :, span] = value.astype(jnp.bfloat16)

        product(turn, 0, store)
        if turn < LEVELS:
            lanes = pl.ds(features, LANES)
            value = mine[level_span(turn), :, lanes].astype(jnp.float32)
            value = value + sibling[slot, :, :, lanes].astype(jnp.float32)
            mine[level_span(turn), :, lanes] = value.astype(jnp.bfloat16)
        if turn + 2 < turns:
            pl.semaphore_signal(credit, inc=1, device_id=(me, 1 - core), device_id_type=MESH)

    def exchange(stream, core_of_rows):
        out = streams[stream].out
        span = pl.ds(pl.multiple_of(core_of_rows * rows, rows), rows)
        return pltpu.make_async_remote_copy(
            out.at[span],
            out.at[span],
            ready_sem.at[stream, 0],
            ready_sem.at[stream, 1],
            device_id=(me, 1 - core),
            device_id_type=MESH,
        )

    def end(stream):
        streams[stream].end_sums(core * rows)
        exchange(stream, core).start()

    left_copy(0).start()
    for copy in rights:
        copy.start()
    for copy in rights:
        copy.wait()
    hand_over(0)
    for turn in range(turns + 2):
        if turn < turns:
            stream = streams[turn // LEVELS]
            settle(turn)
            stream.first(turn % LEVELS)
            if turn + 1 < turns:
                hand_over(turn + 1)
            stream.chain_small(turn % LEVELS)
        if 1 <= turn <= turns:
            streams[(turn - 1) // LEVELS].second((turn - 1) % LEVELS)
        if turn >= 2:
            streams[(turn - 2) // LEVELS].chain_large((turn - 2) % LEVELS)
        if turn == LEVELS + 1:
            streams[0].end_small()
        if turn == LEVELS + 2:
            streams[0].end_sides()
        if turn == LEVELS + 3:
            end(0)
    streams[1].end_small()
    streams[1].end_sides()
    end(1)
    for stream in range(2):
        exchange(stream, 1 - core).wait_recv()
        exchange(stream, core).wait_send()
        streams[stream].end_waits()


def return_sums(grad_in, weighted, terms, w_gate, w_up, w_down, collective_id):
    low, dma = jnp.bfloat16, pltpu.SemaphoreType.DMA
    blocks, rows, depth = grad_in.shape[1:]
    hidden, features = w_down.shape
    wide = features + LANES
    vmem, everywhere = pl.BlockSpec(memory_space=pltpu.VMEM), pl.BlockSpec(memory_space=pl.ANY)
    slots = pltpu.VMEM((2, PLANE, rows, wide), low)
    return pl.pallas_call(
        return_kernel,
        out_shape=[
            jax.ShapeDtypeStruct((2 * rows, wide), jnp.float32),
            jax.ShapeDtypeStruct((2 * rows, features), jnp.float32),
        ],
        in_specs=[everywhere] * 6,
        out_specs=[vmem] * 2,
        scratch_shapes=[
            *scatter_places(blocks, rows, wide),
            *scatter_places(blocks, rows, features),
            slots,
            slots,
            pltpu.VMEM((2, 2, PLANE, rows, depth), low),
            pltpu.VMEM((features, depth), low),
            pltpu.VMEM((hidden, features), low),
            dma((2 * LEVELS,)),
            dma((2 * LEVELS,)),
            dma((2,)),
            dma((3,)),
            dma((2,)),
            dma((2, 2)),
            pltpu.SemaphoreType.REGULAR,
        ],
        compiler_params=pltpu.CompilerParams(
            collective_id=collective_id, has_side_effects=True, vmem_limit_bytes=63 * 1024 * 1024
        ),
    )(grad_in, weighted, terms, w_gate, w_up, w_down)


def kernels_fit():
    return lax.axis_size("gx") == LEVELS * PLANE and lax.axis_size("gy") == 2


def packed_gains(vectors):
    rows = jnp.concatenate([vector.reshape(-1, HEAD_DIM) for vector in vectors], axis=0)
    return jnp.pad(rows, ((0, -rows.shape[0] % 8), (0, 0)))


def unpacked_gains(rows, vectors):
    sums, at = [], 0
    for vector in vectors:
        length = vector.shape[0] // HEAD_DIM
        sums.append(rows[at : at + length].reshape(-1))
        at += length
    return sums


def two_parts(values):
    high = lax.reduce_precision(values, 8, 7)
    return high.astype(jnp.bfloat16), (values - high).astype(jnp.bfloat16)


def sparse_experts(normed_ffn, logits, route_hits, routes, cotangent, w_gate, w_up, w_down):
    sequence_length, model_width = normed_ffn.shape
    experts_all = logits.shape[1]
    devices_gx = lax.axis_size("gx")
    part_width = model_width // lax.axis_size("gy")
    capacity = 5 * sequence_length * TOP // (4 * experts_all)
    pairs_count = sequence_length * TOP
    hits_float = route_hits.astype(jnp.float32)
    chosen = jnp.sum(logits[:, None, :] * hits_float, axis=-1)
    gate_exps = jnp.exp(chosen)
    gate_values = gate_exps / jnp.sum(gate_exps, axis=1, keepdims=True)
    flat_hits = route_hits.reshape(pairs_count, experts_all).astype(jnp.int32)
    slot_rank = jnp.sum((jnp.cumsum(flat_hits, axis=0) - flat_hits) * flat_hits, axis=1)
    slot_dest = routes.reshape(-1) * capacity + slot_rank
    slot_pair = (
        jnp.full((experts_all * capacity,), pairs_count, jnp.int32)
        .at[slot_dest]
        .set(jnp.arange(pairs_count, dtype=jnp.int32))
    )
    slot_token = jnp.where(slot_pair < pairs_count, slot_pair // TOP, sequence_length)

    def to_experts(buffer):
        arrived = lax.all_to_all(buffer, "gx", split_axis=0, concat_axis=0, tiled=True)
        return arrived.reshape(devices_gx * capacity, model_width)

    def from_experts(partial_rows):
        share_rows = lax.psum_scatter(
            partial_rows.astype(jnp.bfloat16), "gy", scatter_dimension=1, tiled=True
        )
        returned = lax.all_to_all(
            share_rows.reshape(devices_gx, capacity, part_width),
            "gx",
            split_axis=0,
            concat_axis=0,
            tiled=True,
        )
        whole_rows = lax.all_gather(returned, "gy", axis=2, tiled=True)
        return whole_rows.reshape(devices_gx * capacity, model_width)

    send_rows = jnp.take(normed_ffn, slot_token, axis=0, mode="fill", fill_value=0)
    expert_in = to_experts(send_rows.reshape(devices_gx, capacity, model_width))
    gate_in = jnp.dot(expert_in, w_gate, preferred_element_type=jnp.float32)
    up_in = jnp.dot(expert_in, w_up, preferred_element_type=jnp.float32)
    gate_sigmoid = jax.nn.sigmoid(gate_in)
    gate_swish = gate_in * gate_sigmoid
    activated = (gate_swish * up_in).astype(jnp.bfloat16)
    expert_part = jnp.dot(activated, w_down, preferred_element_type=jnp.float32)
    expert_out = from_experts(expert_part)
    pair_rows = jnp.take(expert_out, slot_dest, axis=0).reshape(sequence_length, TOP, model_width)
    mixed_rows = jnp.einsum(
        "tk,tkd->td", gate_values, pair_rows, preferred_element_type=jnp.float32
    )
    grad_out_f = cotangent.astype(jnp.float32)
    grad_gates = jnp.einsum("td,tkd->tk", grad_out_f, pair_rows, preferred_element_type=jnp.float32)
    grad_chosen = gate_values * (
        grad_gates - jnp.sum(gate_values * grad_gates, axis=1, keepdims=True)
    )
    grad_logits = jnp.sum(grad_chosen[:, :, None] * hits_float, axis=1).astype(jnp.bfloat16)
    slot_gate = jnp.take(gate_values.reshape(-1), slot_pair, mode="fill", fill_value=0.0)
    grad_send = (
        jnp.take(grad_out_f, slot_token, axis=0, mode="fill", fill_value=0) * slot_gate[:, None]
    )
    grad_expert_out = to_experts(
        grad_send.astype(jnp.bfloat16).reshape(devices_gx, capacity, model_width)
    )
    grad_act = contract(grad_expert_out, w_down, 1, 1)
    down_term = contract(activated, grad_expert_out, 0, 0)
    grad_gate_in = (
        grad_act * up_in * gate_sigmoid * (1.0 + gate_in * (1.0 - gate_sigmoid))
    ).astype(jnp.bfloat16)
    grad_up_in = (grad_act * gate_swish).astype(jnp.bfloat16)
    gate_term = contract(expert_in, grad_gate_in, 0, 0)
    up_term = contract(expert_in, grad_up_in, 0, 0)
    grad_in_part = contract(grad_gate_in, w_gate, 1, 1) + contract(grad_up_in, w_up, 1, 1)
    grad_rows = from_experts(grad_in_part)
    grad_pairs = jnp.take(grad_rows, slot_dest, axis=0).reshape(sequence_length, TOP, model_width)
    grad_rows_sum = jnp.sum(grad_pairs.astype(jnp.float32), axis=1)
    return mixed_rows, grad_rows_sum, grad_logits, (gate_term[None], up_term[None], down_term[None])


def swap_cores(rows):
    return lax.ppermute(rows, "gy", [(0, 1), (1, 0)])


def own_half(rows):
    count = rows.shape[0] // lax.axis_size("gy")
    return lax.dynamic_slice_in_dim(rows, lax.axis_index("gy") * count, count, 0)


def dense_experts(normed_ffn, logits, route_hits, cotangent, w_gate, w_up, w_down):
    sequence_length, model_width = normed_ffn.shape
    experts_all = logits.shape[1]
    gate_exps = jnp.exp(jnp.where(jnp.any(route_hits, axis=1), logits, -1e30))
    gate_all = gate_exps / jnp.sum(gate_exps, axis=1, keepdims=True)
    gate_lanes = jnp.pad(jnp.concatenate(two_parts(gate_all), axis=1), ((0, 0), (0, LANES - 2 * experts_all)))
    row_lanes = jnp.concatenate([own_half(normed_ffn), own_half(gate_lanes)], axis=1)
    weighted, grad_in, terms, gate_term, up_term, down_term = experts_products(
        row_lanes, cotangent, w_gate, w_up, w_down, experts_all, 2
    )
    back, mixed_rows = return_sums(grad_in, weighted, terms, w_gate, w_up, w_down, 3)
    term_lanes = back[:, model_width : model_width + 4 * experts_all]
    grad_gates = jnp.sum(term_lanes.reshape(sequence_length, 4, experts_all), axis=1)
    grad_logits = (
        gate_all * (grad_gates - jnp.sum(gate_all * grad_gates, axis=1, keepdims=True))
    ).astype(jnp.bfloat16)
    return mixed_rows, back[:, :model_width], grad_logits, tuple(
        term[None].astype(jnp.float32) for term in (gate_term, up_term, down_term)
    )


def turn_lanes(values, cosine, sine_table):
    return values * cosine + pltpu.roll(values, HEAD_DIM // 2, 1) * sine_table


def unit_rows(values):
    scale = lax.rsqrt(jnp.mean(values * values, axis=1, keepdims=True) + EPSILON)
    return values * scale, scale


def allowed_pairs(docs_column, docs_row):
    shape = (docs_column.shape[0], docs_row.shape[1])
    keys_at, queries_at = lax.broadcasted_iota(jnp.int32, shape, 0), lax.broadcasted_iota(jnp.int32, shape, 1)
    return (keys_at <= queries_at) & (docs_column == docs_row)


def head_span(head):
    return pl.ds(pl.multiple_of(head * HEAD_DIM, HEAD_DIM), HEAD_DIM)


def weight_copies(w_ref, w_in, w_out, w_sem, wide, last_first):
    groups = list(range(w_in.shape[1] // wide))
    if last_first:
        groups = groups[-1:] + groups[:-1]
    into = [
        (n, pltpu.make_async_copy(w_ref.at[:, pl.ds(n * wide, wide)], w_in.at[:, pl.ds(n * wide, wide)], w_sem.at[n]))
        for n in groups
    ]
    start = w_in.shape[1] + LANES
    out = [
        pltpu.make_async_copy(
            w_ref.at[:, pl.ds(start + n * wide, wide)],
            w_out.at[:, pl.ds(n * wide, wide)],
            w_sem.at[len(groups) + n],
        )
        for n in range(w_out.shape[1] // wide)
    ]
    return into, out


def dot_groups(target, left, right, begin, count, transposed, wide=256):
    def body(i, carry):
        span = pl.ds(pl.multiple_of(begin + i * wide, wide), wide)
        value = dot_nt(left[...], right[span]) if transposed else dot_nn(left[...], right[:, span])
        target[:, span] = value.astype(target.dtype)
        return carry

    lax.fori_loop(0, count // wide, body, 0)


GROUP = 512


def attend_kernel(
    q_heads, kv_heads, tokens_ref, w_ref, cosine_ref, sine_ref, docs_column, docs_row, q_gain, k_gain, attn_gain,
    normed_ref, raw_ref, attended_ref, query_ref, key_ref, value_ref, totals_ref, part_ref, w_in, w_out, w_sem,
):
    into, out = weight_copies(w_ref, w_in, w_out, w_sem, GROUP, True)
    for _, copy in into:
        copy.start()
    for copy in out:
        copy.start()

    def norm_rows(i, carry):
        span = pl.ds(pl.multiple_of(i * 16, 16), 16)
        unit, _ = unit_rows(tokens_ref[span].astype(jnp.float32))
        normed_ref[span] = (unit * attn_gain[...]).astype(jnp.bfloat16)
        return carry

    lax.fori_loop(0, tokens_ref.shape[0] // 16, norm_rows, 0)
    for n, copy in into:
        copy.wait()
        dot_groups(raw_ref, normed_ref, w_in, n * GROUP, GROUP, False)
    cosine, sine_table = cosine_ref[...], sine_ref[...]
    allowed = allowed_pairs(docs_column[...], docs_row[...])
    group, inv_root = q_heads // kv_heads, 1.0 / math.sqrt(HEAD_DIM)
    for kv in range(kv_heads):
        unit, _ = unit_rows(raw_ref[:, head_span(q_heads + kv)])
        key_rows = turn_lanes(unit * k_gain[...], cosine, sine_table).astype(jnp.bfloat16)
        value_rows = raw_ref[:, head_span(q_heads + kv_heads + kv)]
        key_ref[:, head_span(kv)] = key_rows
        value_ref[:, head_span(kv)] = value_rows.astype(jnp.bfloat16)
        value_columns = value_rows.T.astype(jnp.bfloat16)

        def body(index, carry, kv=kv, key_rows=key_rows, value_columns=value_columns):
            head = kv * group + index
            unit, _ = unit_rows(raw_ref[:, head_span(head)])
            query_rows = turn_lanes(unit * q_gain[...], cosine, sine_table).astype(jnp.bfloat16)
            query_ref[:, head_span(head)] = query_rows
            scores = jnp.where(allowed, dot_nt(key_rows, query_rows) * inv_root, -1e30)
            peak = jnp.max(scores, axis=0, keepdims=True)
            exps = jnp.exp(scores - peak)
            total = jnp.sum(exps, axis=0, keepdims=True)
            totals_ref[pl.ds(head, 1), :] = peak + jnp.log(total)
            probs = (exps / total).astype(jnp.bfloat16)
            attended_ref[:, head_span(head)] = dot_nn(value_columns, probs).T.astype(jnp.bfloat16)
            return carry

        lax.fori_loop(0, group, body, 0, unroll=2)
    for copy in out:
        copy.wait()
    dot_groups(part_ref, attended_ref, w_out, 0, w_out.shape[0], True)


def attend_back_kernel(
    q_heads, kv_heads, grad_attn_ref, w_ref, cosine_ref, sine_ref, docs_column, docs_row, q_gain, k_gain,
    raw_ref, query_ref, key_ref, value_ref, totals_ref,
    grad_raw_ref, gains_ref, part_ref, grad_ref, sums_ref, w_in, w_out, w_sem,
):
    into, out = weight_copies(w_ref, w_in, w_out, w_sem, GROUP, False)
    for copy in out:
        copy.start()
    for _, copy in into:
        copy.start()
    for n, copy in enumerate(out):
        copy.wait()
        dot_groups(grad_ref, grad_attn_ref, w_out, n * GROUP, GROUP, False)
    cosine, sine_table = cosine_ref[...], sine_ref[...]
    allowed = allowed_pairs(docs_column[...], docs_row[...])
    group, inv_root = q_heads // kv_heads, 1.0 / math.sqrt(HEAD_DIM)
    gains_ref[...] = jnp.zeros_like(gains_ref)

    def back_to_raw(grad, head, gain, gain_row):
        grad = turn_lanes(grad, cosine, -sine_table)
        unit, scale = unit_rows(raw_ref[:, head_span(head)])
        gains_ref[pl.ds(gain_row, 1), :] += jnp.sum(grad * unit, axis=0, keepdims=True)
        grad = grad * gain
        grad = scale * (grad - unit * jnp.mean(grad * unit, axis=1, keepdims=True))
        grad_raw_ref[:, head_span(head)] = grad.astype(jnp.bfloat16)

    for kv in range(kv_heads):
        key_rows, value_rows = key_ref[:, head_span(kv)], value_ref[:, head_span(kv)]
        key_columns = key_rows.astype(jnp.float32).T.astype(jnp.bfloat16)
        sums_ref[...] = jnp.zeros_like(sums_ref)

        def body(index, carry, kv=kv, key_rows=key_rows, value_rows=value_rows, key_columns=key_columns):
            head = kv * group + index
            query_rows, grad_rows = query_ref[:, head_span(head)], grad_ref[:, head_span(head)]
            scores = jnp.where(allowed, dot_nt(key_rows, query_rows) * inv_root, -1e30)
            probs = jnp.exp(scores - totals_ref[pl.ds(head, 1), :])
            sums_ref[0] += dot_nn(probs.astype(jnp.bfloat16), grad_rows)
            grad_probs = dot_nt(value_rows, grad_rows)
            inner = jnp.sum(probs * grad_probs, axis=0, keepdims=True)
            grad_scores = (probs * (grad_probs - inner)).astype(jnp.bfloat16)
            sums_ref[1] += dot_nn(grad_scores, query_rows)
            grad_queries = dot_nn(key_columns, grad_scores).T * inv_root
            back_to_raw(grad_queries, head, q_gain[...], 0)
            return carry

        lax.fori_loop(0, group, body, 0, unroll=2)
        back_to_raw(sums_ref[1] * inv_root, q_heads + kv, k_gain[...], 1)
        grad_raw_ref[:, head_span(q_heads + kv_heads + kv)] = sums_ref[0].astype(jnp.bfloat16)
    for _, copy in into:
        copy.wait()
    dot_groups(part_ref, grad_raw_ref, w_in, 0, w_in.shape[0], True)


def attention_shared(weights_all, doc_ids, query_norm_gain, k_gain):
    length = doc_ids.shape[1]
    cosine, sine_table = rotary_tables(length, HEAD_DIM)
    cosine, sine_table = cosine[:, 0], sine_table[:, 0]
    return (
        weights_all,
        jnp.concatenate([cosine, cosine], axis=1),
        jnp.concatenate([-sine_table, sine_table], axis=1),
        doc_ids.reshape(length, 1),
        doc_ids.reshape(1, length),
        query_norm_gain.reshape(1, HEAD_DIM),
        k_gain.reshape(1, HEAD_DIM),
    )


def attention_specs(q_heads, kv_heads, features, inputs):
    vmem, everywhere = pl.BlockSpec(memory_space=pltpu.VMEM), pl.BlockSpec(memory_space=pl.ANY)
    wide, out_wide = (q_heads + 2 * kv_heads) * HEAD_DIM, q_heads * HEAD_DIM
    scratch = [
        pltpu.VMEM((features, wide), jnp.bfloat16),
        pltpu.VMEM((features, out_wide), jnp.bfloat16),
        pltpu.SemaphoreType.DMA(((wide + out_wide) // GROUP,)),
    ]
    return [vmem, everywhere] + [vmem] * (inputs - 2), scratch


def attend(tokens, attn_gain, shared, q_heads, kv_heads):
    (length, features), low, shape = tokens.shape, jnp.bfloat16, jax.ShapeDtypeStruct
    in_specs, scratch = attention_specs(q_heads, kv_heads, features, 2 + len(shared))
    return pl.pallas_call(
        functools.partial(attend_kernel, q_heads, kv_heads),
        out_shape=[
            shape((length, features), low),
            shape((length, (q_heads + 2 * kv_heads) * HEAD_DIM), jnp.float32),
            shape((length, q_heads * HEAD_DIM), low),
            shape((length, q_heads * HEAD_DIM), low),
            shape((length, kv_heads * HEAD_DIM), low),
            shape((length, kv_heads * HEAD_DIM), low),
            shape((q_heads, length), jnp.float32),
            shape((length, features), jnp.float32),
        ],
        in_specs=in_specs,
        scratch_shapes=scratch,
        compiler_params=pltpu.CompilerParams(vmem_limit_bytes=48 * 1024 * 1024),
    )(tokens, *shared, attn_gain.reshape(1, features))


def attend_back(grad_attn, shared, kept, q_heads, kv_heads):
    (length, features), shape = grad_attn.shape, jax.ShapeDtypeStruct
    in_specs, scratch = attention_specs(q_heads, kv_heads, features, 1 + len(shared) + len(kept))
    return pl.pallas_call(
        functools.partial(attend_back_kernel, q_heads, kv_heads),
        out_shape=[
            shape((length, (q_heads + 2 * kv_heads) * HEAD_DIM), jnp.bfloat16),
            shape((8, HEAD_DIM), jnp.float32),
            shape((length, features), jnp.float32),
        ],
        in_specs=in_specs,
        scratch_shapes=[
            pltpu.VMEM((length, q_heads * HEAD_DIM), jnp.bfloat16),
            pltpu.VMEM((2, length, HEAD_DIM), jnp.float32),
            *scratch,
        ],
        compiler_params=pltpu.CompilerParams(vmem_limit_bytes=48 * 1024 * 1024),
    )(grad_attn, *shared, *kept)


def on_device(
    tokens_in,
    doc_ids,
    routes,
    q_weight,
    key_matrix,
    value_matrix,
    out_weight,
    router_weight,
    attn_gain,
    ffn_gain,
    query_norm_gain,
    k_gain,
    gate_weight,
    up_weight,
    down_weight,
    cotangent,
):
    sequence_length = tokens_in.shape[0]
    model_width = tokens_in.shape[1]
    devices_gx = lax.axis_size("gx")
    devices_gy = lax.axis_size("gy")
    part_width = model_width // devices_gy
    experts_all = router_weight.shape[1]
    router_lanes = jnp.pad(router_weight, ((0, 0), (0, LANES - experts_all)))
    rows_local = jnp.concatenate([q_weight, key_matrix, value_matrix, router_lanes, out_weight], axis=1)
    dense = kernels_fit() and experts_all <= 2 * TOP
    if dense:
        (weights_all,) = gather_blocks([rows_local], (0,), 1)
        weights_all = weights_all.reshape(-1, rows_local.shape[1])
    else:
        weights_all = lax.all_gather(rows_local, "gx", axis=0, tiled=True)
    q_width, kv_width = q_weight.shape[1], key_matrix.shape[1]
    qkv_width = q_width + 2 * kv_width
    router_full = weights_all[:, qkv_width : qkv_width + experts_all]
    heads_local = q_width // HEAD_DIM
    kv_local = kv_width // HEAD_DIM
    inputs_f = tokens_in.astype(jnp.float32)
    scale_one = root_mean_scale(inputs_f)
    unit_one = inputs_f * scale_one
    shared = attention_shared(weights_all, doc_ids, query_norm_gain, k_gain)
    normalized_input, raw_rows, attended, *kept, attn_part = attend(
        tokens_in, attn_gain, shared, heads_local, kv_local
    )
    attn_total = attn_part + swap_cores(attn_part)
    residual = inputs_f + attn_total
    scale_two = root_mean_scale(residual)
    unit_two = residual * scale_two
    normed_ffn = (unit_two * ffn_gain).astype(jnp.bfloat16)
    logits = jnp.dot(normed_ffn, router_full, preferred_element_type=jnp.float32)
    expert_iota = jnp.arange(experts_all, dtype=jnp.int32)
    route_hits = routes[:, :, None] == expert_iota
    if dense:
        mixed_rows, grad_rows_sum, grad_logits, expert_grads = dense_experts(
            normed_ffn, logits, route_hits, cotangent, gate_weight[0], up_weight[0], down_weight[0]
        )
    else:
        mixed_rows, grad_rows_sum, grad_logits, expert_grads = sparse_experts(
            normed_ffn, logits, route_hits, routes, cotangent, gate_weight[0], up_weight[0], down_weight[0]
        )
    output = (residual + mixed_rows).astype(jnp.bfloat16)
    grad_out_f = cotangent.astype(jnp.float32)
    logit_lanes = jnp.pad(grad_logits, ((0, 0), (0, LANES - experts_all)))
    router_lanes = contract(normed_ffn, logit_lanes, 0, 0)
    grad_ffn_in = contract(grad_logits, router_full, 1, 1) + grad_rows_sum
    ffn_gain_term = jnp.sum(grad_ffn_in * unit_two, axis=0)
    grad_residual = grad_out_f + norm_back(grad_ffn_in * ffn_gain, unit_two, scale_two)
    grad_attn = grad_residual.astype(jnp.bfloat16)
    grad_qkv, head_gains, grad_normed_part = attend_back(
        grad_attn, shared, (raw_rows, *kept), heads_local, kv_local
    )
    q_gain_term, k_gain_term = head_gains[0], head_gains[1]
    grad_normed = grad_normed_part + swap_cores(grad_normed_part)
    attn_gain_term = jnp.sum(grad_normed * unit_one, axis=0)
    own_mask = (jnp.arange(model_width) // part_width == lax.axis_index("gy")).astype(jnp.float32)
    gains = (attn_gain_term * own_mask, ffn_gain_term * own_mask, q_gain_term, k_gain_term)
    if dense:
        router_blocks = router_lanes.astype(jnp.bfloat16).reshape(devices_gx, -1, LANES)
        factors = (normalized_input, grad_qkv, router_blocks, grad_attn, attended)
        lasts = (tokens_in, grad_residual, grad_normed, attn_gain.reshape(1, model_width))
        grad_q, grad_k, grad_v, grad_router, grad_out, gain_rows, grad_input = scatter_sums(
            factors, packed_gains(gains), lasts, kv_width, 4
        )
        gains = unpacked_gains(gain_rows, gains)
    else:
        sums = jnp.concatenate(
            [
                lax.psum_scatter(term, "gx", scatter_dimension=0, tiled=True)
                for term in (
                    contract(normalized_input, grad_qkv, 0, 0),
                    router_lanes,
                    contract(grad_attn, attended, 0, 0),
                )
            ],
            axis=1,
        )
        gains = lax.psum(gains, ("gx", "gy"))
        grad_q = sums[:, :q_width]
        grad_k = sums[:, q_width : q_width + kv_width]
        grad_v = sums[:, q_width + kv_width : qkv_width]
        grad_router = sums[:, qkv_width : qkv_width + LANES]
        grad_out = sums[:, qkv_width + LANES :]
        grad_input = grad_residual + norm_back(grad_normed * attn_gain, unit_one, scale_one)
        grad_input = grad_input.astype(jnp.bfloat16)
    gain_attn, gain_ffn, gain_query, gain_key = gains
    grad_router = grad_router[:, :experts_all]
    return (
        output,
        grad_input,
        grad_q,
        grad_k,
        grad_v,
        grad_out,
        grad_router,
        gain_attn,
        gain_ffn,
        gain_query,
        gain_key,
        expert_grads[0],
        expert_grads[1],
        expert_grads[2],
    )


def solution(mesh):
    return jax.shard_map(
        on_device,
        mesh=mesh,
        in_specs=(
            P("gx", None),
            P("gx", None),
            P("gx", None),
            P("gx", "gy"),
            P("gx", "gy"),
            P("gx", "gy"),
            P("gx", "gy"),
            P("gx", None),
            P(),
            P(),
            P(),
            P(),
            P("gx", None, "gy"),
            P("gx", None, "gy"),
            P("gx", "gy", None),
            P("gx", None),
        ),
        out_specs=(
            P("gx", None),
            P("gx", None),
            P("gx", "gy"),
            P("gx", "gy"),
            P("gx", "gy"),
            P("gx", "gy"),
            P("gx", None),
            P(),
            P(),
            P(),
            P(),
            P("gx", None, "gy"),
            P("gx", None, "gy"),
            P("gx", "gy", None),
        ),
        check_vma=False,
    )
```

```python
import functools
import math

import jax
import jax.numpy as jnp
from jax import lax
from jax.experimental import pallas as pl
from jax.experimental.pallas import tpu as pltpu
from jax.sharding import PartitionSpec as P

QUERY_HEADS = 32
KEY_VALUE_HEADS = 4
HEAD_DIM = 128
LANES = 128
TOP = 8


EPSILON = 1e-06
THETA = 1000000.0


def root_mean_scale(values):
    return lax.rsqrt(jnp.mean(values * values, axis=-1, keepdims=True) + EPSILON)


def rotary_tables(sequence_length, head_width):
    half_width = head_width // 2
    frequencies = THETA ** (-(2.0 * jnp.arange(half_width, dtype=jnp.float32)) / head_width)
    angles = jnp.arange(sequence_length, dtype=jnp.float32)[:, None] * frequencies[None, :]
    return (jnp.cos(angles)[:, None, :], jnp.sin(angles)[:, None, :])


def norm_back(grad_normed, normed_unit, scale_rows):
    return scale_rows * (
        grad_normed - normed_unit * jnp.mean(grad_normed * normed_unit, axis=-1, keepdims=True)
    )


def contract(first_op, second_op, first_dim, second_dim):
    return lax.dot_general(
        first_op,
        second_op,
        (((first_dim,), (second_dim,)), ((), ())),
        preferred_element_type=jnp.float32,
    )


MESH = pl.DeviceIdType.MESH
LEVELS = 4
PLANE = 4


def cut_rows(rows):
    near, far = 3 * rows // 4, rows // 4
    return (
        (0, near),
        ((0, near // 2), (near // 2, near // 2)),
        (near, far),
        ((near, far // 2), (near + far // 2, far // 2)),
    )


def neighbours():
    me, core = lax.axis_index("gx"), lax.axis_index("gy")
    level = me // PLANE
    x_side = me + 1 - 2 * (me % 2)
    y_side = me + 2 - 4 * ((me // 2) % 2)
    return me, core, level, x_side, y_side


def greet(level, targets, with_core, me, core):
    barrier = pltpu.get_barrier_semaphore()

    def hello(device):
        pl.semaphore_signal(barrier, inc=1, device_id=device, device_id_type=MESH)

    for target in targets:
        hello((target, core))
    if with_core:
        hello((me, 1 - core))

    @pl.when(level > 0)
    def _():
        hello((me - PLANE, core))

    @pl.when(level < LEVELS - 1)
    def _():
        hello((me + PLANE, core))

    inner = jnp.where(level > 0, 1, 0) + jnp.where(level < LEVELS - 1, 1, 0)
    pl.semaphore_wait(barrier, len(targets) + int(with_core) + inner)


def when(condition, action):
    if condition is None:
        action()
    else:
        pl.when(condition)(action)


def gather_kernel(count, *refs):
    pieces, out, own, piece_sem = refs[:count], refs[count], refs[count + 1], refs[count + 2]
    copies, lane = [], 0
    for i, piece in enumerate(pieces):
        place = own.at[:, pl.ds(lane, piece.shape[1])]
        copies.append(pltpu.make_async_copy(piece, place, piece_sem.at[i]))
        lane += piece.shape[1]
    for copy in copies:
        copy.start()
    for copy in copies:
        copy.wait()
    steps = gather_steps([own], [out], [None], refs[count + 3 :])
    for step in steps.order:
        step()
    steps.end()


class gather_steps:
    def __init__(self, ins, outs, pairs, sems):
        self.ins, self.outs, self.pairs = ins, outs, pairs
        self.send_sem, self.recv_sem, self.local_sem, self.pair_send, self.pair_recv = sems
        self.me, self.core, self.level, self.x_side, self.y_side = neighbours()
        self.diagonal = self.x_side + self.y_side - self.me
        self.spans = cut_rows(ins[0].shape[0])
        self.has_up, self.has_down = self.level < LEVELS - 1, self.level > 0
        self.up, self.down = (self.me + PLANE, self.core), (self.me - PLANE, self.core)
        self.to_x, self.to_y = (self.x_side, self.core), (self.y_side, self.core)
        self.sent, self.mirrored, self.everyone = [], [], range(len(ins))
        for k in self.everyone:
            self.own_copy(k).start()
        greet(self.level, (self.x_side, self.y_side), any(p is not None for p in pairs), self.me, self.core)
        self.order = [
            self.start,
            self.side_small,
            lambda: self.column(1),
            lambda: self.cross(0),
            lambda: self.column(2),
            self.start_planes,
            lambda: self.cross(1),
            lambda: self.column(3),
            lambda: self.planes(1),
            lambda: self.cross(2),
            lambda: self.planes(2),
            lambda: self.cross(3),
            lambda: self.planes(3),
            lambda: [self.halves(step) for step in range(LEVELS)],
        ]

    def send(self, condition, k, slot, source, first, number, span, target):
        def copy():
            there = self.outs[k].at[pl.ds(first, number), pl.ds(*span)]
            here = there
            if source == "own":
                here, there = self.ins[k].at[pl.ds(*span)], self.outs[k].at[first, pl.ds(*span)]
            return pltpu.make_async_remote_copy(
                here,
                there,
                self.send_sem.at[k, slot],
                self.recv_sem.at[k, slot],
                device_id=target,
                device_id_type=MESH,
            )

        when(condition, lambda: copy().start())
        self.sent.append((condition, copy))

    def mirror(self, condition, k, first, number, span, group):
        if self.pairs[k] is None:
            return
        slot = len(self.mirrored)

        def copy():
            return pltpu.make_async_remote_copy(
                self.outs[k].at[pl.ds(first, number), pl.ds(*span)],
                self.pairs[k].at[pl.ds(first, number), pl.ds(*span)],
                self.pair_send.at[slot],
                self.pair_recv.at[slot],
                device_id=(self.me, 1 - self.core),
                device_id_type=MESH,
            )

        when(condition, lambda: copy().start())
        self.mirrored.append((condition, copy, group))

    def arrive(self, condition, k, slot, first, number, span, group):
        place = self.outs[k].at[pl.ds(first, number), pl.ds(*span)]

        def wait():
            pltpu.make_async_remote_copy(
                place,
                place,
                self.send_sem.at[k, slot],
                self.recv_sem.at[k, slot],
                device_id=self.to_x,
                device_id_type=MESH,
            ).wait_recv()

        when(condition, wait)
        self.mirror(condition, k, first, number, span, group)

    def members(self, step):
        if step == 0:
            return [(None, 0, 0)]
        return [(self.level >= step, step, -step), (self.level + step < LEVELS, 3 + step, step)]

    def slot_of(self, group, index):
        return 6 + 7 * group + index

    last = 6 + 28

    def own_copy(self, k):
        return pltpu.make_async_copy(self.ins[k], self.outs[k].at[self.me], self.local_sem.at[k])

    def start(self):
        whole_a, half_a, whole_b, half_b = self.spans
        last, me = self.last, self.me
        for k in self.everyone:
            self.send(None, k, last, "own", me, 1, whole_b, self.to_x)
            self.send(None, k, last + 1, "own", me, 1, whole_b, self.to_y)
            self.send(self.has_up, k, 0, "own", me, 1, whole_a, self.up)
            self.send(self.has_down, k, 3, "own", me, 1, whole_a, self.down)
            self.send(None, k, self.slot_of(0, 0), "own", me, 1, whole_a, self.to_x)
            self.send(None, k, self.slot_of(1, 0), "own", me, 1, whole_a, self.to_y)

    def side_small(self):
        whole_a, half_a, whole_b, half_b = self.spans
        last = self.last
        for k in self.everyone:
            self.arrive(None, k, last, self.x_side, 1, whole_b, (0, 1))
            self.send(None, k, last + 3, "out", self.x_side, 1, half_b[1], self.to_y)
            self.arrive(None, k, last + 1, self.y_side, 1, whole_b, (0, 1))
            self.send(None, k, last + 2, "out", self.y_side, 1, half_b[0], self.to_x)
        for k in self.everyone:
            self.own_copy(k).wait()
            self.mirror(None, k, self.me, 1, (0, self.ins[k].shape[0]), (0, 0))
            self.arrive(None, k, last + 2, self.diagonal, 1, half_b[0], (0, 1))
            self.arrive(None, k, last + 3, self.diagonal, 1, half_b[1], (0, 1))

    def start_planes(self):
        whole_b = self.spans[2]
        for k in self.everyone:
            self.send(self.has_up, k, self.last + 4, "out", PLANE * self.level, PLANE, whole_b, self.up)
            self.send(self.has_down, k, self.last + 7, "out", PLANE * self.level, PLANE, whole_b, self.down)

    def cross(self, step):
        whole_a, half_a = self.spans[:2]
        for k in self.everyone:
            for condition, index, distance in self.members(step):
                first = self.x_side + PLANE * distance
                self.arrive(condition, k, self.slot_of(0, index), first, 1, whole_a, (distance, 0))
                self.send(condition, k, self.slot_of(3, index), "out", first, 1, half_a[1], self.to_y)
                first = self.y_side + PLANE * distance
                self.arrive(condition, k, self.slot_of(1, index), first, 1, whole_a, (distance, 0))
                self.send(condition, k, self.slot_of(2, index), "out", first, 1, half_a[0], self.to_x)

    def halves(self, step):
        half_a = self.spans[1]
        for k in self.everyone:
            for condition, index, distance in self.members(step):
                first = self.diagonal + PLANE * distance
                self.arrive(condition, k, self.slot_of(2, index), first, 1, half_a[0], (distance, 0))
                self.arrive(condition, k, self.slot_of(3, index), first, 1, half_a[1], (distance, 0))

    def column(self, step):
        whole_a = self.spans[0]
        for k in self.everyone:
            for condition, index, distance in self.members(step):
                first = self.me + PLANE * distance
                rising = distance < 0
                self.arrive(condition, k, step - 1 if rising else 2 + step, first, 1, whole_a, (distance, 0))
                if step < LEVELS - 1:
                    onward = condition & (self.has_up if rising else self.has_down)
                    slot = step if rising else 3 + step
                    self.send(onward, k, slot, "out", first, 1, whole_a, self.up if rising else self.down)
                self.send(condition, k, self.slot_of(0, index), "out", first, 1, whole_a, self.to_x)
                self.send(condition, k, self.slot_of(1, index), "out", first, 1, whole_a, self.to_y)

    def planes(self, step):
        whole_b = self.spans[2]
        for k in self.everyone:
            for condition, index, distance in self.members(step):
                first = PLANE * (self.level + distance)
                rising = distance < 0
                slot = self.last + (3 if rising else 6) + step
                self.arrive(condition, k, slot, first, PLANE, whole_b, (distance, 1))
                if step < LEVELS - 1:
                    onward = condition & (self.has_up if rising else self.has_down)
                    slot = self.last + (4 if rising else 7) + step
                    self.send(onward, k, slot, "out", first, PLANE, whole_b, self.up if rising else self.down)

    def paired_level(self, distance, parts):
        for condition, copy, group in self.mirrored:
            if group[0] == distance and group[1] in parts:
                when(condition, lambda copy=copy: copy().wait_recv())

    def end(self, levels_waited=False):
        for condition, copy in self.sent:
            when(condition, lambda copy=copy: copy().wait_send())
        for condition, copy, group in self.mirrored:
            when(condition, lambda copy=copy: copy().wait_send())
            if not levels_waited:
                when(condition, lambda copy=copy: copy().wait_recv())


GATHER_SLOTS = 6 + 28 + 10


def gather_semaphores(count, paired):
    dma = pltpu.SemaphoreType.DMA
    slots = (count, GATHER_SLOTS)
    pair_slots = (max(1, paired * (GATHER_SLOTS + 1)),)
    return [dma(slots), dma(slots), dma((count,)), dma(pair_slots), dma(pair_slots)]


def gather_blocks(pieces, collective_id):
    rows, width = pieces[0].shape[0], sum(piece.shape[1] for piece in pieces)
    low = pieces[0].dtype
    return pl.pallas_call(
        functools.partial(gather_kernel, len(pieces)),
        out_shape=jax.ShapeDtypeStruct((lax.axis_size("gx"), rows, width), low),
        in_specs=[pl.BlockSpec(memory_space=pl.ANY)] * len(pieces),
        out_specs=pl.BlockSpec(memory_space=pl.ANY),
        scratch_shapes=[
            pltpu.VMEM((rows, width), low),
            pltpu.SemaphoreType.DMA((len(pieces),)),
            *gather_semaphores(1, 0),
        ],
        compiler_params=pltpu.CompilerParams(collective_id=collective_id, has_side_effects=True),
    )(*pieces)


def dot_nn(left, right):
    return lax.dot_general(left, right, (((1,), (0,)), ((), ())), preferred_element_type=jnp.float32)


def dot_nt(left, right):
    return lax.dot_general(left, right, (((1,), (1,)), ((), ())), preferred_element_type=jnp.float32)


def experts_kernel(experts_all, *refs):
    rows_ref, grad_rows_ref, w_gate, w_up, w_down = refs[:5]
    weighted_out, grad_in_out, terms_out, gate_out, up_out, down_out, grads_own, grads_pair = refs[5:13]
    held, grads, w_in, left_in, left_down, weighted_ref, grad_in_ref, terms_ref = refs[13:21]
    sums_in, sums_down, turned, down_low, grad_sem, part_sem, w_sem, out_sem, sum_sem = refs[21:30]
    hidden, width = w_down.shape
    joins = [
        pltpu.make_async_copy(part, w_in.at[:, pl.ds(i * hidden, hidden)], w_sem.at[i])
        for i, part in enumerate((w_gate, w_up))
    ]
    for join in joins:
        join.start()
    rows = rows_ref.shape[0]
    grad_half = grad_rows_ref.at[pl.ds(pl.multiple_of(lax.axis_index("gy") * rows, rows), rows)]
    steps = gather_steps([rows_ref, grad_half], [held.at[0], grads_own], [held.at[1], grads_pair], refs[30:])
    level, core = steps.level, steps.core
    tiles = hidden // LANES
    visits = [
        level,
        jnp.where(level == 0, 1, level - 1),
        jnp.where(level == 0, 2, jnp.where(level == 3, 1, level + 1)),
        jnp.where(level < 2, 3, 0),
    ]

    def fetch(turn, half):
        return pltpu.make_async_copy(
            (grads_own, grads_pair)[half].at[pl.ds(PLANE * visits[turn], PLANE)],
            grads.at[turn % 2, half],
            grad_sem.at[turn % 2, half],
        )

    part_rows = {None: (0, rows), 0: steps.spans[0], 1: steps.spans[2]}

    def fetch_part(part, half):
        span = pl.ds(*part_rows[part])
        return pltpu.make_async_copy(
            (grads_own, grads_pair)[half].at[pl.ds(PLANE * visits[-1], PLANE), span],
            grads.at[(LEVELS - 1) % 2, half, :, span],
            part_sem.at[part, half],
        )

    def fetches(turn, part):
        return [fetch(turn, half) if part is None else fetch_part(part, half) for half in range(2)]

    lane = lax.broadcasted_iota(jnp.int32, (1, LANES), 1)
    expert = steps.me
    gate_pick = (((lane == expert) | (lane == experts_all + expert))).astype(jnp.float32)
    high_lane = (lane == 2 * experts_all * core + expert).astype(jnp.float32)
    low_lane = (lane == 2 * experts_all * core + experts_all + expert).astype(jnp.float32)

    def leave(turn):
        span = pl.ds(PLANE * visits[turn], PLANE)
        pairs = ((weighted_ref, weighted_out), (grad_in_ref, grad_in_out), (terms_ref, terms_out))
        return [
            pltpu.make_async_copy(here.at[:, span], there.at[:, span], out_sem.at[turn, i])
            for i, (here, there) in enumerate(pairs)
        ]

    def forward(turn, begin=0, end=4, part=None):
        first, (row, number) = PLANE * visits[turn], part_rows[part]
        together = 2 if part is None else PLANE
        group, per_half, span_rows = together * number, PLANE // together, pl.ds(row, number)
        if begin == 0:
            for copy in fetches(turn, part):
                copy.wait()

        def body(step, carry):
            half, pair = step // per_half, step % per_half
            at = first + together * pair
            blocks = pl.ds(at, together)
            lanes = held[half, blocks, span_rows, pl.ds(width, LANES)].reshape(group, LANES)
            gate_rows = jnp.sum(lanes.astype(jnp.float32) * gate_pick, axis=1, keepdims=True)
            grad_rows = grads[turn % 2, half, pl.ds(together * pair, together), span_rows].reshape(group, width)
            token_rows = held[half, blocks, span_rows, pl.ds(0, width)].reshape(group, width)
            grad_hidden = dot_nt(grad_rows, w_down[...])
            both = dot_nn(token_rows, w_in[...])
            terms = jnp.zeros((group, 1), jnp.float32)
            column = pl.multiple_of(2 * PLANE * row + step * group, LANES)
            for j in range(tiles):
                gate_in = both[:, j * LANES : (j + 1) * LANES]
                up_in = both[:, hidden + j * LANES : hidden + (j + 1) * LANES]
                back = grad_hidden[:, j * LANES : (j + 1) * LANES]
                gate_sigmoid = 1.0 / (1.0 + jnp.exp(-gate_in))
                gate_swish = gate_in * gate_sigmoid
                activated = gate_swish * up_in
                terms = terms + jnp.sum(activated * back, axis=1, keepdims=True)
                grad_act = gate_rows * back
                weighted = gate_rows * activated
                grad_gate = grad_act * up_in * gate_sigmoid * (1.0 + gate_in * (1.0 - gate_sigmoid))
                grad_up = grad_act * gate_swish
                for value, array, tile, left in (
                    (weighted, weighted_ref, j, left_down),
                    (grad_gate, grad_in_ref, j, left_in),
                    (grad_up, grad_in_ref, tiles + j, left_in),
                ):
                    span = pl.ds(tile * LANES, LANES)
                    low = value.astype(jnp.bfloat16).reshape(together, number, LANES)
                    array[half, blocks, span_rows, span] = low
                    left[span, pl.ds(column, group)] = value.T.astype(jnp.bfloat16)
            high = terms.astype(jnp.bfloat16).astype(jnp.float32)
            spread = high * high_lane + (terms - high) * low_lane
            terms_ref[half, blocks, span_rows] = spread.astype(jnp.bfloat16).reshape(together, number, LANES)
            return carry

        lax.fori_loop(begin, min(end, 2 * per_half), body, 0)
        if end == 4 and part != 0:
            for copy in leave(turn):
                copy.start()

    wide = 256

    def weights(turn, begin=0, end=8, part=None):
        first, (row, number) = PLANE * visits[turn], part_rows[part]
        span_rows, depth = pl.ds(row, number), 2 * PLANE * number
        columns = pl.ds(2 * PLANE * row, depth)

        def body(step, carry):
            span = pl.ds(pl.multiple_of(step * wide, wide), wide)
            token_rows = held[:, pl.ds(first, PLANE), span_rows, span].reshape(depth, wide)
            grad_rows = grads[turn % 2, :, :, span_rows, span].reshape(depth, wide)
            part_in = dot_nn(left_in[:, columns], token_rows)
            part_down = dot_nn(left_down[:, columns], grad_rows)
            if turn:
                part_in = sums_in[:, span] + part_in
                part_down = sums_down[:, span] + part_down
            if part != 1:
                sums_in[:, span] = part_in
                sums_down[:, span] = part_down
            else:
                for i in range(2):
                    turned[i, span] = part_in[i * hidden : (i + 1) * hidden].T.astype(jnp.bfloat16)
                down_low[:, span] = part_down.astype(jnp.bfloat16)
                for copy in leave_sums(step):
                    copy.start()
            return carry

        lax.fori_loop(begin, end, body, 0)

    def leave_sums(step):
        span = pl.ds(pl.multiple_of(step * wide, wide), wide)
        return [
            pltpu.make_async_copy(turned.at[0, span], gate_out.at[span], sum_sem.at[step, 0]),
            pltpu.make_async_copy(turned.at[1, span], up_out.at[span], sum_sem.at[step, 1]),
            pltpu.make_async_copy(down_low.at[:, span], down_out.at[:, span], sum_sem.at[step, 2]),
        ]

    def level_ready(turn, part=None):
        parts = (0, 1) if part is None else (part,)
        if turn == 0:
            steps.paired_level(0, parts)
        for distance in range(-3, 4):
            if turn and distance:
                wanted = visits[turn] == level + distance
                pl.when(wanted)(lambda distance=distance: steps.paired_level(distance, parts))
        for copy in fetches(turn, part):
            copy.start()

    steps.start()
    steps.side_small()
    steps.column(1)
    steps.cross(0)
    for join in joins:
        join.wait()
    steps.column(2)
    steps.start_planes()
    steps.halves(0)
    steps.cross(1)
    level_ready(0)
    forward(0, 0, 4)
    steps.column(3)
    steps.planes(1)
    weights(0, 0, 4)
    steps.cross(2)
    steps.halves(1)
    level_ready(1)
    weights(0, 4, 8)
    forward(1, 0, 4)
    steps.planes(2)
    weights(1, 0, 4)
    steps.cross(3)
    steps.halves(2)
    level_ready(2)
    weights(1, 4, 8)
    forward(2, 0, 4)
    steps.halves(3)
    level_ready(3, 0)
    weights(2, 0, 8)
    forward(3, part=0)
    weights(3, part=0)
    steps.planes(3)
    level_ready(3, 1)
    forward(3, part=1)
    weights(3, part=1)
    for turn in range(LEVELS):
        for copy in leave(turn):
            copy.wait()

    def last_sums(step, carry):
        for copy in leave_sums(step):
            copy.wait()
        return carry

    lax.fori_loop(0, width // wide, last_sums, 0)
    steps.end(levels_waited=True)


def experts_products(rows, grad_rows, w_gate, w_up, w_down, experts_all, collective_id):
    blocks, low, count = lax.axis_size("gx"), jnp.bfloat16, rows.shape[0]
    hidden, width = w_down.shape
    everywhere = pl.BlockSpec(memory_space=pl.ANY)
    block_shape = (2, blocks, count)
    shapes = [
        jax.ShapeDtypeStruct((*block_shape, hidden), low),
        jax.ShapeDtypeStruct((*block_shape, 2 * hidden), low),
        jax.ShapeDtypeStruct((*block_shape, LANES), low),
        jax.ShapeDtypeStruct((width, hidden), low),
        jax.ShapeDtypeStruct((width, hidden), low),
        jax.ShapeDtypeStruct((hidden, width), low),
        *[jax.ShapeDtypeStruct((blocks, count, width), low)] * 2,
    ]
    level_rows = 2 * PLANE * count
    dma = pltpu.SemaphoreType.DMA
    return pl.pallas_call(
        functools.partial(experts_kernel, experts_all),
        out_shape=shapes,
        in_specs=[everywhere] * 4 + [pl.BlockSpec(memory_space=pltpu.VMEM)],
        out_specs=[everywhere] * 8,
        scratch_shapes=[
            pltpu.VMEM((*block_shape, rows.shape[1]), low),
            pltpu.VMEM((2, 2, PLANE, count, width), low),
            pltpu.VMEM((width, 2 * hidden), low),
            pltpu.VMEM((2 * hidden, level_rows), low),
            pltpu.VMEM((hidden, level_rows), low),
            *[pltpu.VMEM(shape.shape, low) for shape in shapes[:3]],
            pltpu.VMEM((2 * hidden, width), jnp.float32),
            pltpu.VMEM((hidden, width), jnp.float32),
            pltpu.VMEM((2, width, hidden), low),
            pltpu.VMEM((hidden, width), low),
            dma((2, 2)),
            dma((2, 2)),
            dma((2,)),
            dma((LEVELS, 3)),
            dma((width // 256, 3)),
            *gather_semaphores(2, 2),
        ],
        compiler_params=pltpu.CompilerParams(
            collective_id=collective_id, has_side_effects=True, vmem_limit_bytes=63 * 1024 * 1024
        ),
    )(rows, grad_rows, w_gate, w_up, w_down)[:6]


class scatter_moves:
    def __init__(self, held, out):
        self.mine, self.half_y, self.half_x, self.full_x, self.full_y, self.slots_a, self.slots_b, self.side_b = held[:8]
        self.send_sem, self.recv_sem, self.chain_send, self.chain_recv = held[8:12]
        self.out = out
        self.me, self.core, level, x_side, y_side = neighbours()
        self.level = level
        self.up, self.down = (self.me + PLANE, self.core), (self.me - PLANE, self.core)
        self.to_x, self.to_y = (x_side, self.core), (y_side, self.core)
        self.x_at, self.y_at, self.own_at = x_side % PLANE, y_side % PLANE, self.me % PLANE
        self.diagonal_at = (x_side + y_side - self.me) % PLANE
        forward = jnp.where(level < 2, 1, 0)
        self.order = [3 * forward, 2 * forward + (1 - forward), level + 1 - 2 * (level % 2), level]
        self.rows, self.width = self.mine.shape[1:]
        self.spans = cut_rows(self.rows)
        self.sent = []

    def send(self, condition, source, target_ref, ssem, rsem, target):
        def copy():
            return pltpu.make_async_remote_copy(
                source, target_ref, ssem, rsem, device_id=target, device_id_type=MESH
            )

        when(condition, lambda: copy().start())
        self.sent.append((condition, copy))

    def arrive(self, condition, target_ref, rsem):
        def wait():
            pltpu.make_async_remote_copy(
                target_ref, target_ref, rsem, rsem, device_id=self.to_x, device_id_type=MESH
            ).wait_recv()

        when(condition, wait)

    def add(self, condition, height, target, *terms, step=16):
        def run():
            def body(i, carry):
                at = pl.multiple_of(i * step, step)
                total = target(at, step)[...].astype(jnp.float32)
                for term in terms:
                    total = total + term(at, step)[...].astype(jnp.float32)
                target(at, step)[...] = total.astype(jnp.bfloat16)
                return carry

            lax.fori_loop(0, height // step, body, 0)

        when(condition, run)

    def rows_of(self, ref, *index, start=0):
        return lambda at, step: ref.at[(*index, pl.ds(start + at, step))]

    def turn_sems(self, turn):
        return [(self.send_sem.at[6 * turn + i], self.recv_sem.at[6 * turn + i]) for i in range(6)]

    def half_spans(self):
        half_a = self.spans[1]
        return half_a[0][1], pl.ds(*half_a[0]), pl.ds(*half_a[1])

    def first(self, turn):
        base, at = PLANE * self.order[turn], self.turn_sems(turn)
        _, lower, upper = self.half_spans()
        mine, to_x, to_y = self.mine, self.to_x, self.to_y
        self.send(None, mine.at[base + self.diagonal_at, lower], self.half_y.at[turn], *at[0], to_y)
        self.send(None, mine.at[base + self.diagonal_at, upper], self.half_x.at[turn], *at[1], to_x)
        self.send(None, mine.at[base + self.x_at, upper], self.full_x.at[turn, upper], *at[2], to_x)
        self.send(None, mine.at[base + self.y_at, lower], self.full_y.at[turn, lower], *at[3], to_y)

    def second(self, turn):
        base, at = PLANE * self.order[turn], self.turn_sems(turn)
        height, lower, upper = self.half_spans()
        mine, rows_of = self.mine, self.rows_of
        self.arrive(None, self.half_y.at[turn], at[0][1])
        self.add(None, height, rows_of(mine, base + self.x_at), rows_of(self.half_y, turn))
        self.send(None, mine.at[base + self.x_at, lower], self.full_x.at[turn, lower], *at[4], self.to_x)
        self.arrive(None, self.half_x.at[turn], at[1][1])
        self.add(None, height, rows_of(mine, base + self.y_at, start=height), rows_of(self.half_x, turn))
        self.send(None, mine.at[base + self.y_at, upper], self.full_y.at[turn, upper], *at[5], self.to_y)

    def chain(self, which, turn, block, slots, spread):
        to_level, level = self.order[turn], self.level
        rising, falling = to_level > level, to_level < level
        begins = (rising & (level == 0)) | (falling & (level == LEVELS - 1))
        middle = (rising | falling) & jnp.logical_not(begins)
        self.arrive(middle, slots.at[to_level], self.chain_recv.at[which, to_level])
        spread(middle, to_level)
        outgoing = self.chain_send.at[which, to_level]
        self.send(rising, block, slots.at[to_level], outgoing, self.chain_recv.at[which, to_level], self.up)
        at = jnp.where(to_level == level - 1, LEVELS, to_level)
        self.send(falling, block, slots.at[at], outgoing, self.chain_recv.at[which, at], self.down)

    def add_small(self, condition, base, slot):
        start, number = self.spans[2]
        for column in range(PLANE):
            self.add(
                condition,
                number,
                self.rows_of(self.mine, base + column, start=start),
                self.rows_of(self.slots_b, slot, column),
            )

    def chain_small(self, turn):
        if turn == LEVELS - 1:
            return
        base = PLANE * self.order[turn]
        block = self.mine.at[pl.ds(base, PLANE), pl.ds(*self.spans[2])]
        self.chain(1, turn, block, self.slots_b, lambda condition, slot: self.add_small(condition, base, slot))

    def plane_arrives(self, turn):
        at = self.turn_sems(turn)
        _, lower, upper = self.half_spans()
        self.arrive(None, self.full_x.at[turn, upper], at[2][1])
        self.arrive(None, self.full_y.at[turn, lower], at[3][1])
        self.arrive(None, self.full_x.at[turn, lower], at[4][1])
        self.arrive(None, self.full_y.at[turn, upper], at[5][1])

    def chain_large(self, turn):
        if turn == LEVELS - 1:
            return
        own, number = PLANE * self.order[turn] + self.own_at, self.spans[0][1]
        rows_of, mine = self.rows_of, self.mine
        self.plane_arrives(turn)
        self.add(None, number, rows_of(mine, own), rows_of(self.full_x, turn), rows_of(self.full_y, turn))
        self.chain(
            0,
            turn,
            mine.at[own, pl.ds(*self.spans[0])],
            self.slots_a,
            lambda condition, slot: self.add(condition, number, rows_of(mine, own), rows_of(self.slots_a, slot)),
        )

    def side(self):
        short = self.spans[3][0][1]
        spans = [pl.ds(0, short), pl.ds(short, short), pl.ds(2 * short, 2 * short), pl.ds(4 * short, 2 * short)]
        return [(self.side_b.at[span], self.send_sem.at[24 + i], self.recv_sem.at[24 + i]) for i, span in enumerate(spans)]

    def arrivals(self):
        return ((self.level > 0, self.level), (self.level < LEVELS - 1, LEVELS))

    def end_small(self):
        base, mine, half_b = PLANE * self.level, self.mine, self.spans[3]
        for condition, slot in self.arrivals():
            self.arrive(condition, self.slots_b.at[slot], self.chain_recv.at[1, slot])
            self.add_small(condition, base, slot)
        side = self.side()
        self.send(None, mine.at[base + self.diagonal_at, pl.ds(*half_b[0])], *side[0], self.to_y)
        self.send(None, mine.at[base + self.diagonal_at, pl.ds(*half_b[1])], *side[1], self.to_x)

    def end_sides(self):
        base, mine, rows_of = PLANE * self.level, self.mine, self.rows_of
        whole_b, half_b = self.spans[2:]
        side, short = self.side(), half_b[0][1]
        self.plane_arrives(LEVELS - 1)
        self.arrive(None, side[0][0], side[0][2])
        self.add(None, short, rows_of(mine, base + self.x_at, start=half_b[0][0]), rows_of(self.side_b))
        self.send(None, mine.at[base + self.x_at, pl.ds(*whole_b)], *side[2], self.to_x)
        self.arrive(None, side[1][0], side[1][2])
        self.add(None, short, rows_of(mine, base + self.y_at, start=half_b[1][0]), rows_of(self.side_b, start=short))
        self.send(None, mine.at[base + self.y_at, pl.ds(*whole_b)], *side[3], self.to_y)

    def end_sums(self, base):
        whole_a, half_a, whole_b, half_b = self.spans
        own, out, mine, step = PLANE * self.level + self.own_at, self.out, self.mine, 16
        full_x, full_y, slots_a, side_b = self.full_x, self.full_y, self.slots_a, self.side_b

        def place(at):
            return pl.ds(pl.multiple_of(base + at, step), step)

        def tail_a(i, carry):
            at = pl.multiple_of(i * step, step)
            span, turn = pl.ds(at, step), LEVELS - 1
            total = mine[own, span].astype(jnp.float32)
            total = total + full_x[turn, span].astype(jnp.float32) + full_y[turn, span].astype(jnp.float32)
            out[place(at)] = total
            return carry

        lax.fori_loop(0, whole_a[1] // step, tail_a, 0)
        for condition, slot in self.arrivals():
            self.arrive(condition, slots_a.at[slot], self.chain_recv.at[0, slot])

            def more(slot=slot):
                def body(i, carry):
                    at = pl.multiple_of(i * step, step)
                    out[place(at)] = out[place(at)] + slots_a[slot, pl.ds(at, step)].astype(jnp.float32)
                    return carry

                lax.fori_loop(0, whole_a[1] // step, body, 0)

            when(condition, more)
        side, short = self.side(), half_b[0][1]
        self.arrive(None, side[2][0], side[2][2])
        self.arrive(None, side[3][0], side[3][2])

        def tail_b(i, carry):
            at = pl.multiple_of(i * step, step)
            total = mine[own, pl.ds(whole_b[0] + at, step)].astype(jnp.float32)
            total = total + side_b[pl.ds(2 * short + at, step)].astype(jnp.float32)
            total = total + side_b[pl.ds(4 * short + at, step)].astype(jnp.float32)
            out[place(whole_b[0] + at)] = total
            return carry

        lax.fori_loop(0, whole_b[1] // step, tail_b, 0)

    def end_waits(self):
        for condition, copy in self.sent:
            when(condition, lambda copy=copy: copy().wait_send())


def scatter_places(blocks, rows, width):
    near, far, low, dma = 3 * rows // 4, rows // 4, jnp.bfloat16, pltpu.SemaphoreType.DMA
    shapes = [
        (blocks, rows, width),
        (LEVELS, near // 2, width),
        (LEVELS, near // 2, width),
        (LEVELS, near, width),
        (LEVELS, near, width),
        (LEVELS + 1, near, width),
        (LEVELS + 1, PLANE, far, width),
        (3 * far, width),
    ]
    return [pltpu.VMEM(shape, low) for shape in shapes] + [dma((28,)), dma((28,)), dma((2, 5)), dma((2, 5))]


PLACES = 12


def scatter_kernel(*refs):
    normed, grad_qkv, router_term, grad_attn, attended, gain_ref = refs[:6]
    tokens, grad_residual, grad_normed, attn_gain = refs[6:10]
    pieces_out, (gain_out, grad_input) = refs[10:15], refs[15:17]
    held, (out, load_sem, leave_sem, gain_slots, gain_send, gain_recv) = refs[17:-6], refs[-6:]
    moves = scatter_moves(held, out)
    me, core, level = moves.me, moves.core, moves.level
    far = me + 2 * PLANE - 4 * PLANE * (level // 2)
    partners = ((me, 1 - core), moves.to_x, moves.to_y, (me + PLANE - 2 * PLANE * (level % 2), core), (far, core))

    def gain_copy(turn):
        return pltpu.make_async_remote_copy(
            gain_slots.at[2 * turn],
            gain_slots.at[2 * turn + 1],
            gain_send.at[turn],
            gain_recv.at[turn],
            device_id=partners[turn],
            device_id_type=MESH,
        )

    def gain_step(turn):
        if turn == 0:
            gain_slots[0] = gain_ref[...]
        else:
            gain_copy(turn - 1).wait_recv()
            gain_slots[2 * turn] = gain_slots[2 * turn - 2] + gain_slots[2 * turn - 1]
        if turn < len(partners):
            gain_copy(turn).start()
        else:
            gain_out[...] = gain_slots[2 * turn]

    router_lane = grad_qkv.shape[1]

    def load(turn):
        span = pl.ds(PLANE * moves.order[turn], PLANE)
        place = moves.mine.at[span, :, pl.ds(router_lane, LANES)]
        return pltpu.make_async_copy(router_term.at[span], place, load_sem.at[turn])

    def products(turn):
        level_rows, wide = PLANE * moves.rows, 256
        span = pl.ds(PLANE * moves.order[turn], PLANE)
        features = pl.ds(pl.multiple_of(moves.order[turn] * level_rows, level_rows), level_rows)
        for left, right, lane in ((normed, grad_qkv, 0), (grad_attn, attended, router_lane + LANES)):
            left_rows = left[:, features].astype(jnp.float32).T.astype(jnp.bfloat16)

            def body(step, carry, left_rows=left_rows, right=right, lane=lane):
                at = pl.multiple_of(step * wide, wide)
                value = dot_nn(left_rows, right[:, pl.ds(at, wide)]).astype(jnp.bfloat16)
                lanes = pl.ds(pl.multiple_of(lane + at, LANES), wide)
                moves.mine[span, :, lanes] = value.reshape(PLANE, moves.rows, wide)
                return carry

            lax.fori_loop(0, right.shape[1] // wide, body, 0)

    def input_rows():
        step = 16

        def body(i, carry):
            span = pl.ds(pl.multiple_of(i * step, step), step)
            unit, scale = unit_rows(tokens[span].astype(jnp.float32))
            grad = grad_normed[span] * attn_gain[...]
            grad = scale * (grad - unit * jnp.mean(grad * unit, axis=1, keepdims=True))
            grad_input[span] = (grad_residual[span] + grad).astype(jnp.bfloat16)
            return carry

        lax.fori_loop(0, tokens.shape[0] // step, body, 0)

    def leave():
        copies, lane = [], 0
        for i, piece in enumerate(pieces_out):
            width = piece.shape[1]
            copies.append(pltpu.make_async_copy(out.at[:, pl.ds(lane, width)], piece, leave_sem.at[i]))
            lane += width
        return copies

    for turn in range(LEVELS):
        load(turn).start()
    products(0)
    greet(level, (moves.to_x[0], moves.to_y[0], far), True, me, core)
    gain_step(0)
    for turn in range(LEVELS):
        if turn:
            products(turn)
        load(turn).wait()
        moves.first(turn)
        moves.chain_small(turn)
    input_rows()
    for turn in range(LEVELS - 1):
        moves.second(turn)
        gain_step(turn + 1)
        if turn:
            moves.chain_large(turn - 1)
    moves.second(LEVELS - 1)
    gain_step(4)
    moves.chain_large(LEVELS - 2)
    moves.end_small()
    moves.end_sides()
    gain_step(5)
    moves.end_sums(0)
    for copy in leave():
        copy.start()
    for turn in range(len(partners)):
        gain_copy(turn).wait_send()
    moves.end_waits()
    for copy in leave():
        copy.wait()


def scatter_sums(factors, gains, lasts, kv_width, collective_id):
    _, grad_qkv, router_term, _, attended = factors
    blocks, rows, _ = router_term.shape
    widths = (grad_qkv.shape[1] - 2 * kv_width, kv_width, kv_width, LANES, attended.shape[1])
    dma, tokens = pltpu.SemaphoreType.DMA, lasts[0]
    vmem, everywhere = pl.BlockSpec(memory_space=pltpu.VMEM), pl.BlockSpec(memory_space=pl.ANY)
    return pl.pallas_call(
        scatter_kernel,
        out_shape=[
            *[jax.ShapeDtypeStruct((rows, width), jnp.float32) for width in widths],
            jax.ShapeDtypeStruct(gains.shape, gains.dtype),
            jax.ShapeDtypeStruct(tokens.shape, tokens.dtype),
        ],
        in_specs=[vmem, vmem, everywhere, vmem, vmem, vmem, vmem, vmem, vmem, vmem],
        out_specs=[everywhere] * 5 + [vmem] * 2,
        scratch_shapes=[
            *scatter_places(blocks, rows, sum(widths)),
            pltpu.VMEM((rows, sum(widths)), jnp.float32),
            dma((LEVELS,)),
            dma((5,)),
            pltpu.VMEM((11, *gains.shape), gains.dtype),
            dma((5,)),
            dma((5,)),
        ],
        compiler_params=pltpu.CompilerParams(
            collective_id=collective_id, has_side_effects=True, vmem_limit_bytes=63 * 1024 * 1024
        ),
    )(*factors, gains, *lasts)


def return_kernel(grad_in, weighted, terms, w_gate, w_up, w_down, back_out, mixed_out, *refs):
    streams = [
        scatter_moves(refs[:PLACES], back_out),
        scatter_moves(refs[PLACES : 2 * PLACES], mixed_out),
    ]
    sibling, away, left, right_in, right_down = refs[2 * PLACES : 2 * PLACES + 5]
    pair_send, pair_recv, left_sem, right_sem, term_sem, ready_sem, credit = refs[2 * PLACES + 5 :]
    me, core, order, rows = streams[0].me, streams[0].core, streams[0].order, streams[0].rows
    hidden, features = w_down.shape
    depths, lefts = (2 * hidden, hidden), (grad_in, weighted)
    turns, wide = 2 * LEVELS, 256
    rights = [
        pltpu.make_async_copy(w_gate, right_in.at[:, pl.ds(0, hidden)], right_sem.at[0]),
        pltpu.make_async_copy(w_up, right_in.at[:, pl.ds(hidden, hidden)], right_sem.at[1]),
        pltpu.make_async_copy(w_down, right_down, right_sem.at[2]),
    ]

    def level_span(turn):
        return pl.ds(PLANE * order[turn % LEVELS], PLANE)

    def left_copy(turn):
        stream = turn // LEVELS
        return pltpu.make_async_copy(
            lefts[stream].at[:, level_span(turn)],
            left.at[turn % 2, :, :, :, pl.ds(0, depths[stream])],
            left_sem.at[turn % 2],
        )

    def term_copy(turn, half):
        lanes = pl.ds(features, LANES)
        place = away.at[turn % 2, :, :, lanes] if half else streams[0].mine.at[level_span(turn), :, lanes]
        return pltpu.make_async_copy(terms.at[half, level_span(turn)], place, term_sem.at[half])

    def width_of(turn):
        return streams[turn // LEVELS].width

    def hand(turn):
        lanes = pl.ds(0, width_of(turn))
        return pltpu.make_async_remote_copy(
            away.at[turn % 2, :, :, lanes],
            sibling.at[turn % 2, :, :, lanes],
            pair_send.at[turn],
            pair_recv.at[turn],
            device_id=(me, 1 - core),
            device_id_type=MESH,
        )

    def product(turn, half, store):
        stream, slot = turn // LEVELS, turn % 2
        factor = left[slot, half, :, :, pl.ds(0, depths[stream])].reshape(PLANE * rows, depths[stream])

        def body(step, carry):
            span = pl.ds(pl.multiple_of(step * wide, wide), wide)
            value = dot_nt(factor, right_in[span]) if stream == 0 else dot_nn(factor, right_down[:, span])
            store(span, value.reshape(PLANE, rows, wide))
            return carry

        lax.fori_loop(0, features // wide, body, 0)

    def hand_over(turn):
        left_copy(turn).wait()
        if turn + 1 < turns:
            left_copy(turn + 1).start()
        if turn < LEVELS:
            term_copy(turn, 1).start()
            term_copy(turn, 0).start()

        def store(span, value):
            away[turn % 2, :, :, span] = value.astype(jnp.bfloat16)

        product(turn, 1, store)
        if turn < LEVELS:
            term_copy(turn, 1).wait()
            term_copy(turn, 0).wait()
        if turn == 0:
            greet(streams[0].level, (streams[0].to_x[0], streams[0].to_y[0]), True, me, core)
        if turn >= 2:
            pl.semaphore_wait(credit, 1)
        hand(turn).start()

    def settle(turn):
        hand(turn).wait()
        mine, slot = streams[turn // LEVELS].mine, turn % 2

        def store(span, value):
            value = value + sibling[slot, :, :, span].astype(jnp.float32)
            mine[level_span(turn), :, span] = value.astype(jnp.bfloat16)

        product(turn, 0, store)
        if turn < LEVELS:
            lanes = pl.ds(features, LANES)
            value = mine[level_span(turn), :, lanes].astype(jnp.float32)
            value = value + sibling[slot, :, :, lanes].astype(jnp.float32)
            mine[level_span(turn), :, lanes] = value.astype(jnp.bfloat16)
        if turn + 2 < turns:
            pl.semaphore_signal(credit, inc=1, device_id=(me, 1 - core), device_id_type=MESH)

    def exchange(stream, core_of_rows):
        out = streams[stream].out
        span = pl.ds(pl.multiple_of(core_of_rows * rows, rows), rows)
        return pltpu.make_async_remote_copy(
            out.at[span],
            out.at[span],
            ready_sem.at[stream, 0],
            ready_sem.at[stream, 1],
            device_id=(me, 1 - core),
            device_id_type=MESH,
        )

    def end(stream):
        streams[stream].end_sums(core * rows)
        exchange(stream, core).start()

    left_copy(0).start()
    for copy in rights:
        copy.start()
    for copy in rights:
        copy.wait()
    hand_over(0)
    for turn in range(turns + 2):
        if turn < turns:
            stream = streams[turn // LEVELS]
            settle(turn)
            stream.first(turn % LEVELS)
            if turn + 1 < turns:
                hand_over(turn + 1)
            stream.chain_small(turn % LEVELS)
        if 1 <= turn <= turns:
            streams[(turn - 1) // LEVELS].second((turn - 1) % LEVELS)
        if turn >= 2:
            streams[(turn - 2) // LEVELS].chain_large((turn - 2) % LEVELS)
        if turn == LEVELS + 1:
            streams[0].end_small()
        if turn == LEVELS + 2:
            streams[0].end_sides()
        if turn == LEVELS + 3:
            end(0)
    streams[1].end_small()
    streams[1].end_sides()
    end(1)
    for stream in range(2):
        exchange(stream, 1 - core).wait_recv()
        exchange(stream, core).wait_send()
        streams[stream].end_waits()


def return_sums(grad_in, weighted, terms, w_gate, w_up, w_down, collective_id):
    low, dma = jnp.bfloat16, pltpu.SemaphoreType.DMA
    blocks, rows, depth = grad_in.shape[1:]
    hidden, features = w_down.shape
    wide = features + LANES
    vmem, everywhere = pl.BlockSpec(memory_space=pltpu.VMEM), pl.BlockSpec(memory_space=pl.ANY)
    slots = pltpu.VMEM((2, PLANE, rows, wide), low)
    return pl.pallas_call(
        return_kernel,
        out_shape=[
            jax.ShapeDtypeStruct((2 * rows, wide), jnp.float32),
            jax.ShapeDtypeStruct((2 * rows, features), jnp.float32),
        ],
        in_specs=[everywhere] * 6,
        out_specs=[vmem] * 2,
        scratch_shapes=[
            *scatter_places(blocks, rows, wide),
            *scatter_places(blocks, rows, features),
            slots,
            slots,
            pltpu.VMEM((2, 2, PLANE, rows, depth), low),
            pltpu.VMEM((features, depth), low),
            pltpu.VMEM((hidden, features), low),
            dma((2 * LEVELS,)),
            dma((2 * LEVELS,)),
            dma((2,)),
            dma((3,)),
            dma((2,)),
            dma((2, 2)),
            pltpu.SemaphoreType.REGULAR,
        ],
        compiler_params=pltpu.CompilerParams(
            collective_id=collective_id, has_side_effects=True, vmem_limit_bytes=63 * 1024 * 1024
        ),
    )(grad_in, weighted, terms, w_gate, w_up, w_down)


def kernels_fit():
    return lax.axis_size("gx") == LEVELS * PLANE and lax.axis_size("gy") == 2


def packed_gains(vectors):
    rows = jnp.concatenate([vector.reshape(-1, HEAD_DIM) for vector in vectors], axis=0)
    return jnp.pad(rows, ((0, -rows.shape[0] % 8), (0, 0)))


def unpacked_gains(rows, vectors):
    sums, at = [], 0
    for vector in vectors:
        length = vector.shape[0] // HEAD_DIM
        sums.append(rows[at : at + length].reshape(-1))
        at += length
    return sums


def two_parts(values):
    high = lax.reduce_precision(values, 8, 7)
    return high.astype(jnp.bfloat16), (values - high).astype(jnp.bfloat16)


def sparse_experts(normed_ffn, logits, route_hits, routes, cotangent, w_gate, w_up, w_down):
    sequence_length, model_width = normed_ffn.shape
    experts_all = logits.shape[1]
    devices_gx = lax.axis_size("gx")
    part_width = model_width // lax.axis_size("gy")
    capacity = 5 * sequence_length * TOP // (4 * experts_all)
    pairs_count = sequence_length * TOP
    hits_float = route_hits.astype(jnp.float32)
    chosen = jnp.sum(logits[:, None, :] * hits_float, axis=-1)
    gate_exps = jnp.exp(chosen)
    gate_values = gate_exps / jnp.sum(gate_exps, axis=1, keepdims=True)
    flat_hits = route_hits.reshape(pairs_count, experts_all).astype(jnp.int32)
    slot_rank = jnp.sum((jnp.cumsum(flat_hits, axis=0) - flat_hits) * flat_hits, axis=1)
    slot_dest = routes.reshape(-1) * capacity + slot_rank
    slot_pair = (
        jnp.full((experts_all * capacity,), pairs_count, jnp.int32)
        .at[slot_dest]
        .set(jnp.arange(pairs_count, dtype=jnp.int32))
    )
    slot_token = jnp.where(slot_pair < pairs_count, slot_pair // TOP, sequence_length)

    def to_experts(buffer):
        arrived = lax.all_to_all(buffer, "gx", split_axis=0, concat_axis=0, tiled=True)
        return arrived.reshape(devices_gx * capacity, model_width)

    def from_experts(partial_rows):
        share_rows = lax.psum_scatter(
            partial_rows.astype(jnp.bfloat16), "gy", scatter_dimension=1, tiled=True
        )
        returned = lax.all_to_all(
            share_rows.reshape(devices_gx, capacity, part_width),
            "gx",
            split_axis=0,
            concat_axis=0,
            tiled=True,
        )
        whole_rows = lax.all_gather(returned, "gy", axis=2, tiled=True)
        return whole_rows.reshape(devices_gx * capacity, model_width)

    send_rows = jnp.take(normed_ffn, slot_token, axis=0, mode="fill", fill_value=0)
    expert_in = to_experts(send_rows.reshape(devices_gx, capacity, model_width))
    gate_in = jnp.dot(expert_in, w_gate, preferred_element_type=jnp.float32)
    up_in = jnp.dot(expert_in, w_up, preferred_element_type=jnp.float32)
    gate_sigmoid = jax.nn.sigmoid(gate_in)
    gate_swish = gate_in * gate_sigmoid
    activated = (gate_swish * up_in).astype(jnp.bfloat16)
    expert_part = jnp.dot(activated, w_down, preferred_element_type=jnp.float32)
    expert_out = from_experts(expert_part)
    pair_rows = jnp.take(expert_out, slot_dest, axis=0).reshape(sequence_length, TOP, model_width)
    mixed_rows = jnp.einsum(
        "tk,tkd->td", gate_values, pair_rows, preferred_element_type=jnp.float32
    )
    grad_out_f = cotangent.astype(jnp.float32)
    grad_gates = jnp.einsum("td,tkd->tk", grad_out_f, pair_rows, preferred_element_type=jnp.float32)
    grad_chosen = gate_values * (
        grad_gates - jnp.sum(gate_values * grad_gates, axis=1, keepdims=True)
    )
    grad_logits = jnp.sum(grad_chosen[:, :, None] * hits_float, axis=1).astype(jnp.bfloat16)
    slot_gate = jnp.take(gate_values.reshape(-1), slot_pair, mode="fill", fill_value=0.0)
    grad_send = (
        jnp.take(grad_out_f, slot_token, axis=0, mode="fill", fill_value=0) * slot_gate[:, None]
    )
    grad_expert_out = to_experts(
        grad_send.astype(jnp.bfloat16).reshape(devices_gx, capacity, model_width)
    )
    grad_act = contract(grad_expert_out, w_down, 1, 1)
    down_term = contract(activated, grad_expert_out, 0, 0)
    grad_gate_in = (
        grad_act * up_in * gate_sigmoid * (1.0 + gate_in * (1.0 - gate_sigmoid))
    ).astype(jnp.bfloat16)
    grad_up_in = (grad_act * gate_swish).astype(jnp.bfloat16)
    gate_term = contract(expert_in, grad_gate_in, 0, 0)
    up_term = contract(expert_in, grad_up_in, 0, 0)
    grad_in_part = contract(grad_gate_in, w_gate, 1, 1) + contract(grad_up_in, w_up, 1, 1)
    grad_rows = from_experts(grad_in_part)
    grad_pairs = jnp.take(grad_rows, slot_dest, axis=0).reshape(sequence_length, TOP, model_width)
    grad_rows_sum = jnp.sum(grad_pairs.astype(jnp.float32), axis=1)
    return mixed_rows, grad_rows_sum, grad_logits, (gate_term[None], up_term[None], down_term[None])


def swap_cores(rows):
    return lax.ppermute(rows, "gy", [(0, 1), (1, 0)])


def own_half(rows):
    count = rows.shape[0] // lax.axis_size("gy")
    return lax.dynamic_slice_in_dim(rows, lax.axis_index("gy") * count, count, 0)


def dense_experts(normed_ffn, logits, route_hits, cotangent, w_gate, w_up, w_down):
    sequence_length, model_width = normed_ffn.shape
    experts_all = logits.shape[1]
    gate_exps = jnp.exp(jnp.where(jnp.any(route_hits, axis=1), logits, -1e30))
    gate_all = gate_exps / jnp.sum(gate_exps, axis=1, keepdims=True)
    gate_lanes = jnp.pad(jnp.concatenate(two_parts(gate_all), axis=1), ((0, 0), (0, LANES - 2 * experts_all)))
    row_lanes = jnp.concatenate([own_half(normed_ffn), own_half(gate_lanes)], axis=1)
    weighted, grad_in, terms, gate_term, up_term, down_term = experts_products(
        row_lanes, cotangent, w_gate, w_up, w_down, experts_all, 2
    )
    back, mixed_rows = return_sums(grad_in, weighted, terms, w_gate, w_up, w_down, 3)
    term_lanes = back[:, model_width : model_width + 4 * experts_all]
    grad_gates = jnp.sum(term_lanes.reshape(sequence_length, 4, experts_all), axis=1)
    grad_logits = (
        gate_all * (grad_gates - jnp.sum(gate_all * grad_gates, axis=1, keepdims=True))
    ).astype(jnp.bfloat16)
    return mixed_rows, back[:, :model_width], grad_logits, tuple(
        term[None].astype(jnp.float32) for term in (gate_term, up_term, down_term)
    )


def turn_lanes(values, cosine, sine_table):
    return values * cosine + pltpu.roll(values, HEAD_DIM // 2, 1) * sine_table


def unit_rows(values):
    scale = lax.rsqrt(jnp.mean(values * values, axis=1, keepdims=True) + EPSILON)
    return values * scale, scale


def allowed_pairs(docs_column, docs_row):
    shape = (docs_column.shape[0], docs_row.shape[1])
    keys_at, queries_at = lax.broadcasted_iota(jnp.int32, shape, 0), lax.broadcasted_iota(jnp.int32, shape, 1)
    return (keys_at <= queries_at) & (docs_column == docs_row)


def head_span(head):
    return pl.ds(pl.multiple_of(head * HEAD_DIM, HEAD_DIM), HEAD_DIM)


def weight_copies(w_ref, w_in, w_out, w_sem, wide, last_first):
    groups = list(range(w_in.shape[1] // wide))
    if last_first:
        groups = groups[-1:] + groups[:-1]
    into = [
        (n, pltpu.make_async_copy(w_ref.at[:, pl.ds(n * wide, wide)], w_in.at[:, pl.ds(n * wide, wide)], w_sem.at[n]))
        for n in groups
    ]
    start = w_in.shape[1] + LANES
    out = [
        pltpu.make_async_copy(
            w_ref.at[:, pl.ds(start + n * wide, wide)],
            w_out.at[:, pl.ds(n * wide, wide)],
            w_sem.at[len(groups) + n],
        )
        for n in range(w_out.shape[1] // wide)
    ]
    return into, out


def dot_groups(target, left, right, begin, count, transposed, wide=256):
    def body(i, carry):
        span = pl.ds(pl.multiple_of(begin + i * wide, wide), wide)
        value = dot_nt(left[...], right[span]) if transposed else dot_nn(left[...], right[:, span])
        target[:, span] = value.astype(target.dtype)
        return carry

    lax.fori_loop(0, count // wide, body, 0)


GROUP = 512


def attend_kernel(
    q_heads, kv_heads, tokens_ref, w_ref, cosine_ref, sine_ref, docs_column, docs_row, q_gain, k_gain, attn_gain,
    normed_ref, raw_ref, attended_ref, query_ref, key_ref, value_ref, totals_ref, part_ref, w_in, w_out, w_sem,
):
    into, out = weight_copies(w_ref, w_in, w_out, w_sem, GROUP, True)
    for _, copy in into:
        copy.start()
    for copy in out:
        copy.start()

    def norm_rows(i, carry):
        span = pl.ds(pl.multiple_of(i * 16, 16), 16)
        unit, _ = unit_rows(tokens_ref[span].astype(jnp.float32))
        normed_ref[span] = (unit * attn_gain[...]).astype(jnp.bfloat16)
        return carry

    lax.fori_loop(0, tokens_ref.shape[0] // 16, norm_rows, 0)
    for n, copy in into:
        copy.wait()
        dot_groups(raw_ref, normed_ref, w_in, n * GROUP, GROUP, False)
    cosine, sine_table = cosine_ref[...], sine_ref[...]
    allowed = allowed_pairs(docs_column[...], docs_row[...])
    group, inv_root = q_heads // kv_heads, 1.0 / math.sqrt(HEAD_DIM)
    for kv in range(kv_heads):
        unit, _ = unit_rows(raw_ref[:, head_span(q_heads + kv)])
        key_rows = turn_lanes(unit * k_gain[...], cosine, sine_table).astype(jnp.bfloat16)
        value_rows = raw_ref[:, head_span(q_heads + kv_heads + kv)]
        key_ref[:, head_span(kv)] = key_rows
        value_ref[:, head_span(kv)] = value_rows.astype(jnp.bfloat16)
        value_columns = value_rows.T.astype(jnp.bfloat16)

        def body(index, carry, kv=kv, key_rows=key_rows, value_columns=value_columns):
            head = kv * group + index
            unit, _ = unit_rows(raw_ref[:, head_span(head)])
            query_rows = turn_lanes(unit * q_gain[...], cosine, sine_table).astype(jnp.bfloat16)
            query_ref[:, head_span(head)] = query_rows
            scores = jnp.where(allowed, dot_nt(key_rows, query_rows) * inv_root, -1e30)
            peak = jnp.max(scores, axis=0, keepdims=True)
            exps = jnp.exp(scores - peak)
            total = jnp.sum(exps, axis=0, keepdims=True)
            totals_ref[pl.ds(head, 1), :] = peak + jnp.log(total)
            probs = (exps / total).astype(jnp.bfloat16)
            attended_ref[:, head_span(head)] = dot_nn(value_columns, probs).T.astype(jnp.bfloat16)
            return carry

        lax.fori_loop(0, group, body, 0, unroll=2)
    for copy in out:
        copy.wait()
    dot_groups(part_ref, attended_ref, w_out, 0, w_out.shape[0], True)


def attend_back_kernel(
    q_heads, kv_heads, grad_attn_ref, w_ref, cosine_ref, sine_ref, docs_column, docs_row, q_gain, k_gain,
    raw_ref, query_ref, key_ref, value_ref, totals_ref,
    grad_raw_ref, gains_ref, part_ref, grad_ref, sums_ref, w_in, w_out, w_sem,
):
    into, out = weight_copies(w_ref, w_in, w_out, w_sem, GROUP, False)
    for copy in out:
        copy.start()
    for _, copy in into:
        copy.start()
    for n, copy in enumerate(out):
        copy.wait()
        dot_groups(grad_ref, grad_attn_ref, w_out, n * GROUP, GROUP, False)
    cosine, sine_table = cosine_ref[...], sine_ref[...]
    allowed = allowed_pairs(docs_column[...], docs_row[...])
    group, inv_root = q_heads // kv_heads, 1.0 / math.sqrt(HEAD_DIM)
    gains_ref[...] = jnp.zeros_like(gains_ref)

    def back_to_raw(grad, head, gain, gain_row):
        grad = turn_lanes(grad, cosine, -sine_table)
        unit, scale = unit_rows(raw_ref[:, head_span(head)])
        gains_ref[pl.ds(gain_row, 1), :] += jnp.sum(grad * unit, axis=0, keepdims=True)
        grad = grad * gain
        grad = scale * (grad - unit * jnp.mean(grad * unit, axis=1, keepdims=True))
        grad_raw_ref[:, head_span(head)] = grad.astype(jnp.bfloat16)

    for kv in range(kv_heads):
        key_rows, value_rows = key_ref[:, head_span(kv)], value_ref[:, head_span(kv)]
        key_columns = key_rows.astype(jnp.float32).T.astype(jnp.bfloat16)
        sums_ref[...] = jnp.zeros_like(sums_ref)

        def body(index, carry, kv=kv, key_rows=key_rows, value_rows=value_rows, key_columns=key_columns):
            head = kv * group + index
            query_rows, grad_rows = query_ref[:, head_span(head)], grad_ref[:, head_span(head)]
            scores = jnp.where(allowed, dot_nt(key_rows, query_rows) * inv_root, -1e30)
            probs = jnp.exp(scores - totals_ref[pl.ds(head, 1), :])
            sums_ref[0] += dot_nn(probs.astype(jnp.bfloat16), grad_rows)
            grad_probs = dot_nt(value_rows, grad_rows)
            inner = jnp.sum(probs * grad_probs, axis=0, keepdims=True)
            grad_scores = (probs * (grad_probs - inner)).astype(jnp.bfloat16)
            sums_ref[1] += dot_nn(grad_scores, query_rows)
            grad_queries = dot_nn(key_columns, grad_scores).T * inv_root
            back_to_raw(grad_queries, head, q_gain[...], 0)
            return carry

        lax.fori_loop(0, group, body, 0, unroll=2)
        back_to_raw(sums_ref[1] * inv_root, q_heads + kv, k_gain[...], 1)
        grad_raw_ref[:, head_span(q_heads + kv_heads + kv)] = sums_ref[0].astype(jnp.bfloat16)
    for _, copy in into:
        copy.wait()
    dot_groups(part_ref, grad_raw_ref, w_in, 0, w_in.shape[0], True)


def attention_shared(weights_all, doc_ids, query_norm_gain, k_gain):
    length = doc_ids.shape[1]
    cosine, sine_table = rotary_tables(length, HEAD_DIM)
    cosine, sine_table = cosine[:, 0], sine_table[:, 0]
    return (
        weights_all,
        jnp.concatenate([cosine, cosine], axis=1),
        jnp.concatenate([-sine_table, sine_table], axis=1),
        doc_ids.reshape(length, 1),
        doc_ids.reshape(1, length),
        query_norm_gain.reshape(1, HEAD_DIM),
        k_gain.reshape(1, HEAD_DIM),
    )


def attention_specs(q_heads, kv_heads, features, inputs):
    vmem, everywhere = pl.BlockSpec(memory_space=pltpu.VMEM), pl.BlockSpec(memory_space=pl.ANY)
    wide, out_wide = (q_heads + 2 * kv_heads) * HEAD_DIM, q_heads * HEAD_DIM
    scratch = [
        pltpu.VMEM((features, wide), jnp.bfloat16),
        pltpu.VMEM((features, out_wide), jnp.bfloat16),
        pltpu.SemaphoreType.DMA(((wide + out_wide) // GROUP,)),
    ]
    return [vmem, everywhere] + [vmem] * (inputs - 2), scratch


def attend(tokens, attn_gain, shared, q_heads, kv_heads):
    (length, features), low, shape = tokens.shape, jnp.bfloat16, jax.ShapeDtypeStruct
    in_specs, scratch = attention_specs(q_heads, kv_heads, features, 2 + len(shared))
    return pl.pallas_call(
        functools.partial(attend_kernel, q_heads, kv_heads),
        out_shape=[
            shape((length, features), low),
            shape((length, (q_heads + 2 * kv_heads) * HEAD_DIM), jnp.float32),
            shape((length, q_heads * HEAD_DIM), low),
            shape((length, q_heads * HEAD_DIM), low),
            shape((length, kv_heads * HEAD_DIM), low),
            shape((length, kv_heads * HEAD_DIM), low),
            shape((q_heads, length), jnp.float32),
            shape((length, features), jnp.float32),
        ],
        in_specs=in_specs,
        scratch_shapes=scratch,
        compiler_params=pltpu.CompilerParams(vmem_limit_bytes=48 * 1024 * 1024),
    )(tokens, *shared, attn_gain.reshape(1, features))


def attend_back(grad_attn, shared, kept, q_heads, kv_heads):
    (length, features), shape = grad_attn.shape, jax.ShapeDtypeStruct
    in_specs, scratch = attention_specs(q_heads, kv_heads, features, 1 + len(shared) + len(kept))
    return pl.pallas_call(
        functools.partial(attend_back_kernel, q_heads, kv_heads),
        out_shape=[
            shape((length, (q_heads + 2 * kv_heads) * HEAD_DIM), jnp.bfloat16),
            shape((8, HEAD_DIM), jnp.float32),
            shape((length, features), jnp.float32),
        ],
        in_specs=in_specs,
        scratch_shapes=[
            pltpu.VMEM((length, q_heads * HEAD_DIM), jnp.bfloat16),
            pltpu.VMEM((2, length, HEAD_DIM), jnp.float32),
            *scratch,
        ],
        compiler_params=pltpu.CompilerParams(vmem_limit_bytes=48 * 1024 * 1024),
    )(grad_attn, *shared, *kept)


def on_device(
    tokens_in,
    doc_ids,
    routes,
    q_weight,
    key_matrix,
    value_matrix,
    out_weight,
    router_weight,
    attn_gain,
    ffn_gain,
    query_norm_gain,
    k_gain,
    gate_weight,
    up_weight,
    down_weight,
    cotangent,
):
    sequence_length = tokens_in.shape[0]
    model_width = tokens_in.shape[1]
    devices_gx = lax.axis_size("gx")
    devices_gy = lax.axis_size("gy")
    part_width = model_width // devices_gy
    experts_all = router_weight.shape[1]
    router_lanes = jnp.pad(router_weight, ((0, 0), (0, LANES - experts_all)))
    pieces = [q_weight, key_matrix, value_matrix, router_lanes, out_weight]
    dense = kernels_fit() and experts_all <= 2 * TOP
    if dense:
        weights_all = gather_blocks(pieces, 1)
        weights_all = weights_all.reshape(-1, weights_all.shape[2])
    else:
        weights_all = lax.all_gather(jnp.concatenate(pieces, axis=1), "gx", axis=0, tiled=True)
    q_width, kv_width = q_weight.shape[1], key_matrix.shape[1]
    qkv_width = q_width + 2 * kv_width
    router_full = weights_all[:, qkv_width : qkv_width + experts_all]
    heads_local = q_width // HEAD_DIM
    kv_local = kv_width // HEAD_DIM
    inputs_f = tokens_in.astype(jnp.float32)
    scale_one = root_mean_scale(inputs_f)
    unit_one = inputs_f * scale_one
    shared = attention_shared(weights_all, doc_ids, query_norm_gain, k_gain)
    normalized_input, raw_rows, attended, *kept, attn_part = attend(
        tokens_in, attn_gain, shared, heads_local, kv_local
    )
    attn_total = attn_part + swap_cores(attn_part)
    residual = inputs_f + attn_total
    scale_two = root_mean_scale(residual)
    unit_two = residual * scale_two
    normed_ffn = (unit_two * ffn_gain).astype(jnp.bfloat16)
    logits = jnp.dot(normed_ffn, router_full, preferred_element_type=jnp.float32)
    expert_iota = jnp.arange(experts_all, dtype=jnp.int32)
    route_hits = routes[:, :, None] == expert_iota
    if dense:
        mixed_rows, grad_rows_sum, grad_logits, expert_grads = dense_experts(
            normed_ffn, logits, route_hits, cotangent, gate_weight[0], up_weight[0], down_weight[0]
        )
    else:
        mixed_rows, grad_rows_sum, grad_logits, expert_grads = sparse_experts(
            normed_ffn, logits, route_hits, routes, cotangent, gate_weight[0], up_weight[0], down_weight[0]
        )
    output = (residual + mixed_rows).astype(jnp.bfloat16)
    grad_out_f = cotangent.astype(jnp.float32)
    logit_lanes = jnp.pad(grad_logits, ((0, 0), (0, LANES - experts_all)))
    router_lanes = contract(normed_ffn, logit_lanes, 0, 0)
    grad_ffn_in = contract(grad_logits, router_full, 1, 1) + grad_rows_sum
    ffn_gain_term = jnp.sum(grad_ffn_in * unit_two, axis=0)
    grad_residual = grad_out_f + norm_back(grad_ffn_in * ffn_gain, unit_two, scale_two)
    grad_attn = grad_residual.astype(jnp.bfloat16)
    grad_qkv, head_gains, grad_normed_part = attend_back(
        grad_attn, shared, (raw_rows, *kept), heads_local, kv_local
    )
    q_gain_term, k_gain_term = head_gains[0], head_gains[1]
    grad_normed = grad_normed_part + swap_cores(grad_normed_part)
    attn_gain_term = jnp.sum(grad_normed * unit_one, axis=0)
    own_mask = (jnp.arange(model_width) // part_width == lax.axis_index("gy")).astype(jnp.float32)
    gains = (attn_gain_term * own_mask, ffn_gain_term * own_mask, q_gain_term, k_gain_term)
    if dense:
        router_blocks = router_lanes.astype(jnp.bfloat16).reshape(devices_gx, -1, LANES)
        factors = (normalized_input, grad_qkv, router_blocks, grad_attn, attended)
        lasts = (tokens_in, grad_residual, grad_normed, attn_gain.reshape(1, model_width))
        grad_q, grad_k, grad_v, grad_router, grad_out, gain_rows, grad_input = scatter_sums(
            factors, packed_gains(gains), lasts, kv_width, 4
        )
        gains = unpacked_gains(gain_rows, gains)
    else:
        sums = jnp.concatenate(
            [
                lax.psum_scatter(term, "gx", scatter_dimension=0, tiled=True)
                for term in (
                    contract(normalized_input, grad_qkv, 0, 0),
                    router_lanes,
                    contract(grad_attn, attended, 0, 0),
                )
            ],
            axis=1,
        )
        gains = lax.psum(gains, ("gx", "gy"))
        grad_q = sums[:, :q_width]
        grad_k = sums[:, q_width : q_width + kv_width]
        grad_v = sums[:, q_width + kv_width : qkv_width]
        grad_router = sums[:, qkv_width : qkv_width + LANES]
        grad_out = sums[:, qkv_width + LANES :]
        grad_input = grad_residual + norm_back(grad_normed * attn_gain, unit_one, scale_one)
        grad_input = grad_input.astype(jnp.bfloat16)
    gain_attn, gain_ffn, gain_query, gain_key = gains
    grad_router = grad_router[:, :experts_all]
    return (
        output,
        grad_input,
        grad_q,
        grad_k,
        grad_v,
        grad_out,
        grad_router,
        gain_attn,
        gain_ffn,
        gain_query,
        gain_key,
        expert_grads[0],
        expert_grads[1],
        expert_grads[2],
    )


def solution(mesh):
    return jax.shard_map(
        on_device,
        mesh=mesh,
        in_specs=(
            P("gx", None),
            P("gx", None),
            P("gx", None),
            P("gx", "gy"),
            P("gx", "gy"),
            P("gx", "gy"),
            P("gx", "gy"),
            P("gx", None),
            P(),
            P(),
            P(),
            P(),
            P("gx", None, "gy"),
            P("gx", None, "gy"),
            P("gx", "gy", None),
            P("gx", None),
        ),
        out_specs=(
            P("gx", None),
            P("gx", None),
            P("gx", "gy"),
            P("gx", "gy"),
            P("gx", "gy"),
            P("gx", "gy"),
            P("gx", None),
            P(),
            P(),
            P(),
            P(),
            P("gx", None, "gy"),
            P("gx", None, "gy"),
            P("gx", "gy", None),
        ),
        check_vma=False,
    )
```

```python
import functools
import math

import jax
import jax.numpy as jnp
from jax import lax
from jax.experimental import pallas as pl
from jax.experimental.pallas import tpu as pltpu
from jax.sharding import PartitionSpec as P

QUERY_HEADS = 32
KEY_VALUE_HEADS = 4
HEAD_DIM = 128
LANES = 128
TOP = 8


EPSILON = 1e-06
THETA = 1000000.0


def root_mean_scale(values):
    return lax.rsqrt(jnp.mean(values * values, axis=-1, keepdims=True) + EPSILON)


def rotary_tables(sequence_length, head_width):
    half_width = head_width // 2
    frequencies = THETA ** (-(2.0 * jnp.arange(half_width, dtype=jnp.float32)) / head_width)
    angles = jnp.arange(sequence_length, dtype=jnp.float32)[:, None] * frequencies[None, :]
    return (jnp.cos(angles)[:, None, :], jnp.sin(angles)[:, None, :])


def norm_back(grad_normed, normed_unit, scale_rows):
    return scale_rows * (
        grad_normed - normed_unit * jnp.mean(grad_normed * normed_unit, axis=-1, keepdims=True)
    )


def contract(first_op, second_op, first_dim, second_dim):
    return lax.dot_general(
        first_op,
        second_op,
        (((first_dim,), (second_dim,)), ((), ())),
        preferred_element_type=jnp.float32,
    )


MESH = pl.DeviceIdType.MESH
LEVELS = 4
PLANE = 4


def cut_rows(rows):
    near, far = 3 * rows // 4, rows // 4
    return (
        (0, near),
        ((0, near // 2), (near // 2, near // 2)),
        (near, far),
        ((near, far // 2), (near + far // 2, far // 2)),
    )


def neighbours():
    me, core = lax.axis_index("gx"), lax.axis_index("gy")
    level = me // PLANE
    x_side = me + 1 - 2 * (me % 2)
    y_side = me + 2 - 4 * ((me // 2) % 2)
    return me, core, level, x_side, y_side


def greet(level, targets, with_core, me, core):
    barrier = pltpu.get_barrier_semaphore()

    def hello(device):
        pl.semaphore_signal(barrier, inc=1, device_id=device, device_id_type=MESH)

    for target in targets:
        hello((target, core))
    if with_core:
        hello((me, 1 - core))

    @pl.when(level > 0)
    def _():
        hello((me - PLANE, core))

    @pl.when(level < LEVELS - 1)
    def _():
        hello((me + PLANE, core))

    inner = jnp.where(level > 0, 1, 0) + jnp.where(level < LEVELS - 1, 1, 0)
    pl.semaphore_wait(barrier, len(targets) + int(with_core) + inner)


def when(condition, action):
    if condition is None:
        action()
    else:
        pl.when(condition)(action)


def gather_kernel(count, *refs):
    pieces, out, own, piece_sem = refs[:count], refs[count], refs[count + 1], refs[count + 2]
    copies, lane = [], 0
    for i, piece in enumerate(pieces):
        place = own.at[:, pl.ds(lane, piece.shape[1])]
        copies.append(pltpu.make_async_copy(piece, place, piece_sem.at[i]))
        lane += piece.shape[1]
    for copy in copies:
        copy.start()
    for copy in copies:
        copy.wait()
    steps = gather_steps([own], [out], [None], refs[count + 3 :])
    for step in steps.order:
        step()
    steps.end()


class gather_steps:
    def __init__(self, ins, outs, pairs, sems):
        self.ins, self.outs, self.pairs = ins, outs, pairs
        self.send_sem, self.recv_sem, self.local_sem, self.pair_send, self.pair_recv = sems
        self.me, self.core, self.level, self.x_side, self.y_side = neighbours()
        self.diagonal = self.x_side + self.y_side - self.me
        self.spans = cut_rows(ins[0].shape[0])
        self.has_up, self.has_down = self.level < LEVELS - 1, self.level > 0
        self.up, self.down = (self.me + PLANE, self.core), (self.me - PLANE, self.core)
        self.to_x, self.to_y = (self.x_side, self.core), (self.y_side, self.core)
        self.sent, self.mirrored, self.everyone = [], [], range(len(ins))
        for k in self.everyone:
            self.own_copy(k).start()
        greet(self.level, (self.x_side, self.y_side), any(p is not None for p in pairs), self.me, self.core)
        self.order = [
            self.start,
            self.side_small,
            lambda: self.column(1),
            lambda: self.cross(0),
            lambda: self.column(2),
            self.start_planes,
            lambda: self.cross(1),
            lambda: self.column(3),
            lambda: self.planes(1),
            lambda: self.cross(2),
            lambda: self.planes(2),
            lambda: self.cross(3),
            lambda: self.planes(3),
            lambda: [self.halves(step) for step in range(LEVELS)],
        ]

    def send(self, condition, k, slot, source, first, number, span, target):
        def copy():
            there = self.outs[k].at[pl.ds(first, number), pl.ds(*span)]
            here = there
            if source == "own":
                here, there = self.ins[k].at[pl.ds(*span)], self.outs[k].at[first, pl.ds(*span)]
            return pltpu.make_async_remote_copy(
                here,
                there,
                self.send_sem.at[k, slot],
                self.recv_sem.at[k, slot],
                device_id=target,
                device_id_type=MESH,
            )

        when(condition, lambda: copy().start())
        self.sent.append((condition, copy))

    def mirror(self, condition, k, first, number, span, group):
        if self.pairs[k] is None:
            return
        slot = len(self.mirrored)

        def copy():
            return pltpu.make_async_remote_copy(
                self.outs[k].at[pl.ds(first, number), pl.ds(*span)],
                self.pairs[k].at[pl.ds(first, number), pl.ds(*span)],
                self.pair_send.at[slot],
                self.pair_recv.at[slot],
                device_id=(self.me, 1 - self.core),
                device_id_type=MESH,
            )

        when(condition, lambda: copy().start())
        self.mirrored.append((condition, copy, group))

    def arrive(self, condition, k, slot, first, number, span, group):
        place = self.outs[k].at[pl.ds(first, number), pl.ds(*span)]

        def wait():
            pltpu.make_async_remote_copy(
                place,
                place,
                self.send_sem.at[k, slot],
                self.recv_sem.at[k, slot],
                device_id=self.to_x,
                device_id_type=MESH,
            ).wait_recv()

        when(condition, wait)
        self.mirror(condition, k, first, number, span, group)

    def members(self, step):
        if step == 0:
            return [(None, 0, 0)]
        return [(self.level >= step, step, -step), (self.level + step < LEVELS, 3 + step, step)]

    def slot_of(self, group, index):
        return 6 + 7 * group + index

    last = 6 + 28

    def own_copy(self, k):
        return pltpu.make_async_copy(self.ins[k], self.outs[k].at[self.me], self.local_sem.at[k])

    def start(self):
        whole_a, half_a, whole_b, half_b = self.spans
        last, me = self.last, self.me
        for k in self.everyone:
            self.send(None, k, last, "own", me, 1, whole_b, self.to_x)
            self.send(None, k, last + 1, "own", me, 1, whole_b, self.to_y)
            self.send(self.has_up, k, 0, "own", me, 1, whole_a, self.up)
            self.send(self.has_down, k, 3, "own", me, 1, whole_a, self.down)
            self.send(None, k, self.slot_of(0, 0), "own", me, 1, whole_a, self.to_x)
            self.send(None, k, self.slot_of(1, 0), "own", me, 1, whole_a, self.to_y)

    def side_small(self):
        whole_a, half_a, whole_b, half_b = self.spans
        last = self.last
        for k in self.everyone:
            self.arrive(None, k, last, self.x_side, 1, whole_b, (0, 1))
            self.send(None, k, last + 3, "out", self.x_side, 1, half_b[1], self.to_y)
            self.arrive(None, k, last + 1, self.y_side, 1, whole_b, (0, 1))
            self.send(None, k, last + 2, "out", self.y_side, 1, half_b[0], self.to_x)
        for k in self.everyone:
            self.own_copy(k).wait()
            self.mirror(None, k, self.me, 1, (0, self.ins[k].shape[0]), (0, 0))
            self.arrive(None, k, last + 2, self.diagonal, 1, half_b[0], (0, 1))
            self.arrive(None, k, last + 3, self.diagonal, 1, half_b[1], (0, 1))

    def start_planes(self):
        whole_b = self.spans[2]
        for k in self.everyone:
            self.send(self.has_up, k, self.last + 4, "out", PLANE * self.level, PLANE, whole_b, self.up)
            self.send(self.has_down, k, self.last + 7, "out", PLANE * self.level, PLANE, whole_b, self.down)

    def cross(self, step):
        whole_a, half_a = self.spans[:2]
        for k in self.everyone:
            for condition, index, distance in self.members(step):
                first = self.x_side + PLANE * distance
                self.arrive(condition, k, self.slot_of(0, index), first, 1, whole_a, (distance, 0))
                self.send(condition, k, self.slot_of(3, index), "out", first, 1, half_a[1], self.to_y)
                first = self.y_side + PLANE * distance
                self.arrive(condition, k, self.slot_of(1, index), first, 1, whole_a, (distance, 0))
                self.send(condition, k, self.slot_of(2, index), "out", first, 1, half_a[0], self.to_x)

    def halves(self, step):
        half_a = self.spans[1]
        for k in self.everyone:
            for condition, index, distance in self.members(step):
                first = self.diagonal + PLANE * distance
                self.arrive(condition, k, self.slot_of(2, index), first, 1, half_a[0], (distance, 0))
                self.arrive(condition, k, self.slot_of(3, index), first, 1, half_a[1], (distance, 0))

    def column(self, step):
        whole_a = self.spans[0]
        for k in self.everyone:
            for condition, index, distance in self.members(step):
                first = self.me + PLANE * distance
                rising = distance < 0
                self.arrive(condition, k, step - 1 if rising else 2 + step, first, 1, whole_a, (distance, 0))
                if step < LEVELS - 1:
                    onward = condition & (self.has_up if rising else self.has_down)
                    slot = step if rising else 3 + step
                    self.send(onward, k, slot, "out", first, 1, whole_a, self.up if rising else self.down)
                self.send(condition, k, self.slot_of(0, index), "out", first, 1, whole_a, self.to_x)
                self.send(condition, k, self.slot_of(1, index), "out", first, 1, whole_a, self.to_y)

    def planes(self, step):
        whole_b = self.spans[2]
        for k in self.everyone:
            for condition, index, distance in self.members(step):
                first = PLANE * (self.level + distance)
                rising = distance < 0
                slot = self.last + (3 if rising else 6) + step
                self.arrive(condition, k, slot, first, PLANE, whole_b, (distance, 1))
                if step < LEVELS - 1:
                    onward = condition & (self.has_up if rising else self.has_down)
                    slot = self.last + (4 if rising else 7) + step
                    self.send(onward, k, slot, "out", first, PLANE, whole_b, self.up if rising else self.down)

    def paired_level(self, distance, parts):
        for condition, copy, group in self.mirrored:
            if group[0] == distance and group[1] in parts:
                when(condition, lambda copy=copy: copy().wait_recv())

    def end(self, levels_waited=False):
        for condition, copy in self.sent:
            when(condition, lambda copy=copy: copy().wait_send())
        for condition, copy, group in self.mirrored:
            when(condition, lambda copy=copy: copy().wait_send())
            if not levels_waited:
                when(condition, lambda copy=copy: copy().wait_recv())


GATHER_SLOTS = 6 + 28 + 10


def gather_semaphores(count, paired):
    dma = pltpu.SemaphoreType.DMA
    slots = (count, GATHER_SLOTS)
    pair_slots = (max(1, paired * (GATHER_SLOTS + 1)),)
    return [dma(slots), dma(slots), dma((count,)), dma(pair_slots), dma(pair_slots)]


def gather_blocks(pieces, collective_id):
    rows, width = pieces[0].shape[0], sum(piece.shape[1] for piece in pieces)
    low = pieces[0].dtype
    return pl.pallas_call(
        functools.partial(gather_kernel, len(pieces)),
        out_shape=jax.ShapeDtypeStruct((lax.axis_size("gx"), rows, width), low),
        in_specs=[pl.BlockSpec(memory_space=pl.ANY)] * len(pieces),
        out_specs=pl.BlockSpec(memory_space=pl.ANY),
        scratch_shapes=[
            pltpu.VMEM((rows, width), low),
            pltpu.SemaphoreType.DMA((len(pieces),)),
            *gather_semaphores(1, 0),
        ],
        compiler_params=pltpu.CompilerParams(collective_id=collective_id, has_side_effects=True),
    )(*pieces)


def dot_nn(left, right):
    return lax.dot_general(left, right, (((1,), (0,)), ((), ())), preferred_element_type=jnp.float32)


def dot_nt(left, right):
    return lax.dot_general(left, right, (((1,), (1,)), ((), ())), preferred_element_type=jnp.float32)


def experts_kernel(experts_all, *refs):
    rows_ref, grad_rows_ref, w_gate, w_up, w_down = refs[:5]
    weighted_out, grad_in_out, terms_out, gate_out, up_out, down_out, grads_own, grads_pair = refs[5:13]
    held, grads, w_in, left_in, left_down, weighted_ref, grad_in_ref, terms_ref = refs[13:21]
    sums_in, sums_down, turned, down_low, grad_sem, part_sem, w_sem, out_sem, sum_sem = refs[21:30]
    hidden, width = w_down.shape
    joins = [
        pltpu.make_async_copy(part, w_in.at[:, pl.ds(i * hidden, hidden)], w_sem.at[i])
        for i, part in enumerate((w_gate, w_up))
    ]
    for join in joins:
        join.start()
    rows = rows_ref.shape[0]
    grad_half = grad_rows_ref.at[pl.ds(pl.multiple_of(lax.axis_index("gy") * rows, rows), rows)]
    steps = gather_steps([rows_ref, grad_half], [held.at[0], grads_own], [held.at[1], grads_pair], refs[30:])
    level, core = steps.level, steps.core
    tiles = hidden // LANES
    visits = [
        level,
        jnp.where(level == 0, 1, level - 1),
        jnp.where(level == 0, 2, jnp.where(level == 3, 1, level + 1)),
        jnp.where(level < 2, 3, 0),
    ]

    def fetch(turn, half):
        return pltpu.make_async_copy(
            (grads_own, grads_pair)[half].at[pl.ds(PLANE * visits[turn], PLANE)],
            grads.at[turn % 2, half],
            grad_sem.at[turn % 2, half],
        )

    part_rows = {None: (0, rows), 0: steps.spans[0], 1: steps.spans[2]}

    def fetch_part(part, half):
        span = pl.ds(*part_rows[part])
        return pltpu.make_async_copy(
            (grads_own, grads_pair)[half].at[pl.ds(PLANE * visits[-1], PLANE), span],
            grads.at[(LEVELS - 1) % 2, half, :, span],
            part_sem.at[part, half],
        )

    def fetches(turn, part):
        return [fetch(turn, half) if part is None else fetch_part(part, half) for half in range(2)]

    lane = lax.broadcasted_iota(jnp.int32, (1, LANES), 1)
    expert = steps.me
    gate_pick = (((lane == expert) | (lane == experts_all + expert))).astype(jnp.float32)
    high_lane = (lane == 2 * experts_all * core + expert).astype(jnp.float32)
    low_lane = (lane == 2 * experts_all * core + experts_all + expert).astype(jnp.float32)

    def leave(turn):
        span = pl.ds(PLANE * visits[turn], PLANE)
        pairs = ((weighted_ref, weighted_out), (grad_in_ref, grad_in_out), (terms_ref, terms_out))
        return [
            pltpu.make_async_copy(here.at[:, span], there.at[:, span], out_sem.at[turn, i])
            for i, (here, there) in enumerate(pairs)
        ]

    def forward(turn, begin=0, end=4, part=None):
        first, (row, number) = PLANE * visits[turn], part_rows[part]
        together = 2 if part is None else PLANE
        group, per_half, span_rows = together * number, PLANE // together, pl.ds(row, number)
        if begin == 0:
            for copy in fetches(turn, part):
                copy.wait()

        def body(step, carry):
            half, pair = step // per_half, step % per_half
            at = first + together * pair
            blocks = pl.ds(at, together)
            lanes = held[half, blocks, span_rows, pl.ds(width, LANES)].reshape(group, LANES)
            gate_rows = jnp.sum(lanes.astype(jnp.float32) * gate_pick, axis=1, keepdims=True)
            grad_rows = grads[turn % 2, half, pl.ds(together * pair, together), span_rows].reshape(group, width)
            token_rows = held[half, blocks, span_rows, pl.ds(0, width)].reshape(group, width)
            grad_hidden = dot_nt(grad_rows, w_down[...])
            both = dot_nn(token_rows, w_in[...])
            terms = jnp.zeros((group, 1), jnp.float32)
            column = pl.multiple_of(2 * PLANE * row + step * group, LANES)
            for j in range(tiles):
                gate_in = both[:, j * LANES : (j + 1) * LANES]
                up_in = both[:, hidden + j * LANES : hidden + (j + 1) * LANES]
                back = grad_hidden[:, j * LANES : (j + 1) * LANES]
                gate_sigmoid = 1.0 / (1.0 + jnp.exp(-gate_in))
                gate_swish = gate_in * gate_sigmoid
                activated = gate_swish * up_in
                terms = terms + jnp.sum(activated * back, axis=1, keepdims=True)
                grad_act = gate_rows * back
                weighted = gate_rows * activated
                grad_gate = grad_act * up_in * gate_sigmoid * (1.0 + gate_in * (1.0 - gate_sigmoid))
                grad_up = grad_act * gate_swish
                for value, array, tile, left in (
                    (weighted, weighted_ref, j, left_down),
                    (grad_gate, grad_in_ref, j, left_in),
                    (grad_up, grad_in_ref, tiles + j, left_in),
                ):
                    span = pl.ds(tile * LANES, LANES)
                    low = value.astype(jnp.bfloat16).reshape(together, number, LANES)
                    array[half, blocks, span_rows, span] = low
                    left[span, pl.ds(column, group)] = value.T.astype(jnp.bfloat16)
            high = terms.astype(jnp.bfloat16).astype(jnp.float32)
            spread = high * high_lane + (terms - high) * low_lane
            terms_ref[half, blocks, span_rows] = spread.astype(jnp.bfloat16).reshape(together, number, LANES)
            return carry

        lax.fori_loop(begin, min(end, 2 * per_half), body, 0)
        if end == 4 and part != 0:
            for copy in leave(turn):
                copy.start()

    wide = 256

    def weights(turn, begin=0, end=8, part=None):
        first, (row, number) = PLANE * visits[turn], part_rows[part]
        span_rows, depth = pl.ds(row, number), 2 * PLANE * number
        columns = pl.ds(2 * PLANE * row, depth)

        def body(step, carry):
            span = pl.ds(pl.multiple_of(step * wide, wide), wide)
            token_rows = held[:, pl.ds(first, PLANE), span_rows, span].reshape(depth, wide)
            grad_rows = grads[turn % 2, :, :, span_rows, span].reshape(depth, wide)
            part_in = dot_nn(left_in[:, columns], token_rows)
            part_down = dot_nn(left_down[:, columns], grad_rows)
            if turn:
                part_in = sums_in[:, span] + part_in
                part_down = sums_down[:, span] + part_down
            if part != 1:
                sums_in[:, span] = part_in
                sums_down[:, span] = part_down
            else:
                for i in range(2):
                    turned[i, span] = part_in[i * hidden : (i + 1) * hidden].T.astype(jnp.bfloat16)
                down_low[:, span] = part_down.astype(jnp.bfloat16)
                for copy in leave_sums(step):
                    copy.start()
            return carry

        lax.fori_loop(begin, end, body, 0)

    def leave_sums(step):
        span = pl.ds(pl.multiple_of(step * wide, wide), wide)
        return [
            pltpu.make_async_copy(turned.at[0, span], gate_out.at[span], sum_sem.at[step, 0]),
            pltpu.make_async_copy(turned.at[1, span], up_out.at[span], sum_sem.at[step, 1]),
            pltpu.make_async_copy(down_low.at[:, span], down_out.at[:, span], sum_sem.at[step, 2]),
        ]

    def level_ready(turn, part=None):
        parts = (0, 1) if part is None else (part,)
        if turn == 0:
            steps.paired_level(0, parts)
        for distance in range(-3, 4):
            if turn and distance:
                wanted = visits[turn] == level + distance
                pl.when(wanted)(lambda distance=distance: steps.paired_level(distance, parts))
        for copy in fetches(turn, part):
            copy.start()

    steps.start()
    steps.side_small()
    steps.column(1)
    steps.cross(0)
    for join in joins:
        join.wait()
    steps.column(2)
    steps.start_planes()
    steps.halves(0)
    steps.cross(1)
    level_ready(0)
    forward(0, 0, 4)
    steps.column(3)
    steps.planes(1)
    weights(0, 0, 4)
    steps.cross(2)
    steps.halves(1)
    level_ready(1)
    weights(0, 4, 8)
    forward(1, 0, 4)
    steps.planes(2)
    weights(1, 0, 4)
    steps.cross(3)
    steps.halves(2)
    level_ready(2)
    weights(1, 4, 8)
    forward(2, 0, 4)
    steps.halves(3)
    level_ready(3, 0)
    weights(2, 0, 8)
    forward(3, part=0)
    weights(3, part=0)
    steps.planes(3)
    level_ready(3, 1)
    forward(3, part=1)
    weights(3, part=1)
    for turn in range(LEVELS):
        for copy in leave(turn):
            copy.wait()

    def last_sums(step, carry):
        for copy in leave_sums(step):
            copy.wait()
        return carry

    lax.fori_loop(0, width // wide, last_sums, 0)
    steps.end(levels_waited=True)


def experts_products(rows, grad_rows, w_gate, w_up, w_down, experts_all, collective_id):
    blocks, low, count = lax.axis_size("gx"), jnp.bfloat16, rows.shape[0]
    hidden, width = w_down.shape
    everywhere = pl.BlockSpec(memory_space=pl.ANY)
    block_shape = (2, blocks, count)
    shapes = [
        jax.ShapeDtypeStruct((*block_shape, hidden), low),
        jax.ShapeDtypeStruct((*block_shape, 2 * hidden), low),
        jax.ShapeDtypeStruct((*block_shape, LANES), low),
        jax.ShapeDtypeStruct((width, hidden), low),
        jax.ShapeDtypeStruct((width, hidden), low),
        jax.ShapeDtypeStruct((hidden, width), low),
        *[jax.ShapeDtypeStruct((blocks, count, width), low)] * 2,
    ]
    level_rows = 2 * PLANE * count
    dma = pltpu.SemaphoreType.DMA
    return pl.pallas_call(
        functools.partial(experts_kernel, experts_all),
        out_shape=shapes,
        in_specs=[everywhere] * 4 + [pl.BlockSpec(memory_space=pltpu.VMEM)],
        out_specs=[everywhere] * 8,
        scratch_shapes=[
            pltpu.VMEM((*block_shape, rows.shape[1]), low),
            pltpu.VMEM((2, 2, PLANE, count, width), low),
            pltpu.VMEM((width, 2 * hidden), low),
            pltpu.VMEM((2 * hidden, level_rows), low),
            pltpu.VMEM((hidden, level_rows), low),
            *[pltpu.VMEM(shape.shape, low) for shape in shapes[:3]],
            pltpu.VMEM((2 * hidden, width), jnp.float32),
            pltpu.VMEM((hidden, width), jnp.float32),
            pltpu.VMEM((2, width, hidden), low),
            pltpu.VMEM((hidden, width), low),
            dma((2, 2)),
            dma((2, 2)),
            dma((2,)),
            dma((LEVELS, 3)),
            dma((width // 256, 3)),
            *gather_semaphores(2, 2),
        ],
        compiler_params=pltpu.CompilerParams(
            collective_id=collective_id, has_side_effects=True, vmem_limit_bytes=63 * 1024 * 1024
        ),
    )(rows, grad_rows, w_gate, w_up, w_down)[:6]


class scatter_moves:
    def __init__(self, held, out):
        self.mine, self.half_y, self.half_x, self.full_x, self.full_y, self.slots_a, self.slots_b, self.side_b = held[:8]
        self.send_sem, self.recv_sem, self.chain_send, self.chain_recv = held[8:12]
        self.out = out
        self.me, self.core, level, x_side, y_side = neighbours()
        self.level = level
        self.up, self.down = (self.me + PLANE, self.core), (self.me - PLANE, self.core)
        self.to_x, self.to_y = (x_side, self.core), (y_side, self.core)
        self.x_at, self.y_at, self.own_at = x_side % PLANE, y_side % PLANE, self.me % PLANE
        self.diagonal_at = (x_side + y_side - self.me) % PLANE
        forward = jnp.where(level < 2, 1, 0)
        self.order = [3 * forward, 2 * forward + (1 - forward), level + 1 - 2 * (level % 2), level]
        self.rows, self.width = self.mine.shape[1:]
        self.spans = cut_rows(self.rows)
        self.sent = []

    def send(self, condition, source, target_ref, ssem, rsem, target):
        def copy():
            return pltpu.make_async_remote_copy(
                source, target_ref, ssem, rsem, device_id=target, device_id_type=MESH
            )

        when(condition, lambda: copy().start())
        self.sent.append((condition, copy))

    def arrive(self, condition, target_ref, rsem):
        def wait():
            pltpu.make_async_remote_copy(
                target_ref, target_ref, rsem, rsem, device_id=self.to_x, device_id_type=MESH
            ).wait_recv()

        when(condition, wait)

    def add(self, condition, height, target, *terms, step=16):
        def run():
            def body(i, carry):
                at = pl.multiple_of(i * step, step)
                total = target(at, step)[...].astype(jnp.float32)
                for term in terms:
                    total = total + term(at, step)[...].astype(jnp.float32)
                target(at, step)[...] = total.astype(jnp.bfloat16)
                return carry

            lax.fori_loop(0, height // step, body, 0)

        when(condition, run)

    def rows_of(self, ref, *index, start=0):
        return lambda at, step: ref.at[(*index, pl.ds(start + at, step))]

    def turn_sems(self, turn):
        return [(self.send_sem.at[6 * turn + i], self.recv_sem.at[6 * turn + i]) for i in range(6)]

    def half_spans(self):
        half_a = self.spans[1]
        return half_a[0][1], pl.ds(*half_a[0]), pl.ds(*half_a[1])

    def first(self, turn):
        base, at = PLANE * self.order[turn], self.turn_sems(turn)
        _, lower, upper = self.half_spans()
        mine, to_x, to_y = self.mine, self.to_x, self.to_y
        self.send(None, mine.at[base + self.diagonal_at, lower], self.half_y.at[turn], *at[0], to_y)
        self.send(None, mine.at[base + self.diagonal_at, upper], self.half_x.at[turn], *at[1], to_x)
        self.send(None, mine.at[base + self.x_at, upper], self.full_x.at[turn, upper], *at[2], to_x)
        self.send(None, mine.at[base + self.y_at, lower], self.full_y.at[turn, lower], *at[3], to_y)

    def second(self, turn):
        base, at = PLANE * self.order[turn], self.turn_sems(turn)
        height, lower, upper = self.half_spans()
        mine, rows_of = self.mine, self.rows_of
        self.arrive(None, self.half_y.at[turn], at[0][1])
        self.add(None, height, rows_of(mine, base + self.x_at), rows_of(self.half_y, turn))
        self.send(None, mine.at[base + self.x_at, lower], self.full_x.at[turn, lower], *at[4], self.to_x)
        self.arrive(None, self.half_x.at[turn], at[1][1])
        self.add(None, height, rows_of(mine, base + self.y_at, start=height), rows_of(self.half_x, turn))
        self.send(None, mine.at[base + self.y_at, upper], self.full_y.at[turn, upper], *at[5], self.to_y)

    def chain(self, which, turn, block, slots, spread):
        to_level, level = self.order[turn], self.level
        rising, falling = to_level > level, to_level < level
        begins = (rising & (level == 0)) | (falling & (level == LEVELS - 1))
        middle = (rising | falling) & jnp.logical_not(begins)
        self.arrive(middle, slots.at[to_level], self.chain_recv.at[which, to_level])
        spread(middle, to_level)
        outgoing = self.chain_send.at[which, to_level]
        self.send(rising, block, slots.at[to_level], outgoing, self.chain_recv.at[which, to_level], self.up)
        at = jnp.where(to_level == level - 1, LEVELS, to_level)
        self.send(falling, block, slots.at[at], outgoing, self.chain_recv.at[which, at], self.down)

    def add_small(self, condition, base, slot):
        start, number = self.spans[2]
        for column in range(PLANE):
            self.add(
                condition,
                number,
                self.rows_of(self.mine, base + column, start=start),
                self.rows_of(self.slots_b, slot, column),
            )

    def chain_small(self, turn):
        if turn == LEVELS - 1:
            return
        base = PLANE * self.order[turn]
        block = self.mine.at[pl.ds(base, PLANE), pl.ds(*self.spans[2])]
        self.chain(1, turn, block, self.slots_b, lambda condition, slot: self.add_small(condition, base, slot))

    def plane_arrives(self, turn):
        at = self.turn_sems(turn)
        _, lower, upper = self.half_spans()
        self.arrive(None, self.full_x.at[turn, upper], at[2][1])
        self.arrive(None, self.full_y.at[turn, lower], at[3][1])
        self.arrive(None, self.full_x.at[turn, lower], at[4][1])
        self.arrive(None, self.full_y.at[turn, upper], at[5][1])

    def chain_large(self, turn):
        if turn == LEVELS - 1:
            return
        own, number = PLANE * self.order[turn] + self.own_at, self.spans[0][1]
        rows_of, mine = self.rows_of, self.mine
        self.plane_arrives(turn)
        self.add(None, number, rows_of(mine, own), rows_of(self.full_x, turn), rows_of(self.full_y, turn))
        self.chain(
            0,
            turn,
            mine.at[own, pl.ds(*self.spans[0])],
            self.slots_a,
            lambda condition, slot: self.add(condition, number, rows_of(mine, own), rows_of(self.slots_a, slot)),
        )

    def side(self):
        short = self.spans[3][0][1]
        spans = [pl.ds(0, short), pl.ds(short, short), pl.ds(2 * short, 2 * short), pl.ds(4 * short, 2 * short)]
        return [(self.side_b.at[span], self.send_sem.at[24 + i], self.recv_sem.at[24 + i]) for i, span in enumerate(spans)]

    def arrivals(self):
        return ((self.level > 0, self.level), (self.level < LEVELS - 1, LEVELS))

    def end_small(self):
        base, mine, half_b = PLANE * self.level, self.mine, self.spans[3]
        for condition, slot in self.arrivals():
            self.arrive(condition, self.slots_b.at[slot], self.chain_recv.at[1, slot])
            self.add_small(condition, base, slot)
        side = self.side()
        self.send(None, mine.at[base + self.diagonal_at, pl.ds(*half_b[0])], *side[0], self.to_y)
        self.send(None, mine.at[base + self.diagonal_at, pl.ds(*half_b[1])], *side[1], self.to_x)

    def end_sides(self):
        base, mine, rows_of = PLANE * self.level, self.mine, self.rows_of
        whole_b, half_b = self.spans[2:]
        side, short = self.side(), half_b[0][1]
        self.plane_arrives(LEVELS - 1)
        self.arrive(None, side[0][0], side[0][2])
        self.add(None, short, rows_of(mine, base + self.x_at, start=half_b[0][0]), rows_of(self.side_b))
        self.send(None, mine.at[base + self.x_at, pl.ds(*whole_b)], *side[2], self.to_x)
        self.arrive(None, side[1][0], side[1][2])
        self.add(None, short, rows_of(mine, base + self.y_at, start=half_b[1][0]), rows_of(self.side_b, start=short))
        self.send(None, mine.at[base + self.y_at, pl.ds(*whole_b)], *side[3], self.to_y)

    def end_sums(self, base):
        whole_a, half_a, whole_b, half_b = self.spans
        own, out, mine, step = PLANE * self.level + self.own_at, self.out, self.mine, 16
        full_x, full_y, slots_a, side_b = self.full_x, self.full_y, self.slots_a, self.side_b

        def place(at):
            return pl.ds(pl.multiple_of(base + at, step), step)

        def tail_a(i, carry):
            at = pl.multiple_of(i * step, step)
            span, turn = pl.ds(at, step), LEVELS - 1
            total = mine[own, span].astype(jnp.float32)
            total = total + full_x[turn, span].astype(jnp.float32) + full_y[turn, span].astype(jnp.float32)
            out[place(at)] = total
            return carry

        lax.fori_loop(0, whole_a[1] // step, tail_a, 0)
        for condition, slot in self.arrivals():
            self.arrive(condition, slots_a.at[slot], self.chain_recv.at[0, slot])

            def more(slot=slot):
                def body(i, carry):
                    at = pl.multiple_of(i * step, step)
                    out[place(at)] = out[place(at)] + slots_a[slot, pl.ds(at, step)].astype(jnp.float32)
                    return carry

                lax.fori_loop(0, whole_a[1] // step, body, 0)

            when(condition, more)
        side, short = self.side(), half_b[0][1]
        self.arrive(None, side[2][0], side[2][2])
        self.arrive(None, side[3][0], side[3][2])

        def tail_b(i, carry):
            at = pl.multiple_of(i * step, step)
            total = mine[own, pl.ds(whole_b[0] + at, step)].astype(jnp.float32)
            total = total + side_b[pl.ds(2 * short + at, step)].astype(jnp.float32)
            total = total + side_b[pl.ds(4 * short + at, step)].astype(jnp.float32)
            out[place(whole_b[0] + at)] = total
            return carry

        lax.fori_loop(0, whole_b[1] // step, tail_b, 0)

    def end_waits(self):
        for condition, copy in self.sent:
            when(condition, lambda copy=copy: copy().wait_send())


def scatter_places(blocks, rows, width):
    near, far, low, dma = 3 * rows // 4, rows // 4, jnp.bfloat16, pltpu.SemaphoreType.DMA
    shapes = [
        (blocks, rows, width),
        (LEVELS, near // 2, width),
        (LEVELS, near // 2, width),
        (LEVELS, near, width),
        (LEVELS, near, width),
        (LEVELS + 1, near, width),
        (LEVELS + 1, PLANE, far, width),
        (3 * far, width),
    ]
    return [pltpu.VMEM(shape, low) for shape in shapes] + [dma((28,)), dma((28,)), dma((2, 5)), dma((2, 5))]


PLACES = 12


def scatter_kernel(*refs):
    normed, grad_qkv, router_term, grad_attn, attended, gain_ref = refs[:6]
    tokens, grad_residual, grad_normed, attn_gain = refs[6:10]
    pieces_out, (gain_out, grad_input) = refs[10:15], refs[15:17]
    held, (out, load_sem, leave_sem, gain_slots, gain_send, gain_recv) = refs[17:-6], refs[-6:]
    moves = scatter_moves(held, out)
    me, core, level = moves.me, moves.core, moves.level
    far = me + 2 * PLANE - 4 * PLANE * (level // 2)
    partners = ((me, 1 - core), moves.to_x, moves.to_y, (me + PLANE - 2 * PLANE * (level % 2), core), (far, core))

    def gain_copy(turn):
        return pltpu.make_async_remote_copy(
            gain_slots.at[2 * turn],
            gain_slots.at[2 * turn + 1],
            gain_send.at[turn],
            gain_recv.at[turn],
            device_id=partners[turn],
            device_id_type=MESH,
        )

    def gain_step(turn):
        if turn == 0:
            gain_slots[0] = gain_ref[...]
        else:
            gain_copy(turn - 1).wait_recv()
            gain_slots[2 * turn] = gain_slots[2 * turn - 2] + gain_slots[2 * turn - 1]
        if turn < len(partners):
            gain_copy(turn).start()
        else:
            gain_out[...] = gain_slots[2 * turn]

    router_lane = grad_qkv.shape[1]

    def load(turn):
        span = pl.ds(PLANE * moves.order[turn], PLANE)
        place = moves.mine.at[span, :, pl.ds(router_lane, LANES)]
        return pltpu.make_async_copy(router_term.at[span], place, load_sem.at[turn])

    def products(turn):
        level_rows, wide = PLANE * moves.rows, 256
        span = pl.ds(PLANE * moves.order[turn], PLANE)
        features = pl.ds(pl.multiple_of(moves.order[turn] * level_rows, level_rows), level_rows)
        for left, right, lane in ((normed, grad_qkv, 0), (grad_attn, attended, router_lane + LANES)):
            left_rows = left[:, features].astype(jnp.float32).T.astype(jnp.bfloat16)

            def body(step, carry, left_rows=left_rows, right=right, lane=lane):
                at = pl.multiple_of(step * wide, wide)
                value = dot_nn(left_rows, right[:, pl.ds(at, wide)]).astype(jnp.bfloat16)
                lanes = pl.ds(pl.multiple_of(lane + at, LANES), wide)
                moves.mine[span, :, lanes] = value.reshape(PLANE, moves.rows, wide)
                return carry

            lax.fori_loop(0, right.shape[1] // wide, body, 0)

    def input_rows():
        step = 16

        def body(i, carry):
            span = pl.ds(pl.multiple_of(i * step, step), step)
            unit, scale = unit_rows(tokens[span].astype(jnp.float32))
            grad = grad_normed[span] * attn_gain[...]
            grad = scale * (grad - unit * jnp.mean(grad * unit, axis=1, keepdims=True))
            grad_input[span] = (grad_residual[span] + grad).astype(jnp.bfloat16)
            return carry

        lax.fori_loop(0, tokens.shape[0] // step, body, 0)

    def leave():
        copies, lane = [], 0
        for i, piece in enumerate(pieces_out):
            width = piece.shape[1]
            copies.append(pltpu.make_async_copy(out.at[:, pl.ds(lane, width)], piece, leave_sem.at[i]))
            lane += width
        return copies

    for turn in range(LEVELS):
        load(turn).start()
    products(0)
    greet(level, (moves.to_x[0], moves.to_y[0], far), True, me, core)
    gain_step(0)
    for turn in range(LEVELS):
        if turn:
            products(turn)
        load(turn).wait()
        moves.first(turn)
        moves.chain_small(turn)
    input_rows()
    for turn in range(LEVELS - 1):
        moves.second(turn)
        gain_step(turn + 1)
        if turn:
            moves.chain_large(turn - 1)
    moves.second(LEVELS - 1)
    gain_step(4)
    moves.chain_large(LEVELS - 2)
    moves.end_small()
    moves.end_sides()
    gain_step(5)
    moves.end_sums(0)
    for copy in leave():
        copy.start()
    for turn in range(len(partners)):
        gain_copy(turn).wait_send()
    moves.end_waits()
    for copy in leave():
        copy.wait()


def scatter_sums(factors, gains, lasts, kv_width, collective_id):
    _, grad_qkv, router_term, _, attended = factors
    blocks, rows, _ = router_term.shape
    widths = (grad_qkv.shape[1] - 2 * kv_width, kv_width, kv_width, LANES, attended.shape[1])
    dma, tokens = pltpu.SemaphoreType.DMA, lasts[0]
    vmem, everywhere = pl.BlockSpec(memory_space=pltpu.VMEM), pl.BlockSpec(memory_space=pl.ANY)
    return pl.pallas_call(
        scatter_kernel,
        out_shape=[
            *[jax.ShapeDtypeStruct((rows, width), jnp.float32) for width in widths],
            jax.ShapeDtypeStruct(gains.shape, gains.dtype),
            jax.ShapeDtypeStruct(tokens.shape, tokens.dtype),
        ],
        in_specs=[vmem, vmem, everywhere, vmem, vmem, vmem, vmem, vmem, vmem, vmem],
        out_specs=[everywhere] * 5 + [vmem] * 2,
        scratch_shapes=[
            *scatter_places(blocks, rows, sum(widths)),
            pltpu.VMEM((rows, sum(widths)), jnp.float32),
            dma((LEVELS,)),
            dma((5,)),
            pltpu.VMEM((11, *gains.shape), gains.dtype),
            dma((5,)),
            dma((5,)),
        ],
        compiler_params=pltpu.CompilerParams(
            collective_id=collective_id, has_side_effects=True, vmem_limit_bytes=63 * 1024 * 1024
        ),
    )(*factors, gains, *lasts)


def return_kernel(grad_in, weighted, terms, w_gate, w_up, w_down, back_out, mixed_out, *refs):
    streams = [
        scatter_moves(refs[:PLACES], back_out),
        scatter_moves(refs[PLACES : 2 * PLACES], mixed_out),
    ]
    sibling, away, left, right_in, right_down = refs[2 * PLACES : 2 * PLACES + 5]
    pair_send, pair_recv, left_sem, right_sem, term_sem, ready_sem, credit = refs[2 * PLACES + 5 :]
    me, core, order, rows = streams[0].me, streams[0].core, streams[0].order, streams[0].rows
    hidden, features = w_down.shape
    depths, lefts = (2 * hidden, hidden), (grad_in, weighted)
    turns, wide = 2 * LEVELS, 256
    rights = [
        pltpu.make_async_copy(w_gate, right_in.at[:, pl.ds(0, hidden)], right_sem.at[0]),
        pltpu.make_async_copy(w_up, right_in.at[:, pl.ds(hidden, hidden)], right_sem.at[1]),
        pltpu.make_async_copy(w_down, right_down, right_sem.at[2]),
    ]

    def level_span(turn):
        return pl.ds(PLANE * order[turn % LEVELS], PLANE)

    def left_copy(turn):
        stream = turn // LEVELS
        return pltpu.make_async_copy(
            lefts[stream].at[:, level_span(turn)],
            left.at[turn % 2, :, :, :, pl.ds(0, depths[stream])],
            left_sem.at[turn % 2],
        )

    def term_copy(turn, half):
        lanes = pl.ds(features, LANES)
        place = away.at[turn % 2, :, :, lanes] if half else streams[0].mine.at[level_span(turn), :, lanes]
        return pltpu.make_async_copy(terms.at[half, level_span(turn)], place, term_sem.at[half])

    def width_of(turn):
        return streams[turn // LEVELS].width

    def hand(turn):
        lanes = pl.ds(0, width_of(turn))
        return pltpu.make_async_remote_copy(
            away.at[turn % 2, :, :, lanes],
            sibling.at[turn % 2, :, :, lanes],
            pair_send.at[turn],
            pair_recv.at[turn],
            device_id=(me, 1 - core),
            device_id_type=MESH,
        )

    def product(turn, half, store):
        stream, slot = turn // LEVELS, turn % 2
        factor = left[slot, half, :, :, pl.ds(0, depths[stream])].reshape(PLANE * rows, depths[stream])

        def body(step, carry):
            span = pl.ds(pl.multiple_of(step * wide, wide), wide)
            value = dot_nt(factor, right_in[span]) if stream == 0 else dot_nn(factor, right_down[:, span])
            store(span, value.reshape(PLANE, rows, wide))
            return carry

        lax.fori_loop(0, features // wide, body, 0)

    def hand_over(turn):
        left_copy(turn).wait()
        if turn + 1 < turns:
            left_copy(turn + 1).start()
        if turn < LEVELS:
            term_copy(turn, 1).start()
            term_copy(turn, 0).start()

        def store(span, value):
            away[turn % 2, :, :, span] = value.astype(jnp.bfloat16)

        product(turn, 1, store)
        if turn < LEVELS:
            term_copy(turn, 1).wait()
            term_copy(turn, 0).wait()
        if turn == 0:
            greet(streams[0].level, (streams[0].to_x[0], streams[0].to_y[0]), True, me, core)
        if turn >= 2:
            pl.semaphore_wait(credit, 1)
        hand(turn).start()

    def settle(turn):
        hand(turn).wait()
        mine, slot = streams[turn // LEVELS].mine, turn % 2

        def store(span, value):
            value = value + sibling[slot, :, :, span].astype(jnp.float32)
            mine[level_span(turn), :, span] = value.astype(jnp.bfloat16)

        product(turn, 0, store)
        if turn < LEVELS:
            lanes = pl.ds(features, LANES)
            value = mine[level_span(turn), :, lanes].astype(jnp.float32)
            value = value + sibling[slot, :, :, lanes].astype(jnp.float32)
            mine[level_span(turn), :, lanes] = value.astype(jnp.bfloat16)
        if turn + 2 < turns:
            pl.semaphore_signal(credit, inc=1, device_id=(me, 1 - core), device_id_type=MESH)

    def exchange(stream, core_of_rows):
        out = streams[stream].out
        span = pl.ds(pl.multiple_of(core_of_rows * rows, rows), rows)
        return pltpu.make_async_remote_copy(
            out.at[span],
            out.at[span],
            ready_sem.at[stream, 0],
            ready_sem.at[stream, 1],
            device_id=(me, 1 - core),
            device_id_type=MESH,
        )

    def end(stream):
        streams[stream].end_sums(core * rows)
        exchange(stream, core).start()

    left_copy(0).start()
    for copy in rights:
        copy.start()
    for copy in rights:
        copy.wait()
    hand_over(0)
    for turn in range(turns + 2):
        if turn < turns:
            stream = streams[turn // LEVELS]
            settle(turn)
            stream.first(turn % LEVELS)
            if turn + 1 < turns:
                hand_over(turn + 1)
            stream.chain_small(turn % LEVELS)
        if 1 <= turn <= turns:
            streams[(turn - 1) // LEVELS].second((turn - 1) % LEVELS)
        if turn >= 2:
            streams[(turn - 2) // LEVELS].chain_large((turn - 2) % LEVELS)
        if turn == LEVELS + 1:
            streams[0].end_small()
        if turn == LEVELS + 2:
            streams[0].end_sides()
        if turn == LEVELS + 3:
            end(0)
    streams[1].end_small()
    streams[1].end_sides()
    end(1)
    for stream in range(2):
        exchange(stream, 1 - core).wait_recv()
        exchange(stream, core).wait_send()
        streams[stream].end_waits()


def return_sums(grad_in, weighted, terms, w_gate, w_up, w_down, collective_id):
    low, dma = jnp.bfloat16, pltpu.SemaphoreType.DMA
    blocks, rows, depth = grad_in.shape[1:]
    hidden, features = w_down.shape
    wide = features + LANES
    vmem, everywhere = pl.BlockSpec(memory_space=pltpu.VMEM), pl.BlockSpec(memory_space=pl.ANY)
    slots = pltpu.VMEM((2, PLANE, rows, wide), low)
    return pl.pallas_call(
        return_kernel,
        out_shape=[
            jax.ShapeDtypeStruct((2 * rows, wide), jnp.float32),
            jax.ShapeDtypeStruct((2 * rows, features), jnp.float32),
        ],
        in_specs=[everywhere] * 6,
        out_specs=[vmem] * 2,
        scratch_shapes=[
            *scatter_places(blocks, rows, wide),
            *scatter_places(blocks, rows, features),
            slots,
            slots,
            pltpu.VMEM((2, 2, PLANE, rows, depth), low),
            pltpu.VMEM((features, depth), low),
            pltpu.VMEM((hidden, features), low),
            dma((2 * LEVELS,)),
            dma((2 * LEVELS,)),
            dma((2,)),
            dma((3,)),
            dma((2,)),
            dma((2, 2)),
            pltpu.SemaphoreType.REGULAR,
        ],
        compiler_params=pltpu.CompilerParams(
            collective_id=collective_id, has_side_effects=True, vmem_limit_bytes=63 * 1024 * 1024
        ),
    )(grad_in, weighted, terms, w_gate, w_up, w_down)


def kernels_fit():
    return lax.axis_size("gx") == LEVELS * PLANE and lax.axis_size("gy") == 2


def packed_gains(vectors):
    rows = jnp.concatenate([vector.reshape(-1, HEAD_DIM) for vector in vectors], axis=0)
    return jnp.pad(rows, ((0, -rows.shape[0] % 8), (0, 0)))


def unpacked_gains(rows, vectors):
    sums, at = [], 0
    for vector in vectors:
        length = vector.shape[0] // HEAD_DIM
        sums.append(rows[at : at + length].reshape(-1))
        at += length
    return sums


def two_parts(values):
    high = lax.reduce_precision(values, 8, 7)
    return high.astype(jnp.bfloat16), (values - high).astype(jnp.bfloat16)


def sparse_experts(normed_ffn, logits, route_hits, routes, cotangent, w_gate, w_up, w_down):
    sequence_length, model_width = normed_ffn.shape
    experts_all = logits.shape[1]
    devices_gx = lax.axis_size("gx")
    part_width = model_width // lax.axis_size("gy")
    capacity = 5 * sequence_length * TOP // (4 * experts_all)
    pairs_count = sequence_length * TOP
    hits_float = route_hits.astype(jnp.float32)
    chosen = jnp.sum(logits[:, None, :] * hits_float, axis=-1)
    gate_exps = jnp.exp(chosen)
    gate_values = gate_exps / jnp.sum(gate_exps, axis=1, keepdims=True)
    flat_hits = route_hits.reshape(pairs_count, experts_all).astype(jnp.int32)
    slot_rank = jnp.sum((jnp.cumsum(flat_hits, axis=0) - flat_hits) * flat_hits, axis=1)
    slot_dest = routes.reshape(-1) * capacity + slot_rank
    slot_pair = (
        jnp.full((experts_all * capacity,), pairs_count, jnp.int32)
        .at[slot_dest]
        .set(jnp.arange(pairs_count, dtype=jnp.int32))
    )
    slot_token = jnp.where(slot_pair < pairs_count, slot_pair // TOP, sequence_length)

    def to_experts(buffer):
        arrived = lax.all_to_all(buffer, "gx", split_axis=0, concat_axis=0, tiled=True)
        return arrived.reshape(devices_gx * capacity, model_width)

    def from_experts(partial_rows):
        share_rows = lax.psum_scatter(
            partial_rows.astype(jnp.bfloat16), "gy", scatter_dimension=1, tiled=True
        )
        returned = lax.all_to_all(
            share_rows.reshape(devices_gx, capacity, part_width),
            "gx",
            split_axis=0,
            concat_axis=0,
            tiled=True,
        )
        whole_rows = lax.all_gather(returned, "gy", axis=2, tiled=True)
        return whole_rows.reshape(devices_gx * capacity, model_width)

    send_rows = jnp.take(normed_ffn, slot_token, axis=0, mode="fill", fill_value=0)
    expert_in = to_experts(send_rows.reshape(devices_gx, capacity, model_width))
    gate_in = jnp.dot(expert_in, w_gate, preferred_element_type=jnp.float32)
    up_in = jnp.dot(expert_in, w_up, preferred_element_type=jnp.float32)
    gate_sigmoid = jax.nn.sigmoid(gate_in)
    gate_swish = gate_in * gate_sigmoid
    activated = (gate_swish * up_in).astype(jnp.bfloat16)
    expert_part = jnp.dot(activated, w_down, preferred_element_type=jnp.float32)
    expert_out = from_experts(expert_part)
    pair_rows = jnp.take(expert_out, slot_dest, axis=0).reshape(sequence_length, TOP, model_width)
    mixed_rows = jnp.einsum(
        "tk,tkd->td", gate_values, pair_rows, preferred_element_type=jnp.float32
    )
    grad_out_f = cotangent.astype(jnp.float32)
    grad_gates = jnp.einsum("td,tkd->tk", grad_out_f, pair_rows, preferred_element_type=jnp.float32)
    grad_chosen = gate_values * (
        grad_gates - jnp.sum(gate_values * grad_gates, axis=1, keepdims=True)
    )
    grad_logits = jnp.sum(grad_chosen[:, :, None] * hits_float, axis=1).astype(jnp.bfloat16)
    slot_gate = jnp.take(gate_values.reshape(-1), slot_pair, mode="fill", fill_value=0.0)
    grad_send = (
        jnp.take(grad_out_f, slot_token, axis=0, mode="fill", fill_value=0) * slot_gate[:, None]
    )
    grad_expert_out = to_experts(
        grad_send.astype(jnp.bfloat16).reshape(devices_gx, capacity, model_width)
    )
    grad_act = contract(grad_expert_out, w_down, 1, 1)
    down_term = contract(activated, grad_expert_out, 0, 0)
    grad_gate_in = (
        grad_act * up_in * gate_sigmoid * (1.0 + gate_in * (1.0 - gate_sigmoid))
    ).astype(jnp.bfloat16)
    grad_up_in = (grad_act * gate_swish).astype(jnp.bfloat16)
    gate_term = contract(expert_in, grad_gate_in, 0, 0)
    up_term = contract(expert_in, grad_up_in, 0, 0)
    grad_in_part = contract(grad_gate_in, w_gate, 1, 1) + contract(grad_up_in, w_up, 1, 1)
    grad_rows = from_experts(grad_in_part)
    grad_pairs = jnp.take(grad_rows, slot_dest, axis=0).reshape(sequence_length, TOP, model_width)
    grad_rows_sum = jnp.sum(grad_pairs.astype(jnp.float32), axis=1)
    return mixed_rows, grad_rows_sum, grad_logits, (gate_term[None], up_term[None], down_term[None])


def swap_cores(rows):
    return lax.ppermute(rows, "gy", [(0, 1), (1, 0)])


def own_half(rows):
    count = rows.shape[0] // lax.axis_size("gy")
    return lax.dynamic_slice_in_dim(rows, lax.axis_index("gy") * count, count, 0)


def dense_experts(normed_ffn, logits, route_hits, cotangent, w_gate, w_up, w_down):
    sequence_length, model_width = normed_ffn.shape
    experts_all = logits.shape[1]
    gate_exps = jnp.exp(jnp.where(jnp.any(route_hits, axis=1), logits, -1e30))
    gate_all = gate_exps / jnp.sum(gate_exps, axis=1, keepdims=True)
    gate_lanes = jnp.pad(jnp.concatenate(two_parts(gate_all), axis=1), ((0, 0), (0, LANES - 2 * experts_all)))
    row_lanes = jnp.concatenate([own_half(normed_ffn), own_half(gate_lanes)], axis=1)
    weighted, grad_in, terms, gate_term, up_term, down_term = experts_products(
        row_lanes, cotangent, w_gate, w_up, w_down, experts_all, 2
    )
    back, mixed_rows = return_sums(grad_in, weighted, terms, w_gate, w_up, w_down, 3)
    term_lanes = back[:, model_width : model_width + 4 * experts_all]
    grad_gates = jnp.sum(term_lanes.reshape(sequence_length, 4, experts_all), axis=1)
    grad_logits = (
        gate_all * (grad_gates - jnp.sum(gate_all * grad_gates, axis=1, keepdims=True))
    ).astype(jnp.bfloat16)
    return mixed_rows, back[:, :model_width], grad_logits, tuple(
        term[None].astype(jnp.float32) for term in (gate_term, up_term, down_term)
    )


def turn_lanes(values, cosine, sine_table):
    return values * cosine + pltpu.roll(values, HEAD_DIM // 2, 1) * sine_table


def unit_rows(values):
    scale = lax.rsqrt(jnp.mean(values * values, axis=1, keepdims=True) + EPSILON)
    return values * scale, scale


def allowed_pairs(docs_column, docs_row):
    shape = (docs_column.shape[0], docs_row.shape[1])
    keys_at, queries_at = lax.broadcasted_iota(jnp.int32, shape, 0), lax.broadcasted_iota(jnp.int32, shape, 1)
    return (keys_at <= queries_at) & (docs_column == docs_row)


def head_span(head):
    return pl.ds(pl.multiple_of(head * HEAD_DIM, HEAD_DIM), HEAD_DIM)


def weight_copies(w_ref, w_in, w_out, w_sem, wide, last_first):
    groups = list(range(w_in.shape[1] // wide))
    if last_first:
        groups = groups[-1:] + groups[:-1]
    into = [
        (n, pltpu.make_async_copy(w_ref.at[:, pl.ds(n * wide, wide)], w_in.at[:, pl.ds(n * wide, wide)], w_sem.at[n]))
        for n in groups
    ]
    start = w_in.shape[1] + LANES
    out = [
        pltpu.make_async_copy(
            w_ref.at[:, pl.ds(start + n * wide, wide)],
            w_out.at[:, pl.ds(n * wide, wide)],
            w_sem.at[len(groups) + n],
        )
        for n in range(w_out.shape[1] // wide)
    ]
    return into, out


def dot_groups(target, left, right, begin, count, transposed, wide=256):
    def body(i, carry):
        span = pl.ds(pl.multiple_of(begin + i * wide, wide), wide)
        value = dot_nt(left[...], right[span]) if transposed else dot_nn(left[...], right[:, span])
        target[:, span] = value.astype(target.dtype)
        return carry

    lax.fori_loop(0, count // wide, body, 0)


GROUP = 512


def attend_kernel(
    q_heads, kv_heads, tokens_ref, w_ref, cosine_ref, sine_ref, docs_column, docs_row, q_gain, k_gain, attn_gain,
    normed_ref, raw_ref, attended_ref, query_ref, key_ref, value_ref, totals_ref, part_ref, w_in, w_out, w_sem,
):
    into, out = weight_copies(w_ref, w_in, w_out, w_sem, GROUP, True)
    for _, copy in into:
        copy.start()
    for copy in out:
        copy.start()

    def norm_rows(i, carry):
        span = pl.ds(pl.multiple_of(i * 16, 16), 16)
        unit, _ = unit_rows(tokens_ref[span].astype(jnp.float32))
        normed_ref[span] = (unit * attn_gain[...]).astype(jnp.bfloat16)
        return carry

    lax.fori_loop(0, tokens_ref.shape[0] // 16, norm_rows, 0)
    for n, copy in into:
        copy.wait()
        dot_groups(raw_ref, normed_ref, w_in, n * GROUP, GROUP, False)
    cosine, sine_table = cosine_ref[...], sine_ref[...]
    allowed = allowed_pairs(docs_column[...], docs_row[...])
    group, inv_root = q_heads // kv_heads, 1.0 / math.sqrt(HEAD_DIM)
    for kv in range(kv_heads):
        unit, _ = unit_rows(raw_ref[:, head_span(q_heads + kv)])
        key_rows = turn_lanes(unit * k_gain[...], cosine, sine_table).astype(jnp.bfloat16)
        value_rows = raw_ref[:, head_span(q_heads + kv_heads + kv)]
        key_ref[:, head_span(kv)] = key_rows
        value_ref[:, head_span(kv)] = value_rows.astype(jnp.bfloat16)
        value_columns = value_rows.T.astype(jnp.bfloat16)

        def body(index, carry, kv=kv, key_rows=key_rows, value_columns=value_columns):
            head = kv * group + index
            unit, _ = unit_rows(raw_ref[:, head_span(head)])
            query_rows = turn_lanes(unit * q_gain[...], cosine, sine_table).astype(jnp.bfloat16)
            query_ref[:, head_span(head)] = query_rows
            scores = jnp.where(allowed, dot_nt(key_rows, query_rows) * inv_root, -1e30)
            peak = jnp.max(scores, axis=0, keepdims=True)
            exps = jnp.exp(scores - peak)
            total = jnp.sum(exps, axis=0, keepdims=True)
            totals_ref[pl.ds(head, 1), :] = peak + jnp.log(total)
            probs = (exps / total).astype(jnp.bfloat16)
            attended_ref[:, head_span(head)] = dot_nn(value_columns, probs).T.astype(jnp.bfloat16)
            return carry

        lax.fori_loop(0, group, body, 0, unroll=4)
    for copy in out:
        copy.wait()
    dot_groups(part_ref, attended_ref, w_out, 0, w_out.shape[0], True)


def attend_back_kernel(
    q_heads, kv_heads, grad_attn_ref, w_ref, cosine_ref, sine_ref, docs_column, docs_row, q_gain, k_gain,
    raw_ref, query_ref, key_ref, value_ref, totals_ref,
    grad_raw_ref, gains_ref, part_ref, grad_ref, sums_ref, w_in, w_out, w_sem,
):
    into, out = weight_copies(w_ref, w_in, w_out, w_sem, GROUP, False)
    for copy in out:
        copy.start()
    for _, copy in into:
        copy.start()
    for n, copy in enumerate(out):
        copy.wait()
        dot_groups(grad_ref, grad_attn_ref, w_out, n * GROUP, GROUP, False)
    cosine, sine_table = cosine_ref[...], sine_ref[...]
    allowed = allowed_pairs(docs_column[...], docs_row[...])
    group, inv_root = q_heads // kv_heads, 1.0 / math.sqrt(HEAD_DIM)
    gains_ref[...] = jnp.zeros_like(gains_ref)

    def back_to_raw(grad, head, gain, gain_row):
        grad = turn_lanes(grad, cosine, -sine_table)
        unit, scale = unit_rows(raw_ref[:, head_span(head)])
        gains_ref[pl.ds(gain_row, 1), :] += jnp.sum(grad * unit, axis=0, keepdims=True)
        grad = grad * gain
        grad = scale * (grad - unit * jnp.mean(grad * unit, axis=1, keepdims=True))
        grad_raw_ref[:, head_span(head)] = grad.astype(jnp.bfloat16)

    for kv in range(kv_heads):
        key_rows, value_rows = key_ref[:, head_span(kv)], value_ref[:, head_span(kv)]
        key_columns = key_rows.astype(jnp.float32).T.astype(jnp.bfloat16)
        sums_ref[...] = jnp.zeros_like(sums_ref)

        def body(index, carry, kv=kv, key_rows=key_rows, value_rows=value_rows, key_columns=key_columns):
            head = kv * group + index
            query_rows, grad_rows = query_ref[:, head_span(head)], grad_ref[:, head_span(head)]
            scores = jnp.where(allowed, dot_nt(key_rows, query_rows) * inv_root, -1e30)
            probs = jnp.exp(scores - totals_ref[pl.ds(head, 1), :])
            sums_ref[0] += dot_nn(probs.astype(jnp.bfloat16), grad_rows)
            grad_probs = dot_nt(value_rows, grad_rows)
            inner = jnp.sum(probs * grad_probs, axis=0, keepdims=True)
            grad_scores = (probs * (grad_probs - inner)).astype(jnp.bfloat16)
            sums_ref[1] += dot_nn(grad_scores, query_rows)
            grad_queries = dot_nn(key_columns, grad_scores).T * inv_root
            back_to_raw(grad_queries, head, q_gain[...], 0)
            return carry

        lax.fori_loop(0, group, body, 0, unroll=4)
        back_to_raw(sums_ref[1] * inv_root, q_heads + kv, k_gain[...], 1)
        grad_raw_ref[:, head_span(q_heads + kv_heads + kv)] = sums_ref[0].astype(jnp.bfloat16)
    for _, copy in into:
        copy.wait()
    dot_groups(part_ref, grad_raw_ref, w_in, 0, w_in.shape[0], True)


def attention_shared(weights_all, doc_ids, query_norm_gain, k_gain):
    length = doc_ids.shape[1]
    cosine, sine_table = rotary_tables(length, HEAD_DIM)
    cosine, sine_table = cosine[:, 0], sine_table[:, 0]
    return (
        weights_all,
        jnp.concatenate([cosine, cosine], axis=1),
        jnp.concatenate([-sine_table, sine_table], axis=1),
        doc_ids.reshape(length, 1),
        doc_ids.reshape(1, length),
        query_norm_gain.reshape(1, HEAD_DIM),
        k_gain.reshape(1, HEAD_DIM),
    )


def attention_specs(q_heads, kv_heads, features, inputs):
    vmem, everywhere = pl.BlockSpec(memory_space=pltpu.VMEM), pl.BlockSpec(memory_space=pl.ANY)
    wide, out_wide = (q_heads + 2 * kv_heads) * HEAD_DIM, q_heads * HEAD_DIM
    scratch = [
        pltpu.VMEM((features, wide), jnp.bfloat16),
        pltpu.VMEM((features, out_wide), jnp.bfloat16),
        pltpu.SemaphoreType.DMA(((wide + out_wide) // GROUP,)),
    ]
    return [vmem, everywhere] + [vmem] * (inputs - 2), scratch


def attend(tokens, attn_gain, shared, q_heads, kv_heads):
    (length, features), low, shape = tokens.shape, jnp.bfloat16, jax.ShapeDtypeStruct
    in_specs, scratch = attention_specs(q_heads, kv_heads, features, 2 + len(shared))
    return pl.pallas_call(
        functools.partial(attend_kernel, q_heads, kv_heads),
        out_shape=[
            shape((length, features), low),
            shape((length, (q_heads + 2 * kv_heads) * HEAD_DIM), jnp.float32),
            shape((length, q_heads * HEAD_DIM), low),
            shape((length, q_heads * HEAD_DIM), low),
            shape((length, kv_heads * HEAD_DIM), low),
            shape((length, kv_heads * HEAD_DIM), low),
            shape((q_heads, length), jnp.float32),
            shape((length, features), jnp.float32),
        ],
        in_specs=in_specs,
        scratch_shapes=scratch,
        compiler_params=pltpu.CompilerParams(vmem_limit_bytes=48 * 1024 * 1024),
    )(tokens, *shared, attn_gain.reshape(1, features))


def attend_back(grad_attn, shared, kept, q_heads, kv_heads):
    (length, features), shape = grad_attn.shape, jax.ShapeDtypeStruct
    in_specs, scratch = attention_specs(q_heads, kv_heads, features, 1 + len(shared) + len(kept))
    return pl.pallas_call(
        functools.partial(attend_back_kernel, q_heads, kv_heads),
        out_shape=[
            shape((length, (q_heads + 2 * kv_heads) * HEAD_DIM), jnp.bfloat16),
            shape((8, HEAD_DIM), jnp.float32),
            shape((length, features), jnp.float32),
        ],
        in_specs=in_specs,
        scratch_shapes=[
            pltpu.VMEM((length, q_heads * HEAD_DIM), jnp.bfloat16),
            pltpu.VMEM((2, length, HEAD_DIM), jnp.float32),
            *scratch,
        ],
        compiler_params=pltpu.CompilerParams(vmem_limit_bytes=48 * 1024 * 1024),
    )(grad_attn, *shared, *kept)


def on_device(
    tokens_in,
    doc_ids,
    routes,
    q_weight,
    key_matrix,
    value_matrix,
    out_weight,
    router_weight,
    attn_gain,
    ffn_gain,
    query_norm_gain,
    k_gain,
    gate_weight,
    up_weight,
    down_weight,
    cotangent,
):
    sequence_length = tokens_in.shape[0]
    model_width = tokens_in.shape[1]
    devices_gx = lax.axis_size("gx")
    devices_gy = lax.axis_size("gy")
    part_width = model_width // devices_gy
    experts_all = router_weight.shape[1]
    router_lanes = jnp.pad(router_weight, ((0, 0), (0, LANES - experts_all)))
    pieces = [q_weight, key_matrix, value_matrix, router_lanes, out_weight]
    dense = kernels_fit() and experts_all <= 2 * TOP
    if dense:
        weights_all = gather_blocks(pieces, 1)
        weights_all = weights_all.reshape(-1, weights_all.shape[2])
    else:
        weights_all = lax.all_gather(jnp.concatenate(pieces, axis=1), "gx", axis=0, tiled=True)
    q_width, kv_width = q_weight.shape[1], key_matrix.shape[1]
    qkv_width = q_width + 2 * kv_width
    router_full = weights_all[:, qkv_width : qkv_width + experts_all]
    heads_local = q_width // HEAD_DIM
    kv_local = kv_width // HEAD_DIM
    inputs_f = tokens_in.astype(jnp.float32)
    scale_one = root_mean_scale(inputs_f)
    unit_one = inputs_f * scale_one
    shared = attention_shared(weights_all, doc_ids, query_norm_gain, k_gain)
    normalized_input, raw_rows, attended, *kept, attn_part = attend(
        tokens_in, attn_gain, shared, heads_local, kv_local
    )
    attn_total = attn_part + swap_cores(attn_part)
    residual = inputs_f + attn_total
    scale_two = root_mean_scale(residual)
    unit_two = residual * scale_two
    normed_ffn = (unit_two * ffn_gain).astype(jnp.bfloat16)
    logits = jnp.dot(normed_ffn, router_full, preferred_element_type=jnp.float32)
    expert_iota = jnp.arange(experts_all, dtype=jnp.int32)
    route_hits = routes[:, :, None] == expert_iota
    if dense:
        mixed_rows, grad_rows_sum, grad_logits, expert_grads = dense_experts(
            normed_ffn, logits, route_hits, cotangent, gate_weight[0], up_weight[0], down_weight[0]
        )
    else:
        mixed_rows, grad_rows_sum, grad_logits, expert_grads = sparse_experts(
            normed_ffn, logits, route_hits, routes, cotangent, gate_weight[0], up_weight[0], down_weight[0]
        )
    output = (residual + mixed_rows).astype(jnp.bfloat16)
    grad_out_f = cotangent.astype(jnp.float32)
    logit_lanes = jnp.pad(grad_logits, ((0, 0), (0, LANES - experts_all)))
    router_lanes = contract(normed_ffn, logit_lanes, 0, 0)
    grad_ffn_in = contract(grad_logits, router_full, 1, 1) + grad_rows_sum
    ffn_gain_term = jnp.sum(grad_ffn_in * unit_two, axis=0)
    grad_residual = grad_out_f + norm_back(grad_ffn_in * ffn_gain, unit_two, scale_two)
    grad_attn = grad_residual.astype(jnp.bfloat16)
    grad_qkv, head_gains, grad_normed_part = attend_back(
        grad_attn, shared, (raw_rows, *kept), heads_local, kv_local
    )
    q_gain_term, k_gain_term = head_gains[0], head_gains[1]
    grad_normed = grad_normed_part + swap_cores(grad_normed_part)
    attn_gain_term = jnp.sum(grad_normed * unit_one, axis=0)
    own_mask = (jnp.arange(model_width) // part_width == lax.axis_index("gy")).astype(jnp.float32)
    gains = (attn_gain_term * own_mask, ffn_gain_term * own_mask, q_gain_term, k_gain_term)
    if dense:
        router_blocks = router_lanes.astype(jnp.bfloat16).reshape(devices_gx, -1, LANES)
        factors = (normalized_input, grad_qkv, router_blocks, grad_attn, attended)
        lasts = (tokens_in, grad_residual, grad_normed, attn_gain.reshape(1, model_width))
        grad_q, grad_k, grad_v, grad_router, grad_out, gain_rows, grad_input = scatter_sums(
            factors, packed_gains(gains), lasts, kv_width, 4
        )
        gains = unpacked_gains(gain_rows, gains)
    else:
        sums = jnp.concatenate(
            [
                lax.psum_scatter(term, "gx", scatter_dimension=0, tiled=True)
                for term in (
                    contract(normalized_input, grad_qkv, 0, 0),
                    router_lanes,
                    contract(grad_attn, attended, 0, 0),
                )
            ],
            axis=1,
        )
        gains = lax.psum(gains, ("gx", "gy"))
        grad_q = sums[:, :q_width]
        grad_k = sums[:, q_width : q_width + kv_width]
        grad_v = sums[:, q_width + kv_width : qkv_width]
        grad_router = sums[:, qkv_width : qkv_width + LANES]
        grad_out = sums[:, qkv_width + LANES :]
        grad_input = grad_residual + norm_back(grad_normed * attn_gain, unit_one, scale_one)
        grad_input = grad_input.astype(jnp.bfloat16)
    gain_attn, gain_ffn, gain_query, gain_key = gains
    grad_router = grad_router[:, :experts_all]
    return (
        output,
        grad_input,
        grad_q,
        grad_k,
        grad_v,
        grad_out,
        grad_router,
        gain_attn,
        gain_ffn,
        gain_query,
        gain_key,
        expert_grads[0],
        expert_grads[1],
        expert_grads[2],
    )


def solution(mesh):
    return jax.shard_map(
        on_device,
        mesh=mesh,
        in_specs=(
            P("gx", None),
            P("gx", None),
            P("gx", None),
            P("gx", "gy"),
            P("gx", "gy"),
            P("gx", "gy"),
            P("gx", "gy"),
            P("gx", None),
            P(),
            P(),
            P(),
            P(),
            P("gx", None, "gy"),
            P("gx", None, "gy"),
            P("gx", "gy", None),
            P("gx", None),
        ),
        out_specs=(
            P("gx", None),
            P("gx", None),
            P("gx", "gy"),
            P("gx", "gy"),
            P("gx", "gy"),
            P("gx", "gy"),
            P("gx", None),
            P(),
            P(),
            P(),
            P(),
            P("gx", None, "gy"),
            P("gx", None, "gy"),
            P("gx", "gy", None),
        ),
        check_vma=False,
    )
```
